32 devices in a mesh: ctx: 8 (over z, y), wshard: 4 (over x, core).
Axes of the slice: x: 2, y: 2, z: 4, core: 2. Of those that a mesh axis runs over, the one named last changes fastest.
Arguments:
- inputs: bfloat16 [4, 1024, 2048], P('wshard', 'ctx'), may hold values from -6 to 6
- cotangent: bfloat16 [4, 1024, 2048], P('wshard', 'ctx'), may hold values from -14 to 14
- w_in: float32 [2048, 8240], P(('ctx', 'wshard')), may hold values from -0.2762136 to 0.2762136
- w_in_m: float32 [2048, 8240], P(('ctx', 'wshard')), may hold values from -12 to 12
- w_in_v: float32 [2048, 8240], P(('ctx', 'wshard')), may hold values from 19.2512 to 77.824
- w_mix: float32 [4096, 2048], P(('ctx', 'wshard')), may hold values from -0.390625 to 0.390625
- w_mix_m: float32 [4096, 2048], P(('ctx', 'wshard')), may hold values from -32 to 32
- w_mix_v: float32 [4096, 2048], P(('ctx', 'wshard')), may hold values from 106.496 to 421.888
- w_up: float32 [2048, 8192], P(('ctx', 'wshard')), may hold values from -0.125 to 0.125
- w_up_m: float32 [2048, 8192], P(('ctx', 'wshard')), may hold values from -20 to 20
- w_up_v: float32 [2048, 8192], P(('ctx', 'wshard')), may hold values from 53.248 to 217.088
- w_down: float32 [4096, 2048], P(('ctx', 'wshard')), may hold values from -0.09375 to 0.09375
- w_down_m: float32 [4096, 2048], P(('ctx', 'wshard')), may hold values from -20 to 20
- w_down_v: float32 [4096, 2048], P(('ctx', 'wshard')), may hold values from 53.248 to 217.088
- vectors: float32 [25232], replicated, may hold values from -12 to 2.5
- vectors_m: float32 [25232], replicated, may hold values from -40 to 40
- vectors_v: float32 [25232], replicated, may hold values from 217.088 to 860.16
Outputs:
- outputs: bfloat16 [4, 1024, 2048], P('wshard', 'ctx')
- input_grad: float32 [4, 1024, 2048], P('wshard', 'ctx')
- new_w_in: float32 [2048, 8240], P(('ctx', 'wshard'))
- new_w_in_m: float32 [2048, 8240], P(('ctx', 'wshard'))
- new_w_in_v: float32 [2048, 8240], P(('ctx', 'wshard'))
- new_w_mix: float32 [4096, 2048], P(('ctx', 'wshard'))
- new_w_mix_m: float32 [4096, 2048], P(('ctx', 'wshard'))
- new_w_mix_v: float32 [4096, 2048], P(('ctx', 'wshard'))
- new_w_up: float32 [2048, 8192], P(('ctx', 'wshard'))
- new_w_up_m: float32 [2048, 8192], P(('ctx', 'wshard'))
- new_w_up_v: float32 [2048, 8192], P(('ctx', 'wshard'))
- new_w_down: float32 [4096, 2048], P(('ctx', 'wshard'))
- new_w_down_m: float32 [4096, 2048], P(('ctx', 'wshard'))
- new_w_down_v: float32 [4096, 2048], P(('ctx', 'wshard'))
- new_vectors: float32 [25232], replicated
- new_vectors_m: float32 [25232], replicated
- new_vectors_v: float32 [25232], replicated
The draws below stay inside these ranges and needn't reach their ends.
All inputs are finite; a program needn't handle non-finite values.
Results may differ from the reference program's by a relative error of at most 0.02.
The reference program's roundings to bfloat16 on the way count: a program that leaves them out, or rounds other values in their place, can miss the bound.
Values may be sent and summed in bfloat16 or wider, within the bound.
A program may use at most 640 MiB of HBM per device.

```python
import math
import jax
import jax.numpy as jnp
from jax import lax

D = 2048
FF = 4096
AH = 8
KVH = 2
HD = 128
MH = 48
MP = 64
NS = 256
CONV = 4
TOK_DEV = 128
STEP = 10
DSSM = 3072
CONVCH = 3584
PROJ = 8240
MIXIN = 4096
NV = 25232
LEN = 1024
SEQS = 4
TOKENS = 4096


def draw_cotangent(key, part):
    key = jax.random.fold_in(key, 11)
    noise = jnp.clip(jax.random.normal(key, (SEQS, LEN, D), jnp.float32), -6.0, 6.0)
    low_end = 0.6
    ratio = 3.0
    flat = (jnp.arange(SEQS)[:, None] * LEN + jnp.arange(LEN)[None, :]).astype(jnp.float32)
    place = flat / max(TOKENS - 1, 1)
    scale = low_end * jnp.exp(place * math.log(ratio))
    return (noise * scale[:, :, None]).astype(jnp.bfloat16)


def draw_w_in(key, part):
    key = jax.random.fold_in(key, 3)
    noise = jnp.clip(jax.random.normal(key, (D, PROJ), jnp.float32), -5.0, 5.0)
    columns = jnp.arange(PROJ)
    factor = jnp.where(columns < AH * HD + KVH * HD, 1.6, 1.0)
    factor = jnp.where(columns >= PROJ - MH, 2.5, factor) / math.sqrt(D)
    return noise * factor[None, :]


def draw_w_mix(key, part):
    key = jax.random.fold_in(key, 5)
    noise = jnp.clip(jax.random.normal(key, (MIXIN, D), jnp.float32), -5.0, 5.0)
    places = jnp.arange(MIXIN)
    factor = jnp.where(places < AH * HD, 2.5 / math.sqrt(AH * HD), 1.0 / math.sqrt(DSSM))
    return noise * factor[:, None]


def rising(count):
    return 0.6 * jnp.exp(jnp.arange(count, dtype=jnp.float32) / max(count - 1, 1) * math.log(3.0))


def draw_vectors(key, part):
    key = jax.random.fold_in(key, 7)
    streams = jax.random.split(key, 8)
    noise = jax.random.uniform(streams[0], (2 * D + DSSM,), jnp.float32, 0.8, 1.25)
    gains = noise * jnp.concatenate([rising(D), rising(D), rising(DSSM)])
    conv_bias = jax.random.uniform(streams[1], (CONVCH,), jnp.float32, -0.5, 0.5)
    conv_weight = jnp.clip(jax.random.normal(streams[2], (CONV * CONVCH,), jnp.float32), -5.0, 5.0) * 0.5
    slow_share = 0.55
    chosen = jax.random.uniform(streams[3], (MH,), jnp.float32) < slow_share
    slow = jax.random.uniform(streams[4], (MH,), jnp.float32, math.log(0.8 / LEN), math.log(2.0 / LEN))
    fast = jax.random.uniform(streams[5], (MH,), jnp.float32, math.log(0.03), math.log(0.12))
    a_log = jnp.where(chosen, slow, fast)
    dt_bias = jax.random.uniform(streams[6], (MH,), jnp.float32, -2.0, 0.0)
    d_skip = jax.random.uniform(streams[7], (MH,), jnp.float32, 0.5, 1.5)
    return jnp.concatenate([gains, conv_bias, conv_weight, a_log, dt_bias, d_skip])


def level_of(stream_key, shape, shards, smallest, largest):
    def one(axis_at, parts):
        draws = jax.random.uniform(jax.random.fold_in(jax.random.fold_in(stream_key, 6), axis_at), (parts,), jnp.float32, smallest / len(shards), largest / len(shards))
        return jnp.repeat(jnp.exp(draws), shape[axis_at] // parts).reshape((-1,) + (1,) * (len(shape) - axis_at - 1))

    level = one(*shards[0])
    for cut in shards[1:]:
        level = level * one(*cut)
    return level


def bell_draw(key, shape, scale, reach, cuts=(), kind=jnp.bfloat16):
    level = level_of(key, shape, cuts, -0.22, 0.18) if cuts else 1.0
    values = jax.random.normal(key, shape, jnp.float32) * scale * level
    return jnp.minimum(jnp.maximum(values, -reach), reach).astype(kind)


def setup_inputs(seed: int = 0) -> dict:
    key_list = jax.random.split(jax.random.key(seed), 18)
    return {
        "inputs": bell_draw(key_list[0], (SEQS, LEN, D), 1.0, 6.0, ((0, 4), (1, 8))),
        "cotangent": draw_cotangent(jax.random.fold_in(key_list[17], 71), 0),
        "w_in": draw_w_in(jax.random.fold_in(key_list[17], 71), 0),
        "w_in_m": bell_draw(key_list[3], (D, PROJ), (0.033 * TOKENS ** 0.5), 12.0, ((0, 32),), jnp.float32),
        "w_in_v": jnp.clip(jnp.exp(math.log(77.824) - 1.3968765 * jax.random.uniform(key_list[4], (D, PROJ), jnp.float32) ** level_of(key_list[4], (D, PROJ), ((0, 32),), -0.2, 0.2)), 19.2512, 77.824),
        "w_mix": draw_w_mix(jax.random.fold_in(key_list[17], 71), 0),
        "w_mix_m": bell_draw(key_list[6], (MIXIN, D), (0.077 * TOKENS ** 0.5), 32.0, ((0, 32),), jnp.float32),
        "w_mix_v": jnp.clip(jnp.exp(math.log(421.888) - 1.3766324 * jax.random.uniform(key_list[7], (MIXIN, D), jnp.float32) ** level_of(key_list[7], (MIXIN, D), ((0, 32),), -0.2, 0.2)), 106.496, 421.888),
        "w_up": bell_draw(key_list[8], (D, 2 * FF), D ** -0.5, 0.125, ((0, 32),), jnp.float32),
        "w_up_m": bell_draw(key_list[9], (D, 2 * FF), (0.055 * TOKENS ** 0.5), 20.0, ((0, 32),), jnp.float32),
        "w_up_v": jnp.clip(jnp.exp(math.log(217.088) - 1.40534252 * jax.random.uniform(key_list[10], (D, 2 * FF), jnp.float32) ** level_of(key_list[10], (D, 2 * FF), ((0, 32),), -0.2, 0.2)), 53.248, 217.088),
        "w_down": bell_draw(key_list[11], (FF, D), FF ** -0.5, 0.09375, ((0, 32),), jnp.float32),
        "w_down_m": bell_draw(key_list[12], (FF, D), (0.055 * TOKENS ** 0.5), 20.0, ((0, 32),), jnp.float32),
        "w_down_v": jnp.clip(jnp.exp(math.log(217.088) - 1.40534252 * jax.random.uniform(key_list[13], (FF, D), jnp.float32) ** level_of(key_list[13], (FF, D), ((0, 32),), -0.2, 0.2)), 53.248, 217.088),
        "vectors": draw_vectors(jax.random.fold_in(key_list[17], 71), 0),
        "vectors_m": bell_draw(key_list[15], (NV,), (0.11 * TOKENS ** 0.5), 40.0, (), jnp.float32),
        "vectors_v": jnp.clip(jnp.exp(jax.random.uniform(key_list[16], (NV,), jnp.float32, math.log(217.088), math.log(860.16))), 217.088, 860.16),
    }


@jax.custom_vjp
def low(v):
    return lax.optimization_barrier(v.astype(jnp.bfloat16)).astype(jnp.float32)

@jax.custom_vjp
def low_back(v):
    return v

def low_keep(v):
    return (low(v), None)

def low_pass(kept, grad):
    return (grad,)

def back_keep(v):
    return (v, None)

def back_low(kept, grad):
    return (low(grad),)
low.defvjp(low_keep, low_pass)
low_back.defvjp(back_keep, back_low)
norm_eps = 1e-05
rope_base = 10000.0
beta_one = 0.9
beta_two = 0.95
adam_eps = 1e-08
decay_weight = 0.1
vector_rate = 0.5
masked_score = -1e+30

def product(left, right):
    return jnp.dot(left, right, precision=lax.Precision.HIGHEST, preferred_element_type=jnp.float32)

def rms_norm(values, gain):
    factor = lax.rsqrt(lax.optimization_barrier(jnp.mean(values * values, axis=-1, keepdims=True)) + norm_eps)
    return values * factor * gain

def rotate(values, positions):
    halfway = values.shape[-1] // 2
    frequency = rope_base ** (-jnp.arange(halfway, dtype=jnp.float32) / halfway)
    angles = positions[:, None] * frequency[None, :]
    cosine = jnp.cos(angles)[:, None, :]
    sine = jnp.sin(angles)[:, None, :]
    first = values[..., :halfway]
    second = values[..., halfway:]
    return jnp.concatenate([first * cosine - second * sine, second * cosine + first * sine], axis=-1)

def split_vectors(vectors):
    extents = (D, D, DSSM, CONVCH, CONV * CONVCH, MH, MH, MH)
    pieces = []
    offset = 0
    for extent in extents:
        pieces.append(lax.slice_in_dim(vectors, offset, offset + extent))
        offset = offset + extent
    pieces[4] = pieces[4].reshape(CONV, CONVCH)
    return pieces

def convolve(extended, conv_weight, conv_bias):
    row_count = extended.shape[0] - CONV + 1
    summed = conv_bias[None, :] + jnp.zeros((row_count, CONVCH), jnp.float32)
    for offset in range(CONV):
        summed = summed + conv_weight[offset][None, :] * extended[offset:offset + row_count]
    return jax.nn.silu(summed)

def cumulate(steps, a_log):
    return jnp.cumsum(-steps * jnp.exp(a_log)[None, :], axis=0)

def block_state(inputs_x, inputs_b, steps, cumul):
    tail = jnp.exp(cumul[-1][None, :] - cumul)
    weighted = inputs_x * (steps * tail)[:, :, None]
    local = jnp.einsum('shp,sn->hpn', weighted, inputs_b, precision=lax.Precision.HIGHEST)
    return (jnp.exp(cumul[-1]), local)

def block_output(inputs_x, inputs_b, inputs_c, steps, cumul, incoming, d_skip):
    row_count = steps.shape[0]
    places = jnp.arange(row_count)
    causal = (places[:, None] >= places[None, :])[:, :, None]
    gaps = jnp.where(causal, cumul[:, None, :] - cumul[None, :, :], 0.0)
    decay = jnp.where(causal, jnp.exp(gaps), 0.0)
    inner = product(inputs_c, inputs_b.T)
    weighted = inputs_x * steps[:, :, None]
    intra = jnp.einsum('tsh,shp->thp', decay * inner[:, :, None], weighted, precision=lax.Precision.HIGHEST)
    carried = jnp.einsum('tn,hpn->thp', inputs_c, incoming, precision=lax.Precision.HIGHEST) * jnp.exp(cumul)[:, :, None]
    return intra + carried + d_skip[None, :, None] * inputs_x

def gate_norm(ssd_out, z_raw, gain_ssm):
    row_count = ssd_out.shape[0]
    gated = ssd_out.reshape(row_count, DSSM) * jax.nn.silu(z_raw)
    return rms_norm(gated, gain_ssm)

def attention(queries, keys, values):
    length = queries.shape[0]
    per_group = AH // KVH
    block_rows = math.gcd(512, length)
    block_count = length // block_rows
    stacked = queries.reshape(block_count, block_rows, KVH, per_group, HD)
    key_pos = jnp.arange(length)
    score_scale = 1.0 / math.sqrt(HD)

    def one_block(item):
        block, index = item
        scores = low_back(jnp.einsum('qkgd,skd->kgqs', block, keys, precision=lax.Precision.HIGHEST) * score_scale)
        query_pos = index * block_rows + jnp.arange(block_rows)
        allowed = key_pos[None, :] <= query_pos[:, None]
        scores = jnp.where(allowed, scores, masked_score)
        highest = lax.optimization_barrier(jnp.max(scores, axis=-1, keepdims=True))
        weights = jnp.exp(scores - highest)
        probs = low(weights / lax.optimization_barrier(jnp.sum(weights, axis=-1, keepdims=True)))
        return jnp.einsum('kgqs,skd->qkgd', probs, values, precision=lax.Precision.HIGHEST)
    result = lax.map(jax.checkpoint(one_block), (stacked, jnp.arange(block_count)))
    return result.reshape(length, AH * HD)

def layer(source, w_in, w_mix, w_up, w_down, vectors):
    gain_attn, gain_ffn, gain_ssm, conv_bias, conv_weight, a_log, dt_bias, d_skip = split_vectors(vectors)
    length = source.shape[0]
    normed = low(rms_norm(source, gain_attn))
    projected = low_back(product(normed, low(w_in)))
    edge_one = AH * HD
    edge_two = edge_one + KVH * HD
    edge_three = edge_two + KVH * HD
    edge_four = edge_three + DSSM
    edge_five = edge_four + CONVCH
    q_raw = projected[:, :edge_one].reshape(length, AH, HD)
    k_raw = projected[:, edge_one:edge_two].reshape(length, KVH, HD)
    v_raw = projected[:, edge_two:edge_three].reshape(length, KVH, HD)
    z_raw = projected[:, edge_three:edge_four]
    xbc_raw = projected[:, edge_four:edge_five]
    dt_raw = projected[:, edge_five:]
    positions = jnp.arange(length).astype(jnp.float32)
    queries = low(rotate(q_raw, positions))
    keys = low(rotate(k_raw, positions))
    values = low(v_raw)
    attended = low(low_back(attention(queries, keys, values)))
    extended = jnp.concatenate([jnp.zeros((CONV - 1, CONVCH), jnp.float32), xbc_raw], axis=0)
    post = convolve(extended, conv_weight, conv_bias)
    steps = jax.nn.softplus(dt_raw + dt_bias)
    block_count = length // TOK_DEV
    blocks = (post[:, :DSSM].reshape(block_count, TOK_DEV, MH, MP), post[:, DSSM:DSSM + NS].reshape(block_count, TOK_DEV, NS), post[:, DSSM + NS:].reshape(block_count, TOK_DEV, NS), steps.reshape(block_count, TOK_DEV, MH))

    def ssd_step(state, block):
        inputs_x, inputs_b, inputs_c, block_steps = block
        cumul = cumulate(block_steps, a_log)
        produced = block_output(inputs_x, inputs_b, inputs_c, block_steps, cumul, state, d_skip)
        decay_total, local = block_state(inputs_x, inputs_b, block_steps, cumul)
        return (decay_total[:, None, None] * state + local, produced)
    ssd_blocks = lax.scan(jax.checkpoint(ssd_step), jnp.zeros((MH, MP, NS), jnp.float32), blocks)[1]
    mixed = low(low_back(gate_norm(ssd_blocks.reshape(length, MH, MP), z_raw, gain_ssm)))
    branch = low_back(product(jnp.concatenate([attended, mixed], axis=1), low(w_mix)))
    middle = source + branch
    normed_two = low(rms_norm(middle, gain_ffn))
    gate_up = low_back(product(normed_two, low(w_up)))
    activated = low(jax.nn.silu(gate_up[:, :FF]) * gate_up[:, FF:])
    return middle + product(activated, low(w_down))

def adamw(weight, moment, second, grad, rate, decay):
    moment = beta_one * moment + (1.0 - beta_one) * grad
    second = beta_two * second + (1.0 - beta_two) * grad * grad
    corrected = moment / (1.0 - beta_one ** STEP)
    divisor = jnp.sqrt(second / (1.0 - beta_two ** STEP)) + adam_eps
    return (weight - rate * (corrected / divisor + decay * weight), moment, second)

def reference(inputs, cotangent, w_in, w_in_m, w_in_v, w_mix, w_mix_m, w_mix_v, w_up, w_up_m, w_up_v, w_down, w_down_m, w_down_v, vectors, vectors_m, vectors_v):
    params = (w_in, w_mix, w_up, w_down, vectors)

    def per_sequence(summed, pair):
        source, upstream = pair
        result, pullback = jax.vjp(layer, source.astype(jnp.float32), w_in, w_mix, w_up, w_down, vectors)
        grads = pullback(upstream.astype(jnp.float32))
        summed = tuple((earlier + fresh for earlier, fresh in zip(summed, grads[1:])))
        return (summed, (result.astype(jnp.bfloat16), grads[0]))
    zeros = tuple((jnp.zeros_like(param) for param in params))
    summed, produced = lax.scan(per_sequence, zeros, (inputs, cotangent))
    outputs, input_grad = produced
    new_in = adamw(w_in, w_in_m, w_in_v, summed[0], 2.0 * D ** (-0.5), decay_weight)
    new_mix = adamw(w_mix, w_mix_m, w_mix_v, summed[1], DSSM ** (-0.5), decay_weight)
    new_up = adamw(w_up, w_up_m, w_up_v, summed[2], D ** (-0.5), decay_weight)
    new_down = adamw(w_down, w_down_m, w_down_v, summed[3], FF ** (-0.5), decay_weight)
    new_vec = adamw(vectors, vectors_m, vectors_v, summed[4], vector_rate, 0.0)
    return (outputs, input_grad, new_in[0], new_in[1], new_in[2], new_mix[0], new_mix[1], new_mix[2], new_up[0], new_up[1], new_up[2], new_down[0], new_down[1], new_down[2], new_vec[0], new_vec[1], new_vec[2])
```

```python
import functools
import math

import jax
import jax.numpy as jnp
from jax import lax
from jax.sharding import PartitionSpec as P

D = 2048
FF = 4096
AH = 8
KVH = 2
HD = 128
MH = 48
MP = 64
NS = 256
CONV = 4
STEP = 10
DSSM = 3072
CONVCH = 3584
ATT = AH * HD
MIXIN = ATT + DSSM
GROUP = AH // KVH
CHUNK = 128
PAD = 128


norm_eps = 1e-05
rope_base = 10000.0
beta_one = 0.9
beta_two = 0.95
adam_eps = 1e-08
decay_weight = 0.1
vector_rate = 0.5
masked_score = -1e30

K_AT = ATT
V_AT = K_AT + KVH * HD
Z_AT = V_AT + KVH * HD
X_AT = Z_AT + DSSM
BC_AT = X_AT + DSSM
DT_AT = BC_AT + 2 * NS
END = DT_AT + MH


def rows_by_rows(left, right):
    return lax.dot_general(
        left, right, (((0,), (0,)), ((), ())), preferred_element_type=jnp.float32
    )


def cols_by_cols(left, right):
    return lax.dot_general(
        left, right, (((1,), (1,)), ((), ())), preferred_element_type=jnp.float32
    )


def plain(left, right):
    return jnp.dot(left, right, preferred_element_type=jnp.float32)


def high(subscripts, *operands):
    return jnp.einsum(subscripts, *operands, precision=lax.Precision.HIGHEST)


def rms_norm(values, gain):
    factor = lax.rsqrt(jnp.mean(values * values, axis=-1, keepdims=True) + norm_eps)
    return values * factor * gain


def rotate(values, positions):
    halfway = values.shape[-1] // 2
    frequency = rope_base ** (-jnp.arange(halfway, dtype=jnp.float32) / halfway)
    angles = positions[:, None] * frequency[None, :]
    cosine = jnp.cos(angles)[:, None, :]
    sine = jnp.sin(angles)[:, None, :]
    first = values[..., :halfway]
    second = values[..., halfway:]
    return jnp.concatenate(
        [first * cosine - second * sine, second * cosine + first * sine], axis=-1
    )


def split_vectors(vectors):
    extents = (D, D, DSSM, CONVCH, CONV * CONVCH, MH, MH, MH)
    pieces = []
    offset = 0
    for extent in extents:
        pieces.append(lax.slice_in_dim(vectors, offset, offset + extent))
        offset = offset + extent
    pieces[4] = pieces[4].reshape(CONV, CONVCH)
    return pieces


def adamw(weight, moment, second, grad, rate, decay):
    moment = beta_one * moment + (1.0 - beta_one) * grad
    second = beta_two * second + (1.0 - beta_two) * grad * grad
    corrected = moment / (1.0 - beta_one**STEP)
    divisor = jnp.sqrt(second / (1.0 - beta_two**STEP)) + adam_eps
    return (weight - rate * (corrected / divisor + decay * weight), moment, second)


class Plan:
    def __init__(self, count):
        self.count = count
        self.R = MIXIN // count
        self.attn = ATT // self.R
        self.ha = self.R // HD
        self.hm = self.R // MP
        self.S = 2 * self.R + 2 * NS + PAD
        self.B = self.R
        self.C = 2 * self.R
        self.T = 2 * self.R + 2 * NS

    def kv_of(self, c):
        return c * self.ha // GROUP


def in_slabs(plan, w):
    R = plan.R
    slabs = []
    blank = lambda k: jnp.zeros((w.shape[0], k), w.dtype)
    for c in range(plan.count):
        if c < plan.attn:
            g = plan.kv_of(c)
            parts = [
                w[:, c * R : (c + 1) * R],
                blank(R),
                w[:, K_AT + g * HD : K_AT + (g + 1) * HD],
                w[:, V_AT + g * HD : V_AT + (g + 1) * HD],
                blank(2 * NS - 2 * HD + PAD),
            ]
        else:
            j = c - plan.attn
            parts = [
                w[:, Z_AT + j * R : Z_AT + (j + 1) * R],
                w[:, X_AT + j * R : X_AT + (j + 1) * R],
                w[:, BC_AT:DT_AT],
                w[:, DT_AT + j * plan.hm : DT_AT + (j + 1) * plan.hm],
                blank(PAD - plan.hm),
            ]
        slabs.append(jnp.concatenate(parts, axis=1))
    return jnp.stack(slabs)


def from_slabs(plan, slabs):
    R, C, T = plan.R, plan.C, plan.T
    slabs = slabs.astype(jnp.float32)
    heads = range(plan.attn)
    spaces = range(plan.attn, plan.count)
    total = lambda items: functools.reduce(lambda a, b: a + b, items)
    parts = [slabs[c][:, :R] for c in heads]
    for at in (C, C + HD):
        for g in range(KVH):
            parts.append(total([slabs[c][:, at : at + HD] for c in heads if plan.kv_of(c) == g]))
    parts += [slabs[c][:, :R] for c in spaces]
    parts += [slabs[c][:, R : 2 * R] for c in spaces]
    parts.append(total([slabs[c][:, C:T] for c in spaces]))
    parts += [slabs[c][:, T : T + plan.hm] for c in spaces]
    return jnp.concatenate(parts, axis=1)


def up_slabs(plan, w):
    G = FF // plan.count
    return jnp.stack(
        [
            jnp.concatenate([w[:, c * G : (c + 1) * G], w[:, FF + c * G : FF + (c + 1) * G]], axis=1)
            for c in range(plan.count)
        ]
    )


def up_from_slabs(plan, slabs):
    G = FF // plan.count
    slabs = slabs.astype(jnp.float32)
    return jnp.concatenate(
        [slabs[c][:, :G] for c in range(plan.count)] + [slabs[c][:, G:] for c in range(plan.count)],
        axis=1,
    )


def gather_ctx(x):
    return lax.all_gather(x, "ctx", axis=0, tiled=True)


def scatter_ctx(x):
    return lax.psum_scatter(
        x.astype(jnp.bfloat16), "ctx", scatter_dimension=0, tiled=True
    ).astype(jnp.float32)


def spread(slabs):
    mine = lax.all_to_all(slabs, "ctx", split_axis=0, concat_axis=0, tiled=True)
    every = lax.all_gather(mine, "wshard", axis=0)
    return every.transpose(1, 0, 2, 3).reshape(D, slabs.shape[2])


def collect(grad, count, ways):
    rows = D // (count * ways)
    grad = grad.astype(jnp.bfloat16).reshape(count, ways, rows, grad.shape[1])
    grad = grad.transpose(1, 0, 2, 3)
    mine = lax.psum_scatter(grad, "wshard", scatter_dimension=0, tiled=True)[0]
    return lax.all_to_all(mine, "ctx", split_axis=0, concat_axis=0, tiled=True)


def attn_inputs(plan, proj):
    length = proj.shape[0]
    positions = jnp.arange(length).astype(jnp.float32)
    queries = rotate(proj[:, : plan.R].reshape(length, plan.ha, HD), positions)
    keys = rotate(proj[:, plan.C : plan.C + HD].reshape(length, 1, HD), positions)[:, 0]
    values = proj[:, plan.C + HD : plan.C + 2 * HD]
    return (
        queries.astype(jnp.bfloat16).transpose(1, 0, 2),
        keys.astype(jnp.bfloat16),
        values.astype(jnp.bfloat16),
    )


def attn_probs(queries, keys, at):
    scores = jnp.einsum("hqd,sd->hqs", queries, keys, preferred_element_type=jnp.float32)
    scores = scores * (1.0 / math.sqrt(HD))
    places = at + jnp.arange(queries.shape[1])
    allowed = jnp.arange(keys.shape[0])[None, :] <= places[:, None]
    scores = jnp.where(allowed[None], scores, masked_score)
    weights = jnp.exp(scores - jnp.max(scores, axis=-1, keepdims=True))
    return weights / jnp.sum(weights, axis=-1, keepdims=True)


def attn_forward(plan, proj):
    queries, keys, values = attn_inputs(plan, proj)
    length = proj.shape[0]
    block = min(512, length)

    def one(at):
        part = lax.dynamic_slice_in_dim(queries, at, block, 1)
        probs = attn_probs(part, keys, at).astype(jnp.bfloat16)
        return jnp.einsum("hqs,sd->qhd", probs, values, preferred_element_type=jnp.float32)

    return lax.map(one, jnp.arange(0, length, block)).reshape(length, plan.R)


def attn_backward(plan, proj, grad):
    (queries, keys, values) = attn_inputs(plan, proj)
    length = proj.shape[0]
    block = min(512, length)
    grads = grad.reshape(length, plan.ha, HD).transpose(1, 0, 2)
    scale = 1.0 / math.sqrt(HD)

    def one(carry, at):
        part = lax.dynamic_slice_in_dim(queries, at, block, 1)
        out_grad = lax.dynamic_slice_in_dim(grads, at, block, 1)
        probs = attn_probs(part, keys, at)
        grad_probs = jnp.einsum("hqd,sd->hqs", out_grad, values, preferred_element_type=jnp.float32)
        delta = jnp.sum(probs * grad_probs, axis=-1, keepdims=True)
        grad_scores = (probs * (grad_probs - delta)).astype(jnp.bfloat16)
        grad_q = jnp.einsum("hqs,sd->qhd", grad_scores, keys, preferred_element_type=jnp.float32)
        grad_k = jnp.einsum("hqs,hqd->sd", grad_scores, part, preferred_element_type=jnp.float32)
        grad_v = jnp.einsum(
            "hqs,hqd->sd",
            probs.astype(jnp.bfloat16),
            out_grad,
            preferred_element_type=jnp.float32,
        )
        return (carry[0] + grad_k, carry[1] + grad_v), grad_q

    empty = jnp.zeros((length, HD), jnp.float32)
    (grad_k, grad_v), grad_q = lax.scan(one, (empty, empty), jnp.arange(0, length, block))
    grad_q = grad_q.reshape(length, plan.ha, HD) * scale
    grad_k = grad_k.reshape(length, 1, HD) * scale
    back = -jnp.arange(length).astype(jnp.float32)
    grad_q = rotate(grad_q, back).reshape(length, plan.R)
    grad_k = rotate(grad_k, back).reshape(length, HD)
    blank = lambda k: jnp.zeros((length, k), jnp.float32)
    return jnp.concatenate(
        [grad_q, blank(plan.R), grad_k, grad_v, blank(plan.S - plan.C - 2 * HD)], axis=1
    )


def space_out(plan, proj, vecs):
    conv_w, conv_b, a_log, dt_bias, d_skip = vecs
    length = proj.shape[0]
    R, hm = plan.R, plan.hm
    z_raw = proj[:, :R]
    xbc = proj[:, R : plan.T]
    dt_raw = proj[:, plan.T : plan.T + hm]
    extended = jnp.concatenate([jnp.zeros((CONV - 1, xbc.shape[1]), jnp.float32), xbc], axis=0)
    summed = conv_b[None, :]
    for offset in range(CONV):
        summed = summed + conv_w[offset][None, :] * extended[offset : offset + length]
    post = jax.nn.silu(summed)
    steps = jax.nn.softplus(dt_raw + dt_bias)
    chunks = length // CHUNK
    x = post[:, :R].reshape(chunks, CHUNK, hm, MP)
    b = post[:, R : R + NS].reshape(chunks, CHUNK, NS)
    c = post[:, R + NS :].reshape(chunks, CHUNK, NS)
    steps = steps.reshape(chunks, CHUNK, hm)
    cumul = jnp.cumsum(-steps * jnp.exp(a_log), axis=1)
    tail = jnp.exp(cumul[:, -1:] - cumul)
    local = high("kshp,ksn->khpn", x * (steps * tail)[..., None], b)
    total = jnp.exp(cumul[:, -1])

    def pass_on(state, item):
        factor, fresh = item
        return factor[:, None, None] * state + fresh, state

    incoming = lax.scan(pass_on, jnp.zeros_like(local[0]), (total, local))[1]
    places = jnp.arange(CHUNK)
    causal = (places[:, None] >= places[None, :])[None, :, :, None]
    gaps = jnp.where(causal, cumul[:, :, None, :] - cumul[:, None, :, :], 0.0)
    decay = jnp.where(causal, jnp.exp(gaps), 0.0)
    inner = high("ktn,ksn->kts", c, b)
    intra = high("ktsh,kshp->kthp", decay * inner[..., None], x * steps[..., None])
    carried = high("ktn,khpn->kthp", c, incoming) * jnp.exp(cumul)[..., None]
    made = intra + carried + d_skip[:, None] * x
    return made.reshape(length, R) * jax.nn.silu(z_raw)


def body(
    inputs,
    cotangent,
    w_in,
    w_in_m,
    w_in_v,
    w_mix,
    w_mix_m,
    w_mix_v,
    w_up,
    w_up_m,
    w_up_v,
    w_down,
    w_down_m,
    w_down_v,
    vectors,
    vectors_m,
    vectors_v,
):
    low = jnp.bfloat16
    count = lax.axis_size("ctx")
    ways = lax.axis_size("wshard")
    place = lax.axis_index("ctx")
    plan = Plan(count)
    R, hm = plan.R, plan.hm
    is_space = place >= plan.attn
    space = jnp.maximum(place - plan.attn, 0)

    gain_attn, gain_ffn, gain_ssm, conv_bias, conv_weight, a_log, dt_bias, d_skip = split_vectors(
        vectors
    )
    in_own = spread(in_slabs(plan, w_in.astype(low)))
    up_own = spread(up_slabs(plan, w_up.astype(low)))
    mix_own = lax.all_gather(w_mix.astype(low), "wshard", axis=0, tiled=True)
    down_own = lax.all_gather(w_down.astype(low), "wshard", axis=0, tiled=True)

    own = lambda a, size, axis=0: lax.dynamic_slice_in_dim(a, space * size, size, axis)
    gain_own = own(gain_ssm, R)
    space_vecs = (
        jnp.concatenate([own(conv_weight, R, 1), conv_weight[:, DSSM:]], axis=1),
        jnp.concatenate([own(conv_bias, R), conv_bias[DSSM:]]),
        own(a_log, hm),
        own(dt_bias, hm),
        own(d_skip, hm),
    )

    source = inputs[0].astype(jnp.float32)
    whole = gather_ctx(inputs[0]).astype(jnp.float32)
    upstream_all = gather_ctx(cotangent[0])
    length = whole.shape[0]
    normed = rms_norm(whole, gain_attn).astype(low)
    proj = plain(normed, in_own)

    made = lax.cond(
        is_space,
        lambda p, v: space_out(plan, p, v),
        lambda p, v: attn_forward(plan, p),
        proj,
        space_vecs,
    )
    square = jnp.where(is_space, jnp.sum(made * made, axis=1), 0.0)
    factor = lax.rsqrt(lax.psum(square, "ctx") / DSSM + norm_eps)
    mixed = jnp.where(is_space, made * factor[:, None] * gain_own, made).astype(low)
    middle = source + scatter_ctx(plain(mixed, mix_own))

    normed_two, two_pull = jax.vjp(rms_norm, middle, gain_ffn)
    two_all = gather_ctx(normed_two.astype(low))
    gate_up = plain(two_all, up_own)
    half = FF // count
    swiglu = lambda g: jax.nn.silu(g[:, :half]) * g[:, half:]
    activated, act_pull = jax.vjp(swiglu, gate_up)
    activated = activated.astype(low)
    outputs = (middle + scatter_ctx(plain(activated, down_own))).astype(low)[None]

    grad_down = rows_by_rows(activated, upstream_all)
    grad_act = cols_by_cols(upstream_all, down_own)
    grad_gate_up = act_pull(grad_act)[0].astype(low)
    grad_up = rows_by_rows(two_all, grad_gate_up)
    grad_two = scatter_ctx(cols_by_cols(grad_gate_up, up_own))
    grad_mid, grad_gain_ffn = two_pull(grad_two)
    grad_middle = cotangent[0].astype(jnp.float32) + grad_mid

    branch_all = gather_ctx(grad_middle.astype(low))
    grad_mix = rows_by_rows(mixed, branch_all)
    grad_made = cols_by_cols(branch_all, mix_own).astype(low)
    wide = grad_made.astype(jnp.float32)
    dots = jnp.where(is_space, jnp.sum(wide * gain_own * made, axis=1), 0.0)
    dots = lax.psum(dots, "ctx")
    grad_gain_own = jnp.sum(wide * made * factor[:, None], axis=0)
    grad_gated = wide * gain_own * factor[:, None] - made * (factor**3 * dots / DSSM)[:, None]

    def space_back(proj, vecs, grad_gated, grad_made):
        pull = jax.vjp(lambda p, v: space_out(plan, p, v), proj, vecs)[1]
        return pull(grad_gated)

    def attn_back(proj, vecs, grad_gated, grad_made):
        return attn_backward(plan, proj, grad_made), jax.tree.map(jnp.zeros_like, vecs)

    grad_proj, grad_vecs = lax.cond(
        is_space, space_back, attn_back, proj, space_vecs, grad_gated, grad_made
    )
    grad_proj = grad_proj.astype(low)
    grad_normed = scatter_ctx(cols_by_cols(grad_proj, in_own))
    grad_in = rows_by_rows(normed, grad_proj)

    pull_source = jax.vjp(rms_norm, source, gain_attn)[1]
    grad_source, grad_gain_attn = pull_source(grad_normed)
    input_grad = (grad_middle + grad_source)[None]

    in_shard = from_slabs(plan, collect(grad_in, count, ways))
    up_shard = up_from_slabs(plan, collect(grad_up, count, ways))
    mix_shard = lax.psum_scatter(
        grad_mix.astype(low), "wshard", scatter_dimension=0, tiled=True
    ).astype(jnp.float32)
    down_shard = lax.psum_scatter(
        grad_down.astype(low), "wshard", scatter_dimension=0, tiled=True
    ).astype(jnp.float32)

    def placed(piece, size, total, axis=0):
        shape = list(piece.shape)
        shape[axis] = total
        start = [0] * piece.ndim
        start[axis] = space * size
        return lax.dynamic_update_slice(jnp.zeros(shape, piece.dtype), piece, start)

    conv_w_grad, conv_b_grad, a_grad, bias_grad, skip_grad = grad_vecs
    grad_gain_own = jnp.where(is_space, grad_gain_own, 0.0)
    vector_local = jnp.concatenate(
        [
            grad_gain_attn,
            grad_gain_ffn,
            placed(grad_gain_own, R, DSSM),
            placed(conv_b_grad[:R], R, DSSM),
            conv_b_grad[R:],
            jnp.concatenate(
                [placed(conv_w_grad[:, :R], R, DSSM, 1), conv_w_grad[:, R:]], axis=1
            ).reshape(CONV * CONVCH),
            placed(a_grad, hm, MH),
            placed(bias_grad, hm, MH),
            placed(skip_grad, hm, MH),
        ]
    )
    vector_grad = lax.psum(vector_local, ("ctx", "wshard"))
    new_in = adamw(w_in, w_in_m, w_in_v, in_shard, 2.0 * D ** (-0.5), decay_weight)
    new_mix = adamw(w_mix, w_mix_m, w_mix_v, mix_shard, DSSM ** (-0.5), decay_weight)
    new_up = adamw(w_up, w_up_m, w_up_v, up_shard, D ** (-0.5), decay_weight)
    new_down = adamw(w_down, w_down_m, w_down_v, down_shard, FF ** (-0.5), decay_weight)
    new_vec = adamw(vectors, vectors_m, vectors_v, vector_grad, vector_rate, 0.0)
    return (outputs, input_grad, *new_in, *new_mix, *new_up, *new_down, *new_vec)


def solution(mesh):
    tokens = P("wshard", "ctx", None)
    weight = P(("ctx", "wshard"), None)
    return jax.shard_map(
        body,
        mesh=mesh,
        in_specs=(tokens,) * 2 + (weight,) * 12 + (P(),) * 3,
        out_specs=(tokens,) * 2 + (weight,) * 12 + (P(),) * 3,
        check_vma=False,
    )
```

```python
import functools
import math

import jax
import jax.numpy as jnp
from jax import lax
from jax.experimental import pallas as pl
from jax.experimental.pallas import tpu as pltpu
from jax.sharding import PartitionSpec as P

D = 2048
FF = 4096
AH = 8
KVH = 2
HD = 128
MH = 48
MP = 64
NS = 256
CONV = 4
STEP = 10
DSSM = 3072
CONVCH = 3584
ATT = AH * HD
MIXIN = ATT + DSSM
GROUP = AH // KVH
CHUNK = 128
PAD = 128
VMEM = 48 * 1024 * 1024


norm_eps = 1e-05
rope_base = 10000.0
beta_one = 0.9
beta_two = 0.95
adam_eps = 1e-08
decay_weight = 0.1
vector_rate = 0.5
masked_score = -1e30

K_AT = ATT
V_AT = K_AT + KVH * HD
Z_AT = V_AT + KVH * HD
X_AT = Z_AT + DSSM
BC_AT = X_AT + DSSM
DT_AT = BC_AT + 2 * NS
END = DT_AT + MH


def rows_by_rows(left, right):
    return lax.dot_general(
        left, right, (((0,), (0,)), ((), ())), preferred_element_type=jnp.float32
    )


def cols_by_cols(left, right):
    return lax.dot_general(
        left, right, (((1,), (1,)), ((), ())), preferred_element_type=jnp.float32
    )


def plain(left, right):
    return jnp.dot(left, right, preferred_element_type=jnp.float32)


def rms_norm(values, gain):
    factor = lax.rsqrt(jnp.mean(values * values, axis=-1, keepdims=True) + norm_eps)
    return values * factor * gain


def split_vectors(vectors):
    extents = (D, D, DSSM, CONVCH, CONV * CONVCH, MH, MH, MH)
    pieces = []
    offset = 0
    for extent in extents:
        pieces.append(lax.slice_in_dim(vectors, offset, offset + extent))
        offset = offset + extent
    pieces[4] = pieces[4].reshape(CONV, CONVCH)
    return pieces


def adamw(weight, moment, second, grad, rate, decay):
    moment = beta_one * moment + (1.0 - beta_one) * grad
    second = beta_two * second + (1.0 - beta_two) * grad * grad
    corrected = moment / (1.0 - beta_one**STEP)
    divisor = jnp.sqrt(second / (1.0 - beta_two**STEP)) + adam_eps
    return (weight - rate * (corrected / divisor + decay * weight), moment, second)


class Plan:
    def __init__(self, count):
        self.count = count
        self.R = MIXIN // count
        self.attn = ATT // self.R
        self.ha = self.R // HD
        self.hm = self.R // MP
        self.S = 2 * self.R + 2 * NS + PAD
        self.B = self.R
        self.C = 2 * self.R
        self.T = 2 * self.R + 2 * NS

    def kv_of(self, c):
        return c * self.ha // GROUP


def in_slabs(plan, w):
    R = plan.R
    slabs = []
    blank = lambda k: jnp.zeros((w.shape[0], k), w.dtype)
    for c in range(plan.count):
        if c < plan.attn:
            g = plan.kv_of(c)
            parts = [
                w[:, c * R : (c + 1) * R],
                blank(R),
                w[:, K_AT + g * HD : K_AT + (g + 1) * HD],
                w[:, V_AT + g * HD : V_AT + (g + 1) * HD],
                blank(2 * NS - 2 * HD + PAD),
            ]
        else:
            j = c - plan.attn
            parts = [
                w[:, Z_AT + j * R : Z_AT + (j + 1) * R],
                w[:, X_AT + j * R : X_AT + (j + 1) * R],
                w[:, BC_AT:DT_AT],
                w[:, DT_AT + j * plan.hm : DT_AT + (j + 1) * plan.hm],
                blank(PAD - plan.hm),
            ]
        slabs.append(jnp.concatenate(parts, axis=1))
    return jnp.stack(slabs)


def from_slabs(plan, slabs):
    R, C, T = plan.R, plan.C, plan.T
    slabs = slabs.astype(jnp.float32)
    heads = range(plan.attn)
    spaces = range(plan.attn, plan.count)
    total = lambda items: functools.reduce(lambda a, b: a + b, items)
    parts = [slabs[c][:, :R] for c in heads]
    for at in (C, C + HD):
        for g in range(KVH):
            parts.append(total([slabs[c][:, at : at + HD] for c in heads if plan.kv_of(c) == g]))
    parts += [slabs[c][:, :R] for c in spaces]
    parts += [slabs[c][:, R : 2 * R] for c in spaces]
    parts.append(total([slabs[c][:, C:T] for c in spaces]))
    parts += [slabs[c][:, T : T + plan.hm] for c in spaces]
    return jnp.concatenate(parts, axis=1)


def up_slabs(plan, w):
    G = FF // plan.count
    return jnp.stack(
        [
            jnp.concatenate([w[:, c * G : (c + 1) * G], w[:, FF + c * G : FF + (c + 1) * G]], axis=1)
            for c in range(plan.count)
        ]
    )


def up_from_slabs(plan, slabs):
    G = FF // plan.count
    slabs = slabs.astype(jnp.float32)
    return jnp.concatenate(
        [slabs[c][:, :G] for c in range(plan.count)] + [slabs[c][:, G:] for c in range(plan.count)],
        axis=1,
    )


def gather_ctx(x):
    return lax.all_gather(x, "ctx", axis=0, tiled=True)


def scatter_ctx(x):
    return lax.psum_scatter(
        x.astype(jnp.bfloat16), "ctx", scatter_dimension=0, tiled=True
    ).astype(jnp.float32)


def spread(slabs):
    mine = lax.all_to_all(slabs, "ctx", split_axis=0, concat_axis=0, tiled=True)
    every = lax.all_gather(mine, "wshard", axis=0)
    return every.transpose(1, 0, 2, 3).reshape(D, slabs.shape[2])


def collect(grad, count, ways):
    rows = D // (count * ways)
    grad = grad.astype(jnp.bfloat16).reshape(count, ways, rows, grad.shape[1])
    grad = grad.transpose(1, 0, 2, 3)
    mine = lax.psum_scatter(grad, "wshard", scatter_dimension=0, tiled=True)[0]
    return lax.all_to_all(mine, "ctx", split_axis=0, concat_axis=0, tiled=True)


def mm(left, right):
    return jnp.dot(
        left.astype(jnp.bfloat16), right.astype(jnp.bfloat16), preferred_element_type=jnp.float32
    )


def mm_nt(left, right):
    return cols_by_cols(left.astype(jnp.bfloat16), right.astype(jnp.bfloat16))


def mm_tn(left, right):
    return rows_by_rows(left.astype(jnp.bfloat16), right.astype(jnp.bfloat16))


def exact(left, right):
    return jnp.dot(
        left, right, precision=lax.Precision.HIGHEST, preferred_element_type=jnp.float32
    )


def iota(shape, axis):
    return lax.broadcasted_iota(jnp.int32, shape, axis)


def rope_tables(length):
    half = HD // 2
    frequency = rope_base ** (-jnp.arange(half, dtype=jnp.float32) / half)
    angles = jnp.arange(length).astype(jnp.float32)[:, None] * frequency[None, :]
    cosine, sine = jnp.cos(angles), jnp.sin(angles)
    return (
        jnp.concatenate([cosine, cosine], axis=1),
        jnp.concatenate([-sine, sine], axis=1),
    )


def turned(values, cosine, sine):
    return values * cosine + pltpu.roll(values, HD // 2, 1) * sine


def attn_stack(plan, q_ref, cosine, sine):
    heads = [
        turned(q_ref[:, h * HD : (h + 1) * HD], cosine, sine).astype(jnp.bfloat16)
        for h in range(plan.ha)
    ]
    return jnp.concatenate(heads, axis=0)


def attn_softmax(stack, keys, at):
    scores = cols_by_cols(stack, keys) * (1.0 / math.sqrt(HD))
    row = iota(scores.shape, 0) & (CHUNK - 1)
    scores = jnp.where(iota(scores.shape, 1) <= row + at, scores, masked_score)
    weights = jnp.exp(scores - jnp.max(scores, axis=1, keepdims=True))
    return weights * (1.0 / jnp.sum(weights, axis=1, keepdims=True))


def attn_fwd_kernel(plan, q_ref, kv_ref, cos_ref, sin_ref, out_ref, keys, values):
    step = pl.program_id(0)

    @pl.when(step == 0)
    def _():
        keys[...] = turned(kv_ref[:, :HD], cos_ref[...], sin_ref[...]).astype(jnp.bfloat16)
        values[...] = kv_ref[:, HD : 2 * HD].astype(jnp.bfloat16)

    at = pl.multiple_of(step * CHUNK, CHUNK)
    rows = pl.ds(at, CHUNK)
    stack = attn_stack(plan, q_ref, cos_ref[rows, :], sin_ref[rows, :])
    probs = attn_softmax(stack, keys[...], at)
    made = mm(probs, values[...])
    for h in range(plan.ha):
        out_ref[:, h * HD : (h + 1) * HD] = made[h * CHUNK : (h + 1) * CHUNK]


def attn_fwd(plan, proj, tables):
    length = proj.shape[0]
    whole = lambda i: (0, 0)
    return pl.pallas_call(
        functools.partial(attn_fwd_kernel, plan),
        grid=(length // CHUNK,),
        out_shape=jax.ShapeDtypeStruct((length, plan.R), jnp.float32),
        in_specs=[
            pl.BlockSpec((CHUNK, plan.R), lambda i: (i, 0)),
            pl.BlockSpec((length, 2 * HD), lambda i: (0, plan.C // (2 * HD))),
            pl.BlockSpec((length, HD), whole),
            pl.BlockSpec((length, HD), whole),
        ],
        out_specs=pl.BlockSpec((CHUNK, plan.R), lambda i: (i, 0)),
        scratch_shapes=[pltpu.VMEM((length, HD), jnp.bfloat16)] * 2,
        compiler_params=pltpu.CompilerParams(vmem_limit_bytes=VMEM),
    )(proj, proj, *tables)


def attn_bwd_kernel(
    plan, q_ref, kv_ref, cos_ref, sin_ref, grad_ref, slab_ref, keys, values, grad_k, grad_v
):
    step = pl.program_id(0)
    scale = 1.0 / math.sqrt(HD)

    @pl.when(step == 0)
    def _():
        keys[...] = turned(kv_ref[:, :HD], cos_ref[...], sin_ref[...]).astype(jnp.bfloat16)
        values[...] = kv_ref[:, HD : 2 * HD].astype(jnp.bfloat16)
        grad_k[...] = jnp.zeros_like(grad_k)
        grad_v[...] = jnp.zeros_like(grad_v)
        slab_ref[...] = jnp.zeros_like(slab_ref)

    at = pl.multiple_of(step * CHUNK, CHUNK)
    rows = pl.ds(at, CHUNK)
    cosine, sine = cos_ref[rows, :], sin_ref[rows, :]
    stack = attn_stack(plan, q_ref, cosine, sine)
    probs = attn_softmax(stack, keys[...], at)
    grads = jnp.concatenate([grad_ref[:, h * HD : (h + 1) * HD] for h in range(plan.ha)], axis=0)
    grad_probs = cols_by_cols(grads, values[...])
    delta = jnp.sum(probs * grad_probs, axis=1, keepdims=True)
    grad_scores = (probs * (grad_probs - delta)).astype(jnp.bfloat16)
    grad_q = mm(grad_scores, keys[...]) * scale
    for h in range(plan.ha):
        slab_ref[rows, h * HD : (h + 1) * HD] = turned(
            grad_q[h * CHUNK : (h + 1) * CHUNK], cosine, -sine
        ).astype(jnp.bfloat16)
    grad_k[...] += mm_tn(grad_scores, stack)
    grad_v[...] += mm_tn(probs, grads)

    @pl.when(step == pl.num_programs(0) - 1)
    def _():
        slab_ref[:, plan.C : plan.C + HD] = turned(
            grad_k[...] * scale, cos_ref[...], -sin_ref[...]
        ).astype(jnp.bfloat16)
        slab_ref[:, plan.C + HD : plan.C + 2 * HD] = grad_v[...].astype(jnp.bfloat16)


def attn_bwd(plan, proj, tables, grad):
    length = proj.shape[0]
    whole = lambda i: (0, 0)
    return pl.pallas_call(
        functools.partial(attn_bwd_kernel, plan),
        grid=(length // CHUNK,),
        out_shape=jax.ShapeDtypeStruct((length, plan.S), jnp.bfloat16),
        in_specs=[
            pl.BlockSpec((CHUNK, plan.R), lambda i: (i, 0)),
            pl.BlockSpec((length, 2 * HD), lambda i: (0, plan.C // (2 * HD))),
            pl.BlockSpec((length, HD), whole),
            pl.BlockSpec((length, HD), whole),
            pl.BlockSpec((CHUNK, plan.R), lambda i: (i, 0)),
        ],
        out_specs=pl.BlockSpec((length, plan.S), whole),
        scratch_shapes=[pltpu.VMEM((length, HD), jnp.bfloat16)] * 2
        + [pltpu.VMEM((length, HD), jnp.float32)] * 2,
        compiler_params=pltpu.CompilerParams(vmem_limit_bytes=VMEM),
    )(proj, proj, *tables, grad)


def head_spread(plan):
    return ((iota((PAD, plan.R), 1) >> 6) == iota((PAD, plan.R), 0)).astype(jnp.float32)


def head_gather(plan):
    return ((iota((plan.R, PAD), 0) >> 6) == iota((plan.R, PAD), 1)).astype(jnp.float32)


def lower_ones():
    shape = (CHUNK, CHUNK)
    return (iota(shape, 0) >= iota(shape, 1)).astype(jnp.float32)


def space_parts(plan, dt_raw, window, conv_ref, head_ref):
    total = conv_ref[4:5, :]
    for k in range(CONV):
        at = 8 - CONV + 1 + k
        total = total + conv_ref[k : k + 1, :] * window[at : at + CHUNK, :]
    raw = dt_raw + head_ref[1:2, :]
    steps = jnp.maximum(raw, 0.0) + jnp.log1p(jnp.exp(-jnp.abs(raw)))
    logs = -steps * jnp.exp(head_ref[0:1, :])
    cumul = exact(lower_ones(), logs)
    return total, raw, steps, logs, cumul


def decay_of(cumul, cumul_t, causal, h):
    gaps = cumul[:, h : h + 1] - cumul_t[h : h + 1, :]
    return jnp.exp(jnp.where(causal, gaps, masked_score))


def space_fwd_kernel(plan, proj_ref, conv_ref, head_ref, gated_ref, made_ref, before_ref, state, window):
    R = plan.R
    step = pl.program_id(0)

    @pl.when(step == 0)
    def _():
        state[...] = jnp.zeros_like(state)
        window[0:8, :] = jnp.zeros((8, window.shape[1]), jnp.float32)

    @pl.when(step > 0)
    def _():
        window[0:8, :] = window[CHUNK : CHUNK + 8, :]

    window[8 : CHUNK + 8, :] = proj_ref[:, R : plan.T]
    total, _, steps, _, cumul = space_parts(
        plan, proj_ref[:, plan.T : plan.T + PAD], window, conv_ref, head_ref
    )
    post = total * jax.nn.sigmoid(total)
    x = post[:, :R]
    b = post[:, R : R + NS].astype(jnp.bfloat16)
    c = post[:, R + NS :].astype(jnp.bfloat16)
    spread_heads = head_spread(plan)
    cumul_t = cumul.T
    last = cumul[CHUNK - 1 : CHUNK, :]
    tail = jnp.exp(last - cumul)
    weighted = x * exact(steps, spread_heads)
    causal = iota((CHUNK, CHUNK), 0) >= iota((CHUNK, CHUNK), 1)
    inner = cols_by_cols(c, b)
    before = state[...]
    before_ref[0] = before.astype(jnp.bfloat16)
    made = mm(c, before) * exact(jnp.exp(cumul), spread_heads)
    made = made + exact(jnp.broadcast_to(head_ref[2:3, :], (8, PAD)), spread_heads)[0:1] * x
    left = iota((CHUNK, 2 * MP), 1) < MP
    weighted_low = weighted.astype(jnp.bfloat16)
    intra = []
    for pair in range(plan.hm // 2):
        lanes = weighted_low[:, pair * 2 * MP : (pair + 1) * 2 * MP]
        one = mm(inner * decay_of(cumul, cumul_t, causal, 2 * pair), lanes)
        two = mm(inner * decay_of(cumul, cumul_t, causal, 2 * pair + 1), lanes)
        intra.append(jnp.where(left, one, two))
    made = made + jnp.concatenate(intra, axis=1)
    state[...] = before * exact(
        jnp.broadcast_to(jnp.exp(last), (8, PAD)), spread_heads
    )[0:1] + mm_tn(b, weighted * exact(tail, spread_heads))
    z = proj_ref[:, :R]
    made_ref[...] = made
    gated_ref[...] = made * (z * jax.nn.sigmoid(z))


def space_fwd(plan, proj, conv, heads):
    length = proj.shape[0]
    chunks = length // CHUNK
    W = plan.T - plan.R
    whole = lambda i: (0, 0)
    rows = lambda i: (i, 0)
    return pl.pallas_call(
        functools.partial(space_fwd_kernel, plan),
        grid=(chunks,),
        out_shape=(
            jax.ShapeDtypeStruct((length, plan.R), jnp.float32),
            jax.ShapeDtypeStruct((length, plan.R), jnp.float32),
            jax.ShapeDtypeStruct((chunks, NS, plan.R), jnp.bfloat16),
        ),
        in_specs=[
            pl.BlockSpec((CHUNK, plan.S), rows),
            pl.BlockSpec((8, W), whole),
            pl.BlockSpec((8, PAD), whole),
        ],
        out_specs=(
            pl.BlockSpec((CHUNK, plan.R), rows),
            pl.BlockSpec((CHUNK, plan.R), rows),
            pl.BlockSpec((1, NS, plan.R), lambda i: (i, 0, 0)),
        ),
        scratch_shapes=[
            pltpu.VMEM((NS, plan.R), jnp.float32),
            pltpu.VMEM((CHUNK + 8, W), jnp.float32),
        ],
        compiler_params=pltpu.CompilerParams(vmem_limit_bytes=VMEM),
    )(proj, conv, heads)


def space_bwd_kernel(
    plan, proj_ref, prev_ref, conv_ref, head_ref, grad_ref, made_ref, before_ref,
    slab_ref, conv_acc, head_acc, skip_acc, d_state, window, d_window,
):
    R, T = plan.R, plan.T
    step = pl.program_id(0)
    chunk = pl.num_programs(0) - 1 - step

    @pl.when(step == 0)
    def _():
        d_state[...] = jnp.zeros_like(d_state)
        d_window[CHUNK : CHUNK + 8, :] = jnp.zeros((8, T - R), jnp.float32)
        conv_acc[...] = jnp.zeros_like(conv_acc)
        head_acc[...] = jnp.zeros_like(head_acc)
        skip_acc[...] = jnp.zeros_like(skip_acc)

    @pl.when(step > 0)
    def _():
        d_window[CHUNK : CHUNK + 8, :] = d_window[0:8, :]

    window[0:8, :] = jnp.where(chunk == 0, 0.0, prev_ref[:, R:T])
    window[8 : CHUNK + 8, :] = proj_ref[:, R:T]
    total, raw, steps, logs, cumul = space_parts(
        plan, proj_ref[:, T : T + PAD], window, conv_ref, head_ref
    )
    sig = jax.nn.sigmoid(total)
    post = total * sig
    x = post[:, :R]
    b = post[:, R : R + NS].astype(jnp.bfloat16)
    c = post[:, R + NS :].astype(jnp.bfloat16)
    spread_heads = head_spread(plan)
    gather_heads = head_gather(plan)
    cumul_t = cumul.T
    last = cumul[CHUNK - 1 : CHUNK, :]
    steps_wide = exact(steps, spread_heads)
    tail_wide = exact(jnp.exp(last - cumul), spread_heads)
    grow_wide = exact(jnp.exp(cumul), spread_heads)
    last_wide = exact(jnp.broadcast_to(jnp.exp(last), (8, PAD)), spread_heads)[0:1]
    skip_wide = exact(jnp.broadcast_to(head_ref[2:3, :], (8, PAD)), spread_heads)[0:1]
    weighted = x * steps_wide
    causal = iota((CHUNK, CHUNK), 0) >= iota((CHUNK, CHUNK), 1)
    inner = cols_by_cols(c, b)

    z = proj_ref[:, :R]
    sig_z = jax.nn.sigmoid(z)
    grad = grad_ref[...]
    d_made = grad * (z * sig_z)
    slab_ref[:, :R] = (grad * made_ref[...] * (sig_z * (1.0 + z * (1.0 - sig_z)))).astype(
        jnp.bfloat16
    )
    skip_acc[0:1, :] += jnp.sum(d_made * x, axis=0, keepdims=True)

    before = before_ref[0]
    d_after = d_state[...]
    d_after_low = d_after.astype(jnp.bfloat16)
    grown = d_made * grow_wide
    grown_low = grown.astype(jnp.bfloat16)
    carried = mm(c, before)
    d_c = mm_nt(grown_low, before)
    pulled = weighted * tail_wide
    d_pulled = mm(b, d_after_low)
    d_b = mm_nt(pulled, d_after_low)
    d_cumul = exact(grown * carried, gather_heads)
    kept = exact(d_pulled * pulled, gather_heads)
    d_cumul = d_cumul - kept
    decayed = jnp.sum(d_after * before.astype(jnp.float32), axis=0, keepdims=True) * last_wide
    d_last = jnp.sum(kept, axis=0, keepdims=True) + exact(
        jnp.broadcast_to(decayed, (8, R)), gather_heads
    )[0:1]
    d_state[...] = d_after * last_wide + mm_tn(c, grown_low)

    left = iota((CHUNK, 2 * MP), 1) < MP
    lane = iota((CHUNK, PAD), 1)
    sub = iota((8, CHUNK), 0)
    weighted_low = weighted.astype(jnp.bfloat16)
    d_made_low = d_made.astype(jnp.bfloat16)
    d_inner = jnp.zeros((CHUNK, CHUNK), jnp.float32)
    columns = jnp.zeros((8, CHUNK), jnp.float32)
    d_weighted = []
    for pair in range(plan.hm // 2):
        at = slice(pair * 2 * MP, (pair + 1) * 2 * MP)
        lanes, d_lanes = weighted_low[:, at], d_made_low[:, at]
        halves = []
        for which in range(2):
            h = 2 * pair + which
            decay = decay_of(cumul, cumul_t, causal, h)
            whole = inner * decay
            halves.append(mm_tn(whole, d_lanes))
            mine = jnp.where(left if which == 0 else ~left, d_lanes, jnp.zeros_like(d_lanes))
            d_whole = cols_by_cols(mine, lanes)
            d_inner = d_inner + d_whole * decay
            slope = d_whole * whole
            d_cumul = d_cumul + jnp.where(lane == h, jnp.sum(slope, axis=1, keepdims=True), 0.0)
            columns = columns + jnp.where(sub == h, jnp.sum(slope, axis=0, keepdims=True), 0.0)
        d_weighted.append(jnp.where(left, halves[0], halves[1]))
    d_weighted = jnp.concatenate(d_weighted, axis=1) + d_pulled * tail_wide
    columns = jnp.concatenate([columns, jnp.zeros((CHUNK - 8, CHUNK), jnp.float32)], axis=0).T
    d_cumul = d_cumul - columns
    d_inner_low = d_inner.astype(jnp.bfloat16)
    d_c = d_c + mm(d_inner_low, b)
    d_b = d_b + mm_tn(d_inner_low, c)
    d_x = d_weighted * steps_wide + skip_wide * d_made
    d_steps = exact(d_weighted * x, gather_heads)
    upper = (iota((CHUNK, CHUNK), 0) <= iota((CHUNK, CHUNK), 1)).astype(jnp.float32)
    d_logs = exact(upper, d_cumul) + d_last
    d_steps = d_steps - jnp.exp(head_ref[0:1, :]) * d_logs
    d_raw = d_steps * jax.nn.sigmoid(raw)
    slab_ref[:, T : T + PAD] = jnp.where(lane < plan.hm, d_raw, 0.0).astype(jnp.bfloat16)
    head_acc[0:1, :] += jnp.sum(d_logs * logs, axis=0, keepdims=True)
    head_acc[1:2, :] += jnp.sum(d_raw, axis=0, keepdims=True)

    d_post = jnp.concatenate([d_x, d_b, d_c], axis=1)
    d_total = d_post * (sig * (1.0 + total * (1.0 - sig)))
    d_window[0:CHUNK, :] = d_total
    d_xbc = jnp.zeros((CHUNK, T - R), jnp.float32)
    for k in range(CONV):
        shift = CONV - 1 - k
        d_xbc = d_xbc + conv_ref[k : k + 1, :] * d_window[shift : shift + CHUNK, :]
        at = 8 - CONV + 1 + k
        conv_acc[k : k + 1, :] += jnp.sum(
            d_total * window[at : at + CHUNK, :], axis=0, keepdims=True
        )
    conv_acc[4:5, :] += jnp.sum(d_total, axis=0, keepdims=True)
    slab_ref[:, R:T] = d_xbc.astype(jnp.bfloat16)


def space_bwd(plan, proj, conv, heads, grad, made, before):
    length = proj.shape[0]
    chunks = length // CHUNK
    W = plan.T - plan.R
    whole = lambda i: (0, 0)
    rows = lambda i: (chunks - 1 - i, 0)
    per = CHUNK // 8
    return pl.pallas_call(
        functools.partial(space_bwd_kernel, plan),
        grid=(chunks,),
        out_shape=(
            jax.ShapeDtypeStruct((length, plan.S), jnp.bfloat16),
            jax.ShapeDtypeStruct((8, W), jnp.float32),
            jax.ShapeDtypeStruct((8, PAD), jnp.float32),
            jax.ShapeDtypeStruct((8, plan.R), jnp.float32),
        ),
        in_specs=[
            pl.BlockSpec((CHUNK, plan.S), rows),
            pl.BlockSpec((8, plan.S), lambda i: (jnp.maximum((chunks - 1 - i) * per - 1, 0), 0)),
            pl.BlockSpec((8, W), whole),
            pl.BlockSpec((8, PAD), whole),
            pl.BlockSpec((CHUNK, plan.R), rows),
            pl.BlockSpec((CHUNK, plan.R), rows),
            pl.BlockSpec((1, NS, plan.R), lambda i: (chunks - 1 - i, 0, 0)),
        ],
        out_specs=(
            pl.BlockSpec((CHUNK, plan.S), rows),
            pl.BlockSpec((8, W), whole),
            pl.BlockSpec((8, PAD), whole),
            pl.BlockSpec((8, plan.R), whole),
        ),
        scratch_shapes=[
            pltpu.VMEM((NS, plan.R), jnp.float32),
            pltpu.VMEM((CHUNK + 8, W), jnp.float32),
            pltpu.VMEM((CHUNK + 8, W), jnp.float32),
        ],
        compiler_params=pltpu.CompilerParams(vmem_limit_bytes=VMEM),
    )(proj, proj, conv, heads, grad, made, before)


def body(
    inputs,
    cotangent,
    w_in,
    w_in_m,
    w_in_v,
    w_mix,
    w_mix_m,
    w_mix_v,
    w_up,
    w_up_m,
    w_up_v,
    w_down,
    w_down_m,
    w_down_v,
    vectors,
    vectors_m,
    vectors_v,
):
    low = jnp.bfloat16
    count = lax.axis_size("ctx")
    ways = lax.axis_size("wshard")
    place = lax.axis_index("ctx")
    plan = Plan(count)
    R, hm = plan.R, plan.hm
    is_space = place >= plan.attn
    space = jnp.maximum(place - plan.attn, 0)

    gain_attn, gain_ffn, gain_ssm, conv_bias, conv_weight, a_log, dt_bias, d_skip = split_vectors(
        vectors
    )
    in_own = spread(in_slabs(plan, w_in.astype(low)))
    up_own = spread(up_slabs(plan, w_up.astype(low)))
    mix_own = lax.all_gather(w_mix.astype(low), "wshard", axis=0, tiled=True)
    down_own = lax.all_gather(w_down.astype(low), "wshard", axis=0, tiled=True)

    own = lambda a, size, axis=0: lax.dynamic_slice_in_dim(a, space * size, size, axis)
    gain_own = own(gain_ssm, R)
    W = plan.T - R
    conv = jnp.concatenate(
        [
            jnp.concatenate([own(conv_weight, R, 1), conv_weight[:, DSSM:]], axis=1),
            jnp.concatenate([own(conv_bias, R), conv_bias[DSSM:]])[None],
            jnp.zeros((8 - CONV - 1, W), jnp.float32),
        ]
    )
    heads = jnp.stack([own(v, hm) for v in (a_log, dt_bias, d_skip)])
    heads = jnp.pad(heads, ((0, 5), (0, PAD - hm)))
    tables = rope_tables(count * inputs.shape[1])

    source = inputs[0].astype(jnp.float32)
    whole = gather_ctx(inputs[0]).astype(jnp.float32)
    upstream_all = gather_ctx(cotangent[0])
    length = whole.shape[0]
    normed = rms_norm(whole, gain_attn).astype(low)
    proj = plain(normed, in_own)

    def space_ahead(proj):
        return space_fwd(plan, proj, conv, heads)

    def attn_ahead(proj):
        made = attn_fwd(plan, proj, tables)
        blank = jnp.zeros((length // CHUNK, NS, R), low)
        return made, jnp.zeros_like(made), blank

    made, raw_made, before = lax.cond(is_space, space_ahead, attn_ahead, proj)
    square = jnp.where(is_space, jnp.sum(made * made, axis=1), 0.0)
    factor = lax.rsqrt(lax.psum(square, "ctx") / DSSM + norm_eps)
    mixed = jnp.where(is_space, made * factor[:, None] * gain_own, made).astype(low)
    middle = source + scatter_ctx(plain(mixed, mix_own))

    normed_two, two_pull = jax.vjp(rms_norm, middle, gain_ffn)
    two_all = gather_ctx(normed_two.astype(low))
    gate_up = plain(two_all, up_own)
    half = FF // count
    swiglu = lambda g: jax.nn.silu(g[:, :half]) * g[:, half:]
    activated, act_pull = jax.vjp(swiglu, gate_up)
    activated = activated.astype(low)
    outputs = (middle + scatter_ctx(plain(activated, down_own))).astype(low)[None]

    grad_down = rows_by_rows(activated, upstream_all)
    grad_act = cols_by_cols(upstream_all, down_own)
    grad_gate_up = act_pull(grad_act)[0].astype(low)
    grad_up = rows_by_rows(two_all, grad_gate_up)
    grad_two = scatter_ctx(cols_by_cols(grad_gate_up, up_own))
    grad_mid, grad_gain_ffn = two_pull(grad_two)
    grad_middle = cotangent[0].astype(jnp.float32) + grad_mid

    branch_all = gather_ctx(grad_middle.astype(low))
    grad_mix = rows_by_rows(mixed, branch_all)
    grad_made = cols_by_cols(branch_all, mix_own).astype(low)
    wide = grad_made.astype(jnp.float32)
    dots = jnp.where(is_space, jnp.sum(wide * gain_own * made, axis=1), 0.0)
    dots = lax.psum(dots, "ctx")
    grad_gain_own = jnp.sum(wide * made * factor[:, None], axis=0)
    grad_gated = wide * gain_own * factor[:, None] - made * (factor**3 * dots / DSSM)[:, None]

    def space_back(proj, grad_gated, grad_made):
        return space_bwd(plan, proj, conv, heads, grad_gated, raw_made, before)

    def attn_back(proj, grad_gated, grad_made):
        blank = lambda k: jnp.zeros((8, k), jnp.float32)
        return attn_bwd(plan, proj, tables, grad_made), blank(W), blank(PAD), blank(R)

    grad_proj, conv_acc, head_acc, skip_acc = lax.cond(
        is_space, space_back, attn_back, proj, grad_gated, grad_made
    )
    grad_normed = scatter_ctx(cols_by_cols(grad_proj, in_own))
    grad_in = rows_by_rows(normed, grad_proj)

    pull_source = jax.vjp(rms_norm, source, gain_attn)[1]
    grad_source, grad_gain_attn = pull_source(grad_normed)
    input_grad = (grad_middle + grad_source)[None]

    in_shard = from_slabs(plan, collect(grad_in, count, ways))
    up_shard = up_from_slabs(plan, collect(grad_up, count, ways))
    mix_shard = lax.psum_scatter(
        grad_mix.astype(low), "wshard", scatter_dimension=0, tiled=True
    ).astype(jnp.float32)
    down_shard = lax.psum_scatter(
        grad_down.astype(low), "wshard", scatter_dimension=0, tiled=True
    ).astype(jnp.float32)

    def placed(piece, size, total, axis=0):
        shape = list(piece.shape)
        shape[axis] = total
        start = [0] * piece.ndim
        start[axis] = space * size
        return lax.dynamic_update_slice(jnp.zeros(shape, piece.dtype), piece, start)

    conv_w_grad, conv_b_grad = conv_acc[:CONV], conv_acc[CONV]
    a_grad, bias_grad = head_acc[0, :hm], head_acc[1, :hm]
    skip_grad = jnp.sum(skip_acc[0].reshape(hm, MP), axis=1)
    grad_gain_own = jnp.where(is_space, grad_gain_own, 0.0)
    vector_local = jnp.concatenate(
        [
            grad_gain_attn,
            grad_gain_ffn,
            placed(grad_gain_own, R, DSSM),
            placed(conv_b_grad[:R], R, DSSM),
            conv_b_grad[R:],
            jnp.concatenate(
                [placed(conv_w_grad[:, :R], R, DSSM, 1), conv_w_grad[:, R:]], axis=1
            ).reshape(CONV * CONVCH),
            placed(a_grad, hm, MH),
            placed(bias_grad, hm, MH),
            placed(skip_grad, hm, MH),
        ]
    )
    vector_grad = lax.psum(vector_local, ("ctx", "wshard"))
    new_in = adamw(w_in, w_in_m, w_in_v, in_shard, 2.0 * D ** (-0.5), decay_weight)
    new_mix = adamw(w_mix, w_mix_m, w_mix_v, mix_shard, DSSM ** (-0.5), decay_weight)
    new_up = adamw(w_up, w_up_m, w_up_v, up_shard, D ** (-0.5), decay_weight)
    new_down = adamw(w_down, w_down_m, w_down_v, down_shard, FF ** (-0.5), decay_weight)
    new_vec = adamw(vectors, vectors_m, vectors_v, vector_grad, vector_rate, 0.0)
    return (outputs, input_grad, *new_in, *new_mix, *new_up, *new_down, *new_vec)


def solution(mesh):
    tokens = P("wshard", "ctx", None)
    weight = P(("ctx", "wshard"), None)
    return jax.shard_map(
        body,
        mesh=mesh,
        in_specs=(tokens,) * 2 + (weight,) * 12 + (P(),) * 3,
        out_specs=(tokens,) * 2 + (weight,) * 12 + (P(),) * 3,
        check_vma=False,
    )
```

```python
import functools
import math

import jax
import jax.numpy as jnp
from jax import lax
from jax.experimental import pallas as pl
from jax.experimental.pallas import tpu as pltpu
from jax.sharding import PartitionSpec as P

D = 2048
FF = 4096
AH = 8
KVH = 2
HD = 128
MH = 48
MP = 64
NS = 256
CONV = 4
STEP = 10
DSSM = 3072
CONVCH = 3584
ATT = AH * HD
MIXIN = ATT + DSSM
GROUP = AH // KVH
CHUNK = 128
PAD = 128
VMEM = 48 * 1024 * 1024


norm_eps = 1e-05
rope_base = 10000.0
beta_one = 0.9
beta_two = 0.95
adam_eps = 1e-08
decay_weight = 0.1
vector_rate = 0.5
masked_score = -1e30

K_AT = ATT
V_AT = K_AT + KVH * HD
Z_AT = V_AT + KVH * HD
X_AT = Z_AT + DSSM
BC_AT = X_AT + DSSM
DT_AT = BC_AT + 2 * NS
END = DT_AT + MH


def rows_by_rows(left, right):
    return lax.dot_general(
        left, right, (((0,), (0,)), ((), ())), preferred_element_type=jnp.float32
    )


def cols_by_cols(left, right):
    return lax.dot_general(
        left, right, (((1,), (1,)), ((), ())), preferred_element_type=jnp.float32
    )


def plain(left, right):
    return jnp.dot(left, right, preferred_element_type=jnp.float32)


def rms_norm(values, gain):
    factor = lax.rsqrt(jnp.mean(values * values, axis=-1, keepdims=True) + norm_eps)
    return values * factor * gain


def split_vectors(vectors):
    extents = (D, D, DSSM, CONVCH, CONV * CONVCH, MH, MH, MH)
    pieces = []
    offset = 0
    for extent in extents:
        pieces.append(lax.slice_in_dim(vectors, offset, offset + extent))
        offset = offset + extent
    pieces[4] = pieces[4].reshape(CONV, CONVCH)
    return pieces


def adamw(weight, moment, second, grad, rate, decay):
    moment = beta_one * moment + (1.0 - beta_one) * grad
    second = beta_two * second + (1.0 - beta_two) * grad * grad
    corrected = moment / (1.0 - beta_one**STEP)
    divisor = jnp.sqrt(second / (1.0 - beta_two**STEP)) + adam_eps
    return (weight - rate * (corrected / divisor + decay * weight), moment, second)


class Plan:
    def __init__(self, count):
        self.count = count
        self.R = MIXIN // count
        self.attn = ATT // self.R
        self.ha = self.R // HD
        self.hm = self.R // MP
        self.S = 2 * self.R + 2 * NS + PAD
        self.B = self.R
        self.C = 2 * self.R
        self.T = 2 * self.R + 2 * NS

    def kv_of(self, c):
        return c * self.ha // GROUP


def in_slabs(plan, w):
    R = plan.R
    slabs = []
    blank = lambda k: jnp.zeros((w.shape[0], k), w.dtype)
    for c in range(plan.count):
        if c < plan.attn:
            g = plan.kv_of(c)
            parts = [
                w[:, c * R : (c + 1) * R],
                blank(R),
                w[:, K_AT + g * HD : K_AT + (g + 1) * HD],
                w[:, V_AT + g * HD : V_AT + (g + 1) * HD],
                blank(2 * NS - 2 * HD + PAD),
            ]
        else:
            j = c - plan.attn
            parts = [
                w[:, Z_AT + j * R : Z_AT + (j + 1) * R],
                w[:, X_AT + j * R : X_AT + (j + 1) * R],
                w[:, BC_AT:DT_AT],
                w[:, DT_AT + j * plan.hm : DT_AT + (j + 1) * plan.hm],
                blank(PAD - plan.hm),
            ]
        slabs.append(jnp.concatenate(parts, axis=1))
    return jnp.stack(slabs)


def from_slabs(plan, slabs):
    R, C, T = plan.R, plan.C, plan.T
    slabs = slabs.astype(jnp.float32)
    heads = range(plan.attn)
    spaces = range(plan.attn, plan.count)
    total = lambda items: functools.reduce(lambda a, b: a + b, items)
    parts = [slabs[c][:, :R] for c in heads]
    for at in (C, C + HD):
        for g in range(KVH):
            parts.append(total([slabs[c][:, at : at + HD] for c in heads if plan.kv_of(c) == g]))
    parts += [slabs[c][:, :R] for c in spaces]
    parts += [slabs[c][:, R : 2 * R] for c in spaces]
    parts.append(total([slabs[c][:, C:T] for c in spaces]))
    parts += [slabs[c][:, T : T + plan.hm] for c in spaces]
    return jnp.concatenate(parts, axis=1)


def up_slabs(plan, w):
    G = FF // plan.count
    return jnp.stack(
        [
            jnp.concatenate([w[:, c * G : (c + 1) * G], w[:, FF + c * G : FF + (c + 1) * G]], axis=1)
            for c in range(plan.count)
        ]
    )


def up_from_slabs(plan, slabs):
    G = FF // plan.count
    slabs = slabs.astype(jnp.float32)
    return jnp.concatenate(
        [slabs[c][:, :G] for c in range(plan.count)] + [slabs[c][:, G:] for c in range(plan.count)],
        axis=1,
    )


def gather_ctx(x):
    return lax.all_gather(x, "ctx", axis=0, tiled=True)


def scatter_ctx(x):
    return lax.psum_scatter(
        x.astype(jnp.bfloat16), "ctx", scatter_dimension=0, tiled=True
    ).astype(jnp.float32)


MESH = pl.DeviceIdType.MESH


def here():
    c, w = lax.axis_index("ctx"), lax.axis_index("wshard")
    return c, w, w + 1 - 2 * (w % 2), (w + 2) % 4


def greet(devices):
    barrier = pltpu.get_barrier_semaphore()
    for device in devices:
        pl.semaphore_signal(barrier, inc=1, device_id=device, device_id_type=MESH)
    pl.semaphore_wait(barrier, len(devices))


def remote(src, dst, send, recv, device):
    return pltpu.make_async_remote_copy(
        src_ref=src, dst_ref=dst, send_sem=send, recv_sem=recv, device_id=device, device_id_type=MESH
    )


def spread_kernel(n, kinds, *refs):
    k = len(kinds)
    sources, targets, sems = refs[:k], refs[k : 2 * k], refs[2 * k :]
    c, w, sib, across = here()
    peers = [(c + s) % n for s in range(1, n)]
    greet([(p, w) for p in peers] + [(c, sib), (c, across)])
    pending = []
    jobs = []
    for kind, src, dst, j in zip(kinds, sources, targets, range(k)):
        a_send, a_recv, x_send, x_recv, k_send, k_recv, own_sem = sems[7 * j : 7 * j + 7]
        many = kind == "cols"
        count = n if many else 1
        mine = src.at[c] if many else src
        own = pltpu.make_async_copy(mine, dst.at[c if many else 0, w], own_sem)
        own.start()
        jobs.append((many, count, mine, dst, a_send, a_recv, x_send, x_recv, k_send, k_recv, own))
    for many, count, mine, dst, _, _, x_send, x_recv, k_send, k_recv, own in jobs:
        at = c if many else 0
        to_x = remote(mine, dst.at[at, w], x_send.at[0], x_recv.at[at], (c, across))
        to_k = remote(mine, dst.at[at, w], k_send.at[0, 0], k_recv.at[0, at], (c, sib))
        to_x.start()
        to_k.start()
        pending += [to_x, to_k]
    for s in range(1, n):
        for src, job in zip(sources, jobs):
            many, _, _, dst, a_send, a_recv = job[:6]
            if many:
                p = (c + s) % n
                out = remote(src.at[p], dst.at[c, w], a_send.at[s], a_recv.at[c], (p, w))
                out.start()
                pending.append(out)

    def pass_on(job, s):
        many, _, _, dst, _, _, x_send, x_recv, k_send, k_recv, _ = job
        q = (c + n - s) % n if many else 0
        got = dst.at[q, across]
        remote(got, got, x_send.at[s], x_recv.at[q], (c, across)).wait_recv()
        out = remote(got, got, k_send.at[1, s], k_recv.at[1, q], (c, sib))
        out.start()
        pending.append(out)

    for s in range(1, n):
        for job in jobs:
            many, _, _, dst, a_send, a_recv, x_send, x_recv, k_send, k_recv, _ = job
            if many:
                q = (c + n - s) % n
                got = dst.at[q, w]
                remote(got, got, a_send.at[s], a_recv.at[q], (q, w)).wait_recv()
                to_x = remote(got, got, x_send.at[s], x_recv.at[q], (c, across))
                to_k = remote(got, got, k_send.at[0, s], k_recv.at[0, q], (c, sib))
                to_x.start()
                to_k.start()
                pending += [to_x, to_k]
        for job in jobs:
            if job[0] or s == 1:
                pass_on(job, s - 1)
    for job in jobs:
        if job[0]:
            pass_on(job, n - 1)
    for job in jobs:
        _, count, _, dst, _, _, _, _, k_send, k_recv, own = job
        for q in range(count):
            for half, place in ((0, sib), (1, (sib + 2) % 4)):
                got = dst.at[q, place]
                remote(got, got, k_send.at[half, 0], k_recv.at[half, q], (c, sib)).wait_recv()
        own.wait()
    for out in pending:
        out.wait_send()


def spread(n, kinds, sources, collective_id):
    shapes, sems = [], []
    for kind, src in zip(kinds, sources):
        count = n if kind == "cols" else 1
        shapes.append(jax.ShapeDtypeStruct((count, 4) + src.shape[-2:], src.dtype))
        sems += [
            pltpu.SemaphoreType.DMA((count,)),
            pltpu.SemaphoreType.DMA((count,)),
            pltpu.SemaphoreType.DMA((count,)),
            pltpu.SemaphoreType.DMA((count,)),
            pltpu.SemaphoreType.DMA((2, count)),
            pltpu.SemaphoreType.DMA((2, count)),
            pltpu.SemaphoreType.DMA,
        ]
    sent = sum(math.prod(s.shape) * 2 for s in shapes)
    outs = pl.pallas_call(
        functools.partial(spread_kernel, n, tuple(kinds)),
        out_shape=tuple(shapes),
        in_specs=[pl.BlockSpec(memory_space=pl.ANY)] * len(kinds),
        out_specs=tuple(pl.BlockSpec(memory_space=pl.ANY) for _ in kinds),
        scratch_shapes=sems,
        cost_estimate=pl.CostEstimate(flops=0, bytes_accessed=16 * sent, transcendentals=0),
        compiler_params=pltpu.CompilerParams(
            collective_id=collective_id, has_side_effects=True, vmem_limit_bytes=VMEM
        ),
    )(*sources)
    return [o.reshape(-1, o.shape[-1]) for o in outs]


def collect_kernel(n, kinds, *refs):
    k = len(kinds)
    sources, targets = refs[:k], refs[k : 2 * k]
    extra = refs[2 * k :]
    c, w, sib, across = here()
    x, core = w // 2, w % 2
    far = 1 - x
    away = any(kind == "cols" for kind in kinds)
    greet(
        ([(((c + s) % n), w) for s in range(1, n)] if away else []) + [(c, sib), (c, across)]
    )
    pending = []
    jobs = []
    for j, kind in enumerate(kinds):
        jobs.append((kind, sources[j], targets[j]) + tuple(extra[10 * j : 10 * j + 10]))

    def order(job, s):
        return (c + s) % n if job[1].shape[0] > 1 else 0

    def count(job):
        return job[1].shape[0]

    most = max(count(job) for job in jobs)
    steps = [s % most for s in range(1, most + 1)]
    for place, slot in ((far, 0), (x, 1)):
        for s in steps:
            for job in jobs:
                if s >= count(job):
                    continue
                _, src, _, kbuf, _, _, _, k_send, k_recv = job[:9]
                q = order(job, s)
                out = remote(
                    src.at[q, place * 2 + 1 - core],
                    kbuf.at[slot, q],
                    k_send.at[slot, s],
                    k_recv.at[slot, q],
                    (c, sib),
                )
                out.start()
                pending.append(out)
    wide = jnp.float32
    for s in steps:
        for job in jobs:
            if s >= count(job):
                continue
            _, src, _, kbuf, stage, xbuf, _, k_send, k_recv, x_send, x_recv = job[:11]
            q = order(job, s)
            got = kbuf.at[0, q]
            remote(got, got, k_send.at[0, s], k_recv.at[0, q], (c, sib)).wait_recv()
            stage[q] = (src[q, far * 2 + core].astype(wide) + kbuf[0, q].astype(wide)).astype(
                stage.dtype
            )
            out = remote(stage.at[q], xbuf.at[q], x_send.at[s], x_recv.at[q], (c, across))
            out.start()
            pending.append(out)
    for s in steps:
        for job in jobs:
            if s >= count(job):
                continue
            kind, src, dst, kbuf, stage, xbuf, done, k_send, k_recv, x_send, x_recv = job[:11]
            a_send, a_recv = job[11], job[12]
            q = order(job, s)
            got = kbuf.at[1, q]
            remote(got, got, k_send.at[1, s], k_recv.at[1, q], (c, sib)).wait_recv()
            got = xbuf.at[q]
            remote(got, got, x_send.at[s], x_recv.at[q], (c, across)).wait_recv()
            total = src[q, x * 2 + core].astype(wide) + kbuf[1, q].astype(wide)
            total = (total + xbuf[q].astype(wide)).astype(stage.dtype)
            if kind == "cols" and s > 0:
                done[q] = total
                out = remote(done.at[q], dst.at[c], a_send.at[s], a_recv.at[c], (q, w))
                out.start()
                pending.append(out)
            else:
                dst[q] = total
    for job in jobs:
        if job[0] == "cols":
            dst, a_send, a_recv = job[2], job[11], job[12]
            for s in range(1, n):
                q = (c + n - s) % n
                got = dst.at[q]
                remote(got, got, a_send.at[s], a_recv.at[q], (q, w)).wait_recv()
    for out in pending:
        out.wait_send()


def collect(n, kinds, sources, collective_id):
    shapes, scratch = [], []
    for kind, src in zip(kinds, sources):
        count, _, rows, size = src.shape
        block = (count, rows, size)
        shapes.append(jax.ShapeDtypeStruct(block, src.dtype))
        scratch += [
            pltpu.VMEM((2,) + block, src.dtype),
            pltpu.VMEM(block, src.dtype),
            pltpu.VMEM(block, src.dtype),
            pltpu.VMEM(block if kind == "cols" else (1, 16, 128), src.dtype),
            pltpu.SemaphoreType.DMA((2, count)),
            pltpu.SemaphoreType.DMA((2, count)),
            pltpu.SemaphoreType.DMA((count,)),
            pltpu.SemaphoreType.DMA((count,)),
            pltpu.SemaphoreType.DMA((count,)),
            pltpu.SemaphoreType.DMA((count,)),
        ]
    sent = sum(math.prod(s.shape) * 2 for s in shapes)
    return pl.pallas_call(
        functools.partial(collect_kernel, n, tuple(kinds)),
        out_shape=tuple(shapes),
        in_specs=[pl.BlockSpec(memory_space=pltpu.VMEM)] * len(kinds),
        out_specs=tuple(pl.BlockSpec(memory_space=pltpu.VMEM) for _ in kinds),
        scratch_shapes=scratch,
        cost_estimate=pl.CostEstimate(flops=0, bytes_accessed=64 * sent, transcendentals=0),
        compiler_params=pltpu.CompilerParams(
            collective_id=collective_id, has_side_effects=True, vmem_limit_bytes=VMEM
        ),
    )(*sources)


def sum_kernel(n, over_all, x_ref, out_ref, kept, got, send, recv):
    c, w, sib, across = here()
    partners = [(c, sib), (c, across)] if over_all else []
    for level in range(n.bit_length() - 1):
        reach = 2**level
        partners.append((c + reach - 2 * reach * ((c // reach) % 2), w))
    greet(partners)
    total = x_ref[...]
    for i, partner in enumerate(partners):
        kept[i] = total
        swap = remote(kept.at[i], got.at[i], send.at[i], recv.at[i], partner)
        swap.start()
        swap.wait()
        total = total + got[i]
    out_ref[...] = total


def sum_over(n, over_all, x, collective_id):
    stages = n.bit_length() - 1 + (2 if over_all else 0)
    return pl.pallas_call(
        functools.partial(sum_kernel, n, over_all),
        out_shape=jax.ShapeDtypeStruct(x.shape, x.dtype),
        in_specs=[pl.BlockSpec(memory_space=pltpu.VMEM)],
        out_specs=pl.BlockSpec(memory_space=pltpu.VMEM),
        scratch_shapes=[
            pltpu.VMEM((stages,) + x.shape, x.dtype),
            pltpu.VMEM((stages,) + x.shape, x.dtype),
            pltpu.SemaphoreType.DMA((stages,)),
            pltpu.SemaphoreType.DMA((stages,)),
        ],
        compiler_params=pltpu.CompilerParams(
            collective_id=collective_id, has_side_effects=True, vmem_limit_bytes=VMEM
        ),
    )(x)


def sum_rows(n, x, collective_id):
    return sum_over(n, False, x.reshape(-1, 128), collective_id).reshape(x.shape)


def sum_vector(n, x, collective_id):
    size = x.shape[0]
    padded = -(-size // 1024) * 1024
    wide = jnp.pad(x, (0, padded - size)).reshape(-1, 128)
    return sum_over(n, True, wide, collective_id).reshape(-1)[:size]


def mm(left, right):
    return jnp.dot(
        left.astype(jnp.bfloat16), right.astype(jnp.bfloat16), preferred_element_type=jnp.float32
    )


def mm_nt(left, right):
    return cols_by_cols(left.astype(jnp.bfloat16), right.astype(jnp.bfloat16))


def mm_tn(left, right):
    return rows_by_rows(left.astype(jnp.bfloat16), right.astype(jnp.bfloat16))


def exact(left, right):
    return jnp.dot(
        left, right, precision=lax.Precision.HIGHEST, preferred_element_type=jnp.float32
    )


def iota(shape, axis):
    return lax.broadcasted_iota(jnp.int32, shape, axis)


def rope_tables(length):
    half = HD // 2
    frequency = rope_base ** (-jnp.arange(half, dtype=jnp.float32) / half)
    angles = jnp.arange(length).astype(jnp.float32)[:, None] * frequency[None, :]
    cosine, sine = jnp.cos(angles), jnp.sin(angles)
    return (
        jnp.concatenate([cosine, cosine], axis=1),
        jnp.concatenate([-sine, sine], axis=1),
    )


def turned(values, cosine, sine):
    return values * cosine + pltpu.roll(values, HD // 2, 1) * sine


def attn_stack(plan, q_ref, cosine, sine):
    heads = [
        turned(q_ref[:, h * HD : (h + 1) * HD], cosine, sine).astype(jnp.bfloat16)
        for h in range(plan.ha)
    ]
    return jnp.concatenate(heads, axis=0)


def attn_softmax(stack, keys, at):
    scores = cols_by_cols(stack, keys) * (1.0 / math.sqrt(HD))
    row = iota(scores.shape, 0) & (CHUNK - 1)
    scores = jnp.where(iota(scores.shape, 1) <= row + at, scores, masked_score)
    weights = jnp.exp(scores - jnp.max(scores, axis=1, keepdims=True))
    return weights * (1.0 / jnp.sum(weights, axis=1, keepdims=True))


def attn_fwd_kernel(plan, q_ref, kv_ref, cos_ref, sin_ref, out_ref, keys, values):
    step = pl.program_id(0)

    @pl.when(step == 0)
    def _():
        keys[...] = turned(kv_ref[:, :HD], cos_ref[...], sin_ref[...]).astype(jnp.bfloat16)
        values[...] = kv_ref[:, HD : 2 * HD].astype(jnp.bfloat16)

    at = pl.multiple_of(step * CHUNK, CHUNK)
    rows = pl.ds(at, CHUNK)
    stack = attn_stack(plan, q_ref, cos_ref[rows, :], sin_ref[rows, :])
    probs = attn_softmax(stack, keys[...], at)
    made = mm(probs, values[...])
    for h in range(plan.ha):
        out_ref[:, h * HD : (h + 1) * HD] = made[h * CHUNK : (h + 1) * CHUNK]


def attn_fwd(plan, proj, tables):
    length = proj.shape[0]
    whole = lambda i: (0, 0)
    return pl.pallas_call(
        functools.partial(attn_fwd_kernel, plan),
        grid=(length // CHUNK,),
        out_shape=jax.ShapeDtypeStruct((length, plan.R), jnp.float32),
        in_specs=[
            pl.BlockSpec((CHUNK, plan.R), lambda i: (i, 0)),
            pl.BlockSpec((length, 2 * HD), lambda i: (0, plan.C // (2 * HD))),
            pl.BlockSpec((length, HD), whole),
            pl.BlockSpec((length, HD), whole),
        ],
        out_specs=pl.BlockSpec((CHUNK, plan.R), lambda i: (i, 0)),
        scratch_shapes=[pltpu.VMEM((length, HD), jnp.bfloat16)] * 2,
        compiler_params=pltpu.CompilerParams(vmem_limit_bytes=VMEM),
    )(proj, proj, *tables)


def attn_bwd_kernel(
    plan, q_ref, kv_ref, cos_ref, sin_ref, grad_ref, slab_ref, keys, values, grad_k, grad_v
):
    step = pl.program_id(0)
    scale = 1.0 / math.sqrt(HD)

    @pl.when(step == 0)
    def _():
        keys[...] = turned(kv_ref[:, :HD], cos_ref[...], sin_ref[...]).astype(jnp.bfloat16)
        values[...] = kv_ref[:, HD : 2 * HD].astype(jnp.bfloat16)
        grad_k[...] = jnp.zeros_like(grad_k)
        grad_v[...] = jnp.zeros_like(grad_v)
        slab_ref[...] = jnp.zeros_like(slab_ref)

    at = pl.multiple_of(step * CHUNK, CHUNK)
    rows = pl.ds(at, CHUNK)
    cosine, sine = cos_ref[rows, :], sin_ref[rows, :]
    stack = attn_stack(plan, q_ref, cosine, sine)
    probs = attn_softmax(stack, keys[...], at)
    grads = jnp.concatenate([grad_ref[:, h * HD : (h + 1) * HD] for h in range(plan.ha)], axis=0)
    grad_probs = cols_by_cols(grads, values[...])
    delta = jnp.sum(probs * grad_probs, axis=1, keepdims=True)
    grad_scores = (probs * (grad_probs - delta)).astype(jnp.bfloat16)
    grad_q = mm(grad_scores, keys[...]) * scale
    for h in range(plan.ha):
        slab_ref[rows, h * HD : (h + 1) * HD] = turned(
            grad_q[h * CHUNK : (h + 1) * CHUNK], cosine, -sine
        ).astype(jnp.bfloat16)
    grad_k[...] += mm_tn(grad_scores, stack)
    grad_v[...] += mm_tn(probs, grads)

    @pl.when(step == pl.num_programs(0) - 1)
    def _():
        slab_ref[:, plan.C : plan.C + HD] = turned(
            grad_k[...] * scale, cos_ref[...], -sin_ref[...]
        ).astype(jnp.bfloat16)
        slab_ref[:, plan.C + HD : plan.C + 2 * HD] = grad_v[...].astype(jnp.bfloat16)


def attn_bwd(plan, proj, tables, grad):
    length = proj.shape[0]
    whole = lambda i: (0, 0)
    return pl.pallas_call(
        functools.partial(attn_bwd_kernel, plan),
        grid=(length // CHUNK,),
        out_shape=jax.ShapeDtypeStruct((length, plan.S), jnp.bfloat16),
        in_specs=[
            pl.BlockSpec((CHUNK, plan.R), lambda i: (i, 0)),
            pl.BlockSpec((length, 2 * HD), lambda i: (0, plan.C // (2 * HD))),
            pl.BlockSpec((length, HD), whole),
            pl.BlockSpec((length, HD), whole),
            pl.BlockSpec((CHUNK, plan.R), lambda i: (i, 0)),
        ],
        out_specs=pl.BlockSpec((length, plan.S), whole),
        scratch_shapes=[pltpu.VMEM((length, HD), jnp.bfloat16)] * 2
        + [pltpu.VMEM((length, HD), jnp.float32)] * 2,
        compiler_params=pltpu.CompilerParams(vmem_limit_bytes=VMEM),
    )(proj, proj, *tables, grad)


def head_spread(plan):
    return ((iota((PAD, plan.R), 1) >> 6) == iota((PAD, plan.R), 0)).astype(jnp.float32)


def head_gather(plan):
    return ((iota((plan.R, PAD), 0) >> 6) == iota((plan.R, PAD), 1)).astype(jnp.float32)


def lower_ones():
    shape = (CHUNK, CHUNK)
    return (iota(shape, 0) >= iota(shape, 1)).astype(jnp.float32)


def space_parts(plan, dt_raw, window, conv_ref, head_ref):
    total = conv_ref[4:5, :]
    for k in range(CONV):
        at = 8 - CONV + 1 + k
        total = total + conv_ref[k : k + 1, :] * window[at : at + CHUNK, :]
    raw = dt_raw + head_ref[1:2, :]
    steps = jnp.maximum(raw, 0.0) + jnp.log1p(jnp.exp(-jnp.abs(raw)))
    logs = -steps * jnp.exp(head_ref[0:1, :])
    cumul = exact(lower_ones(), logs)
    return total, raw, steps, logs, cumul


def decay_of(cumul, cumul_t, causal, h):
    gaps = cumul[:, h : h + 1] - cumul_t[h : h + 1, :]
    return jnp.exp(jnp.where(causal, gaps, masked_score))


def space_fwd_kernel(plan, proj_ref, conv_ref, head_ref, gated_ref, made_ref, before_ref, state, window):
    R = plan.R
    step = pl.program_id(0)

    @pl.when(step == 0)
    def _():
        state[...] = jnp.zeros_like(state)
        window[0:8, :] = jnp.zeros((8, window.shape[1]), jnp.float32)

    @pl.when(step > 0)
    def _():
        window[0:8, :] = window[CHUNK : CHUNK + 8, :]

    window[8 : CHUNK + 8, :] = proj_ref[:, R : plan.T]
    total, _, steps, _, cumul = space_parts(
        plan, proj_ref[:, plan.T : plan.T + PAD], window, conv_ref, head_ref
    )
    post = total * jax.nn.sigmoid(total)
    x = post[:, :R]
    b = post[:, R : R + NS].astype(jnp.bfloat16)
    c = post[:, R + NS :].astype(jnp.bfloat16)
    spread_heads = head_spread(plan)
    cumul_t = cumul.T
    last = cumul[CHUNK - 1 : CHUNK, :]
    tail = jnp.exp(last - cumul)
    weighted = x * exact(steps, spread_heads)
    causal = iota((CHUNK, CHUNK), 0) >= iota((CHUNK, CHUNK), 1)
    inner = cols_by_cols(c, b)
    before = state[...]
    before_ref[0] = before.astype(jnp.bfloat16)
    made = mm(c, before) * exact(jnp.exp(cumul), spread_heads)
    made = made + exact(jnp.broadcast_to(head_ref[2:3, :], (8, PAD)), spread_heads)[0:1] * x
    left = iota((CHUNK, 2 * MP), 1) < MP
    weighted_low = weighted.astype(jnp.bfloat16)
    intra = []
    for pair in range(plan.hm // 2):
        lanes = weighted_low[:, pair * 2 * MP : (pair + 1) * 2 * MP]
        one = mm(inner * decay_of(cumul, cumul_t, causal, 2 * pair), lanes)
        two = mm(inner * decay_of(cumul, cumul_t, causal, 2 * pair + 1), lanes)
        intra.append(jnp.where(left, one, two))
    made = made + jnp.concatenate(intra, axis=1)
    state[...] = before * exact(
        jnp.broadcast_to(jnp.exp(last), (8, PAD)), spread_heads
    )[0:1] + mm_tn(b, weighted * exact(tail, spread_heads))
    z = proj_ref[:, :R]
    made_ref[...] = made
    gated_ref[...] = made * (z * jax.nn.sigmoid(z))


def space_fwd(plan, proj, conv, heads):
    length = proj.shape[0]
    chunks = length // CHUNK
    W = plan.T - plan.R
    whole = lambda i: (0, 0)
    rows = lambda i: (i, 0)
    return pl.pallas_call(
        functools.partial(space_fwd_kernel, plan),
        grid=(chunks,),
        out_shape=(
            jax.ShapeDtypeStruct((length, plan.R), jnp.float32),
            jax.ShapeDtypeStruct((length, plan.R), jnp.float32),
            jax.ShapeDtypeStruct((chunks, NS, plan.R), jnp.bfloat16),
        ),
        in_specs=[
            pl.BlockSpec((CHUNK, plan.S), rows),
            pl.BlockSpec((8, W), whole),
            pl.BlockSpec((8, PAD), whole),
        ],
        out_specs=(
            pl.BlockSpec((CHUNK, plan.R), rows),
            pl.BlockSpec((CHUNK, plan.R), rows),
            pl.BlockSpec((1, NS, plan.R), lambda i: (i, 0, 0)),
        ),
        scratch_shapes=[
            pltpu.VMEM((NS, plan.R), jnp.float32),
            pltpu.VMEM((CHUNK + 8, W), jnp.float32),
        ],
        compiler_params=pltpu.CompilerParams(vmem_limit_bytes=VMEM),
    )(proj, conv, heads)


def space_bwd_kernel(
    plan, proj_ref, prev_ref, conv_ref, head_ref, grad_ref, made_ref, before_ref,
    slab_ref, conv_acc, head_acc, skip_acc, d_state, window, d_window,
):
    R, T = plan.R, plan.T
    step = pl.program_id(0)
    chunk = pl.num_programs(0) - 1 - step

    @pl.when(step == 0)
    def _():
        d_state[...] = jnp.zeros_like(d_state)
        d_window[CHUNK : CHUNK + 8, :] = jnp.zeros((8, T - R), jnp.float32)
        conv_acc[...] = jnp.zeros_like(conv_acc)
        head_acc[...] = jnp.zeros_like(head_acc)
        skip_acc[...] = jnp.zeros_like(skip_acc)

    @pl.when(step > 0)
    def _():
        d_window[CHUNK : CHUNK + 8, :] = d_window[0:8, :]

    window[0:8, :] = jnp.where(chunk == 0, 0.0, prev_ref[:, R:T])
    window[8 : CHUNK + 8, :] = proj_ref[:, R:T]
    total, raw, steps, logs, cumul = space_parts(
        plan, proj_ref[:, T : T + PAD], window, conv_ref, head_ref
    )
    sig = jax.nn.sigmoid(total)
    post = total * sig
    x = post[:, :R]
    b = post[:, R : R + NS].astype(jnp.bfloat16)
    c = post[:, R + NS :].astype(jnp.bfloat16)
    spread_heads = head_spread(plan)
    gather_heads = head_gather(plan)
    cumul_t = cumul.T
    last = cumul[CHUNK - 1 : CHUNK, :]
    steps_wide = exact(steps, spread_heads)
    tail_wide = exact(jnp.exp(last - cumul), spread_heads)
    grow_wide = exact(jnp.exp(cumul), spread_heads)
    last_wide = exact(jnp.broadcast_to(jnp.exp(last), (8, PAD)), spread_heads)[0:1]
    skip_wide = exact(jnp.broadcast_to(head_ref[2:3, :], (8, PAD)), spread_heads)[0:1]
    weighted = x * steps_wide
    causal = iota((CHUNK, CHUNK), 0) >= iota((CHUNK, CHUNK), 1)
    inner = cols_by_cols(c, b)

    z = proj_ref[:, :R]
    sig_z = jax.nn.sigmoid(z)
    grad = grad_ref[...]
    d_made = grad * (z * sig_z)
    slab_ref[:, :R] = (grad * made_ref[...] * (sig_z * (1.0 + z * (1.0 - sig_z)))).astype(
        jnp.bfloat16
    )
    skip_acc[0:1, :] += jnp.sum(d_made * x, axis=0, keepdims=True)

    before = before_ref[0]
    d_after = d_state[...]
    d_after_low = d_after.astype(jnp.bfloat16)
    grown = d_made * grow_wide
    grown_low = grown.astype(jnp.bfloat16)
    carried = mm(c, before)
    d_c = mm_nt(grown_low, before)
    pulled = weighted * tail_wide
    d_pulled = mm(b, d_after_low)
    d_b = mm_nt(pulled, d_after_low)
    d_cumul = exact(grown * carried, gather_heads)
    kept = exact(d_pulled * pulled, gather_heads)
    d_cumul = d_cumul - kept
    decayed = jnp.sum(d_after * before.astype(jnp.float32), axis=0, keepdims=True) * last_wide
    d_last = jnp.sum(kept, axis=0, keepdims=True) + exact(
        jnp.broadcast_to(decayed, (8, R)), gather_heads
    )[0:1]
    d_state[...] = d_after * last_wide + mm_tn(c, grown_low)

    left = iota((CHUNK, 2 * MP), 1) < MP
    lane = iota((CHUNK, PAD), 1)
    sub = iota((8, CHUNK), 0)
    weighted_low = weighted.astype(jnp.bfloat16)
    d_made_low = d_made.astype(jnp.bfloat16)
    d_inner = jnp.zeros((CHUNK, CHUNK), jnp.float32)
    columns = jnp.zeros((8, CHUNK), jnp.float32)
    d_weighted = []
    for pair in range(plan.hm // 2):
        at = slice(pair * 2 * MP, (pair + 1) * 2 * MP)
        lanes, d_lanes = weighted_low[:, at], d_made_low[:, at]
        halves = []
        for which in range(2):
            h = 2 * pair + which
            decay = decay_of(cumul, cumul_t, causal, h)
            whole = inner * decay
            halves.append(mm_tn(whole, d_lanes))
            mine = jnp.where(left if which == 0 else ~left, d_lanes, jnp.zeros_like(d_lanes))
            d_whole = cols_by_cols(mine, lanes)
            d_inner = d_inner + d_whole * decay
            slope = d_whole * whole
            d_cumul = d_cumul + jnp.where(lane == h, jnp.sum(slope, axis=1, keepdims=True), 0.0)
            columns = columns + jnp.where(sub == h, jnp.sum(slope, axis=0, keepdims=True), 0.0)
        d_weighted.append(jnp.where(left, halves[0], halves[1]))
    d_weighted = jnp.concatenate(d_weighted, axis=1) + d_pulled * tail_wide
    columns = jnp.concatenate([columns, jnp.zeros((CHUNK - 8, CHUNK), jnp.float32)], axis=0).T
    d_cumul = d_cumul - columns
    d_inner_low = d_inner.astype(jnp.bfloat16)
    d_c = d_c + mm(d_inner_low, b)
    d_b = d_b + mm_tn(d_inner_low, c)
    d_x = d_weighted * steps_wide + skip_wide * d_made
    d_steps = exact(d_weighted * x, gather_heads)
    upper = (iota((CHUNK, CHUNK), 0) <= iota((CHUNK, CHUNK), 1)).astype(jnp.float32)
    d_logs = exact(upper, d_cumul) + d_last
    d_steps = d_steps - jnp.exp(head_ref[0:1, :]) * d_logs
    d_raw = d_steps * jax.nn.sigmoid(raw)
    slab_ref[:, T : T + PAD] = jnp.where(lane < plan.hm, d_raw, 0.0).astype(jnp.bfloat16)
    head_acc[0:1, :] += jnp.sum(d_logs * logs, axis=0, keepdims=True)
    head_acc[1:2, :] += jnp.sum(d_raw, axis=0, keepdims=True)

    d_post = jnp.concatenate([d_x, d_b, d_c], axis=1)
    d_total = d_post * (sig * (1.0 + total * (1.0 - sig)))
    d_window[0:CHUNK, :] = d_total
    d_xbc = jnp.zeros((CHUNK, T - R), jnp.float32)
    for k in range(CONV):
        shift = CONV - 1 - k
        d_xbc = d_xbc + conv_ref[k : k + 1, :] * d_window[shift : shift + CHUNK, :]
        at = 8 - CONV + 1 + k
        conv_acc[k : k + 1, :] += jnp.sum(
            d_total * window[at : at + CHUNK, :], axis=0, keepdims=True
        )
    conv_acc[4:5, :] += jnp.sum(d_total, axis=0, keepdims=True)
    slab_ref[:, R:T] = d_xbc.astype(jnp.bfloat16)


def space_bwd(plan, proj, conv, heads, grad, made, before):
    length = proj.shape[0]
    chunks = length // CHUNK
    W = plan.T - plan.R
    whole = lambda i: (0, 0)
    rows = lambda i: (chunks - 1 - i, 0)
    per = CHUNK // 8
    return pl.pallas_call(
        functools.partial(space_bwd_kernel, plan),
        grid=(chunks,),
        out_shape=(
            jax.ShapeDtypeStruct((length, plan.S), jnp.bfloat16),
            jax.ShapeDtypeStruct((8, W), jnp.float32),
            jax.ShapeDtypeStruct((8, PAD), jnp.float32),
            jax.ShapeDtypeStruct((8, plan.R), jnp.float32),
        ),
        in_specs=[
            pl.BlockSpec((CHUNK, plan.S), rows),
            pl.BlockSpec((8, plan.S), lambda i: (jnp.maximum((chunks - 1 - i) * per - 1, 0), 0)),
            pl.BlockSpec((8, W), whole),
            pl.BlockSpec((8, PAD), whole),
            pl.BlockSpec((CHUNK, plan.R), rows),
            pl.BlockSpec((CHUNK, plan.R), rows),
            pl.BlockSpec((1, NS, plan.R), lambda i: (chunks - 1 - i, 0, 0)),
        ],
        out_specs=(
            pl.BlockSpec((CHUNK, plan.S), rows),
            pl.BlockSpec((8, W), whole),
            pl.BlockSpec((8, PAD), whole),
            pl.BlockSpec((8, plan.R), whole),
        ),
        scratch_shapes=[
            pltpu.VMEM((NS, plan.R), jnp.float32),
            pltpu.VMEM((CHUNK + 8, W), jnp.float32),
            pltpu.VMEM((CHUNK + 8, W), jnp.float32),
        ],
        compiler_params=pltpu.CompilerParams(vmem_limit_bytes=VMEM),
    )(proj, proj, conv, heads, grad, made, before)


def body(
    inputs,
    cotangent,
    w_in,
    w_in_m,
    w_in_v,
    w_mix,
    w_mix_m,
    w_mix_v,
    w_up,
    w_up_m,
    w_up_v,
    w_down,
    w_down_m,
    w_down_v,
    vectors,
    vectors_m,
    vectors_v,
):
    low = jnp.bfloat16
    count = lax.axis_size("ctx")
    ways = lax.axis_size("wshard")
    place = lax.axis_index("ctx")
    plan = Plan(count)
    R, hm = plan.R, plan.hm
    is_space = place >= plan.attn
    space = jnp.maximum(place - plan.attn, 0)

    gain_attn, gain_ffn, gain_ssm, conv_bias, conv_weight, a_log, dt_bias, d_skip = split_vectors(
        vectors
    )
    in_own, mix_own = spread(
        count, ("cols", "rows"), (in_slabs(plan, w_in.astype(low)), w_mix.astype(low)), 1
    )

    own = lambda a, size, axis=0: lax.dynamic_slice_in_dim(a, space * size, size, axis)
    gain_own = own(gain_ssm, R)
    W = plan.T - R
    conv = jnp.concatenate(
        [
            jnp.concatenate([own(conv_weight, R, 1), conv_weight[:, DSSM:]], axis=1),
            jnp.concatenate([own(conv_bias, R), conv_bias[DSSM:]])[None],
            jnp.zeros((8 - CONV - 1, W), jnp.float32),
        ]
    )
    heads = jnp.stack([own(v, hm) for v in (a_log, dt_bias, d_skip)])
    heads = jnp.pad(heads, ((0, 5), (0, PAD - hm)))
    tables = rope_tables(count * inputs.shape[1])

    source = inputs[0].astype(jnp.float32)
    whole = gather_ctx(inputs[0]).astype(jnp.float32)
    upstream_all = gather_ctx(cotangent[0])
    length = whole.shape[0]
    normed = rms_norm(whole, gain_attn).astype(low)
    proj = plain(normed, in_own)

    def space_ahead(proj):
        return space_fwd(plan, proj, conv, heads)

    def attn_ahead(proj):
        made = attn_fwd(plan, proj, tables)
        blank = jnp.zeros((length // CHUNK, NS, R), low)
        return made, jnp.zeros_like(made), blank

    made, raw_made, before = lax.cond(is_space, space_ahead, attn_ahead, proj)
    square = jnp.where(is_space, jnp.sum(made * made, axis=1), 0.0)
    factor = lax.rsqrt(sum_rows(count, square, 5) / DSSM + norm_eps)
    mixed = jnp.where(is_space, made * factor[:, None] * gain_own, made).astype(low)
    branch = plain(mixed, mix_own).astype(low)
    branch, w_up_late, w_down_late = lax.optimization_barrier((branch, w_up, w_down))
    up_own, down_own = spread(
        count, ("cols", "rows"), (up_slabs(plan, w_up_late.astype(low)), w_down_late.astype(low)), 2
    )
    middle = source + scatter_ctx(branch)

    normed_two, two_pull = jax.vjp(rms_norm, middle, gain_ffn)
    two_all = gather_ctx(normed_two.astype(low))
    gate_up = plain(two_all, up_own)
    half = FF // count
    swiglu = lambda g: jax.nn.silu(g[:, :half]) * g[:, half:]
    activated, act_pull = jax.vjp(swiglu, gate_up)
    activated = activated.astype(low)
    outputs = (middle + scatter_ctx(plain(activated, down_own))).astype(low)[None]

    grad_down = rows_by_rows(activated, upstream_all)
    grad_act = cols_by_cols(upstream_all, down_own)
    grad_gate_up = act_pull(grad_act)[0].astype(low)
    grad_up = rows_by_rows(two_all, grad_gate_up)
    grad_two = scatter_ctx(cols_by_cols(grad_gate_up, up_own))
    grad_mid, grad_gain_ffn = two_pull(grad_two)
    grad_middle = cotangent[0].astype(jnp.float32) + grad_mid

    branch_all = gather_ctx(grad_middle.astype(low))
    grad_mix = rows_by_rows(mixed, branch_all)
    grad_made = cols_by_cols(branch_all, mix_own).astype(low)
    wide = grad_made.astype(jnp.float32)
    dots = jnp.where(is_space, jnp.sum(wide * gain_own * made, axis=1), 0.0)
    dots = sum_rows(count, dots, 6)
    grad_gain_own = jnp.sum(wide * made * factor[:, None], axis=0)
    grad_gated = wide * gain_own * factor[:, None] - made * (factor**3 * dots / DSSM)[:, None]

    def space_back(proj, grad_gated, grad_made):
        return space_bwd(plan, proj, conv, heads, grad_gated, raw_made, before)

    def attn_back(proj, grad_gated, grad_made):
        blank = lambda k: jnp.zeros((8, k), jnp.float32)
        return attn_bwd(plan, proj, tables, grad_made), blank(W), blank(PAD), blank(R)

    grad_proj, conv_acc, head_acc, skip_acc = lax.cond(
        is_space, space_back, attn_back, proj, grad_gated, grad_made
    )
    grad_normed = scatter_ctx(cols_by_cols(grad_proj, in_own))
    grad_in = rows_by_rows(normed, grad_proj)

    pull_source = jax.vjp(rms_norm, source, gain_attn)[1]
    grad_source, grad_gain_attn = pull_source(grad_normed)
    input_grad = (grad_middle + grad_source)[None]

    cut = lambda g, blocks: g.astype(low).reshape(blocks, ways, -1, g.shape[1])
    up_mine, down_mine = collect(
        count, ("rows", "rows"), (cut(grad_up, count), cut(grad_down, 1)), 3
    )
    in_mine, mix_mine = collect(count, ("cols", "rows"), (cut(grad_in, count), cut(grad_mix, 1)), 4)
    in_shard = from_slabs(plan, in_mine)
    up_mine = lax.all_to_all(up_mine, "ctx", split_axis=0, concat_axis=0, tiled=True)
    up_shard = up_from_slabs(plan, up_mine)
    mix_shard = mix_mine[0].astype(jnp.float32)
    down_shard = down_mine[0].astype(jnp.float32)

    def placed(piece, size, total, axis=0):
        shape = list(piece.shape)
        shape[axis] = total
        start = [0] * piece.ndim
        start[axis] = space * size
        return lax.dynamic_update_slice(jnp.zeros(shape, piece.dtype), piece, start)

    conv_w_grad, conv_b_grad = conv_acc[:CONV], conv_acc[CONV]
    a_grad, bias_grad = head_acc[0, :hm], head_acc[1, :hm]
    skip_grad = jnp.sum(skip_acc[0].reshape(hm, MP), axis=1)
    grad_gain_own = jnp.where(is_space, grad_gain_own, 0.0)
    vector_local = jnp.concatenate(
        [
            grad_gain_attn,
            grad_gain_ffn,
            placed(grad_gain_own, R, DSSM),
            placed(conv_b_grad[:R], R, DSSM),
            conv_b_grad[R:],
            jnp.concatenate(
                [placed(conv_w_grad[:, :R], R, DSSM, 1), conv_w_grad[:, R:]], axis=1
            ).reshape(CONV * CONVCH),
            placed(a_grad, hm, MH),
            placed(bias_grad, hm, MH),
            placed(skip_grad, hm, MH),
        ]
    )
    vector_grad = sum_vector(count, vector_local, 7)
    new_in = adamw(w_in, w_in_m, w_in_v, in_shard, 2.0 * D ** (-0.5), decay_weight)
    new_mix = adamw(w_mix, w_mix_m, w_mix_v, mix_shard, DSSM ** (-0.5), decay_weight)
    new_up = adamw(w_up, w_up_m, w_up_v, up_shard, D ** (-0.5), decay_weight)
    new_down = adamw(w_down, w_down_m, w_down_v, down_shard, FF ** (-0.5), decay_weight)
    new_vec = adamw(vectors, vectors_m, vectors_v, vector_grad, vector_rate, 0.0)
    return (outputs, input_grad, *new_in, *new_mix, *new_up, *new_down, *new_vec)


def solution(mesh):
    tokens = P("wshard", "ctx", None)
    weight = P(("ctx", "wshard"), None)
    return jax.shard_map(
        body,
        mesh=mesh,
        in_specs=(tokens,) * 2 + (weight,) * 12 + (P(),) * 3,
        out_specs=(tokens,) * 2 + (weight,) * 12 + (P(),) * 3,
        check_vma=False,
    )
```

```python
import functools
import math

import jax
import jax.numpy as jnp
from jax import lax
from jax.experimental import pallas as pl
from jax.experimental.pallas import tpu as pltpu
from jax.sharding import PartitionSpec as P

D = 2048
FF = 4096
AH = 8
KVH = 2
HD = 128
MH = 48
MP = 64
NS = 256
CONV = 4
STEP = 10
DSSM = 3072
CONVCH = 3584
ATT = AH * HD
MIXIN = ATT + DSSM
GROUP = AH // KVH
CHUNK = 128
PAD = 128
VMEM = 60 * 1024 * 1024


norm_eps = 1e-05
rope_base = 10000.0
beta_one = 0.9
beta_two = 0.95
adam_eps = 1e-08
decay_weight = 0.1
vector_rate = 0.5
masked_score = -1e30

K_AT = ATT
V_AT = K_AT + KVH * HD
Z_AT = V_AT + KVH * HD
X_AT = Z_AT + DSSM
BC_AT = X_AT + DSSM
DT_AT = BC_AT + 2 * NS
END = DT_AT + MH


def rows_by_rows(left, right):
    return lax.dot_general(
        left, right, (((0,), (0,)), ((), ())), preferred_element_type=jnp.float32
    )


def cols_by_cols(left, right):
    return lax.dot_general(
        left, right, (((1,), (1,)), ((), ())), preferred_element_type=jnp.float32
    )


def plain(left, right):
    return jnp.dot(left, right, preferred_element_type=jnp.float32)


def rms_norm(values, gain):
    factor = lax.rsqrt(jnp.mean(values * values, axis=-1, keepdims=True) + norm_eps)
    return values * factor * gain


def split_vectors(vectors):
    extents = (D, D, DSSM, CONVCH, CONV * CONVCH, MH, MH, MH)
    pieces = []
    offset = 0
    for extent in extents:
        pieces.append(lax.slice_in_dim(vectors, offset, offset + extent))
        offset = offset + extent
    pieces[4] = pieces[4].reshape(CONV, CONVCH)
    return pieces


def adamw(weight, moment, second, grad, rate, decay):
    moment = beta_one * moment + (1.0 - beta_one) * grad
    second = beta_two * second + (1.0 - beta_two) * grad * grad
    corrected = moment / (1.0 - beta_one**STEP)
    divisor = jnp.sqrt(second / (1.0 - beta_two**STEP)) + adam_eps
    return (weight - rate * (corrected / divisor + decay * weight), moment, second)


class Plan:
    def __init__(self, count):
        self.count = count
        self.R = MIXIN // count
        self.attn = ATT // self.R
        self.ha = self.R // HD
        self.hm = self.R // MP
        self.B = self.R
        self.A = self.R + max(self.R, 2 * HD)
        self.K = 2 * NS + PAD
        self.W = self.R + 2 * NS

    def kv_of(self, c):
        return c * self.ha // GROUP


def from_slabs(plan, slabs, shared):
    R, B = plan.R, plan.B
    slabs = slabs.astype(jnp.float32)
    shared = shared.astype(jnp.float32)
    heads = range(plan.attn)
    spaces = range(plan.attn, plan.count)
    total = lambda items: functools.reduce(lambda a, b: a + b, items)
    parts = [slabs[c][:, :R] for c in heads]
    for at in (B, B + HD):
        for g in range(KVH):
            parts.append(total([slabs[c][:, at : at + HD] for c in heads if plan.kv_of(c) == g]))
    parts += [slabs[c][:, :R] for c in spaces]
    parts += [slabs[c][:, B : B + R] for c in spaces]
    parts.append(total([shared[c][:, : END - BC_AT] for c in spaces]))
    return jnp.concatenate(parts, axis=1)


def up_from_slabs(plan, slabs):
    G = FF // plan.count
    slabs = slabs.astype(jnp.float32)
    return jnp.concatenate(
        [slabs[c][:, :G] for c in range(plan.count)] + [slabs[c][:, G:] for c in range(plan.count)],
        axis=1,
    )


def gather_ctx(x):
    return lax.all_gather(x, "ctx", axis=0, tiled=True)


def scatter_ctx(x):
    return lax.psum_scatter(
        x.astype(jnp.bfloat16), "ctx", scatter_dimension=0, tiled=True
    ).astype(jnp.float32)


MESH = pl.DeviceIdType.MESH


def here():
    c, w = lax.axis_index("ctx"), lax.axis_index("wshard")
    return c, w, w + 1 - 2 * (w % 2), (w + 2) % 4


def greet(devices):
    barrier = pltpu.get_barrier_semaphore()
    for device in devices:
        pl.semaphore_signal(barrier, inc=1, device_id=device, device_id_type=MESH)
    pl.semaphore_wait(barrier, len(devices))


def remote(src, dst, send, recv, device):
    return pltpu.make_async_remote_copy(
        src_ref=src, dst_ref=dst, send_sem=send, recv_sem=recv, device_id=device, device_id_type=MESH
    )


def collect_job(n, kinds, sources, targets, extra):
    c, w, sib, across = here()
    x, core = w // 2, w % 2
    far = 1 - x
    pending = []
    jobs = []
    for j, kind in enumerate(kinds):
        jobs.append((kind, sources[j], targets[j]) + tuple(extra[10 * j : 10 * j + 10]))

    def order(job, s):
        return (c + s) % n if job[1].shape[0] > 1 else 0

    def count(job):
        return job[1].shape[0]

    most = max(count(job) for job in jobs)
    steps = [s % most for s in range(1, most + 1)]
    for place, slot in ((far, 0), (x, 1)):
        for s in steps:
            for job in jobs:
                if s >= count(job):
                    continue
                _, src, _, kbuf, _, _, _, k_send, k_recv = job[:9]
                q = order(job, s)
                out = remote(
                    src.at[q, place * 2 + 1 - core],
                    kbuf.at[slot, q],
                    k_send.at[slot, s],
                    k_recv.at[slot, q],
                    (c, sib),
                )
                out.start()
                pending.append(out)
    yield
    wide = jnp.float32
    for s in steps:
        for job in jobs:
            if s >= count(job):
                continue
            _, src, _, kbuf, stage, xbuf, _, k_send, k_recv, x_send, x_recv = job[:11]
            q = order(job, s)
            got = kbuf.at[0, q]
            remote(got, got, k_send.at[0, s], k_recv.at[0, q], (c, sib)).wait_recv()
            stage[q] = (src[q, far * 2 + core].astype(wide) + kbuf[0, q].astype(wide)).astype(
                stage.dtype
            )
            out = remote(stage.at[q], xbuf.at[q], x_send.at[s], x_recv.at[q], (c, across))
            out.start()
            pending.append(out)
    yield
    for s in steps:
        for job in jobs:
            if s >= count(job):
                continue
            kind, src, dst, kbuf, stage, xbuf, done, k_send, k_recv, x_send, x_recv = job[:11]
            a_send, a_recv = job[11], job[12]
            q = order(job, s)
            got = kbuf.at[1, q]
            remote(got, got, k_send.at[1, s], k_recv.at[1, q], (c, sib)).wait_recv()
            got = xbuf.at[q]
            remote(got, got, x_send.at[s], x_recv.at[q], (c, across)).wait_recv()
            total = src[q, x * 2 + core].astype(wide) + kbuf[1, q].astype(wide)
            total = (total + xbuf[q].astype(wide)).astype(stage.dtype)
            if kind == "cols" and s > 0:
                done[q] = total
                out = remote(done.at[q], dst.at[c], a_send.at[s], a_recv.at[c], (q, w))
                out.start()
                pending.append(out)
            else:
                dst[q] = total
        yield
    for job in jobs:
        if job[0] == "cols":
            dst, a_send, a_recv = job[2], job[11], job[12]
            for s in range(1, n):
                q = (c + n - s) % n
                got = dst.at[q]
                remote(got, got, a_send.at[s], a_recv.at[q], (q, w)).wait_recv()
    for out in pending:
        out.wait_send()


def collect_shapes(kinds, sources):
    shapes, scratch = [], []
    for kind, src in zip(kinds, sources):
        count, _, rows, size = src.shape
        block = (count, rows, size)
        shapes.append(jax.ShapeDtypeStruct(block, src.dtype))
        scratch += [
            pltpu.VMEM((2,) + block, src.dtype),
            pltpu.VMEM(block, src.dtype),
            pltpu.VMEM(block, src.dtype),
            pltpu.VMEM(block if kind == "cols" else (1, 16, 128), src.dtype),
            pltpu.SemaphoreType.DMA((2, count)),
            pltpu.SemaphoreType.DMA((2, count)),
            pltpu.SemaphoreType.DMA((count,)),
            pltpu.SemaphoreType.DMA((count,)),
            pltpu.SemaphoreType.DMA((count,)),
            pltpu.SemaphoreType.DMA((count,)),
        ]
    return shapes, scratch


def row_sum_kernel(n, x_ref, out_ref, got, send, recv):
    c, w = lax.axis_index("ctx"), lax.axis_index("wshard")
    greet([((c + s) % n, w) for s in range(1, n)])
    copies = [
        remote(x_ref, got.at[c], send.at[s], recv.at[c], ((c + s) % n, w)) for s in range(1, n)
    ]
    for copy in copies:
        copy.start()
    total = x_ref[...]
    for s in range(1, n):
        q = (c + n - s) % n
        remote(x_ref, got.at[q], send.at[s], recv.at[q], (q, w)).wait_recv()
        total = total + got[q]
    out_ref[...] = total
    for copy in copies:
        copy.wait_send()


def sum_rows(n, x, collective_id):
    block = x.reshape(-1, 128)
    return pl.pallas_call(
        functools.partial(row_sum_kernel, n),
        out_shape=jax.ShapeDtypeStruct(block.shape, x.dtype),
        in_specs=[pl.BlockSpec(memory_space=pltpu.VMEM)],
        out_specs=pl.BlockSpec(memory_space=pltpu.VMEM),
        scratch_shapes=[
            pltpu.VMEM((n,) + block.shape, x.dtype),
            pltpu.SemaphoreType.DMA((n,)),
            pltpu.SemaphoreType.DMA((n,)),
        ],
        compiler_params=pltpu.CompilerParams(
            collective_id=collective_id, has_side_effects=True, vmem_limit_bytes=VMEM
        ),
    )(block).reshape(x.shape)


def sum_job(n, x_ref, out_ref, kept, got, send, recv):
    c, w, sib, across = here()
    partners = [(c, sib), (c, across)]
    for level in range(n.bit_length() - 1):
        reach = 2**level
        partners.append((c + reach - 2 * reach * ((c // reach) % 2), w))
    out_ref[...] = x_ref[...]
    for i, partner in enumerate(partners):
        kept[i] = out_ref[...]
        swap = remote(kept.at[i], got.at[i], send.at[i], recv.at[i], partner)
        swap.start()
        yield
        swap.wait()
        out_ref[...] += got[i]


def sum_scratch(n, shape):
    stages = n.bit_length() + 1
    return [
        pltpu.VMEM((stages,) + shape, jnp.float32),
        pltpu.VMEM((stages,) + shape, jnp.float32),
        pltpu.SemaphoreType.DMA((stages,)),
        pltpu.SemaphoreType.DMA((stages,)),
    ]


def share_job(sources, targets, sems):
    c, w, sib, across = here()
    pending = []
    for j, (src, dst) in enumerate(zip(sources, targets)):
        x_send, x_recv, k_send, k_recv, own_sem = sems[5 * j : 5 * j + 5]
        for q in range(src.shape[0]):
            own = pltpu.make_async_copy(src.at[q], dst.at[q, w], own_sem.at[q])
            to_x = remote(src.at[q], dst.at[q, w], x_send.at[q], x_recv.at[q], (c, across))
            to_k = remote(src.at[q], dst.at[q, w], k_send.at[0, q], k_recv.at[0, q], (c, sib))
            for copy in (to_x, to_k, own):
                copy.start()
            pending += [to_x.wait_send, to_k.wait_send, own.wait]
    yield
    for j, dst in enumerate(targets):
        x_send, x_recv, k_send, k_recv, own_sem = sems[5 * j : 5 * j + 5]
        for q in range(dst.shape[0]):
            got = dst.at[q, across]
            remote(got, got, x_send.at[q], x_recv.at[q], (c, across)).wait_recv()
            out = remote(got, got, k_send.at[1, q], k_recv.at[1, q], (c, sib))
            out.start()
            pending.append(out.wait_send)
    yield
    for j, dst in enumerate(targets):
        x_send, x_recv, k_send, k_recv, own_sem = sems[5 * j : 5 * j + 5]
        for q in range(dst.shape[0]):
            for half, place in ((0, sib), (1, (sib + 2) % 4)):
                got = dst.at[q, place]
                remote(got, got, k_send.at[half, q], k_recv.at[half, q], (c, sib)).wait_recv()
    for wait in pending:
        wait()


def share_shapes(sources):
    shapes, sems = [], []
    for src in sources:
        count = src.shape[0]
        shapes.append(jax.ShapeDtypeStruct((count, 4) + src.shape[1:], src.dtype))
        sems += [
            pltpu.SemaphoreType.DMA((count,)),
            pltpu.SemaphoreType.DMA((count,)),
            pltpu.SemaphoreType.DMA((2, count)),
            pltpu.SemaphoreType.DMA((2, count)),
            pltpu.SemaphoreType.DMA((count,)),
        ]
    return shapes, sems


def advance(*jobs):
    jobs = list(jobs)
    while jobs:
        for job in list(jobs):
            try:
                next(job)
            except StopIteration:
                jobs.remove(job)


class Line:
    def __init__(self, n):
        self.c, self.w, self.sib, self.across = here()
        self.n, self.N = n, n // 2
        self.at, self.side = self.c // 2, self.c % 2
        self.pair = (self.c + 1 - 2 * self.side, self.w)
        self.left = (self.c - 2, self.w)
        self.right = (self.c + 2, self.w)
        self.has_left = self.at > 0
        self.has_right = self.at < self.N - 1

    def greet(self, others=()):
        barrier = pltpu.get_barrier_semaphore()
        signal = lambda d: pl.semaphore_signal(barrier, inc=1, device_id=d, device_id_type=MESH)
        sure = [self.pair] + list(others)
        for device in sure:
            signal(device)
        pl.when(self.has_left)(lambda: signal(self.left))
        pl.when(self.has_right)(lambda: signal(self.right))
        beside = (self.at + self.N - 1) // self.N + (2 * self.N - 2 - self.at) // self.N
        pl.semaphore_wait(barrier, len(sure) + beside)


def scatter_job(line, block, total, ystage, ybuf, zbuf, sems):
    y_send, y_recv, r_send, r_recv, l_send, l_recv = sems
    N, at, side = line.N, line.at, line.side
    wide = jnp.float32

    def both_ways(d):
        return ((at + d, at + d < N), (at - d, at - d >= 0)) if d else ((at, None),)

    def guarded(keep, step):
        if keep is None:
            step()
        else:
            pl.when(keep)(step)

    def y_copy(b):
        return remote(ystage.at[b], ybuf.at[b], y_send.at[b], y_recv.at[b], line.pair)

    def r_copy(b, slot):
        return remote(ybuf.at[b], zbuf.at[slot], r_send.at[b], r_recv.at[b], line.right)

    def l_copy(b, slot):
        return remote(ybuf.at[b], zbuf.at[slot], l_send.at[b], l_recv.at[b], line.left)

    for d in range(N - 1, -1, -1):
        for b, keep in both_ways(d):

            def first(b=b):
                ystage[b] = block(2 * b + 1 - side).astype(ystage.dtype)
                y_copy(b).start()

            guarded(keep, first)
        yield
    for d in range(N - 1, 0, -1):
        for b, keep, ahead in ((at + d, at + d < N, True), (at - d, at - d >= 0, False)):

            def relay(b=b, ahead=ahead):
                mine = block(2 * b + side)
                y_copy(b).wait_recv()
                mine = mine + ybuf[b].astype(wide)
                came = line.has_left if ahead else line.has_right

                @pl.when(came)
                def _():
                    (r_copy if ahead else l_copy)(b, b).wait_recv()
                    ybuf[b] = (mine + zbuf[b].astype(wide)).astype(ybuf.dtype)

                @pl.when(jnp.logical_not(came))
                def _():
                    ybuf[b] = mine.astype(ybuf.dtype)

                if ahead:
                    pl.when(b == at + 1)(lambda: r_copy(b, b).start())
                    pl.when(b > at + 1)(lambda: r_copy(b, b).start())
                else:
                    pl.when(b == at - 1)(lambda: l_copy(b, N).start())
                    pl.when(b < at - 1)(lambda: l_copy(b, b).start())

            guarded(keep, relay)
        yield
    mine = block(2 * at + side)
    y_copy(at).wait_recv()
    total[...] = mine + ybuf[at].astype(wide)

    @pl.when(line.has_left)
    def _():
        r_copy(at, at).wait_recv()
        total[...] += zbuf[at].astype(wide)

    @pl.when(line.has_right)
    def _():
        l_copy(at, N).wait_recv()
        total[...] += zbuf[N].astype(wide)

    for d in range(N):
        for b, keep in both_ways(d):
            guarded(keep, lambda b=b: y_copy(b).wait_send())
    for d in range(1, N):
        pl.when(at + d < N)(lambda d=d: r_copy(at + d, at + d).wait_send())
        pl.when(at - d >= 0)(lambda d=d: l_copy(at - d, at - d).wait_send())


def gather_job(line, own, out, sems):
    r_send, l_send, y_send, recv, own_sem = sems
    n, N, at, side, c = line.n, line.N, line.at, line.side, line.c
    local = pltpu.make_async_copy(own, out(c), own_sem)
    local.start()

    def send(src, q, sem, device):
        return remote(src, out(q), sem.at[q // 2], recv.at[q], device)

    pl.when(line.has_right)(lambda: send(own, c, r_send, line.right).start())
    pl.when(line.has_left)(lambda: send(own, c, l_send, line.left).start())
    send(own, c, y_send, line.pair).start()
    yield
    for d in range(1, N):
        for q, keep, ahead in ((c - 2 * d, at - d >= 0, True), (c + 2 * d, at + d < N, False)):

            def relay(q=q, ahead=ahead):
                got = out(q)
                send(got, q, y_send, line.pair).wait_recv()
                if ahead:
                    pl.when(line.has_right)(lambda: send(got, q, r_send, line.right).start())
                else:
                    pl.when(line.has_left)(lambda: send(got, q, l_send, line.left).start())
                send(got, q, y_send, line.pair).start()

            pl.when(keep)(relay)
        yield
    for b in range(N):
        q = 2 * b + 1 - side
        send(out(q), q, y_send, line.pair).wait_recv()
    local.wait()
    for b in range(N):
        q = 2 * b + side
        got = out(q)
        send(got, q, y_send, line.pair).wait_send()
        pl.when(jnp.logical_and(b <= at, line.has_right))(
            lambda q=q, got=got: send(got, q, r_send, line.right).wait_send()
        )
        pl.when(jnp.logical_and(b >= at, line.has_left))(
            lambda q=q, got=got: send(got, q, l_send, line.left).wait_send()
        )


def scatter_scratch(n, rows):
    N = n // 2
    return [
        pltpu.VMEM((N, rows, D), jnp.bfloat16),
        pltpu.VMEM((N, rows, D), jnp.bfloat16),
        pltpu.VMEM((N + 1, rows, D), jnp.bfloat16),
        pltpu.VMEM((rows, D), jnp.float32),
    ] + [pltpu.SemaphoreType.DMA((N,))] * 6


def gather_scratch(n, rows):
    N = n // 2
    return [
        pltpu.VMEM((rows, D), jnp.bfloat16),
        pltpu.SemaphoreType.DMA((N,)),
        pltpu.SemaphoreType.DMA((N,)),
        pltpu.SemaphoreType.DMA((N,)),
        pltpu.SemaphoreType.DMA((n,)),
        pltpu.SemaphoreType.DMA,
    ]


def rms_factor(values):
    return lax.rsqrt(jnp.mean(values * values, axis=1, keepdims=True) + norm_eps)


def rms_back(values, gain, grad):
    factor = rms_factor(values)
    scaled = grad * gain
    inner = jnp.mean(scaled * values, axis=1, keepdims=True)
    d_gain = jnp.sum(grad * (values * factor), axis=0, keepdims=True)
    return factor * scaled - values * (factor * factor * factor * inner), d_gain


def matmul_block(left, right, turned_right, rows):
    def block(place):
        part = left[pl.ds(pl.multiple_of(place * rows, rows), rows), :]
        if turned_right:
            return cols_by_cols(part, right[...])
        return plain(part, right[...])

    return block


def finish(job):
    for _ in job:
        pass


def start_kernel(plan, n, x, w_in, w_up, w_mix, w_down, *refs):
    tokens, in_all, shared_all, up_some, mix_all, down_some = refs[:6]
    in_low, shared_low, up_low, mix_low, down_low = refs[6:11]
    t_sems = refs[11:16]
    a_send, a_recv, x_send, x_recv, k_send, k_recv, own_sem = refs[16:]
    line = Line(n)
    c, w, sib, across = line.c, line.w, line.sib, line.across
    greet([((c + s) % n, w) for s in range(1, n)] + [(c, sib), (c, across)])
    R, B, G = plan.R, plan.B, FF // n
    low = jnp.bfloat16
    inputs = gather_job(line, x, lambda q: tokens.at[q], t_sems)
    next(inputs)
    passed, pending = [], []

    def pass_on(number, view, src=None):
        src = view(w) if src is None else src
        to_x = remote(src, view(w), x_send.at[number], x_recv.at[number], (c, across))
        to_k = remote(src, view(w), k_send.at[0, number], k_recv.at[0, number], (c, sib))
        to_x.start()
        to_k.start()
        pending.append(to_x)
        pending.append(to_k)
        passed.append((number, view))

    mix_low[...] = w_mix[...].astype(low)
    pass_on(2 * n, lambda place: mix_all.at[0, place], mix_low)
    shared_low[...] = jnp.zeros_like(shared_low)
    shared_low[:, : END - BC_AT] = w_in[:, BC_AT:END].astype(low)
    for p in range(n):
        if p < plan.attn:
            g = plan.kv_of(p)
            in_low[p, :, :R] = w_in[:, p * R : (p + 1) * R].astype(low)
            in_low[p, :, B : B + HD] = w_in[:, K_AT + g * HD : K_AT + (g + 1) * HD].astype(low)
            in_low[p, :, B + HD : B + 2 * HD] = w_in[
                :, V_AT + g * HD : V_AT + (g + 1) * HD
            ].astype(low)
            if B + 2 * HD < plan.A:
                rest = plan.A - B - 2 * HD
                in_low[p, :, B + 2 * HD :] = jnp.zeros((in_low.shape[1], rest), low)
        else:
            j = p - plan.attn
            in_low[p, :, :R] = w_in[:, Z_AT + j * R : Z_AT + (j + 1) * R].astype(low)
            in_low[p, :, B : B + R] = w_in[:, X_AT + j * R : X_AT + (j + 1) * R].astype(low)
            if B + R < plan.A:
                in_low[p, :, B + R :] = jnp.zeros((in_low.shape[1], plan.A - B - R), low)

    def column_copies(s):
        p = (c + s) % n
        ends = ((in_low.at[p], in_all), (shared_low, shared_all))
        return [
            remote(src, dst.at[c, w], a_send.at[k, s], a_recv.at[k, c], (p, w))
            for k, (src, dst) in enumerate(ends)
        ]

    def send_columns(steps):
        for s in steps:
            for copy in column_copies(s):
                copy.start()
                pending.append(copy)

    in_view = lambda q: lambda place: in_all.at[q, place]
    shared_view = lambda q: lambda place: shared_all.at[q, place]

    def take_columns(steps):
        for s in steps:
            q = (c + n - s) % n
            for k, view in ((0, in_view), (1, shared_view)):
                got = view(q)(w)
                remote(got, got, a_send.at[k, s], a_recv.at[k, q], (q, w)).wait_recv()
                pass_on(k * n + q, view(q))

    done = [0]

    def seconds(upto):
        while done[0] < min(upto, len(passed)):
            number, view = passed[done[0]]
            got = view(across)
            remote(got, got, x_send.at[number], x_recv.at[number], (c, across)).wait_recv()
            out = remote(got, got, k_send.at[1, number], k_recv.at[1, number], (c, sib))
            out.start()
            pending.append(out)
            done[0] += 1

    cuts = [round(1 + (n - 1) * i / 3) for i in range(4)]
    parts = [range(cuts[i], cuts[i + 1]) for i in range(3)]
    send_columns(parts[0])
    pass_on(c, in_view(c), in_low.at[c])
    pass_on(n + c, shared_view(c), shared_low)
    down_low[...] = w_down[...].astype(low)
    for p in range(n):
        up_low[p, :, :G] = w_up[:, p * G : (p + 1) * G].astype(low)
        up_low[p, :, G:] = w_up[:, FF + p * G : FF + (p + 1) * G].astype(low)
    locals_started = []
    own = (
        (in_low.at[c], in_all.at[c, w]),
        (shared_low, shared_all.at[c, w]),
        (mix_low, mix_all.at[0, w]),
        (up_low.at[c], up_some.at[c]),
        (down_low, down_some.at[0]),
    )
    for i, (src, dst) in enumerate(own):
        copy = pltpu.make_async_copy(src, dst, own_sem.at[i])
        copy.start()
        locals_started.append(copy)
    for step in range(3):
        for _ in range(line.N // 4):
            next(inputs, None)
        if step < 2:
            send_columns(parts[step + 1])
        else:
            for s in range(1, n):
                p = (c + s) % n
                out = remote(
                    up_low.at[p], up_some.at[c], a_send.at[2, s], a_recv.at[2, c], (p, w)
                )
                out.start()
                pending.append(out)
        take_columns(parts[step])
        seconds(len(passed) - 4)
    finish(inputs)
    seconds(len(passed))
    for s in range(1, n):
        q = (c + n - s) % n
        got = up_some.at[q]
        remote(got, got, a_send.at[2, s], a_recv.at[2, q], (q, w)).wait_recv()
    for number, view in passed:
        for half, place in ((0, sib), (1, (sib + 2) % 4)):
            got = view(place)
            remote(got, got, k_send.at[half, number], k_recv.at[half, number], (c, sib)).wait_recv()
    for copy in locals_started:
        copy.wait()
    for out in pending:
        out.wait_send()


def branch_kernel(n, refs_in, refs_out, scratch):
    left, right, source, gain, up, down = refs_in
    middle, normed, up_all, down_all = refs_out
    line = Line(n)
    line.greet([(line.c, line.sib), (line.c, line.across)])
    rows = source.shape[0]
    ystage, ybuf, zbuf, total = scratch[:4]
    own = scratch[10]
    share = share_job((up, down), (up_all, down_all), scratch[16:])
    main = scatter_job(
        line, matmul_block(left, right, False, rows), total, ystage, ybuf, zbuf, scratch[4:10]
    )
    next(main)
    next(share)
    finish(main)
    value = source[...].astype(jnp.float32) + total[...]
    middle[...] = value
    own[...] = (value * rms_factor(value) * gain[...]).astype(own.dtype)
    spread_out = gather_job(line, own, lambda q: normed.at[q], scratch[11:16])
    next(spread_out)
    next(share)
    finish(spread_out)
    finish(share)


def feed_back_kernel(n, refs_in, refs_out, scratch):
    left, right, cotangent, middle, gain, up, down = refs_in
    grad, d_gain, low_all, up_sum, down_sum = refs_out
    line = Line(n)
    others = [((line.c + s) % n, line.w) for s in range(1, n)]
    greet(others + [(line.c, line.sib), (line.c, line.across)])
    rows = cotangent.shape[0]
    ystage, ybuf, zbuf, total = scratch[:4]
    own = scratch[10]
    sums = collect_job(n, ("cols", "rows"), (up, down), (up_sum, down_sum), scratch[16:])
    main = scatter_job(
        line, matmul_block(left, right, True, rows), total, ystage, ybuf, zbuf, scratch[4:10]
    )
    next(main)
    next(sums)
    for _ in range(line.N - 1):
        next(main)
    next(sums)
    finish(main)
    for _ in range(n):
        next(sums)
    back, gain_row = rms_back(middle[...], gain[...], total[...])
    value = cotangent[...].astype(jnp.float32) + back
    grad[...] = value
    d_gain[...] = jnp.broadcast_to(gain_row, d_gain.shape)
    own[...] = value.astype(own.dtype)
    spread_out = gather_job(line, own, lambda q: low_all.at[q], scratch[11:16])
    for _ in range(line.N):
        next(spread_out)
    finish(sums)
    finish(spread_out)


SUMS = ("cols", "cols", "rows")


def source_back_kernel(n, refs_in, refs_out, scratch):
    (left, left_two, right, right_two, source, grad_middle, gain, vector) = refs_in[:8]
    w_in, w_shared, w_mix = refs_in[8:]
    grad, vector_sum, in_sum, shared_sum, mix_sum = refs_out
    line = Line(n)
    others = [((line.c + s) % n, line.w) for s in range(1, n)]
    greet(others + [(line.c, line.sib), (line.c, line.across)])
    rows = source.shape[0]
    ystage, ybuf, zbuf, total = scratch[:4]
    sums = collect_job(
        n, SUMS, (w_in, w_shared, w_mix), (in_sum, shared_sum, mix_sum), scratch[10:-4]
    )
    one = matmul_block(left, right, True, rows)
    two = matmul_block(left_two, right_two, True, rows)
    main = scatter_job(
        line, lambda place: one(place) + two(place), total, ystage, ybuf, zbuf, scratch[4:10]
    )
    count = len(scratch) - 4
    vectors = sum_job(n, vector, vector_sum, *scratch[count:])
    next(main)
    next(sums)
    next(vectors)
    for _ in range(line.N - 1):
        next(main)
    next(sums)
    for _ in main:
        next(vectors, None)
        next(sums)
        next(sums)
    for _ in range(n - 2 * line.N + 2):
        next(sums)
    back, _ = rms_back(source[...].astype(jnp.float32), gain[...], total[...])
    grad[...] = grad_middle[...] + back
    finish(vectors)
    finish(sums)


def flow_call(kernel, n, rows, args, outs, gathers, away, extra, collective_id):
    inside = pl.BlockSpec(memory_space=pltpu.VMEM)
    outside = pl.BlockSpec(memory_space=pl.ANY)
    side_args, side_shapes, side_scratch = extra
    shapes = list(outs)
    specs = [inside] * len(outs)
    scratch = scatter_scratch(n, rows)
    if gathers:
        shapes.append(jax.ShapeDtypeStruct((n, rows, D), jnp.bfloat16))
        specs.append(outside)
        scratch = scratch + gather_scratch(n, rows)
    side = outside if away else inside
    in_specs = [inside] * len(args) + [side] * len(side_args)
    specs = specs + [side] * len(side_shapes)
    shapes = shapes + list(side_shapes)
    first, second = len(in_specs), len(in_specs) + len(specs)

    def run(*refs):
        kernel(n, refs[:first], refs[first:second], refs[second:])

    return pl.pallas_call(
        run,
        out_shape=tuple(shapes),
        in_specs=in_specs,
        out_specs=tuple(specs),
        scratch_shapes=scratch + list(side_scratch),
        cost_estimate=pl.CostEstimate(flops=0, bytes_accessed=2 * 10**8, transcendentals=0),
        compiler_params=pltpu.CompilerParams(
            collective_id=collective_id, has_side_effects=True, vmem_limit_bytes=VMEM
        ),
    )(*args, *side_args)


def start_call(plan, n, x, w_in, w_up, w_mix, w_down, collective_id):
    rows = w_in.shape[0]
    low = jnp.bfloat16
    G = FF // n
    shapes = (
        jax.ShapeDtypeStruct((n,) + x.shape, low),
        jax.ShapeDtypeStruct((n, 4, rows, plan.A), low),
        jax.ShapeDtypeStruct((n, 4, rows, plan.K), low),
        jax.ShapeDtypeStruct((n, rows, 2 * G), low),
        jax.ShapeDtypeStruct((1, 4) + w_mix.shape, low),
        jax.ShapeDtypeStruct((1,) + w_down.shape, low),
    )
    dma = pltpu.SemaphoreType.DMA
    outside = pl.BlockSpec(memory_space=pl.ANY)
    inside = pl.BlockSpec(memory_space=pltpu.VMEM)
    blocks = 2 * n + 1
    outs = pl.pallas_call(
        functools.partial(start_kernel, plan, n),
        out_shape=shapes,
        in_specs=[outside] + [inside] * 4,
        out_specs=(outside,) * 6,
        scratch_shapes=[
            pltpu.VMEM((n, rows, plan.A), low),
            pltpu.VMEM((rows, plan.K), low),
            pltpu.VMEM((n, rows, 2 * G), low),
            pltpu.VMEM(w_mix.shape, low),
            pltpu.VMEM(w_down.shape, low),
        ]
        + gather_scratch(n, 16)[1:]
        + [dma((3, n)), dma((3, n))]
        + [dma((blocks,)), dma((blocks,)), dma((2, blocks)), dma((2, blocks))]
        + [dma((5,))],
        cost_estimate=pl.CostEstimate(flops=0, bytes_accessed=2 * 10**8, transcendentals=0),
        compiler_params=pltpu.CompilerParams(
            collective_id=collective_id, has_side_effects=True, vmem_limit_bytes=VMEM
        ),
    )(x, w_in, w_up, w_mix, w_down)
    flat = lambda o: o.reshape(-1, o.shape[-1])
    tokens, in_all, shared_all, up_some, mix_all, down_some = outs
    return flat(tokens), flat(in_all), flat(shared_all), up_some, flat(mix_all), down_some


def mm(left, right):
    return jnp.dot(
        left.astype(jnp.bfloat16), right.astype(jnp.bfloat16), preferred_element_type=jnp.float32
    )


def mm_nt(left, right):
    return cols_by_cols(left.astype(jnp.bfloat16), right.astype(jnp.bfloat16))


def mm_tn(left, right):
    return rows_by_rows(left.astype(jnp.bfloat16), right.astype(jnp.bfloat16))


def exact(left, right):
    return jnp.dot(
        left, right, precision=lax.Precision.HIGHEST, preferred_element_type=jnp.float32
    )


def iota(shape, axis):
    return lax.broadcasted_iota(jnp.int32, shape, axis)


def rope_tables(length):
    half = HD // 2
    frequency = rope_base ** (-jnp.arange(half, dtype=jnp.float32) / half)
    angles = jnp.arange(length).astype(jnp.float32)[:, None] * frequency[None, :]
    cosine, sine = jnp.cos(angles), jnp.sin(angles)
    return (
        jnp.concatenate([cosine, cosine], axis=1),
        jnp.concatenate([-sine, sine], axis=1),
    )


def turned(values, cosine, sine):
    return values * cosine + pltpu.roll(values, HD // 2, 1) * sine


def attn_stack(plan, q_ref, cosine, sine):
    heads = [
        turned(q_ref[:, h * HD : (h + 1) * HD], cosine, sine).astype(jnp.bfloat16)
        for h in range(plan.ha)
    ]
    return jnp.concatenate(heads, axis=0)


def attn_softmax(stack, keys, at):
    scores = cols_by_cols(stack, keys) * (1.0 / math.sqrt(HD))
    row = iota(scores.shape, 0) & (CHUNK - 1)
    scores = jnp.where(iota(scores.shape, 1) <= row + at, scores, masked_score)
    weights = jnp.exp(scores - jnp.max(scores, axis=1, keepdims=True))
    return weights * (1.0 / jnp.sum(weights, axis=1, keepdims=True))


def attn_fwd_kernel(plan, q_ref, k_ref, v_ref, cos_ref, sin_ref, out_ref, keys, values):
    step = pl.program_id(0)

    @pl.when(step == 0)
    def _():
        keys[...] = turned(k_ref[...], cos_ref[...], sin_ref[...]).astype(jnp.bfloat16)
        values[...] = v_ref[...].astype(jnp.bfloat16)

    at = pl.multiple_of(step * CHUNK, CHUNK)
    rows = pl.ds(at, CHUNK)
    stack = attn_stack(plan, q_ref, cos_ref[rows, :], sin_ref[rows, :])
    probs = attn_softmax(stack, keys[...], at)
    made = mm(probs, values[...])
    for h in range(plan.ha):
        out_ref[:, h * HD : (h + 1) * HD] = made[h * CHUNK : (h + 1) * CHUNK]


def attn_fwd(plan, proj, tables):
    length = proj.shape[0]
    whole = lambda i: (0, 0)
    return pl.pallas_call(
        functools.partial(attn_fwd_kernel, plan),
        grid=(length // CHUNK,),
        out_shape=jax.ShapeDtypeStruct((length, plan.R), jnp.float32),
        in_specs=[
            pl.BlockSpec((CHUNK, plan.R), lambda i: (i, 0)),
            pl.BlockSpec((length, HD), lambda i: (0, plan.B // HD)),
            pl.BlockSpec((length, HD), lambda i: (0, plan.B // HD + 1)),
            pl.BlockSpec((length, HD), whole),
            pl.BlockSpec((length, HD), whole),
        ],
        out_specs=pl.BlockSpec((CHUNK, plan.R), lambda i: (i, 0)),
        scratch_shapes=[pltpu.VMEM((length, HD), jnp.bfloat16)] * 2,
        compiler_params=pltpu.CompilerParams(vmem_limit_bytes=VMEM),
    )(proj, proj, proj, *tables)


def attn_bwd_kernel(
    plan, q_ref, k_ref, v_ref, cos_ref, sin_ref, grad_ref, slab_ref, keys, values, grad_k, grad_v
):
    step = pl.program_id(0)
    scale = 1.0 / math.sqrt(HD)

    @pl.when(step == 0)
    def _():
        keys[...] = turned(k_ref[...], cos_ref[...], sin_ref[...]).astype(jnp.bfloat16)
        values[...] = v_ref[...].astype(jnp.bfloat16)
        grad_k[...] = jnp.zeros_like(grad_k)
        grad_v[...] = jnp.zeros_like(grad_v)
        slab_ref[...] = jnp.zeros_like(slab_ref)

    at = pl.multiple_of(step * CHUNK, CHUNK)
    rows = pl.ds(at, CHUNK)
    cosine, sine = cos_ref[rows, :], sin_ref[rows, :]
    stack = attn_stack(plan, q_ref, cosine, sine)
    probs = attn_softmax(stack, keys[...], at)
    grads = jnp.concatenate([grad_ref[:, h * HD : (h + 1) * HD] for h in range(plan.ha)], axis=0)
    grad_probs = cols_by_cols(grads, values[...])
    delta = jnp.sum(probs * grad_probs, axis=1, keepdims=True)
    grad_scores = (probs * (grad_probs - delta)).astype(jnp.bfloat16)
    grad_q = mm(grad_scores, keys[...]) * scale
    for h in range(plan.ha):
        slab_ref[rows, h * HD : (h + 1) * HD] = turned(
            grad_q[h * CHUNK : (h + 1) * CHUNK], cosine, -sine
        ).astype(jnp.bfloat16)
    grad_k[...] += mm_tn(grad_scores, stack)
    grad_v[...] += mm_tn(probs, grads)

    @pl.when(step == pl.num_programs(0) - 1)
    def _():
        slab_ref[:, plan.B : plan.B + HD] = turned(
            grad_k[...] * scale, cos_ref[...], -sin_ref[...]
        ).astype(jnp.bfloat16)
        slab_ref[:, plan.B + HD : plan.B + 2 * HD] = grad_v[...].astype(jnp.bfloat16)


def attn_bwd(plan, proj, tables, grad):
    length = proj.shape[0]
    whole = lambda i: (0, 0)
    return pl.pallas_call(
        functools.partial(attn_bwd_kernel, plan),
        grid=(length // CHUNK,),
        out_shape=jax.ShapeDtypeStruct((length, plan.A), jnp.bfloat16),
        in_specs=[
            pl.BlockSpec((CHUNK, plan.R), lambda i: (i, 0)),
            pl.BlockSpec((length, HD), lambda i: (0, plan.B // HD)),
            pl.BlockSpec((length, HD), lambda i: (0, plan.B // HD + 1)),
            pl.BlockSpec((length, HD), whole),
            pl.BlockSpec((length, HD), whole),
            pl.BlockSpec((CHUNK, plan.R), lambda i: (i, 0)),
        ],
        out_specs=pl.BlockSpec((length, plan.A), whole),
        scratch_shapes=[pltpu.VMEM((length, HD), jnp.bfloat16)] * 2
        + [pltpu.VMEM((length, HD), jnp.float32)] * 2,
        compiler_params=pltpu.CompilerParams(vmem_limit_bytes=VMEM),
    )(proj, proj, proj, *tables, grad)


def head_spread(plan):
    return ((iota((PAD, plan.R), 1) >> 6) == iota((PAD, plan.R), 0)).astype(jnp.float32)


def head_gather(plan):
    return ((iota((plan.R, PAD), 0) >> 6) == iota((plan.R, PAD), 1)).astype(jnp.float32)


def lower_ones():
    shape = (CHUNK, CHUNK)
    return (iota(shape, 0) >= iota(shape, 1)).astype(jnp.float32)


def space_parts(plan, dt_raw, window, conv_ref, head_ref, pick_ref):
    total = conv_ref[4:5, :]
    for k in range(CONV):
        at = 8 - CONV + 1 + k
        total = total + conv_ref[k : k + 1, :] * window[at : at + CHUNK, :]
    raw = exact(dt_raw, pick_ref[...]) + head_ref[1:2, :]
    steps = jnp.maximum(raw, 0.0) + jnp.log1p(jnp.exp(-jnp.abs(raw)))
    logs = -steps * jnp.exp(head_ref[0:1, :])
    cumul = exact(lower_ones(), logs)
    return total, raw, steps, logs, cumul


def decay_of(cumul, cumul_t, causal, h):
    gaps = cumul[:, h : h + 1] - cumul_t[h : h + 1, :]
    return jnp.exp(jnp.where(causal, gaps, masked_score))


def space_fwd_kernel(
    plan, proj_ref, shared_ref, conv_ref, head_ref, pick_ref, gated_ref, made_ref, before_ref, state, window
):
    R = plan.R
    step = pl.program_id(0)

    @pl.when(step == 0)
    def _():
        state[...] = jnp.zeros_like(state)
        window[0:8, :] = jnp.zeros((8, window.shape[1]), jnp.float32)

    @pl.when(step > 0)
    def _():
        window[0:8, :] = window[CHUNK : CHUNK + 8, :]

    window[8 : CHUNK + 8, :R] = proj_ref[:, plan.B : plan.B + R]
    window[8 : CHUNK + 8, R:] = shared_ref[:, : 2 * NS]
    total, _, steps, _, cumul = space_parts(
        plan, shared_ref[:, 2 * NS :], window, conv_ref, head_ref, pick_ref
    )
    post = total * jax.nn.sigmoid(total)
    x = post[:, :R]
    b = post[:, R : R + NS].astype(jnp.bfloat16)
    c = post[:, R + NS :].astype(jnp.bfloat16)
    spread_heads = head_spread(plan)
    cumul_t = cumul.T
    last = cumul[CHUNK - 1 : CHUNK, :]
    tail = jnp.exp(last - cumul)
    weighted = x * exact(steps, spread_heads)
    causal = iota((CHUNK, CHUNK), 0) >= iota((CHUNK, CHUNK), 1)
    inner = cols_by_cols(c, b)
    before = state[...]
    before_ref[0] = before.astype(jnp.bfloat16)
    made = mm(c, before) * exact(jnp.exp(cumul), spread_heads)
    made = made + exact(jnp.broadcast_to(head_ref[2:3, :], (8, PAD)), spread_heads)[0:1] * x
    left = iota((CHUNK, 2 * MP), 1) < MP
    weighted_low = weighted.astype(jnp.bfloat16)
    intra = []
    for pair in range(plan.hm // 2):
        lanes = weighted_low[:, pair * 2 * MP : (pair + 1) * 2 * MP]
        one = mm(inner * decay_of(cumul, cumul_t, causal, 2 * pair), lanes)
        two = mm(inner * decay_of(cumul, cumul_t, causal, 2 * pair + 1), lanes)
        intra.append(jnp.where(left, one, two))
    made = made + jnp.concatenate(intra, axis=1)
    state[...] = before * exact(
        jnp.broadcast_to(jnp.exp(last), (8, PAD)), spread_heads
    )[0:1] + mm_tn(b, weighted * exact(tail, spread_heads))
    z = proj_ref[:, :R]
    made_ref[...] = made
    gated_ref[...] = made * (z * jax.nn.sigmoid(z))


def space_fwd(plan, proj, shared, conv, heads, pick):
    length = proj.shape[0]
    chunks = length // CHUNK
    W = plan.W
    whole = lambda i: (0, 0)
    rows = lambda i: (i, 0)
    return pl.pallas_call(
        functools.partial(space_fwd_kernel, plan),
        grid=(chunks,),
        out_shape=(
            jax.ShapeDtypeStruct((length, plan.R), jnp.float32),
            jax.ShapeDtypeStruct((length, plan.R), jnp.float32),
            jax.ShapeDtypeStruct((chunks, NS, plan.R), jnp.bfloat16),
        ),
        in_specs=[
            pl.BlockSpec((CHUNK, plan.A), rows),
            pl.BlockSpec((CHUNK, plan.K), rows),
            pl.BlockSpec((8, W), whole),
            pl.BlockSpec((8, PAD), whole),
            pl.BlockSpec((PAD, PAD), whole),
        ],
        out_specs=(
            pl.BlockSpec((CHUNK, plan.R), rows),
            pl.BlockSpec((CHUNK, plan.R), rows),
            pl.BlockSpec((1, NS, plan.R), lambda i: (i, 0, 0)),
        ),
        scratch_shapes=[
            pltpu.VMEM((NS, plan.R), jnp.float32),
            pltpu.VMEM((CHUNK + 8, W), jnp.float32),
        ],
        compiler_params=pltpu.CompilerParams(vmem_limit_bytes=VMEM),
    )(proj, shared, conv, heads, pick)


def space_bwd_kernel(
    plan, proj_ref, shared_ref, prev_ref, prev_shared, conv_ref, head_ref, pick_ref, grad_ref, made_ref,
    before_ref, slab_ref, slab_shared, conv_acc, head_acc, skip_acc, d_state, window, d_window,
):
    R = plan.R
    step = pl.program_id(0)
    chunk = pl.num_programs(0) - 1 - step

    @pl.when(step == 0)
    def _():
        d_state[...] = jnp.zeros_like(d_state)
        d_window[CHUNK : CHUNK + 8, :] = jnp.zeros((8, plan.W), jnp.float32)
        conv_acc[...] = jnp.zeros_like(conv_acc)
        head_acc[...] = jnp.zeros_like(head_acc)
        skip_acc[...] = jnp.zeros_like(skip_acc)

    @pl.when(step > 0)
    def _():
        d_window[CHUNK : CHUNK + 8, :] = d_window[0:8, :]

    window[0:8, :R] = jnp.where(chunk == 0, 0.0, prev_ref[:, plan.B : plan.B + R])
    window[0:8, R:] = jnp.where(chunk == 0, 0.0, prev_shared[:, : 2 * NS])
    window[8 : CHUNK + 8, :R] = proj_ref[:, plan.B : plan.B + R]
    window[8 : CHUNK + 8, R:] = shared_ref[:, : 2 * NS]
    total, raw, steps, logs, cumul = space_parts(
        plan, shared_ref[:, 2 * NS :], window, conv_ref, head_ref, pick_ref
    )
    sig = jax.nn.sigmoid(total)
    post = total * sig
    x = post[:, :R]
    b = post[:, R : R + NS].astype(jnp.bfloat16)
    c = post[:, R + NS :].astype(jnp.bfloat16)
    spread_heads = head_spread(plan)
    gather_heads = head_gather(plan)
    cumul_t = cumul.T
    last = cumul[CHUNK - 1 : CHUNK, :]
    steps_wide = exact(steps, spread_heads)
    tail_wide = exact(jnp.exp(last - cumul), spread_heads)
    grow_wide = exact(jnp.exp(cumul), spread_heads)
    last_wide = exact(jnp.broadcast_to(jnp.exp(last), (8, PAD)), spread_heads)[0:1]
    skip_wide = exact(jnp.broadcast_to(head_ref[2:3, :], (8, PAD)), spread_heads)[0:1]
    weighted = x * steps_wide
    causal = iota((CHUNK, CHUNK), 0) >= iota((CHUNK, CHUNK), 1)
    inner = cols_by_cols(c, b)

    z = proj_ref[:, :R]
    sig_z = jax.nn.sigmoid(z)
    grad = grad_ref[...]
    d_made = grad * (z * sig_z)
    slab_ref[:, :R] = (grad * made_ref[...] * (sig_z * (1.0 + z * (1.0 - sig_z)))).astype(
        jnp.bfloat16
    )
    skip_acc[0:1, :] += jnp.sum(d_made * x, axis=0, keepdims=True)

    before = before_ref[0]
    d_after = d_state[...]
    d_after_low = d_after.astype(jnp.bfloat16)
    grown = d_made * grow_wide
    grown_low = grown.astype(jnp.bfloat16)
    carried = mm(c, before)
    d_c = mm_nt(grown_low, before)
    pulled = weighted * tail_wide
    d_pulled = mm(b, d_after_low)
    d_b = mm_nt(pulled, d_after_low)
    d_cumul = exact(grown * carried, gather_heads)
    kept = exact(d_pulled * pulled, gather_heads)
    d_cumul = d_cumul - kept
    decayed = jnp.sum(d_after * before.astype(jnp.float32), axis=0, keepdims=True) * last_wide
    d_last = jnp.sum(kept, axis=0, keepdims=True) + exact(
        jnp.broadcast_to(decayed, (8, R)), gather_heads
    )[0:1]
    d_state[...] = d_after * last_wide + mm_tn(c, grown_low)

    left = iota((CHUNK, 2 * MP), 1) < MP
    lane = iota((CHUNK, PAD), 1)
    sub = iota((8, CHUNK), 0)
    weighted_low = weighted.astype(jnp.bfloat16)
    d_made_low = d_made.astype(jnp.bfloat16)
    d_inner = jnp.zeros((CHUNK, CHUNK), jnp.float32)
    columns = jnp.zeros((8, CHUNK), jnp.float32)
    d_weighted = []
    for pair in range(plan.hm // 2):
        at = slice(pair * 2 * MP, (pair + 1) * 2 * MP)
        lanes, d_lanes = weighted_low[:, at], d_made_low[:, at]
        halves = []
        for which in range(2):
            h = 2 * pair + which
            decay = decay_of(cumul, cumul_t, causal, h)
            whole = inner * decay
            halves.append(mm_tn(whole, d_lanes))
            mine = jnp.where(left if which == 0 else ~left, d_lanes, jnp.zeros_like(d_lanes))
            d_whole = cols_by_cols(mine, lanes)
            d_inner = d_inner + d_whole * decay
            slope = d_whole * whole
            d_cumul = d_cumul + jnp.where(lane == h, jnp.sum(slope, axis=1, keepdims=True), 0.0)
            columns = columns + jnp.where(sub == h, jnp.sum(slope, axis=0, keepdims=True), 0.0)
        d_weighted.append(jnp.where(left, halves[0], halves[1]))
    d_weighted = jnp.concatenate(d_weighted, axis=1) + d_pulled * tail_wide
    columns = jnp.concatenate([columns, jnp.zeros((CHUNK - 8, CHUNK), jnp.float32)], axis=0).T
    d_cumul = d_cumul - columns
    d_inner_low = d_inner.astype(jnp.bfloat16)
    d_c = d_c + mm(d_inner_low, b)
    d_b = d_b + mm_tn(d_inner_low, c)
    d_x = d_weighted * steps_wide + skip_wide * d_made
    d_steps = exact(d_weighted * x, gather_heads)
    upper = (iota((CHUNK, CHUNK), 0) <= iota((CHUNK, CHUNK), 1)).astype(jnp.float32)
    d_logs = exact(upper, d_cumul) + d_last
    d_steps = d_steps - jnp.exp(head_ref[0:1, :]) * d_logs
    d_raw = d_steps * jax.nn.sigmoid(raw)
    d_raw = jnp.where(lane < plan.hm, d_raw, 0.0)
    slab_shared[:, 2 * NS :] = lax.dot_general(
        d_raw,
        pick_ref[...],
        (((1,), (1,)), ((), ())),
        precision=lax.Precision.HIGHEST,
        preferred_element_type=jnp.float32,
    ).astype(jnp.bfloat16)
    head_acc[0:1, :] += jnp.sum(d_logs * logs, axis=0, keepdims=True)
    head_acc[1:2, :] += jnp.sum(d_raw, axis=0, keepdims=True)

    d_post = jnp.concatenate([d_x, d_b, d_c], axis=1)
    d_total = d_post * (sig * (1.0 + total * (1.0 - sig)))
    d_window[0:CHUNK, :] = d_total
    d_xbc = jnp.zeros((CHUNK, plan.W), jnp.float32)
    for k in range(CONV):
        shift = CONV - 1 - k
        d_xbc = d_xbc + conv_ref[k : k + 1, :] * d_window[shift : shift + CHUNK, :]
        at = 8 - CONV + 1 + k
        conv_acc[k : k + 1, :] += jnp.sum(
            d_total * window[at : at + CHUNK, :], axis=0, keepdims=True
        )
    conv_acc[4:5, :] += jnp.sum(d_total, axis=0, keepdims=True)
    slab_ref[:, plan.B : plan.B + R] = d_xbc[:, :R].astype(jnp.bfloat16)
    slab_shared[:, : 2 * NS] = d_xbc[:, R:].astype(jnp.bfloat16)
    if plan.B + R < plan.A:
        slab_ref[:, plan.B + R :] = jnp.zeros((CHUNK, plan.A - plan.B - R), jnp.bfloat16)


def space_bwd(plan, proj, shared, conv, heads, pick, grad, made, before):
    length = proj.shape[0]
    chunks = length // CHUNK
    W = plan.W
    whole = lambda i: (0, 0)
    rows = lambda i: (chunks - 1 - i, 0)
    per = CHUNK // 8
    return pl.pallas_call(
        functools.partial(space_bwd_kernel, plan),
        grid=(chunks,),
        out_shape=(
            jax.ShapeDtypeStruct((length, plan.A), jnp.bfloat16),
            jax.ShapeDtypeStruct((length, plan.K), jnp.bfloat16),
            jax.ShapeDtypeStruct((8, W), jnp.float32),
            jax.ShapeDtypeStruct((8, PAD), jnp.float32),
            jax.ShapeDtypeStruct((8, plan.R), jnp.float32),
        ),
        in_specs=[
            pl.BlockSpec((CHUNK, plan.A), rows),
            pl.BlockSpec((CHUNK, plan.K), rows),
            pl.BlockSpec((8, plan.A), lambda i: (jnp.maximum((chunks - 1 - i) * per - 1, 0), 0)),
            pl.BlockSpec((8, plan.K), lambda i: (jnp.maximum((chunks - 1 - i) * per - 1, 0), 0)),
            pl.BlockSpec((8, W), whole),
            pl.BlockSpec((8, PAD), whole),
            pl.BlockSpec((PAD, PAD), whole),
            pl.BlockSpec((CHUNK, plan.R), rows),
            pl.BlockSpec((CHUNK, plan.R), rows),
            pl.BlockSpec((1, NS, plan.R), lambda i: (chunks - 1 - i, 0, 0)),
        ],
        out_specs=(
            pl.BlockSpec((CHUNK, plan.A), rows),
            pl.BlockSpec((CHUNK, plan.K), rows),
            pl.BlockSpec((8, W), whole),
            pl.BlockSpec((8, PAD), whole),
            pl.BlockSpec((8, plan.R), whole),
        ),
        scratch_shapes=[
            pltpu.VMEM((NS, plan.R), jnp.float32),
            pltpu.VMEM((CHUNK + 8, W), jnp.float32),
            pltpu.VMEM((CHUNK + 8, W), jnp.float32),
        ],
        compiler_params=pltpu.CompilerParams(vmem_limit_bytes=VMEM),
    )(proj, shared, proj, shared, conv, heads, pick, grad, made, before)


def body(
    inputs,
    cotangent,
    w_in,
    w_in_m,
    w_in_v,
    w_mix,
    w_mix_m,
    w_mix_v,
    w_up,
    w_up_m,
    w_up_v,
    w_down,
    w_down_m,
    w_down_v,
    vectors,
    vectors_m,
    vectors_v,
):
    low = jnp.bfloat16
    count = lax.axis_size("ctx")
    ways = lax.axis_size("wshard")
    place = lax.axis_index("ctx")
    plan = Plan(count)
    R, hm = plan.R, plan.hm
    is_space = place >= plan.attn
    space = jnp.maximum(place - plan.attn, 0)

    gain_attn, gain_ffn, gain_ssm, conv_bias, conv_weight, a_log, dt_bias, d_skip = split_vectors(
        vectors
    )
    whole, in_own, shared_own, up_some, mix_own, down_some = start_call(
        plan, count, inputs[0], w_in, w_up, w_mix, w_down, 1
    )

    own = lambda a, size, axis=0: lax.dynamic_slice_in_dim(a, space * size, size, axis)
    gain_own = own(gain_ssm, R)
    W = plan.W
    conv = jnp.concatenate(
        [
            jnp.concatenate([own(conv_weight, R, 1), conv_weight[:, DSSM:]], axis=1),
            jnp.concatenate([own(conv_bias, R), conv_bias[DSSM:]])[None],
            jnp.zeros((8 - CONV - 1, W), jnp.float32),
        ]
    )
    heads = jnp.stack([own(v, hm) for v in (a_log, dt_bias, d_skip)])
    heads = jnp.pad(heads, ((0, 5), (0, PAD - hm)))
    column = lax.broadcasted_iota(jnp.int32, (PAD, PAD), 1)
    row = lax.broadcasted_iota(jnp.int32, (PAD, PAD), 0)
    pick = jnp.logical_and(row == column + space * hm, column < hm).astype(jnp.float32)
    tables = rope_tables(count * inputs.shape[1])

    source = inputs[0].astype(jnp.float32)
    whole = whole.astype(jnp.float32)
    in_own, cotangent_late = lax.optimization_barrier((in_own, cotangent[0]))
    upstream_all = gather_ctx(cotangent_late)
    length = whole.shape[0]
    rows = inputs.shape[1]
    unit = whole * lax.rsqrt(jnp.mean(whole * whole, axis=-1, keepdims=True) + norm_eps)
    normed = (unit * gain_attn).astype(low)
    unit = unit.astype(low)
    proj = plain(normed, in_own)
    shared = plain(normed, shared_own)

    def space_ahead(proj, shared):
        return space_fwd(plan, proj, shared, conv, heads, pick)

    def attn_ahead(proj, shared):
        made = attn_fwd(plan, proj, tables)
        blank = jnp.zeros((length // CHUNK, NS, R), low)
        return made, jnp.zeros_like(made), blank

    made, raw_made, before = lax.cond(is_space, space_ahead, attn_ahead, proj, shared)
    square = jnp.where(is_space, jnp.sum(made * made, axis=1), 0.0)
    factor = lax.rsqrt(sum_rows(count, square, 5) / DSSM + norm_eps)
    mixed = jnp.where(is_space, made * factor[:, None] * gain_own, made).astype(low)
    wide = lambda *shape: jax.ShapeDtypeStruct(shape, jnp.float32)
    side = (up_some, down_some)
    middle, two_all, up_own, down_own = flow_call(
        branch_kernel,
        count,
        rows,
        (mixed, mix_own, inputs[0], gain_ffn[None]),
        (wide(rows, D),),
        True,
        True,
        (side, *share_shapes(side)),
        8,
    )
    two_all = two_all.reshape(length, D)
    up_own, down_own = up_own.reshape(D, -1), down_own.reshape(-1, D)

    gate_up = plain(two_all, up_own)
    half = FF // count
    swiglu = lambda g: jax.nn.silu(g[:, :half]) * g[:, half:]
    activated, act_pull = jax.vjp(swiglu, gate_up)
    activated = activated.astype(low)
    late = plain(activated, down_own).astype(low)
    grad_down = rows_by_rows(activated, upstream_all)
    grad_act = cols_by_cols(upstream_all, down_own)
    grad_gate_up = act_pull(grad_act)[0].astype(low)
    grad_up = rows_by_rows(two_all, grad_gate_up)
    cut = lambda g, blocks: g.astype(low).reshape(blocks, ways, -1, g.shape[1])
    side = (cut(grad_up, count), cut(grad_down, 1))
    grad_gate_up, late = lax.optimization_barrier((grad_gate_up, late))
    grad_middle, grad_gain_ffn, branch_all, up_mine, down_mine = flow_call(
        feed_back_kernel,
        count,
        rows,
        (grad_gate_up, up_own, cotangent[0], middle, gain_ffn[None]),
        (wide(rows, D), wide(8, D)),
        True,
        False,
        (side, *collect_shapes(("cols", "rows"), side)),
        9,
    )
    grad_gain_ffn = grad_gain_ffn[0]
    branch_all = branch_all.reshape(length, D)
    branch_all, late = lax.optimization_barrier((branch_all, late))
    late = scatter_ctx(late)
    grad_mix = rows_by_rows(mixed, branch_all)
    grad_made = cols_by_cols(branch_all, mix_own).astype(low)
    made_wide = grad_made.astype(jnp.float32)
    dots = jnp.where(is_space, jnp.sum(made_wide * gain_own * made, axis=1), 0.0)
    dots = sum_rows(count, dots, 6)
    grad_gain_own = jnp.sum(made_wide * made * factor[:, None], axis=0)
    grad_gated = made_wide * gain_own * factor[:, None] - made * (factor**3 * dots / DSSM)[:, None]

    def space_back(proj, shared, grad_gated, grad_made):
        return space_bwd(plan, proj, shared, conv, heads, pick, grad_gated, raw_made, before)

    def attn_back(proj, shared, grad_gated, grad_made):
        blank = lambda k: jnp.zeros((8, k), jnp.float32)
        none = jnp.zeros(shared.shape, low)
        return attn_bwd(plan, proj, tables, grad_made), none, blank(W), blank(PAD), blank(R)

    grad_proj, grad_shared, conv_acc, head_acc, skip_acc = lax.cond(
        is_space, space_back, attn_back, proj, shared, grad_gated, grad_made
    )
    grad_in = rows_by_rows(unit, grad_proj)
    grad_in_shared = rows_by_rows(unit, grad_shared)
    grad_gain_attn = jnp.sum(grad_in * in_own, axis=1) + jnp.sum(grad_in_shared * shared_own, axis=1)
    grad_in = grad_in * gain_attn[:, None]
    grad_in_shared = grad_in_shared * gain_attn[:, None]
    grad_proj, late = lax.optimization_barrier((grad_proj, late))
    outputs = (middle + late).astype(low)[None]
    def placed(piece, size, total, axis=0):
        shape = list(piece.shape)
        shape[axis] = total
        start = [0] * piece.ndim
        start[axis] = space * size
        return lax.dynamic_update_slice(jnp.zeros(shape, piece.dtype), piece, start)

    conv_w_grad, conv_b_grad = conv_acc[:CONV], conv_acc[CONV]
    a_grad, bias_grad = head_acc[0, :hm], head_acc[1, :hm]
    skip_grad = jnp.sum(skip_acc[0].reshape(hm, MP), axis=1)
    grad_gain_own = jnp.where(is_space, grad_gain_own, 0.0)
    vector_local = jnp.concatenate(
        [
            grad_gain_attn,
            grad_gain_ffn,
            placed(grad_gain_own, R, DSSM),
            placed(conv_b_grad[:R], R, DSSM),
            conv_b_grad[R:],
            jnp.concatenate(
                [placed(conv_w_grad[:, :R], R, DSSM, 1), conv_w_grad[:, R:]], axis=1
            ).reshape(CONV * CONVCH),
            placed(a_grad, hm, MH),
            placed(bias_grad, hm, MH),
            placed(skip_grad, hm, MH),
        ]
    )
    pad = -vectors.shape[0] % 1024
    vector_local = jnp.pad(vector_local, (0, pad)).reshape(-1, 128)
    side = (cut(grad_in, count), cut(grad_in_shared, count), cut(grad_mix, 1))
    side_shapes, side_scratch = collect_shapes(SUMS, side)
    input_grad, vector_sum, in_mine, shared_mine, mix_mine = flow_call(
        source_back_kernel,
        count,
        rows,
        (
            grad_proj,
            grad_shared,
            in_own,
            shared_own,
            inputs[0],
            grad_middle,
            gain_attn[None],
            vector_local,
        ),
        (wide(rows, D), wide(*vector_local.shape)),
        False,
        False,
        (side, side_shapes, side_scratch + sum_scratch(count, vector_local.shape)),
        10,
    )
    input_grad = input_grad[None]

    in_shard = from_slabs(plan, in_mine, shared_mine)
    up_shard = up_from_slabs(plan, up_mine)
    mix_shard = mix_mine[0].astype(jnp.float32)
    down_shard = down_mine[0].astype(jnp.float32)

    vector_grad = vector_sum.reshape(-1)[: vectors.shape[0]]
    new_in = adamw(w_in, w_in_m, w_in_v, in_shard, 2.0 * D ** (-0.5), decay_weight)
    new_mix = adamw(w_mix, w_mix_m, w_mix_v, mix_shard, DSSM ** (-0.5), decay_weight)
    new_up = adamw(w_up, w_up_m, w_up_v, up_shard, D ** (-0.5), decay_weight)
    new_down = adamw(w_down, w_down_m, w_down_v, down_shard, FF ** (-0.5), decay_weight)
    new_vec = adamw(vectors, vectors_m, vectors_v, vector_grad, vector_rate, 0.0)
    return (outputs, input_grad, *new_in, *new_mix, *new_up, *new_down, *new_vec)


def solution(mesh):
    tokens = P("wshard", "ctx", None)
    weight = P(("ctx", "wshard"), None)
    return jax.shard_map(
        body,
        mesh=mesh,
        in_specs=(tokens,) * 2 + (weight,) * 12 + (P(),) * 3,
        out_specs=(tokens,) * 2 + (weight,) * 12 + (P(),) * 3,
        check_vma=False,
    )
```

```python
import functools
import math

import jax
import jax.numpy as jnp
from jax import lax
from jax.experimental import pallas as pl
from jax.experimental.pallas import tpu as pltpu
from jax.sharding import PartitionSpec as P

D = 2048
FF = 4096
AH = 8
KVH = 2
HD = 128
MH = 48
MP = 64
NS = 256
CONV = 4
STEP = 10
DSSM = 3072
CONVCH = 3584
ATT = AH * HD
MIXIN = ATT + DSSM
GROUP = AH // KVH
CHUNK = 128
PAD = 128
VMEM = 60 * 1024 * 1024


norm_eps = 1e-05
rope_base = 10000.0
beta_one = 0.9
beta_two = 0.95
adam_eps = 1e-08
decay_weight = 0.1
vector_rate = 0.5
masked_score = -1e30

K_AT = ATT
V_AT = K_AT + KVH * HD
Z_AT = V_AT + KVH * HD
X_AT = Z_AT + DSSM
BC_AT = X_AT + DSSM
DT_AT = BC_AT + 2 * NS
END = DT_AT + MH


def rows_by_rows(left, right):
    return lax.dot_general(
        left, right, (((0,), (0,)), ((), ())), preferred_element_type=jnp.float32
    )


def cols_by_cols(left, right):
    return lax.dot_general(
        left, right, (((1,), (1,)), ((), ())), preferred_element_type=jnp.float32
    )


def plain(left, right):
    return jnp.dot(left, right, preferred_element_type=jnp.float32)


def rms_norm(values, gain):
    factor = lax.rsqrt(jnp.mean(values * values, axis=-1, keepdims=True) + norm_eps)
    return values * factor * gain


def split_vectors(vectors):
    extents = (D, D, DSSM, CONVCH, CONV * CONVCH, MH, MH, MH)
    pieces = []
    offset = 0
    for extent in extents:
        pieces.append(lax.slice_in_dim(vectors, offset, offset + extent))
        offset = offset + extent
    pieces[4] = pieces[4].reshape(CONV, CONVCH)
    return pieces


def adamw(weight, moment, second, grad, rate, decay):
    moment = beta_one * moment + (1.0 - beta_one) * grad
    second = beta_two * second + (1.0 - beta_two) * grad * grad
    corrected = moment / (1.0 - beta_one**STEP)
    divisor = jnp.sqrt(second / (1.0 - beta_two**STEP)) + adam_eps
    return (weight - rate * (corrected / divisor + decay * weight), moment, second)


class Plan:
    def __init__(self, count):
        self.count = count
        self.R = MIXIN // count
        self.attn = ATT // self.R
        self.ha = self.R // HD
        self.hm = self.R // MP
        self.B = self.R
        self.A = self.R + max(self.R, 2 * HD)
        self.K = 2 * NS + PAD
        self.W = self.R + 2 * NS

    def kv_of(self, c):
        return c * self.ha // GROUP


def from_slabs(plan, slabs, shared):
    R, B = plan.R, plan.B
    slabs = slabs.astype(jnp.float32)
    shared = shared.astype(jnp.float32)
    heads = range(plan.attn)
    spaces = range(plan.attn, plan.count)
    total = lambda items: functools.reduce(lambda a, b: a + b, items)
    parts = [slabs[c][:, :R] for c in heads]
    for at in (B, B + HD):
        for g in range(KVH):
            parts.append(total([slabs[c][:, at : at + HD] for c in heads if plan.kv_of(c) == g]))
    parts += [slabs[c][:, :R] for c in spaces]
    parts += [slabs[c][:, B : B + R] for c in spaces]
    parts.append(total([shared[c][:, : END - BC_AT] for c in spaces]))
    return jnp.concatenate(parts, axis=1)


def up_from_slabs(plan, slabs):
    G = FF // plan.count
    slabs = slabs.astype(jnp.float32)
    return jnp.concatenate(
        [slabs[c][:, :G] for c in range(plan.count)] + [slabs[c][:, G:] for c in range(plan.count)],
        axis=1,
    )


def gather_ctx(x):
    return lax.all_gather(x, "ctx", axis=0, tiled=True)


def scatter_ctx(x):
    return lax.psum_scatter(
        x.astype(jnp.bfloat16), "ctx", scatter_dimension=0, tiled=True
    ).astype(jnp.float32)


MESH = pl.DeviceIdType.MESH


def here():
    c, w = lax.axis_index("ctx"), lax.axis_index("wshard")
    return c, w, w + 1 - 2 * (w % 2), (w + 2) % 4


def greet(devices):
    barrier = pltpu.get_barrier_semaphore()
    for device in devices:
        pl.semaphore_signal(barrier, inc=1, device_id=device, device_id_type=MESH)
    pl.semaphore_wait(barrier, len(devices))


def remote(src, dst, send, recv, device):
    return pltpu.make_async_remote_copy(
        src_ref=src, dst_ref=dst, send_sem=send, recv_sem=recv, device_id=device, device_id_type=MESH
    )


def collect_job(n, kinds, sources, targets, extra):
    c, w, sib, across = here()
    x, core = w // 2, w % 2
    far = 1 - x
    pending = []
    jobs = []
    for j, kind in enumerate(kinds):
        jobs.append((kind, sources[j], targets[j]) + tuple(extra[10 * j : 10 * j + 10]))

    def order(job, s):
        return (c + s) % n if job[1].shape[0] > 1 else 0

    def count(job):
        return job[1].shape[0]

    most = max(count(job) for job in jobs)
    steps = [s % most for s in range(1, most + 1)]
    for place, slot in ((far, 0), (x, 1)):
        for s in steps:
            for job in jobs:
                if s >= count(job):
                    continue
                _, src, _, kbuf, _, _, _, k_send, k_recv = job[:9]
                q = order(job, s)
                out = remote(
                    src.at[q, place * 2 + 1 - core],
                    kbuf.at[slot, q],
                    k_send.at[slot, s],
                    k_recv.at[slot, q],
                    (c, sib),
                )
                out.start()
                pending.append(out)
    yield
    wide = jnp.float32
    for s in steps:
        for job in jobs:
            if s >= count(job):
                continue
            _, src, _, kbuf, stage, xbuf, _, k_send, k_recv, x_send, x_recv = job[:11]
            q = order(job, s)
            got = kbuf.at[0, q]
            remote(got, got, k_send.at[0, s], k_recv.at[0, q], (c, sib)).wait_recv()
            stage[q] = (src[q, far * 2 + core].astype(wide) + kbuf[0, q].astype(wide)).astype(
                stage.dtype
            )
            out = remote(stage.at[q], xbuf.at[q], x_send.at[s], x_recv.at[q], (c, across))
            out.start()
            pending.append(out)
    yield
    for s in steps:
        for job in jobs:
            if s >= count(job):
                continue
            kind, src, dst, kbuf, stage, xbuf, done, k_send, k_recv, x_send, x_recv = job[:11]
            a_send, a_recv = job[11], job[12]
            q = order(job, s)
            got = kbuf.at[1, q]
            remote(got, got, k_send.at[1, s], k_recv.at[1, q], (c, sib)).wait_recv()
            got = xbuf.at[q]
            remote(got, got, x_send.at[s], x_recv.at[q], (c, across)).wait_recv()
            total = src[q, x * 2 + core].astype(wide) + kbuf[1, q].astype(wide)
            total = (total + xbuf[q].astype(wide)).astype(stage.dtype)
            if kind == "cols" and s > 0:
                done[q] = total
                out = remote(done.at[q], dst.at[c], a_send.at[s], a_recv.at[c], (q, w))
                out.start()
                pending.append(out)
            else:
                dst[q] = total
        yield
    for job in jobs:
        if job[0] == "cols":
            dst, a_send, a_recv = job[2], job[11], job[12]
            for s in range(1, n):
                q = (c + n - s) % n
                got = dst.at[q]
                remote(got, got, a_send.at[s], a_recv.at[q], (q, w)).wait_recv()
    for out in pending:
        out.wait_send()


def home_job(n, source, target, send, recv):
    c, w = lax.axis_index("ctx"), lax.axis_index("wshard")
    target[c] = source[c]
    copies = [
        remote(source.at[(c + s) % n], target.at[c], send.at[s], recv.at[c], ((c + s) % n, w))
        for s in range(1, n)
    ]
    for copy in copies:
        copy.start()
    yield
    for s in range(1, n):
        q = (c + n - s) % n
        remote(source.at[q], target.at[q], send.at[s], recv.at[q], (q, w)).wait_recv()
    for copy in copies:
        copy.wait_send()


def collect_shapes(kinds, sources):
    shapes, scratch = [], []
    for kind, src in zip(kinds, sources):
        count, _, rows, size = src.shape
        block = (count, rows, size)
        shapes.append(jax.ShapeDtypeStruct(block, src.dtype))
        scratch += [
            pltpu.VMEM((2,) + block, src.dtype),
            pltpu.VMEM(block, src.dtype),
            pltpu.VMEM(block, src.dtype),
            pltpu.VMEM(block if kind == "cols" else (1, 16, 128), src.dtype),
            pltpu.SemaphoreType.DMA((2, count)),
            pltpu.SemaphoreType.DMA((2, count)),
            pltpu.SemaphoreType.DMA((count,)),
            pltpu.SemaphoreType.DMA((count,)),
            pltpu.SemaphoreType.DMA((count,)),
            pltpu.SemaphoreType.DMA((count,)),
        ]
    return shapes, scratch


def row_sum_kernel(n, x_ref, out_ref, got, send, recv):
    c, w = lax.axis_index("ctx"), lax.axis_index("wshard")
    greet([((c + s) % n, w) for s in range(1, n)])
    copies = [
        remote(x_ref, got.at[c], send.at[s], recv.at[c], ((c + s) % n, w)) for s in range(1, n)
    ]
    for copy in copies:
        copy.start()
    total = x_ref[...]
    for s in range(1, n):
        q = (c + n - s) % n
        remote(x_ref, got.at[q], send.at[s], recv.at[q], (q, w)).wait_recv()
        total = total + got[q]
    out_ref[...] = total
    for copy in copies:
        copy.wait_send()


def sum_rows(n, x, collective_id):
    block = x.reshape(-1, 128)
    return pl.pallas_call(
        functools.partial(row_sum_kernel, n),
        out_shape=jax.ShapeDtypeStruct(block.shape, x.dtype),
        in_specs=[pl.BlockSpec(memory_space=pltpu.VMEM)],
        out_specs=pl.BlockSpec(memory_space=pltpu.VMEM),
        scratch_shapes=[
            pltpu.VMEM((n,) + block.shape, x.dtype),
            pltpu.SemaphoreType.DMA((n,)),
            pltpu.SemaphoreType.DMA((n,)),
        ],
        compiler_params=pltpu.CompilerParams(
            collective_id=collective_id, has_side_effects=True, vmem_limit_bytes=VMEM
        ),
    )(block).reshape(x.shape)


def sum_job(n, x_ref, out_ref, kept, got, send, recv):
    c, w, sib, across = here()
    partners = [(c, sib)]
    for level in range(n.bit_length() - 1):
        reach = 2**level
        partners.append((c + reach - 2 * reach * ((c // reach) % 2), w))
    partners.append((c, across))
    out_ref[...] = x_ref[...]
    for i, partner in enumerate(partners):
        kept[i] = out_ref[...]
        swap = remote(kept.at[i], got.at[i], send.at[i], recv.at[i], partner)
        swap.start()
        yield
        swap.wait()
        out_ref[...] += got[i]


def sum_scratch(n, shape):
    stages = n.bit_length() + 1
    return [
        pltpu.VMEM((stages,) + shape, jnp.float32),
        pltpu.VMEM((stages,) + shape, jnp.float32),
        pltpu.SemaphoreType.DMA((stages,)),
        pltpu.SemaphoreType.DMA((stages,)),
    ]


def share_job(sources, targets, sems):
    c, w, sib, across = here()
    pending = []
    for j, (src, dst) in enumerate(zip(sources, targets)):
        x_send, x_recv, k_send, k_recv, own_sem = sems[5 * j : 5 * j + 5]
        for q in range(src.shape[0]):
            own = pltpu.make_async_copy(src.at[q], dst.at[q, w], own_sem.at[q])
            to_x = remote(src.at[q], dst.at[q, w], x_send.at[q], x_recv.at[q], (c, across))
            to_k = remote(src.at[q], dst.at[q, w], k_send.at[0, q], k_recv.at[0, q], (c, sib))
            for copy in (to_x, to_k, own):
                copy.start()
            pending += [to_x.wait_send, to_k.wait_send, own.wait]
    yield
    for j, dst in enumerate(targets):
        x_send, x_recv, k_send, k_recv, own_sem = sems[5 * j : 5 * j + 5]
        for q in range(dst.shape[0]):
            got = dst.at[q, across]
            remote(got, got, x_send.at[q], x_recv.at[q], (c, across)).wait_recv()
            out = remote(got, got, k_send.at[1, q], k_recv.at[1, q], (c, sib))
            out.start()
            pending.append(out.wait_send)
    yield
    for j, dst in enumerate(targets):
        x_send, x_recv, k_send, k_recv, own_sem = sems[5 * j : 5 * j + 5]
        for q in range(dst.shape[0]):
            for half, place in ((0, sib), (1, (sib + 2) % 4)):
                got = dst.at[q, place]
                remote(got, got, k_send.at[half, q], k_recv.at[half, q], (c, sib)).wait_recv()
    for wait in pending:
        wait()


def share_shapes(sources):
    shapes, sems = [], []
    for src in sources:
        count = src.shape[0]
        shapes.append(jax.ShapeDtypeStruct((count, 4) + src.shape[1:], src.dtype))
        sems += [
            pltpu.SemaphoreType.DMA((count,)),
            pltpu.SemaphoreType.DMA((count,)),
            pltpu.SemaphoreType.DMA((2, count)),
            pltpu.SemaphoreType.DMA((2, count)),
            pltpu.SemaphoreType.DMA((count,)),
        ]
    return shapes, sems


def advance(*jobs):
    jobs = list(jobs)
    while jobs:
        for job in list(jobs):
            try:
                next(job)
            except StopIteration:
                jobs.remove(job)


class Line:
    def __init__(self, n):
        self.c, self.w, self.sib, self.across = here()
        self.n, self.N = n, n // 2
        self.at, self.side = self.c // 2, self.c % 2
        self.pair = (self.c + 1 - 2 * self.side, self.w)
        self.left = (self.c - 2, self.w)
        self.right = (self.c + 2, self.w)
        self.has_left = self.at > 0
        self.has_right = self.at < self.N - 1

    def greet(self, others=()):
        barrier = pltpu.get_barrier_semaphore()
        signal = lambda d: pl.semaphore_signal(barrier, inc=1, device_id=d, device_id_type=MESH)
        sure = [self.pair] + list(others)
        for device in sure:
            signal(device)
        pl.when(self.has_left)(lambda: signal(self.left))
        pl.when(self.has_right)(lambda: signal(self.right))
        beside = (self.at + self.N - 1) // self.N + (2 * self.N - 2 - self.at) // self.N
        pl.semaphore_wait(barrier, len(sure) + beside)


def scatter_job(line, block, total, ystage, ybuf, zbuf, sems):
    y_send, y_recv, r_send, r_recv, l_send, l_recv = sems
    N, at, side = line.N, line.at, line.side
    wide = jnp.float32

    def both_ways(d):
        return ((at + d, at + d < N), (at - d, at - d >= 0)) if d else ((at, None),)

    def guarded(keep, step):
        if keep is None:
            step()
        else:
            pl.when(keep)(step)

    def y_copy(b):
        return remote(ystage.at[b], ybuf.at[b], y_send.at[b], y_recv.at[b], line.pair)

    def r_copy(b, slot):
        return remote(ybuf.at[b], zbuf.at[slot], r_send.at[b], r_recv.at[b], line.right)

    def l_copy(b, slot):
        return remote(ybuf.at[b], zbuf.at[slot], l_send.at[b], l_recv.at[b], line.left)

    for d in range(N - 1, -1, -1):
        for b, keep in both_ways(d):

            def first(b=b):
                ystage[b] = block(2 * b + 1 - side).astype(ystage.dtype)
                y_copy(b).start()

            guarded(keep, first)
        yield
    for d in range(N - 1, 0, -1):
        for b, keep, ahead in ((at + d, at + d < N, True), (at - d, at - d >= 0, False)):

            def relay(b=b, ahead=ahead):
                mine = block(2 * b + side)
                y_copy(b).wait_recv()
                mine = mine + ybuf[b].astype(wide)
                came = line.has_left if ahead else line.has_right

                @pl.when(came)
                def _():
                    (r_copy if ahead else l_copy)(b, b).wait_recv()
                    ybuf[b] = (mine + zbuf[b].astype(wide)).astype(ybuf.dtype)

                @pl.when(jnp.logical_not(came))
                def _():
                    ybuf[b] = mine.astype(ybuf.dtype)

                if ahead:
                    pl.when(b == at + 1)(lambda: r_copy(b, b).start())
                    pl.when(b > at + 1)(lambda: r_copy(b, b).start())
                else:
                    pl.when(b == at - 1)(lambda: l_copy(b, N).start())
                    pl.when(b < at - 1)(lambda: l_copy(b, b).start())

            guarded(keep, relay)
        yield
    mine = block(2 * at + side)
    y_copy(at).wait_recv()
    total[...] = mine + ybuf[at].astype(wide)

    @pl.when(line.has_left)
    def _():
        r_copy(at, at).wait_recv()
        total[...] += zbuf[at].astype(wide)

    @pl.when(line.has_right)
    def _():
        l_copy(at, N).wait_recv()
        total[...] += zbuf[N].astype(wide)

    for d in range(N):
        for b, keep in both_ways(d):
            guarded(keep, lambda b=b: y_copy(b).wait_send())
    for d in range(1, N):
        pl.when(at + d < N)(lambda d=d: r_copy(at + d, at + d).wait_send())
        pl.when(at - d >= 0)(lambda d=d: l_copy(at - d, at - d).wait_send())


def scatter_line_job(line, values, stage, slots, pair_slot, total, sems):
    r_send, r_recv, l_send, l_recv, p_send, p_recv = sems
    n, N, at, side = line.n, line.N, line.at, line.side
    wide = jnp.float32

    def copy(q, slot, ahead):
        send, recv = (r_send, r_recv) if ahead else (l_send, l_recv)
        device = line.right if ahead else line.left
        return remote(stage.at[q], slots.at[slot], send.at[q], recv.at[q], device)

    for d in range(N - 1, 0, -1):
        for b, keep, ahead in ((at + d, at + d < N, True), (at - d, at - d >= 0, False)):

            def relay(b=b, ahead=ahead):
                came = line.has_left if ahead else line.has_right
                for y in range(2):
                    q = 2 * b + y

                    @pl.when(came)
                    def _(q=q):
                        copy(q, q, ahead).wait_recv()
                        stage[q] = (values[q].astype(wide) + slots[q].astype(wide)).astype(stage.dtype)

                    @pl.when(jnp.logical_not(came))
                    def _(q=q):
                        stage[q] = values[q]

                    if ahead:
                        copy(q, q, True).start()
                    else:
                        pl.when(b == at - 1)(lambda q=q, y=y: copy(q, n + y, False).start())
                        pl.when(b < at - 1)(lambda q=q: copy(q, q, False).start())

            pl.when(keep)(relay)
        yield

    def reach(q, y_slot):
        pl.when(line.has_left)(lambda: copy(q, q, True).wait_recv())
        pl.when(line.has_right)(lambda: copy(q, y_slot, False).wait_recv())
        left = jnp.where(line.has_left, slots[q].astype(wide), 0.0)
        right = jnp.where(line.has_right, slots[y_slot].astype(wide), 0.0)
        return values[q].astype(wide) + left + right

    other = 2 * at + 1 - side
    stage[other] = reach(other, n + 1 - side).astype(stage.dtype)
    swap = remote(stage.at[other], pair_slot, p_send, p_recv, line.pair)
    swap.start()
    mine = reach(2 * at + side, n + side)
    yield
    swap.wait()
    total[...] = mine + pair_slot[...].astype(wide)
    for d in range(1, N):
        for y in range(2):
            pl.when(at + d < N)(lambda d=d, y=y: copy(2 * (at + d) + y, 0, True).wait_send())
            pl.when(at - d >= 0)(lambda d=d, y=y: copy(2 * (at - d) + y, 0, False).wait_send())


def gather_job(line, own, out, sems):
    r_send, l_send, y_send, recv, own_sem = sems
    n, N, at, side, c = line.n, line.N, line.at, line.side, line.c
    local = pltpu.make_async_copy(own, out(c), own_sem)
    local.start()

    def send(src, q, sem, device):
        return remote(src, out(q), sem.at[q // 2], recv.at[q], device)

    pl.when(line.has_right)(lambda: send(own, c, r_send, line.right).start())
    pl.when(line.has_left)(lambda: send(own, c, l_send, line.left).start())
    send(own, c, y_send, line.pair).start()
    yield
    for d in range(1, N):
        for q, keep, ahead in ((c - 2 * d, at - d >= 0, True), (c + 2 * d, at + d < N, False)):

            def relay(q=q, ahead=ahead):
                got = out(q)
                send(got, q, y_send, line.pair).wait_recv()
                if ahead:
                    pl.when(line.has_right)(lambda: send(got, q, r_send, line.right).start())
                else:
                    pl.when(line.has_left)(lambda: send(got, q, l_send, line.left).start())
                send(got, q, y_send, line.pair).start()

            pl.when(keep)(relay)
        yield
    for b in range(N):
        q = 2 * b + 1 - side
        send(out(q), q, y_send, line.pair).wait_recv()
    local.wait()
    for b in range(N):
        q = 2 * b + side
        got = out(q)
        send(got, q, y_send, line.pair).wait_send()
        pl.when(jnp.logical_and(b <= at, line.has_right))(
            lambda q=q, got=got: send(got, q, r_send, line.right).wait_send()
        )
        pl.when(jnp.logical_and(b >= at, line.has_left))(
            lambda q=q, got=got: send(got, q, l_send, line.left).wait_send()
        )


def gather_pair_job(line, own, out, sems):
    r_send, l_send, y_send, recv, own_sem = sems
    n, N, at, c = line.n, line.N, line.at, line.c
    local = pltpu.make_async_copy(own, out(c), own_sem)
    local.start()

    def send(src, q, sem, device):
        return remote(src, out(q), sem.at[q], recv.at[q], device)

    def ahead(src, q, act):
        pl.when(line.has_right)(lambda: act(send(src, q, r_send, line.right)))

    def back(src, q, act):
        pl.when(line.has_left)(lambda: act(send(src, q, l_send, line.left)))

    start = lambda copy: copy.start()
    to_pair = remote(own, out(c), y_send.at[0], recv.at[c], line.pair)
    to_pair.start()
    ahead(own, c, start)
    back(own, c, start)
    yield
    q = line.pair[0]
    got = out(q)
    send(got, q, r_send, line.pair).wait_recv()
    ahead(got, q, start)
    back(got, q, start)
    yield
    for d in range(1, N):
        for b, keep, forward in ((at - d, at - d >= 0, True), (at + d, at + d < N, False)):

            def relay(b=b, forward=forward):
                for y in range(2):
                    got = out(2 * b + y)
                    send(got, 2 * b + y, r_send, line.pair).wait_recv()
                    (ahead if forward else back)(got, 2 * b + y, start)

            pl.when(keep)(relay)
        yield
    local.wait()
    to_pair.wait_send()
    done = lambda copy: copy.wait_send()
    for b in range(N):
        for y in range(2):
            q = 2 * b + y
            pl.when(b <= at)(lambda q=q: ahead(out(q), q, done))
            pl.when(b >= at)(lambda q=q: back(out(q), q, done))


def minor_rows(rows):
    return rows // 8


def scatter_steps(line, product, rows, total, scratch):
    n, N = line.n, line.N
    few = minor_rows(rows)
    many = rows - few
    ystage, ybuf, zbuf, values, stage, slots, pair_slot = scratch[:7]
    main_sems, minor_sems = scratch[7:13], scratch[13:19]
    first = product(lambda q: (q * rows + many, few), range(n))
    values[...] = first.astype(values.dtype).reshape(values.shape)
    minor = scatter_line_job(
        line, values, stage, slots, pair_slot, total.at[pl.ds(many, few)], minor_sems
    )
    block = lambda place: product(lambda q: (q * rows, many), [place])
    main = scatter_job(line, block, total.at[pl.ds(0, many)], ystage, ybuf, zbuf, main_sems)
    next(minor)
    for _ in range(N):
        next(main)
        yield
    for _ in range(N - 1):
        next(minor, None)
        next(main)
        yield
    finish(minor)
    finish(main)


def gather_steps(line, own, out, rows, scratch):
    few = minor_rows(rows)
    many = rows - few
    minor = gather_pair_job(
        line, own.at[pl.ds(many, few)], lambda q: out(q, many, few), scratch[5:10]
    )
    main = gather_job(line, own.at[pl.ds(0, many)], lambda q: out(q, 0, many), scratch[:5])
    next(minor)
    next(main)
    yield
    for _ in range(line.N - 1):
        next(minor)
        next(main)
        yield
    finish(minor)
    finish(main)


SCATTER = 19
GATHER = 10


def scatter_scratch(n, rows):
    N = n // 2
    few = minor_rows(rows)
    many = rows - few
    low, dma = jnp.bfloat16, pltpu.SemaphoreType.DMA
    return (
        [
            pltpu.VMEM((N, many, D), low),
            pltpu.VMEM((N, many, D), low),
            pltpu.VMEM((N + 1, many, D), low),
            pltpu.VMEM((n, few, D), low),
            pltpu.VMEM((n, few, D), low),
            pltpu.VMEM((n + 2, few, D), low),
            pltpu.VMEM((few, D), low),
        ]
        + [dma((N,))] * 6
        + [dma((n,))] * 4
        + [dma, dma]
    )


def gather_scratch(n):
    N = n // 2
    dma = pltpu.SemaphoreType.DMA
    return [dma((N,)), dma((N,)), dma((N,)), dma((n,)), dma] + [
        dma((n,)),
        dma((n,)),
        dma((1,)),
        dma((n,)),
        dma,
    ]


def rms_factor(values):
    return lax.rsqrt(jnp.mean(values * values, axis=1, keepdims=True) + norm_eps)


def rms_back(values, gain, grad):
    factor = rms_factor(values)
    scaled = grad * gain
    inner = jnp.mean(scaled * values, axis=1, keepdims=True)
    d_gain = jnp.sum(grad * (values * factor), axis=0, keepdims=True)
    return factor * scaled - values * (factor * factor * factor * inner), d_gain


def matmul_rows(*pairs):
    def product(place, blocks):
        total = 0.0
        for left, right in pairs:
            parts = []
            for q in blocks:
                first, count = place(q)
                if not isinstance(first, int):
                    first = pl.multiple_of(first, 16)
                parts.append(left[pl.ds(first, count), :])
            part = parts[0] if len(parts) == 1 else jnp.concatenate(parts, axis=0)
            if right.shape[0] == left.shape[1]:
                total = total + plain(part, right[...])
            else:
                total = total + cols_by_cols(part, right[...])
        return total

    return product


def finish(job):
    for _ in job:
        pass


def start_kernel(plan, n, x, w_in, w_up, w_mix, w_down, *refs):
    tokens, in_all, shared_all, up_some, mix_all, down_some = refs[:6]
    in_low, shared_low, up_low, mix_low, down_low = refs[6:11]
    t_sems = refs[11 : 11 + GATHER]
    a_send, a_recv, x_send, x_recv, k_send, k_recv, own_sem = refs[11 + GATHER :]
    line = Line(n)
    c, w, sib, across = line.c, line.w, line.sib, line.across
    greet([((c + s) % n, w) for s in range(1, n)] + [(c, sib), (c, across)])
    R, B, G = plan.R, plan.B, FF // n
    low = jnp.bfloat16
    place = lambda q, first, count: tokens.at[q, pl.ds(first, count)]
    inputs = gather_steps(line, x, place, x.shape[0], t_sems)
    next(inputs)
    passed, pending = [], []

    def pass_on(number, view, src=None):
        src = view(w) if src is None else src
        to_x = remote(src, view(w), x_send.at[number], x_recv.at[number], (c, across))
        to_k = remote(src, view(w), k_send.at[0, number], k_recv.at[0, number], (c, sib))
        to_x.start()
        to_k.start()
        pending.append(to_x)
        pending.append(to_k)
        passed.append((number, view))

    mix_low[...] = w_mix[...].astype(low)
    pass_on(2 * n, lambda place: mix_all.at[0, place], mix_low)
    shared_low[...] = jnp.zeros_like(shared_low)
    shared_low[:, : END - BC_AT] = w_in[:, BC_AT:END].astype(low)
    for p in range(n):
        if p < plan.attn:
            g = plan.kv_of(p)
            in_low[p, :, :R] = w_in[:, p * R : (p + 1) * R].astype(low)
            in_low[p, :, B : B + HD] = w_in[:, K_AT + g * HD : K_AT + (g + 1) * HD].astype(low)
            in_low[p, :, B + HD : B + 2 * HD] = w_in[
                :, V_AT + g * HD : V_AT + (g + 1) * HD
            ].astype(low)
            if B + 2 * HD < plan.A:
                rest = plan.A - B - 2 * HD
                in_low[p, :, B + 2 * HD :] = jnp.zeros((in_low.shape[1], rest), low)
        else:
            j = p - plan.attn
            in_low[p, :, :R] = w_in[:, Z_AT + j * R : Z_AT + (j + 1) * R].astype(low)
            in_low[p, :, B : B + R] = w_in[:, X_AT + j * R : X_AT + (j + 1) * R].astype(low)
            if B + R < plan.A:
                in_low[p, :, B + R :] = jnp.zeros((in_low.shape[1], plan.A - B - R), low)

    def column_copies(s):
        p = (c + s) % n
        ends = ((in_low.at[p], in_all), (shared_low, shared_all))
        return [
            remote(src, dst.at[c, w], a_send.at[k, s], a_recv.at[k, c], (p, w))
            for k, (src, dst) in enumerate(ends)
        ]

    def send_columns(steps):
        for s in steps:
            for copy in column_copies(s):
                copy.start()
                pending.append(copy)

    in_view = lambda q: lambda place: in_all.at[q, place]
    shared_view = lambda q: lambda place: shared_all.at[q, place]

    def take_columns(steps):
        for s in steps:
            q = (c + n - s) % n
            for k, view in ((0, in_view), (1, shared_view)):
                got = view(q)(w)
                remote(got, got, a_send.at[k, s], a_recv.at[k, q], (q, w)).wait_recv()
                pass_on(k * n + q, view(q))

    done = [0]

    def seconds(upto):
        while done[0] < min(upto, len(passed)):
            number, view = passed[done[0]]
            got = view(across)
            remote(got, got, x_send.at[number], x_recv.at[number], (c, across)).wait_recv()
            out = remote(got, got, k_send.at[1, number], k_recv.at[1, number], (c, sib))
            out.start()
            pending.append(out)
            done[0] += 1

    cuts = [round(1 + (n - 1) * i / 3) for i in range(4)]
    parts = [range(cuts[i], cuts[i + 1]) for i in range(3)]
    send_columns(parts[0])
    pass_on(c, in_view(c), in_low.at[c])
    pass_on(n + c, shared_view(c), shared_low)
    down_low[...] = w_down[...].astype(low)
    for p in range(n):
        up_low[p, :, :G] = w_up[:, p * G : (p + 1) * G].astype(low)
        up_low[p, :, G:] = w_up[:, FF + p * G : FF + (p + 1) * G].astype(low)
    locals_started = []
    own = (
        (in_low.at[c], in_all.at[c, w]),
        (shared_low, shared_all.at[c, w]),
        (mix_low, mix_all.at[0, w]),
        (up_low.at[c], up_some.at[c]),
        (down_low, down_some.at[0]),
    )
    for i, (src, dst) in enumerate(own):
        copy = pltpu.make_async_copy(src, dst, own_sem.at[i])
        copy.start()
        locals_started.append(copy)
    for step in range(3):
        for _ in range(line.N // 4):
            next(inputs, None)
        if step < 2:
            send_columns(parts[step + 1])
        else:
            for s in range(1, n):
                p = (c + s) % n
                out = remote(
                    up_low.at[p], up_some.at[c], a_send.at[2, s], a_recv.at[2, c], (p, w)
                )
                out.start()
                pending.append(out)
        take_columns(parts[step])
        seconds(len(passed) - 4)
    finish(inputs)
    seconds(len(passed))
    for s in range(1, n):
        q = (c + n - s) % n
        got = up_some.at[q]
        remote(got, got, a_send.at[2, s], a_recv.at[2, q], (q, w)).wait_recv()
    for number, view in passed:
        for half, place in ((0, sib), (1, (sib + 2) % 4)):
            got = view(place)
            remote(got, got, k_send.at[half, number], k_recv.at[half, number], (c, sib)).wait_recv()
    for copy in locals_started:
        copy.wait()
    for out in pending:
        out.wait_send()


def branch_kernel(n, refs_in, refs_out, scratch):
    left, right, source, gain, up, down = refs_in
    middle, normed, up_all, down_all = refs_out
    line = Line(n)
    line.greet([(line.c, line.sib), (line.c, line.across)])
    rows = source.shape[0]
    total, own = scratch[:2]
    share = share_job((up, down), (up_all, down_all), scratch[2 + SCATTER + GATHER :])
    main = scatter_steps(line, matmul_rows((left, right)), rows, total, scratch[2:])
    next(main)
    next(share)
    finish(main)
    value = source[...].astype(jnp.float32) + total[...]
    middle[...] = value
    own[...] = (value * rms_factor(value) * gain[...]).astype(own.dtype)
    place = lambda q, first, count: normed.at[q, pl.ds(first, count)]
    spread_out = gather_steps(line, own, place, rows, scratch[2 + SCATTER :])
    next(spread_out)
    next(share)
    finish(spread_out)
    finish(share)


def feed_back_kernel(n, refs_in, refs_out, scratch):
    left, right, cotangent, middle, gain, active, w_down, up, down = refs_in
    grad, d_gain, result, low_all, up_sum, down_sum = refs_out
    line = Line(n)
    line.greet([(line.c, line.sib), (line.c, line.across)])
    rows = cotangent.shape[0]
    total, own = scratch[:2]
    late_scratch = scratch[2 + SCATTER + GATHER :]
    both = result.shape[0] == rows
    skip = SCATTER + 1 if both else 0
    sums = collect_job(n, ("rows", "rows"), (up, down), (up_sum, down_sum), late_scratch[skip:])
    main = scatter_steps(line, matmul_rows((left, right)), rows, total, scratch[2:])
    next(main)
    next(sums)
    for _ in range(line.N - 1):
        next(main)
    next(sums)
    finish(main)
    back, gain_row = rms_back(middle[...], gain[...], total[...])
    value = cotangent[...].astype(jnp.float32) + back
    grad[...] = value
    d_gain[...] = jnp.broadcast_to(gain_row, d_gain.shape)
    own[...] = value.astype(own.dtype)
    place = lambda q, first, count: low_all.at[q, pl.ds(first, count)]
    spread_out = gather_steps(line, own, place, rows, scratch[2 + SCATTER :])
    next(spread_out)
    if both:
        late = scatter_steps(
            line, matmul_rows((active, w_down)), rows, late_scratch[0], late_scratch[1:]
        )
        for _ in range(line.N - 1):
            next(late)
            next(spread_out)
        for _ in range(line.N):
            next(late)
    finish(spread_out)
    finish(sums)
    if both:
        finish(late)
        result[...] = (middle[...] + late_scratch[0][...]).astype(result.dtype)


SUMS = ("cols", "cols", "rows")


def source_back_kernel(n, refs_in, refs_out, scratch):
    (left, left_two, right, right_two, source, grad_middle, gain, vector, up) = refs_in[:9]
    w_in, w_shared, w_mix = refs_in[9:]
    grad, vector_sum, up_home, in_sum, shared_sum, mix_sum = refs_out
    line = Line(n)
    others = [((line.c + s) % n, line.w) for s in range(1, n)]
    greet(others + [(line.c, line.sib), (line.c, line.across)])
    rows = source.shape[0]
    total = scratch[0]
    sums = collect_job(
        n, SUMS, (w_in, w_shared, w_mix), (in_sum, shared_sum, mix_sum), scratch[2 + SCATTER : -6]
    )
    product = matmul_rows((left, right), (left_two, right_two))
    main = scatter_steps(line, product, rows, total, scratch[2:])
    last = len(scratch)
    vectors = sum_job(n, vector, vector_sum, *scratch[last - 6 : last - 2])
    home = home_job(n, up, up_home, *scratch[last - 2 :])
    next(vectors)
    next(vectors)
    next(home)
    next(main)
    next(sums)
    for _ in range(line.N - 1):
        next(vectors, None)
        next(main)
    finish(vectors)
    next(sums)
    for _ in main:
        next(sums)
        next(sums)
    for _ in range(n - 2 * line.N + 2):
        next(sums)
    back, _ = rms_back(source[...].astype(jnp.float32), gain[...], total[...])
    grad[...] = grad_middle[...] + back
    finish(home)
    finish(sums)


def flow_call(kernel, n, rows, args, outs, gathers, away, extra, collective_id):
    inside = pl.BlockSpec(memory_space=pltpu.VMEM)
    outside = pl.BlockSpec(memory_space=pl.ANY)
    side_args, side_shapes, side_scratch = extra
    shapes = list(outs)
    specs = [inside] * len(outs)
    scratch = [
        pltpu.VMEM((rows, D), jnp.float32),
        pltpu.VMEM((rows, D) if gathers else (16, 128), jnp.bfloat16),
    ]
    scratch = scratch + scatter_scratch(n, rows)
    if gathers:
        shapes.append(jax.ShapeDtypeStruct((n, rows, D), jnp.bfloat16))
        specs.append(outside)
        scratch = scratch + gather_scratch(n)
    side = outside if away else inside
    in_specs = [inside] * len(args) + [side] * len(side_args)
    specs = specs + [side] * len(side_shapes)
    shapes = shapes + list(side_shapes)
    first, second = len(in_specs), len(in_specs) + len(specs)

    def run(*refs):
        kernel(n, refs[:first], refs[first:second], refs[second:])

    return pl.pallas_call(
        run,
        out_shape=tuple(shapes),
        in_specs=in_specs,
        out_specs=tuple(specs),
        scratch_shapes=scratch + list(side_scratch),
        cost_estimate=pl.CostEstimate(flops=0, bytes_accessed=2 * 10**8, transcendentals=0),
        compiler_params=pltpu.CompilerParams(
            collective_id=collective_id, has_side_effects=True, vmem_limit_bytes=VMEM
        ),
    )(*args, *side_args)


def start_call(plan, n, x, w_in, w_up, w_mix, w_down, collective_id):
    rows = w_in.shape[0]
    low = jnp.bfloat16
    G = FF // n
    shapes = (
        jax.ShapeDtypeStruct((n,) + x.shape, low),
        jax.ShapeDtypeStruct((n, 4, rows, plan.A), low),
        jax.ShapeDtypeStruct((n, 4, rows, plan.K), low),
        jax.ShapeDtypeStruct((n, rows, 2 * G), low),
        jax.ShapeDtypeStruct((1, 4) + w_mix.shape, low),
        jax.ShapeDtypeStruct((1,) + w_down.shape, low),
    )
    dma = pltpu.SemaphoreType.DMA
    outside = pl.BlockSpec(memory_space=pl.ANY)
    inside = pl.BlockSpec(memory_space=pltpu.VMEM)
    blocks = 2 * n + 1
    outs = pl.pallas_call(
        functools.partial(start_kernel, plan, n),
        out_shape=shapes,
        in_specs=[outside] + [inside] * 4,
        out_specs=(outside,) * 6,
        scratch_shapes=[
            pltpu.VMEM((n, rows, plan.A), low),
            pltpu.VMEM((rows, plan.K), low),
            pltpu.VMEM((n, rows, 2 * G), low),
            pltpu.VMEM(w_mix.shape, low),
            pltpu.VMEM(w_down.shape, low),
        ]
        + gather_scratch(n)
        + [dma((3, n)), dma((3, n))]
        + [dma((blocks,)), dma((blocks,)), dma((2, blocks)), dma((2, blocks))]
        + [dma((5,))],
        cost_estimate=pl.CostEstimate(flops=0, bytes_accessed=2 * 10**8, transcendentals=0),
        compiler_params=pltpu.CompilerParams(
            collective_id=collective_id, has_side_effects=True, vmem_limit_bytes=VMEM
        ),
    )(x, w_in, w_up, w_mix, w_down)
    flat = lambda o: o.reshape(-1, o.shape[-1])
    tokens, in_all, shared_all, up_some, mix_all, down_some = outs
    return flat(tokens), flat(in_all), flat(shared_all), up_some, flat(mix_all), down_some


def mm(left, right):
    return jnp.dot(
        left.astype(jnp.bfloat16), right.astype(jnp.bfloat16), preferred_element_type=jnp.float32
    )


def mm_nt(left, right):
    return cols_by_cols(left.astype(jnp.bfloat16), right.astype(jnp.bfloat16))


def mm_tn(left, right):
    return rows_by_rows(left.astype(jnp.bfloat16), right.astype(jnp.bfloat16))


def pieces(values, count):
    found = []
    for _ in range(count):
        part = values.astype(jnp.bfloat16)
        found.append(part)
        values = values - part.astype(jnp.float32)
    return found


def by_marks(values, marks, count=2):
    return plain(
        jnp.concatenate(pieces(values, count), axis=1), jnp.concatenate([marks] * count, axis=0)
    )


def marks_by(marks, values, count=3):
    return plain(
        jnp.concatenate([marks] * count, axis=1), jnp.concatenate(pieces(values, count), axis=0)
    )


def iota(shape, axis):
    return lax.broadcasted_iota(jnp.int32, shape, axis)


def rope_tables(length):
    half = HD // 2
    frequency = rope_base ** (-jnp.arange(half, dtype=jnp.float32) / half)
    angles = jnp.arange(length).astype(jnp.float32)[:, None] * frequency[None, :]
    cosine, sine = jnp.cos(angles), jnp.sin(angles)
    return (
        jnp.concatenate([cosine, cosine], axis=1),
        jnp.concatenate([-sine, sine], axis=1),
    )


def turned(values, cosine, sine):
    return values * cosine + pltpu.roll(values, HD // 2, 1) * sine


def attn_stack(plan, q_ref, cosine, sine):
    heads = [
        turned(q_ref[:, h * HD : (h + 1) * HD], cosine, sine).astype(jnp.bfloat16)
        for h in range(plan.ha)
    ]
    return jnp.concatenate(heads, axis=0)


def by_extent(step, length, run):
    parts = 4
    per = length // CHUNK // parts
    for part in range(parts):
        pl.when(step // per == part)(functools.partial(run, (part + 1) * per * CHUNK))


def attn_softmax(stack, keys, at):
    scores = cols_by_cols(stack, keys) * (1.0 / math.sqrt(HD))
    row = iota(scores.shape, 0) & (CHUNK - 1)
    scores = jnp.where(iota(scores.shape, 1) <= row + at, scores, masked_score)
    weights = jnp.exp(scores - jnp.max(scores, axis=1, keepdims=True))
    return weights * (1.0 / jnp.sum(weights, axis=1, keepdims=True))


def attn_fwd_kernel(plan, q_ref, k_ref, v_ref, cos_ref, sin_ref, out_ref, keys, values):
    step = pl.program_id(0)

    @pl.when(step == 0)
    def _():
        keys[...] = turned(k_ref[...], cos_ref[...], sin_ref[...]).astype(jnp.bfloat16)
        values[...] = v_ref[...].astype(jnp.bfloat16)

    at = pl.multiple_of(step * CHUNK, CHUNK)
    rows = pl.ds(at, CHUNK)
    stack = attn_stack(plan, q_ref, cos_ref[rows, :], sin_ref[rows, :])

    def run(extent):
        probs = attn_softmax(stack, keys[:extent, :], at)
        made = mm(probs, values[:extent, :])
        for h in range(plan.ha):
            out_ref[:, h * HD : (h + 1) * HD] = made[h * CHUNK : (h + 1) * CHUNK]

    by_extent(step, keys.shape[0], run)


def attn_fwd(plan, proj, tables):
    length = proj.shape[0]
    whole = lambda i: (0, 0)
    return pl.pallas_call(
        functools.partial(attn_fwd_kernel, plan),
        grid=(length // CHUNK,),
        out_shape=jax.ShapeDtypeStruct((length, plan.R), jnp.float32),
        in_specs=[
            pl.BlockSpec((CHUNK, plan.R), lambda i: (i, 0)),
            pl.BlockSpec((length, HD), lambda i: (0, plan.B // HD)),
            pl.BlockSpec((length, HD), lambda i: (0, plan.B // HD + 1)),
            pl.BlockSpec((length, HD), whole),
            pl.BlockSpec((length, HD), whole),
        ],
        out_specs=pl.BlockSpec((CHUNK, plan.R), lambda i: (i, 0)),
        scratch_shapes=[pltpu.VMEM((length, HD), jnp.bfloat16)] * 2,
        compiler_params=pltpu.CompilerParams(vmem_limit_bytes=VMEM),
    )(proj, proj, proj, *tables)


def attn_bwd_kernel(
    plan, q_ref, k_ref, v_ref, cos_ref, sin_ref, grad_ref, slab_ref, keys, values, grad_k, grad_v
):
    step = pl.program_id(0)
    scale = 1.0 / math.sqrt(HD)

    @pl.when(step == 0)
    def _():
        keys[...] = turned(k_ref[...], cos_ref[...], sin_ref[...]).astype(jnp.bfloat16)
        values[...] = v_ref[...].astype(jnp.bfloat16)
        grad_k[...] = jnp.zeros_like(grad_k)
        grad_v[...] = jnp.zeros_like(grad_v)
        slab_ref[...] = jnp.zeros_like(slab_ref)

    at = pl.multiple_of(step * CHUNK, CHUNK)
    rows = pl.ds(at, CHUNK)
    cosine, sine = cos_ref[rows, :], sin_ref[rows, :]
    stack = attn_stack(plan, q_ref, cosine, sine)
    grads = jnp.concatenate([grad_ref[:, h * HD : (h + 1) * HD] for h in range(plan.ha)], axis=0)

    def run(extent):
        probs = attn_softmax(stack, keys[:extent, :], at)
        grad_probs = cols_by_cols(grads, values[:extent, :])
        delta = jnp.sum(probs * grad_probs, axis=1, keepdims=True)
        grad_scores = (probs * (grad_probs - delta)).astype(jnp.bfloat16)
        grad_q = mm(grad_scores, keys[:extent, :]) * scale
        for h in range(plan.ha):
            slab_ref[rows, h * HD : (h + 1) * HD] = turned(
                grad_q[h * CHUNK : (h + 1) * CHUNK], cosine, -sine
            ).astype(jnp.bfloat16)
        grad_k[:extent, :] += mm_tn(grad_scores, stack)
        grad_v[:extent, :] += mm_tn(probs, grads)

    by_extent(step, keys.shape[0], run)

    @pl.when(step == pl.num_programs(0) - 1)
    def _():
        slab_ref[:, plan.B : plan.B + HD] = turned(
            grad_k[...] * scale, cos_ref[...], -sin_ref[...]
        ).astype(jnp.bfloat16)
        slab_ref[:, plan.B + HD : plan.B + 2 * HD] = grad_v[...].astype(jnp.bfloat16)


def attn_bwd(plan, proj, tables, grad):
    length = proj.shape[0]
    whole = lambda i: (0, 0)
    return pl.pallas_call(
        functools.partial(attn_bwd_kernel, plan),
        grid=(length // CHUNK,),
        out_shape=jax.ShapeDtypeStruct((length, plan.A), jnp.bfloat16),
        in_specs=[
            pl.BlockSpec((CHUNK, plan.R), lambda i: (i, 0)),
            pl.BlockSpec((length, HD), lambda i: (0, plan.B // HD)),
            pl.BlockSpec((length, HD), lambda i: (0, plan.B // HD + 1)),
            pl.BlockSpec((length, HD), whole),
            pl.BlockSpec((length, HD), whole),
            pl.BlockSpec((CHUNK, plan.R), lambda i: (i, 0)),
        ],
        out_specs=pl.BlockSpec((length, plan.A), whole),
        scratch_shapes=[pltpu.VMEM((length, HD), jnp.bfloat16)] * 2
        + [pltpu.VMEM((length, HD), jnp.float32)] * 2,
        compiler_params=pltpu.CompilerParams(vmem_limit_bytes=VMEM),
    )(proj, proj, proj, *tables, grad)


def head_spread(plan):
    return ((iota((PAD, plan.R), 1) >> 6) == iota((PAD, plan.R), 0)).astype(jnp.bfloat16)


def head_gather(plan):
    return ((iota((plan.R, PAD), 0) >> 6) == iota((plan.R, PAD), 1)).astype(jnp.bfloat16)


def lower_ones():
    shape = (CHUNK, CHUNK)
    return (iota(shape, 0) >= iota(shape, 1)).astype(jnp.bfloat16)


def space_parts(plan, dt_raw, window, conv_ref, head_ref, pick_ref):
    total = conv_ref[4:5, :]
    for k in range(CONV):
        at = 8 - CONV + 1 + k
        total = total + conv_ref[k : k + 1, :] * window[at : at + CHUNK, :]
    raw = by_marks(dt_raw, pick_ref[...], 3) + head_ref[1:2, :]
    steps = jnp.maximum(raw, 0.0) + jnp.log1p(jnp.exp(-jnp.abs(raw)))
    logs = -steps * jnp.exp(head_ref[0:1, :])
    cumul = marks_by(lower_ones(), logs)
    return total, raw, steps, logs, cumul


def decay_of(cumul, cumul_t, causal, h):
    gaps = cumul[:, h : h + 1] - cumul_t[h : h + 1, :]
    return jnp.exp(jnp.where(causal, gaps, masked_score))


def space_fwd_kernel(
    plan, proj_ref, shared_ref, conv_ref, head_ref, pick_ref, gated_ref, made_ref, before_ref, state, window
):
    R = plan.R
    step = pl.program_id(0)

    @pl.when(step == 0)
    def _():
        state[...] = jnp.zeros_like(state)
        window[0:8, :] = jnp.zeros((8, window.shape[1]), jnp.float32)

    @pl.when(step > 0)
    def _():
        window[0:8, :] = window[CHUNK : CHUNK + 8, :]

    window[8 : CHUNK + 8, :R] = proj_ref[:, plan.B : plan.B + R]
    window[8 : CHUNK + 8, R:] = shared_ref[:, : 2 * NS]
    total, _, steps, _, cumul = space_parts(
        plan, shared_ref[:, 2 * NS :], window, conv_ref, head_ref, pick_ref
    )
    post = total * jax.nn.sigmoid(total)
    x = post[:, :R]
    b = post[:, R : R + NS].astype(jnp.bfloat16)
    c = post[:, R + NS :].astype(jnp.bfloat16)
    spread_heads = head_spread(plan)
    cumul_t = cumul.T
    last = cumul[CHUNK - 1 : CHUNK, :]
    tail = jnp.exp(last - cumul)
    weighted = x * by_marks(steps, spread_heads)
    causal = iota((CHUNK, CHUNK), 0) >= iota((CHUNK, CHUNK), 1)
    inner = cols_by_cols(c, b)
    before = state[...]
    before_ref[0] = before.astype(jnp.bfloat16)
    made = mm(c, before) * by_marks(jnp.exp(cumul), spread_heads)
    made = made + by_marks(jnp.broadcast_to(head_ref[2:3, :], (8, PAD)), spread_heads)[0:1] * x
    left = iota((CHUNK, 2 * MP), 1) < MP
    weighted_low = weighted.astype(jnp.bfloat16)
    intra = []
    for pair in range(plan.hm // 2):
        lanes = weighted_low[:, pair * 2 * MP : (pair + 1) * 2 * MP]
        one = mm(inner * decay_of(cumul, cumul_t, causal, 2 * pair), lanes)
        two = mm(inner * decay_of(cumul, cumul_t, causal, 2 * pair + 1), lanes)
        intra.append(jnp.where(left, one, two))
    made = made + jnp.concatenate(intra, axis=1)
    state[...] = before * by_marks(
        jnp.broadcast_to(jnp.exp(last), (8, PAD)), spread_heads
    )[0:1] + mm_tn(b, weighted * by_marks(tail, spread_heads))
    z = proj_ref[:, :R]
    made_ref[...] = made
    gated_ref[...] = made * (z * jax.nn.sigmoid(z))


def space_fwd(plan, proj, shared, conv, heads, pick):
    length = proj.shape[0]
    chunks = length // CHUNK
    W = plan.W
    whole = lambda i: (0, 0)
    rows = lambda i: (i, 0)
    return pl.pallas_call(
        functools.partial(space_fwd_kernel, plan),
        grid=(chunks,),
        out_shape=(
            jax.ShapeDtypeStruct((length, plan.R), jnp.float32),
            jax.ShapeDtypeStruct((length, plan.R), jnp.float32),
            jax.ShapeDtypeStruct((chunks, NS, plan.R), jnp.bfloat16),
        ),
        in_specs=[
            pl.BlockSpec((CHUNK, plan.A), rows),
            pl.BlockSpec((CHUNK, plan.K), rows),
            pl.BlockSpec((8, W), whole),
            pl.BlockSpec((8, PAD), whole),
            pl.BlockSpec((PAD, PAD), whole),
        ],
        out_specs=(
            pl.BlockSpec((CHUNK, plan.R), rows),
            pl.BlockSpec((CHUNK, plan.R), rows),
            pl.BlockSpec((1, NS, plan.R), lambda i: (i, 0, 0)),
        ),
        scratch_shapes=[
            pltpu.VMEM((NS, plan.R), jnp.float32),
            pltpu.VMEM((CHUNK + 8, W), jnp.float32),
        ],
        compiler_params=pltpu.CompilerParams(vmem_limit_bytes=VMEM),
    )(proj, shared, conv, heads, pick)


def space_bwd_kernel(
    plan, proj_ref, shared_ref, prev_ref, prev_shared, conv_ref, head_ref, pick_ref, grad_ref, made_ref,
    before_ref, slab_ref, slab_shared, conv_acc, head_acc, skip_acc, d_state, window, d_window,
):
    R = plan.R
    step = pl.program_id(0)
    chunk = pl.num_programs(0) - 1 - step

    @pl.when(step == 0)
    def _():
        d_state[...] = jnp.zeros_like(d_state)
        d_window[CHUNK : CHUNK + 8, :] = jnp.zeros((8, plan.W), jnp.float32)
        conv_acc[...] = jnp.zeros_like(conv_acc)
        head_acc[...] = jnp.zeros_like(head_acc)
        skip_acc[...] = jnp.zeros_like(skip_acc)

    @pl.when(step > 0)
    def _():
        d_window[CHUNK : CHUNK + 8, :] = d_window[0:8, :]

    window[0:8, :R] = jnp.where(chunk == 0, 0.0, prev_ref[:, plan.B : plan.B + R])
    window[0:8, R:] = jnp.where(chunk == 0, 0.0, prev_shared[:, : 2 * NS])
    window[8 : CHUNK + 8, :R] = proj_ref[:, plan.B : plan.B + R]
    window[8 : CHUNK + 8, R:] = shared_ref[:, : 2 * NS]
    total, raw, steps, logs, cumul = space_parts(
        plan, shared_ref[:, 2 * NS :], window, conv_ref, head_ref, pick_ref
    )
    sig = jax.nn.sigmoid(total)
    post = total * sig
    x = post[:, :R]
    b = post[:, R : R + NS].astype(jnp.bfloat16)
    c = post[:, R + NS :].astype(jnp.bfloat16)
    spread_heads = head_spread(plan)
    gather_heads = head_gather(plan)
    cumul_t = cumul.T
    last = cumul[CHUNK - 1 : CHUNK, :]
    steps_wide = by_marks(steps, spread_heads)
    tail_wide = by_marks(jnp.exp(last - cumul), spread_heads)
    grow_wide = by_marks(jnp.exp(cumul), spread_heads)
    last_wide = by_marks(jnp.broadcast_to(jnp.exp(last), (8, PAD)), spread_heads)[0:1]
    skip_wide = by_marks(jnp.broadcast_to(head_ref[2:3, :], (8, PAD)), spread_heads)[0:1]
    weighted = x * steps_wide
    causal = iota((CHUNK, CHUNK), 0) >= iota((CHUNK, CHUNK), 1)
    inner = cols_by_cols(c, b)

    z = proj_ref[:, :R]
    sig_z = jax.nn.sigmoid(z)
    grad = grad_ref[...]
    d_made = grad * (z * sig_z)
    slab_ref[:, :R] = (grad * made_ref[...] * (sig_z * (1.0 + z * (1.0 - sig_z)))).astype(
        jnp.bfloat16
    )
    skip_acc[0:1, :] += jnp.sum(d_made * x, axis=0, keepdims=True)

    before = before_ref[0]
    d_after = d_state[...]
    d_after_low = d_after.astype(jnp.bfloat16)
    grown = d_made * grow_wide
    grown_low = grown.astype(jnp.bfloat16)
    carried = mm(c, before)
    d_c = mm_nt(grown_low, before)
    pulled = weighted * tail_wide
    d_pulled = mm(b, d_after_low)
    d_b = mm_nt(pulled, d_after_low)
    d_cumul = by_marks(grown * carried, gather_heads)
    kept = by_marks(d_pulled * pulled, gather_heads)
    d_cumul = d_cumul - kept
    decayed = jnp.sum(d_after * before.astype(jnp.float32), axis=0, keepdims=True) * last_wide
    d_last = jnp.sum(kept, axis=0, keepdims=True) + by_marks(
        jnp.broadcast_to(decayed, (8, R)), gather_heads
    )[0:1]
    d_state[...] = d_after * last_wide + mm_tn(c, grown_low)

    left = iota((CHUNK, 2 * MP), 1) < MP
    lane = iota((CHUNK, PAD), 1)
    sub = iota((8, CHUNK), 0)
    weighted_low = weighted.astype(jnp.bfloat16)
    d_made_low = d_made.astype(jnp.bfloat16)
    d_inner = jnp.zeros((CHUNK, CHUNK), jnp.float32)
    columns = jnp.zeros((8, CHUNK), jnp.float32)
    d_weighted = []
    for pair in range(plan.hm // 2):
        at = slice(pair * 2 * MP, (pair + 1) * 2 * MP)
        lanes, d_lanes = weighted_low[:, at], d_made_low[:, at]
        halves = []
        for which in range(2):
            h = 2 * pair + which
            decay = decay_of(cumul, cumul_t, causal, h)
            whole = inner * decay
            halves.append(mm_tn(whole, d_lanes))
            mine = jnp.where(left if which == 0 else ~left, d_lanes, jnp.zeros_like(d_lanes))
            d_whole = cols_by_cols(mine, lanes)
            d_inner = d_inner + d_whole * decay
            slope = d_whole * whole
            d_cumul = d_cumul + jnp.where(lane == h, jnp.sum(slope, axis=1, keepdims=True), 0.0)
            columns = columns + jnp.where(sub == h, jnp.sum(slope, axis=0, keepdims=True), 0.0)
        d_weighted.append(jnp.where(left, halves[0], halves[1]))
    d_weighted = jnp.concatenate(d_weighted, axis=1) + d_pulled * tail_wide
    columns = jnp.concatenate([columns, jnp.zeros((CHUNK - 8, CHUNK), jnp.float32)], axis=0).T
    d_cumul = d_cumul - columns
    d_inner_low = d_inner.astype(jnp.bfloat16)
    d_c = d_c + mm(d_inner_low, b)
    d_b = d_b + mm_tn(d_inner_low, c)
    d_x = d_weighted * steps_wide + skip_wide * d_made
    d_steps = by_marks(d_weighted * x, gather_heads)
    upper = (iota((CHUNK, CHUNK), 0) <= iota((CHUNK, CHUNK), 1)).astype(jnp.bfloat16)
    d_logs = marks_by(upper, d_cumul) + d_last
    d_steps = d_steps - jnp.exp(head_ref[0:1, :]) * d_logs
    d_raw = d_steps * jax.nn.sigmoid(raw)
    d_raw = jnp.where(lane < plan.hm, d_raw, 0.0)
    slab_shared[:, 2 * NS :] = cols_by_cols(d_raw.astype(jnp.bfloat16), pick_ref[...]).astype(
        jnp.bfloat16
    )
    head_acc[0:1, :] += jnp.sum(d_logs * logs, axis=0, keepdims=True)
    head_acc[1:2, :] += jnp.sum(d_raw, axis=0, keepdims=True)

    d_post = jnp.concatenate([d_x, d_b, d_c], axis=1)
    d_total = d_post * (sig * (1.0 + total * (1.0 - sig)))
    d_window[0:CHUNK, :] = d_total
    d_xbc = jnp.zeros((CHUNK, plan.W), jnp.float32)
    for k in range(CONV):
        shift = CONV - 1 - k
        d_xbc = d_xbc + conv_ref[k : k + 1, :] * d_window[shift : shift + CHUNK, :]
        at = 8 - CONV + 1 + k
        conv_acc[k : k + 1, :] += jnp.sum(
            d_total * window[at : at + CHUNK, :], axis=0, keepdims=True
        )
    conv_acc[4:5, :] += jnp.sum(d_total, axis=0, keepdims=True)
    slab_ref[:, plan.B : plan.B + R] = d_xbc[:, :R].astype(jnp.bfloat16)
    slab_shared[:, : 2 * NS] = d_xbc[:, R:].astype(jnp.bfloat16)
    if plan.B + R < plan.A:
        slab_ref[:, plan.B + R :] = jnp.zeros((CHUNK, plan.A - plan.B - R), jnp.bfloat16)


def space_bwd(plan, proj, shared, conv, heads, pick, grad, made, before):
    length = proj.shape[0]
    chunks = length // CHUNK
    W = plan.W
    whole = lambda i: (0, 0)
    rows = lambda i: (chunks - 1 - i, 0)
    per = CHUNK // 8
    return pl.pallas_call(
        functools.partial(space_bwd_kernel, plan),
        grid=(chunks,),
        out_shape=(
            jax.ShapeDtypeStruct((length, plan.A), jnp.bfloat16),
            jax.ShapeDtypeStruct((length, plan.K), jnp.bfloat16),
            jax.ShapeDtypeStruct((8, W), jnp.float32),
            jax.ShapeDtypeStruct((8, PAD), jnp.float32),
            jax.ShapeDtypeStruct((8, plan.R), jnp.float32),
        ),
        in_specs=[
            pl.BlockSpec((CHUNK, plan.A), rows),
            pl.BlockSpec((CHUNK, plan.K), rows),
            pl.BlockSpec((8, plan.A), lambda i: (jnp.maximum((chunks - 1 - i) * per - 1, 0), 0)),
            pl.BlockSpec((8, plan.K), lambda i: (jnp.maximum((chunks - 1 - i) * per - 1, 0), 0)),
            pl.BlockSpec((8, W), whole),
            pl.BlockSpec((8, PAD), whole),
            pl.BlockSpec((PAD, PAD), whole),
            pl.BlockSpec((CHUNK, plan.R), rows),
            pl.BlockSpec((CHUNK, plan.R), rows),
            pl.BlockSpec((1, NS, plan.R), lambda i: (chunks - 1 - i, 0, 0)),
        ],
        out_specs=(
            pl.BlockSpec((CHUNK, plan.A), rows),
            pl.BlockSpec((CHUNK, plan.K), rows),
            pl.BlockSpec((8, W), whole),
            pl.BlockSpec((8, PAD), whole),
            pl.BlockSpec((8, plan.R), whole),
        ),
        scratch_shapes=[
            pltpu.VMEM((NS, plan.R), jnp.float32),
            pltpu.VMEM((CHUNK + 8, W), jnp.float32),
            pltpu.VMEM((CHUNK + 8, W), jnp.float32),
        ],
        compiler_params=pltpu.CompilerParams(vmem_limit_bytes=VMEM),
    )(proj, shared, proj, shared, conv, heads, pick, grad, made, before)


def body(
    inputs,
    cotangent,
    w_in,
    w_in_m,
    w_in_v,
    w_mix,
    w_mix_m,
    w_mix_v,
    w_up,
    w_up_m,
    w_up_v,
    w_down,
    w_down_m,
    w_down_v,
    vectors,
    vectors_m,
    vectors_v,
):
    low = jnp.bfloat16
    count = lax.axis_size("ctx")
    ways = lax.axis_size("wshard")
    place = lax.axis_index("ctx")
    plan = Plan(count)
    R, hm = plan.R, plan.hm
    is_space = place >= plan.attn
    space = jnp.maximum(place - plan.attn, 0)

    gain_attn, gain_ffn, gain_ssm, conv_bias, conv_weight, a_log, dt_bias, d_skip = split_vectors(
        vectors
    )
    whole, in_own, shared_own, up_some, mix_own, down_some = start_call(
        plan, count, inputs[0], w_in, w_up, w_mix, w_down, 1
    )

    own = lambda a, size, axis=0: lax.dynamic_slice_in_dim(a, space * size, size, axis)
    gain_own = own(gain_ssm, R)
    W = plan.W
    conv = jnp.concatenate(
        [
            jnp.concatenate([own(conv_weight, R, 1), conv_weight[:, DSSM:]], axis=1),
            jnp.concatenate([own(conv_bias, R), conv_bias[DSSM:]])[None],
            jnp.zeros((8 - CONV - 1, W), jnp.float32),
        ]
    )
    heads = jnp.stack([own(v, hm) for v in (a_log, dt_bias, d_skip)])
    heads = jnp.pad(heads, ((0, 5), (0, PAD - hm)))
    column = lax.broadcasted_iota(jnp.int32, (PAD, PAD), 1)
    row = lax.broadcasted_iota(jnp.int32, (PAD, PAD), 0)
    pick = jnp.logical_and(row == column + space * hm, column < hm).astype(low)
    tables = rope_tables(count * inputs.shape[1])

    source = inputs[0].astype(jnp.float32)
    whole = whole.astype(jnp.float32)
    in_own, cotangent_late = lax.optimization_barrier((in_own, cotangent[0]))
    upstream_all = gather_ctx(cotangent_late)
    length = whole.shape[0]
    rows = inputs.shape[1]
    unit = whole * lax.rsqrt(jnp.mean(whole * whole, axis=-1, keepdims=True) + norm_eps)
    normed = (unit * gain_attn).astype(low)
    unit = unit.astype(low)
    proj = plain(normed, in_own)
    shared = plain(normed, shared_own)

    def space_ahead(proj, shared):
        return space_fwd(plan, proj, shared, conv, heads, pick)

    def attn_ahead(proj, shared):
        made = attn_fwd(plan, proj, tables)
        blank = jnp.zeros((length // CHUNK, NS, R), low)
        return made, jnp.zeros_like(made), blank

    made, raw_made, before = lax.cond(is_space, space_ahead, attn_ahead, proj, shared)
    square = jnp.where(is_space, jnp.sum(made * made, axis=1), 0.0)
    factor = lax.rsqrt(sum_rows(count, square, 5) / DSSM + norm_eps)
    mixed = jnp.where(is_space, made * factor[:, None] * gain_own, made).astype(low)
    wide = lambda *shape: jax.ShapeDtypeStruct(shape, jnp.float32)
    side = (up_some, down_some)
    middle, two_all, up_own, down_own = flow_call(
        branch_kernel,
        count,
        rows,
        (mixed, mix_own, inputs[0], gain_ffn[None]),
        (wide(rows, D),),
        True,
        True,
        (side, *share_shapes(side)),
        8,
    )
    two_all = two_all.reshape(length, D)
    up_own, down_own = up_own.reshape(D, -1), down_own.reshape(-1, D)

    gate_up = plain(two_all, up_own)
    half = FF // count
    swiglu = lambda g: jax.nn.silu(g[:, :half]) * g[:, half:]
    activated, act_pull = jax.vjp(swiglu, gate_up)
    activated = activated.astype(low)
    grad_down = rows_by_rows(activated, upstream_all)
    grad_act = cols_by_cols(upstream_all, down_own)
    grad_gate_up = act_pull(grad_act)[0].astype(low)
    grad_up = rows_by_rows(two_all, grad_gate_up)
    cut = lambda g, blocks: g.astype(low).reshape(blocks, ways, -1, g.shape[1])
    side = (cut(grad_up, count), cut(grad_down, 1))
    roomy = length <= 1024
    side_shapes, side_scratch = collect_shapes(("rows", "rows"), side)
    if roomy:
        side_scratch = (
            [pltpu.VMEM((rows, D), jnp.float32)] + scatter_scratch(count, rows) + side_scratch
        )
    result = jax.ShapeDtypeStruct((rows if roomy else 16, D), low)
    grad_middle, grad_gain_ffn, outputs, branch_all, up_mine, down_mine = flow_call(
        feed_back_kernel,
        count,
        rows,
        (
            grad_gate_up,
            up_own,
            cotangent[0],
            middle,
            gain_ffn[None],
            activated if roomy else activated[:16],
            down_own,
        ),
        (wide(rows, D), wide(8, D), result),
        True,
        False,
        (side, side_shapes, side_scratch),
        9,
    )
    grad_gain_ffn = grad_gain_ffn[0]
    branch_all = branch_all.reshape(length, D)
    if not roomy:
        late = lax.optimization_barrier((branch_all, plain(activated, down_own).astype(low)))[1]
        outputs = (middle + scatter_ctx(late)).astype(low)
    outputs = outputs[None]
    grad_mix = rows_by_rows(mixed, branch_all)
    grad_made = cols_by_cols(branch_all, mix_own).astype(low)
    made_wide = grad_made.astype(jnp.float32)
    dots = jnp.where(is_space, jnp.sum(made_wide * gain_own * made, axis=1), 0.0)
    dots = sum_rows(count, dots, 6)
    grad_gain_own = jnp.sum(made_wide * made * factor[:, None], axis=0)
    grad_gated = made_wide * gain_own * factor[:, None] - made * (factor**3 * dots / DSSM)[:, None]

    def space_back(proj, shared, grad_gated, grad_made):
        return space_bwd(plan, proj, shared, conv, heads, pick, grad_gated, raw_made, before)

    def attn_back(proj, shared, grad_gated, grad_made):
        blank = lambda k: jnp.zeros((8, k), jnp.float32)
        none = jnp.zeros(shared.shape, low)
        return attn_bwd(plan, proj, tables, grad_made), none, blank(W), blank(PAD), blank(R)

    grad_proj, grad_shared, conv_acc, head_acc, skip_acc = lax.cond(
        is_space, space_back, attn_back, proj, shared, grad_gated, grad_made
    )
    grad_in = rows_by_rows(unit, grad_proj)
    grad_in_shared = rows_by_rows(unit, grad_shared)
    grad_gain_attn = jnp.sum(grad_in * in_own, axis=1) + jnp.sum(grad_in_shared * shared_own, axis=1)
    grad_in = grad_in * gain_attn[:, None]
    grad_in_shared = grad_in_shared * gain_attn[:, None]
    def placed(piece, size, total, axis=0):
        shape = list(piece.shape)
        shape[axis] = total
        start = [0] * piece.ndim
        start[axis] = space * size
        return lax.dynamic_update_slice(jnp.zeros(shape, piece.dtype), piece, start)

    conv_w_grad, conv_b_grad = conv_acc[:CONV], conv_acc[CONV]
    a_grad, bias_grad = head_acc[0, :hm], head_acc[1, :hm]
    skip_grad = jnp.sum(skip_acc[0].reshape(hm, MP), axis=1)
    grad_gain_own = jnp.where(is_space, grad_gain_own, 0.0)
    vector_local = jnp.concatenate(
        [
            grad_gain_attn,
            grad_gain_ffn,
            placed(grad_gain_own, R, DSSM),
            placed(conv_b_grad[:R], R, DSSM),
            conv_b_grad[R:],
            jnp.concatenate(
                [placed(conv_w_grad[:, :R], R, DSSM, 1), conv_w_grad[:, R:]], axis=1
            ).reshape(CONV * CONVCH),
            placed(a_grad, hm, MH),
            placed(bias_grad, hm, MH),
            placed(skip_grad, hm, MH),
        ]
    )
    pad = -vectors.shape[0] % 1024
    vector_local = jnp.pad(vector_local, (0, pad)).reshape(-1, 128)
    side = (cut(grad_in, count), cut(grad_in_shared, count), cut(grad_mix, 1))
    side_shapes, side_scratch = collect_shapes(SUMS, side)
    home_sems = [pltpu.SemaphoreType.DMA((count,))] * 2
    input_grad, vector_sum, up_mine, in_mine, shared_mine, mix_mine = flow_call(
        source_back_kernel,
        count,
        rows,
        (
            grad_proj,
            grad_shared,
            in_own,
            shared_own,
            inputs[0],
            grad_middle,
            gain_attn[None],
            vector_local,
            up_mine,
        ),
        (wide(rows, D), wide(*vector_local.shape), jax.ShapeDtypeStruct(up_mine.shape, low)),
        False,
        False,
        (side, side_shapes, side_scratch + sum_scratch(count, vector_local.shape) + home_sems),
        10,
    )
    input_grad = input_grad[None]

    in_shard = from_slabs(plan, in_mine, shared_mine)
    up_shard = up_from_slabs(plan, up_mine)
    mix_shard = mix_mine[0].astype(jnp.float32)
    down_shard = down_mine[0].astype(jnp.float32)

    vector_grad = vector_sum.reshape(-1)[: vectors.shape[0]]
    new_in = adamw(w_in, w_in_m, w_in_v, in_shard, 2.0 * D ** (-0.5), decay_weight)
    new_mix = adamw(w_mix, w_mix_m, w_mix_v, mix_shard, DSSM ** (-0.5), decay_weight)
    new_up = adamw(w_up, w_up_m, w_up_v, up_shard, D ** (-0.5), decay_weight)
    new_down = adamw(w_down, w_down_m, w_down_v, down_shard, FF ** (-0.5), decay_weight)
    new_vec = adamw(vectors, vectors_m, vectors_v, vector_grad, vector_rate, 0.0)
    return (outputs, input_grad, *new_in, *new_mix, *new_up, *new_down, *new_vec)


def solution(mesh):
    tokens = P("wshard", "ctx", None)
    weight = P(("ctx", "wshard"), None)
    return jax.shard_map(
        body,
        mesh=mesh,
        in_specs=(tokens,) * 2 + (weight,) * 12 + (P(),) * 3,
        out_specs=(tokens,) * 2 + (weight,) * 12 + (P(),) * 3,
        check_vma=False,
    )
```

```python
import functools
import math

import jax
import jax.numpy as jnp
from jax import lax
from jax.experimental import pallas as pl
from jax.experimental.pallas import tpu as pltpu
from jax.sharding import PartitionSpec as P

D = 2048
FF = 4096
AH = 8
KVH = 2
HD = 128
MH = 48
MP = 64
NS = 256
CONV = 4
STEP = 10
DSSM = 3072
CONVCH = 3584
ATT = AH * HD
MIXIN = ATT + DSSM
GROUP = AH // KVH
CHUNK = 128
PAD = 128
VMEM = 60 * 1024 * 1024


norm_eps = 1e-05
rope_base = 10000.0
beta_one = 0.9
beta_two = 0.95
adam_eps = 1e-08
decay_weight = 0.1
vector_rate = 0.5
masked_score = -1e30

K_AT = ATT
V_AT = K_AT + KVH * HD
Z_AT = V_AT + KVH * HD
X_AT = Z_AT + DSSM
BC_AT = X_AT + DSSM
DT_AT = BC_AT + 2 * NS
END = DT_AT + MH


def rows_by_rows(left, right):
    return lax.dot_general(
        left, right, (((0,), (0,)), ((), ())), preferred_element_type=jnp.float32
    )


def cols_by_cols(left, right):
    return lax.dot_general(
        left, right, (((1,), (1,)), ((), ())), preferred_element_type=jnp.float32
    )


def plain(left, right):
    return jnp.dot(left, right, preferred_element_type=jnp.float32)


def rms_norm(values, gain):
    factor = lax.rsqrt(jnp.mean(values * values, axis=-1, keepdims=True) + norm_eps)
    return values * factor * gain


def split_vectors(vectors):
    extents = (D, D, DSSM, CONVCH, CONV * CONVCH, MH, MH, MH)
    pieces = []
    offset = 0
    for extent in extents:
        pieces.append(lax.slice_in_dim(vectors, offset, offset + extent))
        offset = offset + extent
    pieces[4] = pieces[4].reshape(CONV, CONVCH)
    return pieces


def adamw(weight, moment, second, grad, rate, decay):
    moment = beta_one * moment + (1.0 - beta_one) * grad
    second = beta_two * second + (1.0 - beta_two) * grad * grad
    corrected = moment / (1.0 - beta_one**STEP)
    divisor = jnp.sqrt(second / (1.0 - beta_two**STEP)) + adam_eps
    return (weight - rate * (corrected / divisor + decay * weight), moment, second)


class Plan:
    def __init__(self, count):
        self.count = count
        self.R = MIXIN // count
        self.attn = ATT // self.R
        self.ha = self.R // HD
        self.hm = self.R // MP
        self.B = self.R
        self.A = self.R + max(self.R, 2 * HD)
        self.K = 2 * NS + PAD
        self.W = self.R + 2 * NS

    def kv_of(self, c):
        return c * self.ha // GROUP


def from_slabs(plan, slabs, shared):
    R, B = plan.R, plan.B
    slabs = slabs.astype(jnp.float32)
    shared = shared.astype(jnp.float32)
    heads = range(plan.attn)
    spaces = range(plan.attn, plan.count)
    total = lambda items: functools.reduce(lambda a, b: a + b, items)
    parts = [slabs[c][:, :R] for c in heads]
    for at in (B, B + HD):
        for g in range(KVH):
            parts.append(total([slabs[c][:, at : at + HD] for c in heads if plan.kv_of(c) == g]))
    parts += [slabs[c][:, :R] for c in spaces]
    parts += [slabs[c][:, B : B + R] for c in spaces]
    parts.append(total([shared[c][:, : END - BC_AT] for c in spaces]))
    return jnp.concatenate(parts, axis=1)


def up_from_slabs(plan, slabs):
    G = FF // plan.count
    slabs = slabs.astype(jnp.float32)
    return jnp.concatenate(
        [slabs[c][:, :G] for c in range(plan.count)] + [slabs[c][:, G:] for c in range(plan.count)],
        axis=1,
    )


def gather_ctx(x):
    return lax.all_gather(x, "ctx", axis=0, tiled=True)


def scatter_ctx(x):
    return lax.psum_scatter(
        x.astype(jnp.bfloat16), "ctx", scatter_dimension=0, tiled=True
    ).astype(jnp.float32)


MESH = pl.DeviceIdType.MESH


def here():
    c, w = lax.axis_index("ctx"), lax.axis_index("wshard")
    return c, w, w + 1 - 2 * (w % 2), (w + 2) % 4


def greet(devices):
    barrier = pltpu.get_barrier_semaphore()
    for device in devices:
        pl.semaphore_signal(barrier, inc=1, device_id=device, device_id_type=MESH)
    pl.semaphore_wait(barrier, len(devices))


def remote(src, dst, send, recv, device):
    return pltpu.make_async_remote_copy(
        src_ref=src, dst_ref=dst, send_sem=send, recv_sem=recv, device_id=device, device_id_type=MESH
    )


def collect_job(n, kinds, sources, targets, extra):
    c, w, sib, across = here()
    x, core = w // 2, w % 2
    far = 1 - x
    pending = []
    jobs = []
    for j, kind in enumerate(kinds):
        jobs.append((kind, sources[j], targets[j]) + tuple(extra[10 * j : 10 * j + 10]))

    def order(job, s):
        return (c + s) % n if job[1].shape[0] > 1 else 0

    def count(job):
        return job[1].shape[0]

    most = max(count(job) for job in jobs)
    steps = [s % most for s in range(1, most + 1)]
    for place, slot in ((far, 0), (x, 1)):
        for s in steps:
            for job in jobs:
                if s >= count(job):
                    continue
                _, src, _, kbuf, _, _, _, k_send, k_recv = job[:9]
                q = order(job, s)
                out = remote(
                    src.at[q, place * 2 + 1 - core],
                    kbuf.at[slot, q],
                    k_send.at[slot, s],
                    k_recv.at[slot, q],
                    (c, sib),
                )
                out.start()
                pending.append(out)
    yield
    wide = jnp.float32
    for s in steps:
        for job in jobs:
            if s >= count(job):
                continue
            _, src, _, kbuf, stage, xbuf, _, k_send, k_recv, x_send, x_recv = job[:11]
            q = order(job, s)
            got = kbuf.at[0, q]
            remote(got, got, k_send.at[0, s], k_recv.at[0, q], (c, sib)).wait_recv()
            stage[q] = (src[q, far * 2 + core].astype(wide) + kbuf[0, q].astype(wide)).astype(
                stage.dtype
            )
            out = remote(stage.at[q], xbuf.at[q], x_send.at[s], x_recv.at[q], (c, across))
            out.start()
            pending.append(out)
    yield
    for s in steps:
        for job in jobs:
            if s >= count(job):
                continue
            kind, src, dst, kbuf, stage, xbuf, done, k_send, k_recv, x_send, x_recv = job[:11]
            a_send, a_recv = job[11], job[12]
            q = order(job, s)
            got = kbuf.at[1, q]
            remote(got, got, k_send.at[1, s], k_recv.at[1, q], (c, sib)).wait_recv()
            got = xbuf.at[q]
            remote(got, got, x_send.at[s], x_recv.at[q], (c, across)).wait_recv()
            total = src[q, x * 2 + core].astype(wide) + kbuf[1, q].astype(wide)
            total = (total + xbuf[q].astype(wide)).astype(stage.dtype)
            if kind == "cols" and s > 0:
                done[q] = total
                out = remote(done.at[q], dst.at[c], a_send.at[s], a_recv.at[c], (q, w))
                out.start()
                pending.append(out)
            else:
                dst[q] = total
        yield
    for job in jobs:
        if job[0] == "cols":
            dst, a_send, a_recv = job[2], job[11], job[12]
            for s in range(1, n):
                q = (c + n - s) % n
                got = dst.at[q]
                remote(got, got, a_send.at[s], a_recv.at[q], (q, w)).wait_recv()
    for out in pending:
        out.wait_send()


def home_job(n, source, target, send, recv):
    c, w = lax.axis_index("ctx"), lax.axis_index("wshard")
    target[c] = source[c]
    copies = [
        remote(source.at[(c + s) % n], target.at[c], send.at[s], recv.at[c], ((c + s) % n, w))
        for s in range(1, n)
    ]
    for copy in copies:
        copy.start()
    yield
    for s in range(1, n):
        q = (c + n - s) % n
        remote(source.at[q], target.at[q], send.at[s], recv.at[q], (q, w)).wait_recv()
    for copy in copies:
        copy.wait_send()


def collect_shapes(kinds, sources):
    shapes, scratch = [], []
    for kind, src in zip(kinds, sources):
        count, _, rows, size = src.shape
        block = (count, rows, size)
        shapes.append(jax.ShapeDtypeStruct(block, src.dtype))
        scratch += [
            pltpu.VMEM((2,) + block, src.dtype),
            pltpu.VMEM(block, src.dtype),
            pltpu.VMEM(block, src.dtype),
            pltpu.VMEM(block if kind == "cols" else (1, 16, 128), src.dtype),
            pltpu.SemaphoreType.DMA((2, count)),
            pltpu.SemaphoreType.DMA((2, count)),
            pltpu.SemaphoreType.DMA((count,)),
            pltpu.SemaphoreType.DMA((count,)),
            pltpu.SemaphoreType.DMA((count,)),
            pltpu.SemaphoreType.DMA((count,)),
        ]
    return shapes, scratch


def row_sum_kernel(n, x_ref, out_ref, got, send, recv):
    c, w = lax.axis_index("ctx"), lax.axis_index("wshard")
    greet([((c + s) % n, w) for s in range(1, n)])
    copies = [
        remote(x_ref, got.at[c], send.at[s], recv.at[c], ((c + s) % n, w)) for s in range(1, n)
    ]
    for copy in copies:
        copy.start()
    total = x_ref[...]
    for s in range(1, n):
        q = (c + n - s) % n
        remote(x_ref, got.at[q], send.at[s], recv.at[q], (q, w)).wait_recv()
        total = total + got[q]
    out_ref[...] = total
    for copy in copies:
        copy.wait_send()


def sum_rows(n, x, collective_id):
    block = x.reshape(-1, 128)
    return pl.pallas_call(
        functools.partial(row_sum_kernel, n),
        out_shape=jax.ShapeDtypeStruct(block.shape, x.dtype),
        in_specs=[pl.BlockSpec(memory_space=pltpu.VMEM)],
        out_specs=pl.BlockSpec(memory_space=pltpu.VMEM),
        scratch_shapes=[
            pltpu.VMEM((n,) + block.shape, x.dtype),
            pltpu.SemaphoreType.DMA((n,)),
            pltpu.SemaphoreType.DMA((n,)),
        ],
        compiler_params=pltpu.CompilerParams(
            collective_id=collective_id, has_side_effects=True, vmem_limit_bytes=VMEM
        ),
    )(block).reshape(x.shape)


def sum_job(n, x_ref, out_ref, kept, got, send, recv):
    c, w, sib, across = here()
    partners = [(c, sib), (c, across)]
    for level in list(range(1, n.bit_length() - 1)) + [0]:
        reach = 2**level
        partners.append((c + reach - 2 * reach * ((c // reach) % 2), w))
    out_ref[...] = x_ref[...]
    for i, partner in enumerate(partners):
        kept[i] = out_ref[...]
        swap = remote(kept.at[i], got.at[i], send.at[i], recv.at[i], partner)
        swap.start()
        yield
        swap.wait()
        out_ref[...] += got[i]


def sum_scratch(n, shape):
    stages = n.bit_length() + 1
    return [
        pltpu.VMEM((stages,) + shape, jnp.float32),
        pltpu.VMEM((stages,) + shape, jnp.float32),
        pltpu.SemaphoreType.DMA((stages,)),
        pltpu.SemaphoreType.DMA((stages,)),
    ]


def share_job(sources, targets, sems):
    c, w, sib, across = here()
    pending = []
    for j, (src, dst) in enumerate(zip(sources, targets)):
        x_send, x_recv, k_send, k_recv, own_sem = sems[5 * j : 5 * j + 5]
        for q in range(src.shape[0]):
            own = pltpu.make_async_copy(src.at[q], dst.at[q, w], own_sem.at[q])
            to_x = remote(src.at[q], dst.at[q, w], x_send.at[q], x_recv.at[q], (c, across))
            to_k = remote(src.at[q], dst.at[q, w], k_send.at[0, q], k_recv.at[0, q], (c, sib))
            for copy in (to_x, to_k, own):
                copy.start()
            pending += [to_x.wait_send, to_k.wait_send, own.wait]
    yield
    for j, dst in enumerate(targets):
        x_send, x_recv, k_send, k_recv, own_sem = sems[5 * j : 5 * j + 5]
        for q in range(dst.shape[0]):
            got = dst.at[q, across]
            remote(got, got, x_send.at[q], x_recv.at[q], (c, across)).wait_recv()
            out = remote(got, got, k_send.at[1, q], k_recv.at[1, q], (c, sib))
            out.start()
            pending.append(out.wait_send)
    yield
    for j, dst in enumerate(targets):
        x_send, x_recv, k_send, k_recv, own_sem = sems[5 * j : 5 * j + 5]
        for q in range(dst.shape[0]):
            for half, place in ((0, sib), (1, (sib + 2) % 4)):
                got = dst.at[q, place]
                remote(got, got, k_send.at[half, q], k_recv.at[half, q], (c, sib)).wait_recv()
    for wait in pending:
        wait()


def share_shapes(sources):
    shapes, sems = [], []
    for src in sources:
        count = src.shape[0]
        shapes.append(jax.ShapeDtypeStruct((count, 4) + src.shape[1:], src.dtype))
        sems += [
            pltpu.SemaphoreType.DMA((count,)),
            pltpu.SemaphoreType.DMA((count,)),
            pltpu.SemaphoreType.DMA((2, count)),
            pltpu.SemaphoreType.DMA((2, count)),
            pltpu.SemaphoreType.DMA((count,)),
        ]
    return shapes, sems


def advance(*jobs):
    jobs = list(jobs)
    while jobs:
        for job in list(jobs):
            try:
                next(job)
            except StopIteration:
                jobs.remove(job)


class Line:
    def __init__(self, n):
        self.c, self.w, self.sib, self.across = here()
        self.n, self.N = n, n // 2
        self.at, self.side = self.c // 2, self.c % 2
        self.pair = (self.c + 1 - 2 * self.side, self.w)
        self.left = (self.c - 2, self.w)
        self.right = (self.c + 2, self.w)
        self.has_left = self.at > 0
        self.has_right = self.at < self.N - 1

    def greet(self, others=()):
        barrier = pltpu.get_barrier_semaphore()
        signal = lambda d: pl.semaphore_signal(barrier, inc=1, device_id=d, device_id_type=MESH)
        sure = [self.pair] + list(others)
        for device in sure:
            signal(device)
        pl.when(self.has_left)(lambda: signal(self.left))
        pl.when(self.has_right)(lambda: signal(self.right))
        beside = (self.at + self.N - 1) // self.N + (2 * self.N - 2 - self.at) // self.N
        pl.semaphore_wait(barrier, len(sure) + beside)


def scatter_job(line, theirs, mine_of, total, ybuf, zbuf, sems):
    y_send, y_recv, r_send, r_recv, l_send, l_recv = sems
    N, at, side = line.N, line.at, line.side
    wide = jnp.float32

    def both_ways(d):
        return ((at + d, at + d < N), (at - d, at - d >= 0)) if d else ((at, None),)

    def guarded(keep, step):
        if keep is None:
            step()
        else:
            pl.when(keep)(step)

    def y_copy(b, src=None):
        src = ybuf.at[b] if src is None else src
        return remote(src, ybuf.at[b], y_send.at[b], y_recv.at[b], line.pair)

    def r_copy(b, slot):
        return remote(ybuf.at[b], zbuf.at[slot], r_send.at[b], r_recv.at[b], line.right)

    def l_copy(b, slot):
        return remote(ybuf.at[b], zbuf.at[slot], l_send.at[b], l_recv.at[b], line.left)

    for d in range(N - 1, -1, -1):
        for b, keep in both_ways(d):

            def first(b=b):
                y_copy(b, theirs(b)).start()

            guarded(keep, first)
        yield
    for d in range(N - 1, 0, -1):
        for b, keep, ahead in ((at + d, at + d < N, True), (at - d, at - d >= 0, False)):

            def relay(b=b, ahead=ahead):
                mine = mine_of(b)
                y_copy(b).wait_recv()
                mine = mine + ybuf[b].astype(wide)
                came = line.has_left if ahead else line.has_right

                @pl.when(came)
                def _():
                    (r_copy if ahead else l_copy)(b, b).wait_recv()
                    ybuf[b] = (mine + zbuf[b].astype(wide)).astype(ybuf.dtype)

                @pl.when(jnp.logical_not(came))
                def _():
                    ybuf[b] = mine.astype(ybuf.dtype)

                if ahead:
                    pl.when(b == at + 1)(lambda: r_copy(b, b).start())
                    pl.when(b > at + 1)(lambda: r_copy(b, b).start())
                else:
                    pl.when(b == at - 1)(lambda: l_copy(b, N).start())
                    pl.when(b < at - 1)(lambda: l_copy(b, b).start())

            guarded(keep, relay)
        yield
    mine = mine_of(at)
    y_copy(at).wait_recv()
    total[...] = mine + ybuf[at].astype(wide)

    @pl.when(line.has_left)
    def _():
        r_copy(at, at).wait_recv()
        total[...] += zbuf[at].astype(wide)

    @pl.when(line.has_right)
    def _():
        l_copy(at, N).wait_recv()
        total[...] += zbuf[N].astype(wide)

    for d in range(N):
        for b, keep in both_ways(d):
            guarded(keep, lambda b=b: y_copy(b).wait_send())
    for d in range(1, N):
        pl.when(at + d < N)(lambda d=d: r_copy(at + d, at + d).wait_send())
        pl.when(at - d >= 0)(lambda d=d: l_copy(at - d, at - d).wait_send())


def scatter_line_job(line, value, stage, slots, pair_slot, total, sems):
    r_send, r_recv, l_send, l_recv, p_send, p_recv = sems
    n, N, at, side = line.n, line.N, line.at, line.side
    wide = jnp.float32

    def copy(q, slot, ahead):
        send, recv = (r_send, r_recv) if ahead else (l_send, l_recv)
        device = line.right if ahead else line.left
        return remote(stage.at[q], slots.at[slot], send.at[q], recv.at[q], device)

    for d in range(N - 1, 0, -1):
        for b, keep, ahead in ((at + d, at + d < N, True), (at - d, at - d >= 0, False)):

            def relay(b=b, ahead=ahead):
                came = line.has_left if ahead else line.has_right
                for y in range(2):
                    q = 2 * b + y

                    @pl.when(came)
                    def _(q=q, y=y):
                        copy(q, q, ahead).wait_recv()
                        stage[q] = (value(b, y) + slots[q].astype(wide)).astype(stage.dtype)

                    @pl.when(jnp.logical_not(came))
                    def _(q=q, y=y):
                        stage[q] = value(b, y).astype(stage.dtype)

                    if ahead:
                        copy(q, q, True).start()
                    else:
                        pl.when(b == at - 1)(lambda q=q, y=y: copy(q, n + y, False).start())
                        pl.when(b < at - 1)(lambda q=q: copy(q, q, False).start())

            pl.when(keep)(relay)
        yield

    def reach(y):
        q, y_slot = 2 * at + y, n + y
        pl.when(line.has_left)(lambda: copy(q, q, True).wait_recv())
        pl.when(line.has_right)(lambda: copy(q, y_slot, False).wait_recv())
        left = jnp.where(line.has_left, slots[q].astype(wide), 0.0)
        right = jnp.where(line.has_right, slots[y_slot].astype(wide), 0.0)
        return value(at, y) + left + right

    other = 2 * at + 1 - side
    stage[other] = reach(1 - side).astype(stage.dtype)
    swap = remote(stage.at[other], pair_slot, p_send, p_recv, line.pair)
    swap.start()
    mine = reach(side)
    yield
    swap.wait()
    total[...] = mine + pair_slot[...].astype(wide)
    for d in range(1, N):
        for y in range(2):
            pl.when(at + d < N)(lambda d=d, y=y: copy(2 * (at + d) + y, 0, True).wait_send())
            pl.when(at - d >= 0)(lambda d=d, y=y: copy(2 * (at - d) + y, 0, False).wait_send())


def gather_job(line, own, out, sems, use=None):
    r_send, l_send, y_send, recv, own_sem = sems
    n, N, at, side, c = line.n, line.N, line.at, line.side, line.c
    local = pltpu.make_async_copy(own, out(c), own_sem)
    local.start()

    def send(src, q, sem, device):
        return remote(src, out(q), sem.at[q // 2], recv.at[q], device)

    use = use or (lambda q: None)
    pair = c + 1 - 2 * side

    def other(d):
        for q, keep in ((pair - 2 * d, at - d >= 0), (pair + 2 * d, at + d < N))[: 1 + (d > 0)]:

            def take(q=q):
                send(out(q), q, y_send, line.pair).wait_recv()
                use(q)

            pl.when(keep)(take)

    pl.when(line.has_right)(lambda: send(own, c, r_send, line.right).start())
    pl.when(line.has_left)(lambda: send(own, c, l_send, line.left).start())
    send(own, c, y_send, line.pair).start()
    yield
    local.wait()
    use(c)
    for d in range(1, N):
        for q, keep, ahead in ((c - 2 * d, at - d >= 0, True), (c + 2 * d, at + d < N, False)):

            def relay(q=q, ahead=ahead):
                got = out(q)
                send(got, q, y_send, line.pair).wait_recv()
                if ahead:
                    pl.when(line.has_right)(lambda: send(got, q, r_send, line.right).start())
                else:
                    pl.when(line.has_left)(lambda: send(got, q, l_send, line.left).start())
                send(got, q, y_send, line.pair).start()
                use(q)

            pl.when(keep)(relay)
        yield
    for d in range(N):
        other(d)
    for b in range(N):
        q = 2 * b + side
        got = out(q)
        send(got, q, y_send, line.pair).wait_send()
        pl.when(jnp.logical_and(b <= at, line.has_right))(
            lambda q=q, got=got: send(got, q, r_send, line.right).wait_send()
        )
        pl.when(jnp.logical_and(b >= at, line.has_left))(
            lambda q=q, got=got: send(got, q, l_send, line.left).wait_send()
        )


def gather_pair_job(line, own, out, sems):
    r_send, l_send, y_send, recv, own_sem = sems
    n, N, at, c = line.n, line.N, line.at, line.c
    local = pltpu.make_async_copy(own, out(c), own_sem)
    local.start()

    def send(src, q, sem, device):
        return remote(src, out(q), sem.at[q], recv.at[q], device)

    def ahead(src, q, act):
        pl.when(line.has_right)(lambda: act(send(src, q, r_send, line.right)))

    def back(src, q, act):
        pl.when(line.has_left)(lambda: act(send(src, q, l_send, line.left)))

    start = lambda copy: copy.start()
    to_pair = remote(own, out(c), y_send.at[0], recv.at[c], line.pair)
    to_pair.start()
    ahead(own, c, start)
    back(own, c, start)
    yield
    local.wait()
    q = line.pair[0]
    got = out(q)
    send(got, q, r_send, line.pair).wait_recv()
    ahead(got, q, start)
    back(got, q, start)
    yield
    for d in range(1, N):
        for b, keep, forward in ((at - d, at - d >= 0, True), (at + d, at + d < N, False)):

            def relay(b=b, forward=forward):
                for y in range(2):
                    got = out(2 * b + y)
                    send(got, 2 * b + y, r_send, line.pair).wait_recv()
                    (ahead if forward else back)(got, 2 * b + y, start)

            pl.when(keep)(relay)
        yield
    to_pair.wait_send()
    done = lambda copy: copy.wait_send()
    for b in range(N):
        for y in range(2):
            q = 2 * b + y
            pl.when(b <= at)(lambda q=q: ahead(out(q), q, done))
            pl.when(b >= at)(lambda q=q: back(out(q), q, done))


def minor_rows(rows):
    return rows // 8


def scatter_steps(line, product, rows, total, made, scratch):
    N, side = line.N, line.side
    if len(made.shape) == 3:

        def theirs(b):
            made[b] = product(2 * b * rows + (1 - side) * rows, rows).astype(made.dtype)
            return made.at[b]

        yield from scatter_job(
            line,
            theirs,
            lambda b: product(2 * b * rows + side * rows, rows),
            total,
            *scratch[:2],
            scratch[2:8],
        )
        return
    few = minor_rows(rows)
    many = rows - few
    ybuf, zbuf = scratch[:2]
    stage, slots, pair_slot = scratch[8:11]
    wide = jnp.float32

    def theirs(b):
        both = product(2 * b * rows, 2 * rows).astype(made.dtype)
        made[b] = both.reshape(2, rows, D)
        return made.at[b, 1 - side, pl.ds(0, many)]

    minor = scatter_line_job(
        line,
        lambda b, y: made[b, y, many:, :].astype(wide),
        stage,
        slots,
        pair_slot,
        total.at[pl.ds(many, few)],
        scratch[11:17],
    )
    main = scatter_job(
        line,
        theirs,
        lambda b: made[b, side, :many, :].astype(wide),
        total.at[pl.ds(0, many)],
        ybuf,
        zbuf,
        scratch[2:8],
    )
    for _ in range(N):
        next(main)
        yield
    next(minor)
    for _ in range(N - 1):
        next(minor, None)
        next(main)
        yield
    finish(minor)
    finish(main)


def gather_steps(line, own, out, rows, scratch, use=None):
    few = minor_rows(rows)
    many = rows - few
    minor = gather_pair_job(
        line, own.at[pl.ds(many, few)], lambda q: out(q, many, few), scratch[5:10]
    )
    main = gather_job(line, own.at[pl.ds(0, many)], lambda q: out(q, 0, many), scratch[:5], use)
    next(minor)
    next(main)
    yield
    next(minor)
    for _ in range(line.N - 1):
        next(minor)
        next(main)
        yield
    finish(minor)
    finish(main)


GATHER = 10


def scatter_shapes(n, rows, roomy):
    N = n // 2
    few = minor_rows(rows) if roomy else 0
    many = rows - few
    low, dma = jnp.bfloat16, pltpu.SemaphoreType.DMA
    made = pltpu.VMEM((N, 2, rows, D) if roomy else (N, rows, D), low)
    scratch = [
        pltpu.VMEM((N, many, D), low),
        pltpu.VMEM((N + 1, many, D), low),
    ] + [dma((N,))] * 6
    if roomy:
        scratch += [
            pltpu.VMEM((n, few, D), low),
            pltpu.VMEM((n + 2, few, D), low),
            pltpu.VMEM((few, D), low),
        ]
        scratch += [dma((n,))] * 4 + [dma, dma]
    return made, scratch


def gather_scratch(n):
    N = n // 2
    dma = pltpu.SemaphoreType.DMA
    return [dma((N,)), dma((N,)), dma((N,)), dma((n,)), dma] + [
        dma((n,)),
        dma((n,)),
        dma((1,)),
        dma((n,)),
        dma,
    ]


def rms_factor(values):
    return lax.rsqrt(jnp.mean(values * values, axis=1, keepdims=True) + norm_eps)


def rms_back(values, gain, grad):
    factor = rms_factor(values)
    scaled = grad * gain
    inner = jnp.mean(scaled * values, axis=1, keepdims=True)
    d_gain = jnp.sum(grad * (values * factor), axis=0, keepdims=True)
    return factor * scaled - values * (factor * factor * factor * inner), d_gain


def matmul_rows(*pairs):
    def product(first, count):
        total = 0.0
        for left, right in pairs:
            part = left[pl.ds(pl.multiple_of(first, 16), count), :]
            if right.shape[0] == left.shape[1]:
                total = total + plain(part, right[...])
            else:
                total = total + cols_by_cols(part, right[...])
        return total

    return product


def finish(job):
    for _ in job:
        pass


def start_kernel(plan, n, x, w_in, w_up, w_mix, w_down, *refs):
    tokens, in_all, shared_all, up_some, mix_all, down_some = refs[:6]
    in_low, shared_low, up_low, mix_low, down_low = refs[6:11]
    t_sems = refs[11 : 11 + GATHER]
    a_send, a_recv, x_send, x_recv, k_send, k_recv, own_sem = refs[11 + GATHER :]
    line = Line(n)
    c, w, sib, across = line.c, line.w, line.sib, line.across
    greet([((c + s) % n, w) for s in range(1, n)] + [(c, sib), (c, across)])
    R, B, G = plan.R, plan.B, FF // n
    low = jnp.bfloat16
    place = lambda q, first, count: tokens.at[q, pl.ds(first, count)]
    inputs = gather_steps(line, x, place, x.shape[0], t_sems)
    next(inputs)
    passed, pending = [], []

    def pass_on(number, view, src=None):
        src = view(w) if src is None else src
        to_x = remote(src, view(w), x_send.at[number], x_recv.at[number], (c, across))
        to_k = remote(src, view(w), k_send.at[0, number], k_recv.at[0, number], (c, sib))
        to_x.start()
        to_k.start()
        pending.append(to_x)
        pending.append(to_k)
        passed.append((number, view))

    mix_low[...] = w_mix[...].astype(low)
    pass_on(2 * n, lambda place: mix_all.at[0, place], mix_low)
    shared_low[...] = jnp.zeros_like(shared_low)
    shared_low[:, : END - BC_AT] = w_in[:, BC_AT:END].astype(low)
    for p in range(n):
        if p < plan.attn:
            g = plan.kv_of(p)
            in_low[p, :, :R] = w_in[:, p * R : (p + 1) * R].astype(low)
            in_low[p, :, B : B + HD] = w_in[:, K_AT + g * HD : K_AT + (g + 1) * HD].astype(low)
            in_low[p, :, B + HD : B + 2 * HD] = w_in[
                :, V_AT + g * HD : V_AT + (g + 1) * HD
            ].astype(low)
            if B + 2 * HD < plan.A:
                rest = plan.A - B - 2 * HD
                in_low[p, :, B + 2 * HD :] = jnp.zeros((in_low.shape[1], rest), low)
        else:
            j = p - plan.attn
            in_low[p, :, :R] = w_in[:, Z_AT + j * R : Z_AT + (j + 1) * R].astype(low)
            in_low[p, :, B : B + R] = w_in[:, X_AT + j * R : X_AT + (j + 1) * R].astype(low)
            if B + R < plan.A:
                in_low[p, :, B + R :] = jnp.zeros((in_low.shape[1], plan.A - B - R), low)

    def column_copies(s):
        p = (c + s) % n
        ends = ((in_low.at[p], in_all), (shared_low, shared_all))
        return [
            remote(src, dst.at[c, w], a_send.at[k, s], a_recv.at[k, c], (p, w))
            for k, (src, dst) in enumerate(ends)
        ]

    def send_columns(steps):
        for s in steps:
            for copy in column_copies(s):
                copy.start()
                pending.append(copy)

    in_view = lambda q: lambda place: in_all.at[q, place]
    shared_view = lambda q: lambda place: shared_all.at[q, place]

    def take_columns(steps):
        for s in steps:
            q = (c + n - s) % n
            for k, view in ((0, in_view), (1, shared_view)):
                got = view(q)(w)
                remote(got, got, a_send.at[k, s], a_recv.at[k, q], (q, w)).wait_recv()
                pass_on(k * n + q, view(q))

    done = [0]

    def seconds(upto):
        while done[0] < min(upto, len(passed)):
            number, view = passed[done[0]]
            got = view(across)
            remote(got, got, x_send.at[number], x_recv.at[number], (c, across)).wait_recv()
            out = remote(got, got, k_send.at[1, number], k_recv.at[1, number], (c, sib))
            out.start()
            pending.append(out)
            done[0] += 1

    cuts = [round(1 + (n - 1) * i / 3) for i in range(4)]
    parts = [range(cuts[i], cuts[i + 1]) for i in range(3)]
    send_columns(parts[0])
    pass_on(c, in_view(c), in_low.at[c])
    pass_on(n + c, shared_view(c), shared_low)
    down_low[...] = w_down[...].astype(low)
    for p in range(n):
        up_low[p, :, :G] = w_up[:, p * G : (p + 1) * G].astype(low)
        up_low[p, :, G:] = w_up[:, FF + p * G : FF + (p + 1) * G].astype(low)
    locals_started = []
    own = (
        (in_low.at[c], in_all.at[c, w]),
        (shared_low, shared_all.at[c, w]),
        (mix_low, mix_all.at[0, w]),
        (up_low.at[c], up_some.at[c]),
        (down_low, down_some.at[0]),
    )
    for i, (src, dst) in enumerate(own):
        copy = pltpu.make_async_copy(src, dst, own_sem.at[i])
        copy.start()
        locals_started.append(copy)
    for step in range(3):
        for _ in range(line.N // 4):
            next(inputs, None)
        if step < 2:
            send_columns(parts[step + 1])
        else:
            for s in range(1, n):
                p = (c + s) % n
                out = remote(
                    up_low.at[p], up_some.at[c], a_send.at[2, s], a_recv.at[2, c], (p, w)
                )
                out.start()
                pending.append(out)
        take_columns(parts[step])
        seconds(len(passed) - 4)
    finish(inputs)
    seconds(len(passed))
    for s in range(1, n):
        q = (c + n - s) % n
        got = up_some.at[q]
        remote(got, got, a_send.at[2, s], a_recv.at[2, q], (q, w)).wait_recv()
    for number, view in passed:
        for half, place in ((0, sib), (1, (sib + 2) % 4)):
            got = view(place)
            remote(got, got, k_send.at[half, number], k_recv.at[half, number], (c, sib)).wait_recv()
    for copy in locals_started:
        copy.wait()
    for out in pending:
        out.wait_send()


def branch_kernel(n, refs_in, refs_out, scratch):
    left, right, source, gain, up, down = refs_in
    middle, gates, normed, up_all, down_all = refs_out
    line = Line(n)
    line.greet([(line.c, line.sib), (line.c, line.across)])
    rows = source.shape[0]
    (total, own, made), (flow, gather, extra) = scratch[:3], scratch[3:]
    share = share_job((up, down), (up_all, down_all), extra)
    main = scatter_steps(line, matmul_rows((left, right)), rows, total, made, flow)
    next(main)
    next(share)
    finish(main)
    value = source[...].astype(jnp.float32) + total[...]
    middle[...] = value
    own[...] = (value * rms_factor(value) * gain[...]).astype(own.dtype)
    place = lambda q, first, count: normed.at[q, pl.ds(first, count)]

    def use(q):
        gates[pl.ds(pl.multiple_of(q * rows, rows), rows), :] = plain(
            normed[q], up_all[...].reshape(D, -1)
        )

    fused = gates.shape[0] == n * rows
    spread_out = gather_steps(
        line, own, place, rows, gather, use if fused else None
    )
    next(spread_out)
    next(share)
    finish(share)
    finish(spread_out)


def feed_back_kernel(n, refs_in, refs_out, scratch):
    left, right, cotangent, middle, gain, active, w_down, w_mix, normed, upstream, up, down = refs_in
    grad, d_gain, result, made, low_all, up_sum, down_sum = refs_out
    line = Line(n)
    line.greet([(line.c, line.sib), (line.c, line.across)])
    rows = cotangent.shape[0]
    (total, own, terms), (flow, gather, extra) = scratch[:3], scratch[3:]
    both = result.shape[0] == rows
    pieces = []
    if both:
        (late_total, up, down, normed_part, upstream_part, part_sem), extra = extra[:6], extra[6:]
        late_flow, extra = extra[: len(flow)], extra[len(flow) :]
        width = D // n
        height = down.shape[2]

        def fetch(q):
            columns = pl.ds(q * width, width)
            return [
                pltpu.make_async_copy(a.at[:, columns], b.at[q % 2], part_sem.at[i, q % 2])
                for i, (a, b) in enumerate(((normed, normed_part), (upstream, upstream_part)))
            ]

        def piece(q):
            for copy in fetch(q):
                copy.wait()
            if q + 1 < n:
                for copy in fetch(q + 1):
                    copy.start()
            part = rows_by_rows(normed_part[q % 2], left[...])
            up[q] = part.astype(up.dtype).reshape(up.shape[1:])
            part = rows_by_rows(active[...], upstream_part[q % 2]).astype(down.dtype)
            for k in range(4):
                down[0, k, :, q * width : (q + 1) * width] = part[k * height : (k + 1) * height]

        for copy in fetch(0):
            copy.start()
        pieces = [functools.partial(piece, q) for q in range(n)]
    sums = collect_job(n, ("rows", "rows"), (up, down), (up_sum, down_sum), extra)
    main = scatter_steps(line, matmul_rows((left, right)), rows, total, terms, flow)
    for _ in range(line.N):
        next(main)
    if not both:
        next(sums)
    per = -(-len(pieces) // max(line.N - 1, 1))
    for step in range(line.N - 1):
        for piece in pieces[step * per : (step + 1) * per]:
            piece()
        next(main)
    if both:
        next(sums)
    next(sums)
    finish(main)
    back, gain_row = rms_back(middle[...], gain[...], total[...])
    value = cotangent[...].astype(jnp.float32) + back
    grad[...] = value
    d_gain[...] = jnp.broadcast_to(gain_row, d_gain.shape)
    own[...] = value.astype(own.dtype)
    place = lambda q, first, count: low_all.at[q, pl.ds(first, count)]

    def use(q):
        made[pl.ds(pl.multiple_of(q * rows, rows), rows), :] = cols_by_cols(
            low_all[q], w_mix[...]
        ).astype(made.dtype)

    spread_out = gather_steps(
        line, own, place, rows, gather, use if both else None
    )
    next(spread_out)
    if both:
        late = scatter_steps(
            line, matmul_rows((active, w_down)), rows, late_total, terms, late_flow
        )
        for _ in range(line.N - 1):
            next(late)
            next(spread_out)
        for _ in range(line.N):
            next(late)
    finish(spread_out)
    finish(sums)
    if both:
        finish(late)
        result[...] = (middle[...] + late_total[...]).astype(result.dtype)


SUMS = ("cols", "cols", "rows")


def source_back_kernel(n, refs_in, refs_out, scratch):
    (left, left_two, right, right_two, source, grad_middle, gain, vector, up) = refs_in[:9]
    w_in, w_shared, w_mix = refs_in[9:]
    grad, vector_sum, up_home, in_sum, shared_sum, mix_sum = refs_out
    line = Line(n)
    others = [((line.c + s) % n, line.w) for s in range(1, n)]
    greet(others + [(line.c, line.sib), (line.c, line.across)])
    rows = source.shape[0]
    (total, _, made), (flow, _, extra) = scratch[:3], scratch[3:]
    sums = collect_job(n, SUMS, (w_in, w_shared, w_mix), (in_sum, shared_sum, mix_sum), extra[:-6])
    product = matmul_rows((left, right), (left_two, right_two))
    main = scatter_steps(line, product, rows, total, made, flow)
    vectors = sum_job(n, vector, vector_sum, *extra[-6:-2])
    home = home_job(n, up, up_home, *extra[-2:])
    next(vectors)
    next(home)
    next(main)
    next(sums)
    for _ in range(line.N - 1):
        next(main)
    next(vectors)
    next(sums)
    for _ in main:
        next(vectors, None)
        next(sums)
        next(sums)
    for _ in range(n - 2 * line.N + 2):
        next(sums)
    finish(vectors)
    back, _ = rms_back(source[...].astype(jnp.float32), gain[...], total[...])
    grad[...] = grad_middle[...] + back
    finish(home)
    finish(sums)


def flow_call(
    kernel, n, rows, args, outs, gathers, away, extra, collective_id, near=False, far_args=()
):
    inside = pl.BlockSpec(memory_space=pltpu.VMEM)
    outside = pl.BlockSpec(memory_space=pl.ANY)
    side_args, side_shapes, side_scratch = extra
    shapes = list(outs)
    specs = [inside] * len(outs)
    scratch = [
        pltpu.VMEM((rows, D), jnp.float32),
        pltpu.VMEM((rows, D) if gathers else (16, 128), jnp.bfloat16),
    ]
    made, flow = scatter_shapes(n, rows, args[0].shape[0] <= 1024)
    gather = []
    if gathers:
        shapes.append(jax.ShapeDtypeStruct((n, rows, D), jnp.bfloat16))
        specs.append(inside if near else outside)
        gather = gather_scratch(n)
    scratch = scratch + [made] + flow + gather + list(side_scratch)
    ends = 3 + len(flow), 3 + len(flow) + len(gather)
    side = outside if away else inside
    in_specs = [inside] * len(args) + [outside] * len(far_args) + [side] * len(side_args)
    specs = specs + [inside if near else side] * len(side_shapes)
    shapes = shapes + list(side_shapes)
    first, second = len(in_specs), len(in_specs) + len(specs)

    def run(*refs):
        parts = refs[second:]
        groups = parts[3 : ends[0]], parts[ends[0] : ends[1]], parts[ends[1] :]
        kernel(n, refs[:first], refs[first:second], tuple(parts[:3]) + groups)

    return pl.pallas_call(
        run,
        out_shape=tuple(shapes),
        in_specs=in_specs,
        out_specs=tuple(specs),
        scratch_shapes=scratch,
        cost_estimate=pl.CostEstimate(flops=0, bytes_accessed=2 * 10**8, transcendentals=0),
        compiler_params=pltpu.CompilerParams(
            collective_id=collective_id, has_side_effects=True, vmem_limit_bytes=VMEM
        ),
    )(*args, *far_args, *side_args)


def start_call(plan, n, x, w_in, w_up, w_mix, w_down, collective_id):
    rows = w_in.shape[0]
    low = jnp.bfloat16
    G = FF // n
    shapes = (
        jax.ShapeDtypeStruct((n,) + x.shape, low),
        jax.ShapeDtypeStruct((n, 4, rows, plan.A), low),
        jax.ShapeDtypeStruct((n, 4, rows, plan.K), low),
        jax.ShapeDtypeStruct((n, rows, 2 * G), low),
        jax.ShapeDtypeStruct((1, 4) + w_mix.shape, low),
        jax.ShapeDtypeStruct((1,) + w_down.shape, low),
    )
    dma = pltpu.SemaphoreType.DMA
    outside = pl.BlockSpec(memory_space=pl.ANY)
    inside = pl.BlockSpec(memory_space=pltpu.VMEM)
    blocks = 2 * n + 1
    outs = pl.pallas_call(
        functools.partial(start_kernel, plan, n),
        out_shape=shapes,
        in_specs=[outside] + [inside] * 4,
        out_specs=(outside,) * 6,
        scratch_shapes=[
            pltpu.VMEM((n, rows, plan.A), low),
            pltpu.VMEM((rows, plan.K), low),
            pltpu.VMEM((n, rows, 2 * G), low),
            pltpu.VMEM(w_mix.shape, low),
            pltpu.VMEM(w_down.shape, low),
        ]
        + gather_scratch(n)
        + [dma((3, n)), dma((3, n))]
        + [dma((blocks,)), dma((blocks,)), dma((2, blocks)), dma((2, blocks))]
        + [dma((5,))],
        cost_estimate=pl.CostEstimate(flops=0, bytes_accessed=2 * 10**8, transcendentals=0),
        compiler_params=pltpu.CompilerParams(
            collective_id=collective_id, has_side_effects=True, vmem_limit_bytes=VMEM
        ),
    )(x, w_in, w_up, w_mix, w_down)
    flat = lambda o: o.reshape(-1, o.shape[-1])
    tokens, in_all, shared_all, up_some, mix_all, down_some = outs
    return flat(tokens), flat(in_all), flat(shared_all), up_some, flat(mix_all), down_some


def mm(left, right):
    return jnp.dot(
        left.astype(jnp.bfloat16), right.astype(jnp.bfloat16), preferred_element_type=jnp.float32
    )


def mm_nt(left, right):
    return cols_by_cols(left.astype(jnp.bfloat16), right.astype(jnp.bfloat16))


def mm_tn(left, right):
    return rows_by_rows(left.astype(jnp.bfloat16), right.astype(jnp.bfloat16))


def pieces(values, count):
    found = []
    for _ in range(count):
        part = values.astype(jnp.bfloat16)
        found.append(part)
        values = values - part.astype(jnp.float32)
    return found


def by_marks(values, marks, count=2):
    return plain(
        jnp.concatenate(pieces(values, count), axis=1), jnp.concatenate([marks] * count, axis=0)
    )


def marks_by(marks, values, count=3):
    return plain(
        jnp.concatenate([marks] * count, axis=1), jnp.concatenate(pieces(values, count), axis=0)
    )


def iota(shape, axis):
    return lax.broadcasted_iota(jnp.int32, shape, axis)


def rope_tables(length):
    half = HD // 2
    frequency = rope_base ** (-jnp.arange(half, dtype=jnp.float32) / half)
    angles = jnp.arange(length).astype(jnp.float32)[:, None] * frequency[None, :]
    cosine, sine = jnp.cos(angles), jnp.sin(angles)
    return (
        jnp.concatenate([cosine, cosine], axis=1),
        jnp.concatenate([-sine, sine], axis=1),
    )


def turned(values, cosine, sine):
    return values * cosine + pltpu.roll(values, HD // 2, 1) * sine


def attn_stack(plan, q_ref, cosine, sine):
    heads = [
        turned(q_ref[:, h * HD : (h + 1) * HD], cosine, sine).astype(jnp.bfloat16)
        for h in range(plan.ha)
    ]
    return jnp.concatenate(heads, axis=0)


def by_extent(step, length, run):
    parts = 4
    per = length // CHUNK // parts
    for part in range(parts):
        pl.when(step // per == part)(functools.partial(run, (part + 1) * per * CHUNK))


def attn_softmax(stack, keys, at):
    scores = cols_by_cols(stack, keys) * (1.0 / math.sqrt(HD))
    row = iota(scores.shape, 0) & (CHUNK - 1)
    scores = jnp.where(iota(scores.shape, 1) <= row + at, scores, masked_score)
    weights = jnp.exp(scores - jnp.max(scores, axis=1, keepdims=True))
    return weights * (1.0 / jnp.sum(weights, axis=1, keepdims=True))


def attn_fwd_kernel(plan, q_ref, k_ref, v_ref, cos_ref, sin_ref, out_ref, keys, values):
    step = pl.program_id(0)

    @pl.when(step == 0)
    def _():
        keys[...] = turned(k_ref[...], cos_ref[...], sin_ref[...]).astype(jnp.bfloat16)
        values[...] = v_ref[...].astype(jnp.bfloat16)

    at = pl.multiple_of(step * CHUNK, CHUNK)
    rows = pl.ds(at, CHUNK)
    stack = attn_stack(plan, q_ref, cos_ref[rows, :], sin_ref[rows, :])

    def run(extent):
        probs = attn_softmax(stack, keys[:extent, :], at)
        made = mm(probs, values[:extent, :])
        for h in range(plan.ha):
            out_ref[:, h * HD : (h + 1) * HD] = made[h * CHUNK : (h + 1) * CHUNK]

    by_extent(step, keys.shape[0], run)


def attn_fwd(plan, proj, tables):
    length = proj.shape[0]
    whole = lambda i: (0, 0)
    return pl.pallas_call(
        functools.partial(attn_fwd_kernel, plan),
        grid=(length // CHUNK,),
        out_shape=jax.ShapeDtypeStruct((length, plan.R), jnp.float32),
        in_specs=[
            pl.BlockSpec((CHUNK, plan.R), lambda i: (i, 0)),
            pl.BlockSpec((length, HD), lambda i: (0, plan.B // HD)),
            pl.BlockSpec((length, HD), lambda i: (0, plan.B // HD + 1)),
            pl.BlockSpec((length, HD), whole),
            pl.BlockSpec((length, HD), whole),
        ],
        out_specs=pl.BlockSpec((CHUNK, plan.R), lambda i: (i, 0)),
        scratch_shapes=[pltpu.VMEM((length, HD), jnp.bfloat16)] * 2,
        compiler_params=pltpu.CompilerParams(vmem_limit_bytes=VMEM),
    )(proj, proj, proj, *tables)


def attn_bwd_kernel(
    plan, q_ref, k_ref, v_ref, cos_ref, sin_ref, grad_ref, slab_ref, keys, values, grad_k, grad_v
):
    step = pl.program_id(0)
    scale = 1.0 / math.sqrt(HD)

    @pl.when(step == 0)
    def _():
        keys[...] = turned(k_ref[...], cos_ref[...], sin_ref[...]).astype(jnp.bfloat16)
        values[...] = v_ref[...].astype(jnp.bfloat16)
        grad_k[...] = jnp.zeros_like(grad_k)
        grad_v[...] = jnp.zeros_like(grad_v)
        slab_ref[...] = jnp.zeros_like(slab_ref)

    at = pl.multiple_of(step * CHUNK, CHUNK)
    rows = pl.ds(at, CHUNK)
    cosine, sine = cos_ref[rows, :], sin_ref[rows, :]
    stack = attn_stack(plan, q_ref, cosine, sine)
    grads = jnp.concatenate([grad_ref[:, h * HD : (h + 1) * HD] for h in range(plan.ha)], axis=0)

    def run(extent):
        probs = attn_softmax(stack, keys[:extent, :], at)
        grad_probs = cols_by_cols(grads, values[:extent, :])
        delta = jnp.sum(probs * grad_probs, axis=1, keepdims=True)
        grad_scores = (probs * (grad_probs - delta)).astype(jnp.bfloat16)
        grad_q = mm(grad_scores, keys[:extent, :]) * scale
        for h in range(plan.ha):
            slab_ref[rows, h * HD : (h + 1) * HD] = turned(
                grad_q[h * CHUNK : (h + 1) * CHUNK], cosine, -sine
            ).astype(jnp.bfloat16)
        grad_k[:extent, :] += mm_tn(grad_scores, stack)
        grad_v[:extent, :] += mm_tn(probs, grads)

    by_extent(step, keys.shape[0], run)

    @pl.when(step == pl.num_programs(0) - 1)
    def _():
        slab_ref[:, plan.B : plan.B + HD] = turned(
            grad_k[...] * scale, cos_ref[...], -sin_ref[...]
        ).astype(jnp.bfloat16)
        slab_ref[:, plan.B + HD : plan.B + 2 * HD] = grad_v[...].astype(jnp.bfloat16)


def attn_bwd(plan, proj, tables, grad):
    length = proj.shape[0]
    whole = lambda i: (0, 0)
    return pl.pallas_call(
        functools.partial(attn_bwd_kernel, plan),
        grid=(length // CHUNK,),
        out_shape=jax.ShapeDtypeStruct((length, plan.A), jnp.bfloat16),
        in_specs=[
            pl.BlockSpec((CHUNK, plan.R), lambda i: (i, 0)),
            pl.BlockSpec((length, HD), lambda i: (0, plan.B // HD)),
            pl.BlockSpec((length, HD), lambda i: (0, plan.B // HD + 1)),
            pl.BlockSpec((length, HD), whole),
            pl.BlockSpec((length, HD), whole),
            pl.BlockSpec((CHUNK, plan.R), lambda i: (i, 0)),
        ],
        out_specs=pl.BlockSpec((length, plan.A), whole),
        scratch_shapes=[pltpu.VMEM((length, HD), jnp.bfloat16)] * 2
        + [pltpu.VMEM((length, HD), jnp.float32)] * 2,
        compiler_params=pltpu.CompilerParams(vmem_limit_bytes=VMEM),
    )(proj, proj, proj, *tables, grad)


def head_spread(plan):
    return ((iota((PAD, plan.R), 1) >> 6) == iota((PAD, plan.R), 0)).astype(jnp.bfloat16)


def head_gather(plan):
    return ((iota((plan.R, PAD), 0) >> 6) == iota((plan.R, PAD), 1)).astype(jnp.bfloat16)


def lower_ones():
    shape = (CHUNK, CHUNK)
    return (iota(shape, 0) >= iota(shape, 1)).astype(jnp.bfloat16)


def space_parts(plan, dt_raw, window, conv_ref, head_ref, pick_ref):
    total = conv_ref[4:5, :]
    for k in range(CONV):
        at = 8 - CONV + 1 + k
        total = total + conv_ref[k : k + 1, :] * window[at : at + CHUNK, :]
    raw = by_marks(dt_raw, pick_ref[...], 3) + head_ref[1:2, :]
    steps = jnp.maximum(raw, 0.0) + jnp.log1p(jnp.exp(-jnp.abs(raw)))
    logs = -steps * jnp.exp(head_ref[0:1, :])
    cumul = marks_by(lower_ones(), logs)
    return total, raw, steps, logs, cumul


def decay_of(cumul, cumul_t, causal, h):
    gaps = cumul[:, h : h + 1] - cumul_t[h : h + 1, :]
    return jnp.exp(jnp.where(causal, gaps, masked_score))


def space_fwd_kernel(
    plan, proj_ref, shared_ref, conv_ref, head_ref, pick_ref, gated_ref, made_ref, before_ref, state, window
):
    R = plan.R
    step = pl.program_id(0)

    @pl.when(step == 0)
    def _():
        state[...] = jnp.zeros_like(state)
        window[0:8, :] = jnp.zeros((8, window.shape[1]), jnp.float32)

    @pl.when(step > 0)
    def _():
        window[0:8, :] = window[CHUNK : CHUNK + 8, :]

    window[8 : CHUNK + 8, :R] = proj_ref[:, plan.B : plan.B + R]
    window[8 : CHUNK + 8, R:] = shared_ref[:, : 2 * NS]
    total, _, steps, _, cumul = space_parts(
        plan, shared_ref[:, 2 * NS :], window, conv_ref, head_ref, pick_ref
    )
    post = total * jax.nn.sigmoid(total)
    x = post[:, :R]
    b = post[:, R : R + NS].astype(jnp.bfloat16)
    c = post[:, R + NS :].astype(jnp.bfloat16)
    spread_heads = head_spread(plan)
    cumul_t = cumul.T
    last = cumul[CHUNK - 1 : CHUNK, :]
    tail = jnp.exp(last - cumul)
    weighted = x * by_marks(steps, spread_heads)
    causal = iota((CHUNK, CHUNK), 0) >= iota((CHUNK, CHUNK), 1)
    inner = cols_by_cols(c, b)
    before = state[...]
    before_ref[0] = before.astype(jnp.bfloat16)
    made = mm(c, before) * by_marks(jnp.exp(cumul), spread_heads)
    made = made + by_marks(jnp.broadcast_to(head_ref[2:3, :], (8, PAD)), spread_heads)[0:1] * x
    left = iota((CHUNK, 2 * MP), 1) < MP
    weighted_low = weighted.astype(jnp.bfloat16)
    intra = []
    for pair in range(plan.hm // 2):
        lanes = weighted_low[:, pair * 2 * MP : (pair + 1) * 2 * MP]
        one = mm(inner * decay_of(cumul, cumul_t, causal, 2 * pair), lanes)
        two = mm(inner * decay_of(cumul, cumul_t, causal, 2 * pair + 1), lanes)
        intra.append(jnp.where(left, one, two))
    made = made + jnp.concatenate(intra, axis=1)
    state[...] = before * by_marks(
        jnp.broadcast_to(jnp.exp(last), (8, PAD)), spread_heads
    )[0:1] + mm_tn(b, weighted * by_marks(tail, spread_heads))
    z = proj_ref[:, :R]
    made_ref[...] = made
    gated_ref[...] = made * (z * jax.nn.sigmoid(z))


def space_fwd(plan, proj, shared, conv, heads, pick):
    length = proj.shape[0]
    chunks = length // CHUNK
    W = plan.W
    whole = lambda i: (0, 0)
    rows = lambda i: (i, 0)
    return pl.pallas_call(
        functools.partial(space_fwd_kernel, plan),
        grid=(chunks,),
        out_shape=(
            jax.ShapeDtypeStruct((length, plan.R), jnp.float32),
            jax.ShapeDtypeStruct((length, plan.R), jnp.float32),
            jax.ShapeDtypeStruct((chunks, NS, plan.R), jnp.bfloat16),
        ),
        in_specs=[
            pl.BlockSpec((CHUNK, plan.A), rows),
            pl.BlockSpec((CHUNK, plan.K), rows),
            pl.BlockSpec((8, W), whole),
            pl.BlockSpec((8, PAD), whole),
            pl.BlockSpec((PAD, PAD), whole),
        ],
        out_specs=(
            pl.BlockSpec((CHUNK, plan.R), rows),
            pl.BlockSpec((CHUNK, plan.R), rows),
            pl.BlockSpec((1, NS, plan.R), lambda i: (i, 0, 0)),
        ),
        scratch_shapes=[
            pltpu.VMEM((NS, plan.R), jnp.float32),
            pltpu.VMEM((CHUNK + 8, W), jnp.float32),
        ],
        compiler_params=pltpu.CompilerParams(vmem_limit_bytes=VMEM),
    )(proj, shared, conv, heads, pick)


def space_bwd_kernel(
    plan, proj_ref, shared_ref, prev_ref, prev_shared, conv_ref, head_ref, pick_ref, grad_ref, made_ref,
    before_ref, slab_ref, slab_shared, conv_acc, head_acc, skip_acc, d_state, window, d_window,
):
    R = plan.R
    step = pl.program_id(0)
    chunk = pl.num_programs(0) - 1 - step

    @pl.when(step == 0)
    def _():
        d_state[...] = jnp.zeros_like(d_state)
        d_window[CHUNK : CHUNK + 8, :] = jnp.zeros((8, plan.W), jnp.float32)
        conv_acc[...] = jnp.zeros_like(conv_acc)
        head_acc[...] = jnp.zeros_like(head_acc)
        skip_acc[...] = jnp.zeros_like(skip_acc)

    @pl.when(step > 0)
    def _():
        d_window[CHUNK : CHUNK + 8, :] = d_window[0:8, :]

    window[0:8, :R] = jnp.where(chunk == 0, 0.0, prev_ref[:, plan.B : plan.B + R])
    window[0:8, R:] = jnp.where(chunk == 0, 0.0, prev_shared[:, : 2 * NS])
    window[8 : CHUNK + 8, :R] = proj_ref[:, plan.B : plan.B + R]
    window[8 : CHUNK + 8, R:] = shared_ref[:, : 2 * NS]
    total, raw, steps, logs, cumul = space_parts(
        plan, shared_ref[:, 2 * NS :], window, conv_ref, head_ref, pick_ref
    )
    sig = jax.nn.sigmoid(total)
    post = total * sig
    x = post[:, :R]
    b = post[:, R : R + NS].astype(jnp.bfloat16)
    c = post[:, R + NS :].astype(jnp.bfloat16)
    spread_heads = head_spread(plan)
    gather_heads = head_gather(plan)
    cumul_t = cumul.T
    last = cumul[CHUNK - 1 : CHUNK, :]
    steps_wide = by_marks(steps, spread_heads)
    tail_wide = by_marks(jnp.exp(last - cumul), spread_heads)
    grow_wide = by_marks(jnp.exp(cumul), spread_heads)
    last_wide = by_marks(jnp.broadcast_to(jnp.exp(last), (8, PAD)), spread_heads)[0:1]
    skip_wide = by_marks(jnp.broadcast_to(head_ref[2:3, :], (8, PAD)), spread_heads)[0:1]
    weighted = x * steps_wide
    causal = iota((CHUNK, CHUNK), 0) >= iota((CHUNK, CHUNK), 1)
    inner = cols_by_cols(c, b)

    z = proj_ref[:, :R]
    sig_z = jax.nn.sigmoid(z)
    grad = grad_ref[...]
    d_made = grad * (z * sig_z)
    slab_ref[:, :R] = (grad * made_ref[...] * (sig_z * (1.0 + z * (1.0 - sig_z)))).astype(
        jnp.bfloat16
    )
    skip_acc[0:1, :] += jnp.sum(d_made * x, axis=0, keepdims=True)

    before = before_ref[0]
    d_after = d_state[...]
    d_after_low = d_after.astype(jnp.bfloat16)
    grown = d_made * grow_wide
    grown_low = grown.astype(jnp.bfloat16)
    carried = mm(c, before)
    d_c = mm_nt(grown_low, before)
    pulled = weighted * tail_wide
    d_pulled = mm(b, d_after_low)
    d_b = mm_nt(pulled, d_after_low)
    d_cumul = by_marks(grown * carried, gather_heads)
    kept = by_marks(d_pulled * pulled, gather_heads)
    d_cumul = d_cumul - kept
    decayed = jnp.sum(d_after * before.astype(jnp.float32), axis=0, keepdims=True) * last_wide
    d_last = jnp.sum(kept, axis=0, keepdims=True) + by_marks(
        jnp.broadcast_to(decayed, (8, R)), gather_heads
    )[0:1]
    d_state[...] = d_after * last_wide + mm_tn(c, grown_low)

    left = iota((CHUNK, 2 * MP), 1) < MP
    lane = iota((CHUNK, PAD), 1)
    sub = iota((8, CHUNK), 0)
    weighted_low = weighted.astype(jnp.bfloat16)
    d_made_low = d_made.astype(jnp.bfloat16)
    d_inner = jnp.zeros((CHUNK, CHUNK), jnp.float32)
    columns = jnp.zeros((8, CHUNK), jnp.float32)
    d_weighted = []
    for pair in range(plan.hm // 2):
        at = slice(pair * 2 * MP, (pair + 1) * 2 * MP)
        lanes, d_lanes = weighted_low[:, at], d_made_low[:, at]
        halves = []
        for which in range(2):
            h = 2 * pair + which
            decay = decay_of(cumul, cumul_t, causal, h)
            whole = inner * decay
            halves.append(mm_tn(whole, d_lanes))
            mine = jnp.where(left if which == 0 else ~left, d_lanes, jnp.zeros_like(d_lanes))
            d_whole = cols_by_cols(mine, lanes)
            d_inner = d_inner + d_whole * decay
            slope = d_whole * whole
            d_cumul = d_cumul + jnp.where(lane == h, jnp.sum(slope, axis=1, keepdims=True), 0.0)
            columns = columns + jnp.where(sub == h, jnp.sum(slope, axis=0, keepdims=True), 0.0)
        d_weighted.append(jnp.where(left, halves[0], halves[1]))
    d_weighted = jnp.concatenate(d_weighted, axis=1) + d_pulled * tail_wide
    columns = jnp.concatenate([columns, jnp.zeros((CHUNK - 8, CHUNK), jnp.float32)], axis=0).T
    d_cumul = d_cumul - columns
    d_inner_low = d_inner.astype(jnp.bfloat16)
    d_c = d_c + mm(d_inner_low, b)
    d_b = d_b + mm_tn(d_inner_low, c)
    d_x = d_weighted * steps_wide + skip_wide * d_made
    d_steps = by_marks(d_weighted * x, gather_heads)
    upper = (iota((CHUNK, CHUNK), 0) <= iota((CHUNK, CHUNK), 1)).astype(jnp.bfloat16)
    d_logs = marks_by(upper, d_cumul) + d_last
    d_steps = d_steps - jnp.exp(head_ref[0:1, :]) * d_logs
    d_raw = d_steps * jax.nn.sigmoid(raw)
    d_raw = jnp.where(lane < plan.hm, d_raw, 0.0)
    slab_shared[:, 2 * NS :] = cols_by_cols(d_raw.astype(jnp.bfloat16), pick_ref[...]).astype(
        jnp.bfloat16
    )
    head_acc[0:1, :] += jnp.sum(d_logs * logs, axis=0, keepdims=True)
    head_acc[1:2, :] += jnp.sum(d_raw, axis=0, keepdims=True)

    d_post = jnp.concatenate([d_x, d_b, d_c], axis=1)
    d_total = d_post * (sig * (1.0 + total * (1.0 - sig)))
    d_window[0:CHUNK, :] = d_total
    d_xbc = jnp.zeros((CHUNK, plan.W), jnp.float32)
    for k in range(CONV):
        shift = CONV - 1 - k
        d_xbc = d_xbc + conv_ref[k : k + 1, :] * d_window[shift : shift + CHUNK, :]
        at = 8 - CONV + 1 + k
        conv_acc[k : k + 1, :] += jnp.sum(
            d_total * window[at : at + CHUNK, :], axis=0, keepdims=True
        )
    conv_acc[4:5, :] += jnp.sum(d_total, axis=0, keepdims=True)
    slab_ref[:, plan.B : plan.B + R] = d_xbc[:, :R].astype(jnp.bfloat16)
    slab_shared[:, : 2 * NS] = d_xbc[:, R:].astype(jnp.bfloat16)
    if plan.B + R < plan.A:
        slab_ref[:, plan.B + R :] = jnp.zeros((CHUNK, plan.A - plan.B - R), jnp.bfloat16)


def space_bwd(plan, proj, shared, conv, heads, pick, grad, made, before):
    length = proj.shape[0]
    chunks = length // CHUNK
    W = plan.W
    whole = lambda i: (0, 0)
    rows = lambda i: (chunks - 1 - i, 0)
    per = CHUNK // 8
    return pl.pallas_call(
        functools.partial(space_bwd_kernel, plan),
        grid=(chunks,),
        out_shape=(
            jax.ShapeDtypeStruct((length, plan.A), jnp.bfloat16),
            jax.ShapeDtypeStruct((length, plan.K), jnp.bfloat16),
            jax.ShapeDtypeStruct((8, W), jnp.float32),
            jax.ShapeDtypeStruct((8, PAD), jnp.float32),
            jax.ShapeDtypeStruct((8, plan.R), jnp.float32),
        ),
        in_specs=[
            pl.BlockSpec((CHUNK, plan.A), rows),
            pl.BlockSpec((CHUNK, plan.K), rows),
            pl.BlockSpec((8, plan.A), lambda i: (jnp.maximum((chunks - 1 - i) * per - 1, 0), 0)),
            pl.BlockSpec((8, plan.K), lambda i: (jnp.maximum((chunks - 1 - i) * per - 1, 0), 0)),
            pl.BlockSpec((8, W), whole),
            pl.BlockSpec((8, PAD), whole),
            pl.BlockSpec((PAD, PAD), whole),
            pl.BlockSpec((CHUNK, plan.R), rows),
            pl.BlockSpec((CHUNK, plan.R), rows),
            pl.BlockSpec((1, NS, plan.R), lambda i: (chunks - 1 - i, 0, 0)),
        ],
        out_specs=(
            pl.BlockSpec((CHUNK, plan.A), rows),
            pl.BlockSpec((CHUNK, plan.K), rows),
            pl.BlockSpec((8, W), whole),
            pl.BlockSpec((8, PAD), whole),
            pl.BlockSpec((8, plan.R), whole),
        ),
        scratch_shapes=[
            pltpu.VMEM((NS, plan.R), jnp.float32),
            pltpu.VMEM((CHUNK + 8, W), jnp.float32),
            pltpu.VMEM((CHUNK + 8, W), jnp.float32),
        ],
        compiler_params=pltpu.CompilerParams(vmem_limit_bytes=VMEM),
    )(proj, shared, proj, shared, conv, heads, pick, grad, made, before)


def body(
    inputs,
    cotangent,
    w_in,
    w_in_m,
    w_in_v,
    w_mix,
    w_mix_m,
    w_mix_v,
    w_up,
    w_up_m,
    w_up_v,
    w_down,
    w_down_m,
    w_down_v,
    vectors,
    vectors_m,
    vectors_v,
):
    low = jnp.bfloat16
    count = lax.axis_size("ctx")
    ways = lax.axis_size("wshard")
    place = lax.axis_index("ctx")
    plan = Plan(count)
    R, hm = plan.R, plan.hm
    is_space = place >= plan.attn
    space = jnp.maximum(place - plan.attn, 0)

    gain_attn, gain_ffn, gain_ssm, conv_bias, conv_weight, a_log, dt_bias, d_skip = split_vectors(
        vectors
    )
    whole, in_own, shared_own, up_some, mix_own, down_some = start_call(
        plan, count, inputs[0], w_in, w_up, w_mix, w_down, 1
    )

    own = lambda a, size, axis=0: lax.dynamic_slice_in_dim(a, space * size, size, axis)
    gain_own = own(gain_ssm, R)
    W = plan.W
    conv = jnp.concatenate(
        [
            jnp.concatenate([own(conv_weight, R, 1), conv_weight[:, DSSM:]], axis=1),
            jnp.concatenate([own(conv_bias, R), conv_bias[DSSM:]])[None],
            jnp.zeros((8 - CONV - 1, W), jnp.float32),
        ]
    )
    heads = jnp.stack([own(v, hm) for v in (a_log, dt_bias, d_skip)])
    heads = jnp.pad(heads, ((0, 5), (0, PAD - hm)))
    column = lax.broadcasted_iota(jnp.int32, (PAD, PAD), 1)
    row = lax.broadcasted_iota(jnp.int32, (PAD, PAD), 0)
    pick = jnp.logical_and(row == column + space * hm, column < hm).astype(low)
    tables = rope_tables(count * inputs.shape[1])

    source = inputs[0].astype(jnp.float32)
    whole = whole.astype(jnp.float32)
    in_own, cotangent_late = lax.optimization_barrier((in_own, cotangent[0]))
    upstream_all = gather_ctx(cotangent_late)
    length = whole.shape[0]
    rows = inputs.shape[1]
    unit = whole * lax.rsqrt(jnp.mean(whole * whole, axis=-1, keepdims=True) + norm_eps)
    normed = (unit * gain_attn).astype(low)
    unit = unit.astype(low)
    proj = plain(normed, in_own)
    shared = plain(normed, shared_own)

    def space_ahead(proj, shared):
        return space_fwd(plan, proj, shared, conv, heads, pick)

    def attn_ahead(proj, shared):
        made = attn_fwd(plan, proj, tables)
        blank = jnp.zeros((length // CHUNK, NS, R), low)
        return made, jnp.zeros_like(made), blank

    made, raw_made, before = lax.cond(is_space, space_ahead, attn_ahead, proj, shared)
    square = jnp.where(is_space, jnp.sum(made * made, axis=1), 0.0)
    factor = lax.rsqrt(sum_rows(count, square, 5) / DSSM + norm_eps)
    mixed = jnp.where(is_space, made * factor[:, None] * gain_own, made).astype(low)
    wide = lambda *shape: jax.ShapeDtypeStruct(shape, jnp.float32)
    side = (up_some, down_some)
    roomy = length <= 1024
    middle, gate_up, two_all, up_own, down_own = flow_call(
        branch_kernel,
        count,
        rows,
        (mixed, mix_own, inputs[0], gain_ffn[None]),
        (wide(rows, D), wide(length if roomy else 8, 2 * FF // count)),
        True,
        True,
        (side, *share_shapes(side)),
        8,
        roomy,
    )
    two_all = two_all.reshape(length, D)
    up_own, down_own = up_own.reshape(D, -1), down_own.reshape(-1, D)

    if not roomy:
        gate_up = plain(two_all, up_own)
    half = FF // count
    swiglu = lambda g: jax.nn.silu(g[:, :half]) * g[:, half:]
    activated, act_pull = jax.vjp(swiglu, gate_up)
    activated = activated.astype(low)
    grad_act = cols_by_cols(upstream_all, down_own)
    grad_gate_up = act_pull(grad_act)[0].astype(low)
    cut = lambda g, blocks: g.astype(low).reshape(blocks, ways, -1, g.shape[1])
    if roomy:
        up_block = (count, ways, D // (count * ways), 2 * FF // count)
        down_block = (1, ways, FF // (count * ways), D)
        side = [jax.ShapeDtypeStruct(block, low) for block in (up_block, down_block)]
        side_shapes, side_scratch = collect_shapes(("rows", "rows"), side)
        side_scratch = (
            [pltpu.VMEM((rows, D), jnp.float32)]
            + [pltpu.VMEM(block, low) for block in (up_block, down_block)]
            + [pltpu.VMEM((2, length, D // count), low)] * 2
            + [pltpu.SemaphoreType.DMA((2, 2))]
            + scatter_shapes(count, rows, True)[1]
            + side_scratch
        )
        blank = jnp.zeros((1, 1, 16, 128), low)
        side = (blank, blank)
    else:
        side = (cut(rows_by_rows(two_all, grad_gate_up), count), cut(rows_by_rows(activated, upstream_all), 1))
        side_shapes, side_scratch = collect_shapes(("rows", "rows"), side)
    some = lambda a: a if roomy else a[:16]
    result = jax.ShapeDtypeStruct((rows if roomy else 16, D), low)
    grad_middle, grad_gain_ffn, outputs, grad_made, branch_all, up_mine, down_mine = flow_call(
        feed_back_kernel,
        count,
        rows,
        (
            grad_gate_up,
            up_own,
            cotangent[0],
            middle,
            gain_ffn[None],
            some(activated),
            some(down_own),
            some(mix_own),
        ),
        (
            wide(rows, D),
            wide(8, D),
            result,
            jax.ShapeDtypeStruct((length if roomy else 16, R), low),
        ),
        True,
        False,
        (side, side_shapes, side_scratch),
        9,
        roomy,
        (two_all, upstream_all),
    )
    grad_gain_ffn = grad_gain_ffn[0]
    branch_all = branch_all.reshape(length, D)
    if not roomy:
        late = lax.optimization_barrier((branch_all, plain(activated, down_own).astype(low)))[1]
        outputs = (middle + scatter_ctx(late)).astype(low)
    outputs = outputs[None]
    grad_mix = rows_by_rows(mixed, branch_all)
    if not roomy:
        grad_made = cols_by_cols(branch_all, mix_own).astype(low)
    made_wide = grad_made.astype(jnp.float32)
    dots = jnp.where(is_space, jnp.sum(made_wide * gain_own * made, axis=1), 0.0)
    dots = sum_rows(count, dots, 6)
    grad_gain_own = jnp.sum(made_wide * made * factor[:, None], axis=0)
    grad_gated = made_wide * gain_own * factor[:, None] - made * (factor**3 * dots / DSSM)[:, None]

    def space_back(proj, shared, grad_gated, grad_made):
        return space_bwd(plan, proj, shared, conv, heads, pick, grad_gated, raw_made, before)

    def attn_back(proj, shared, grad_gated, grad_made):
        blank = lambda k: jnp.zeros((8, k), jnp.float32)
        none = jnp.zeros(shared.shape, low)
        return attn_bwd(plan, proj, tables, grad_made), none, blank(W), blank(PAD), blank(R)

    grad_proj, grad_shared, conv_acc, head_acc, skip_acc = lax.cond(
        is_space, space_back, attn_back, proj, shared, grad_gated, grad_made
    )
    grad_in = rows_by_rows(unit, grad_proj)
    grad_in_shared = rows_by_rows(unit, grad_shared)
    grad_gain_attn = jnp.sum(grad_in * in_own, axis=1) + jnp.sum(grad_in_shared * shared_own, axis=1)
    grad_in = grad_in * gain_attn[:, None]
    grad_in_shared = grad_in_shared * gain_attn[:, None]
    def placed(piece, size, total, axis=0):
        shape = list(piece.shape)
        shape[axis] = total
        start = [0] * piece.ndim
        start[axis] = space * size
        return lax.dynamic_update_slice(jnp.zeros(shape, piece.dtype), piece, start)

    conv_w_grad, conv_b_grad = conv_acc[:CONV], conv_acc[CONV]
    a_grad, bias_grad = head_acc[0, :hm], head_acc[1, :hm]
    skip_grad = jnp.sum(skip_acc[0].reshape(hm, MP), axis=1)
    grad_gain_own = jnp.where(is_space, grad_gain_own, 0.0)
    vector_local = jnp.concatenate(
        [
            grad_gain_attn,
            grad_gain_ffn,
            placed(grad_gain_own, R, DSSM),
            placed(conv_b_grad[:R], R, DSSM),
            conv_b_grad[R:],
            jnp.concatenate(
                [placed(conv_w_grad[:, :R], R, DSSM, 1), conv_w_grad[:, R:]], axis=1
            ).reshape(CONV * CONVCH),
            placed(a_grad, hm, MH),
            placed(bias_grad, hm, MH),
            placed(skip_grad, hm, MH),
        ]
    )
    pad = -vectors.shape[0] % 1024
    vector_local = jnp.pad(vector_local, (0, pad)).reshape(-1, 128)
    side = (cut(grad_in, count), cut(grad_in_shared, count), cut(grad_mix, 1))
    side_shapes, side_scratch = collect_shapes(SUMS, side)
    home_sems = [pltpu.SemaphoreType.DMA((count,))] * 2
    input_grad, vector_sum, up_mine, in_mine, shared_mine, mix_mine = flow_call(
        source_back_kernel,
        count,
        rows,
        (
            grad_proj,
            grad_shared,
            in_own,
            shared_own,
            inputs[0],
            grad_middle,
            gain_attn[None],
            vector_local,
            up_mine,
        ),
        (wide(rows, D), wide(*vector_local.shape), jax.ShapeDtypeStruct(up_mine.shape, low)),
        False,
        False,
        (side, side_shapes, side_scratch + sum_scratch(count, vector_local.shape) + home_sems),
        10,
    )
    input_grad = input_grad[None]

    in_shard = from_slabs(plan, in_mine, shared_mine)
    up_shard = up_from_slabs(plan, up_mine)
    mix_shard = mix_mine[0].astype(jnp.float32)
    down_shard = down_mine[0].astype(jnp.float32)

    vector_grad = vector_sum.reshape(-1)[: vectors.shape[0]]
    new_in = adamw(w_in, w_in_m, w_in_v, in_shard, 2.0 * D ** (-0.5), decay_weight)
    new_mix = adamw(w_mix, w_mix_m, w_mix_v, mix_shard, DSSM ** (-0.5), decay_weight)
    new_up = adamw(w_up, w_up_m, w_up_v, up_shard, D ** (-0.5), decay_weight)
    new_down = adamw(w_down, w_down_m, w_down_v, down_shard, FF ** (-0.5), decay_weight)
    new_vec = adamw(vectors, vectors_m, vectors_v, vector_grad, vector_rate, 0.0)
    return (outputs, input_grad, *new_in, *new_mix, *new_up, *new_down, *new_vec)


def solution(mesh):
    tokens = P("wshard", "ctx", None)
    weight = P(("ctx", "wshard"), None)
    return jax.shard_map(
        body,
        mesh=mesh,
        in_specs=(tokens,) * 2 + (weight,) * 12 + (P(),) * 3,
        out_specs=(tokens,) * 2 + (weight,) * 12 + (P(),) * 3,
        check_vma=False,
    )
```

```python
import functools
import math

import jax
import jax.numpy as jnp
from jax import lax
from jax.experimental import pallas as pl
from jax.experimental.pallas import tpu as pltpu
from jax.sharding import PartitionSpec as P

D = 2048
FF = 4096
AH = 8
KVH = 2
HD = 128
MH = 48
MP = 64
NS = 256
CONV = 4
STEP = 10
DSSM = 3072
CONVCH = 3584
ATT = AH * HD
MIXIN = ATT + DSSM
GROUP = AH // KVH
CHUNK = 128
PAD = 128
VMEM = 60 * 1024 * 1024


norm_eps = 1e-05
rope_base = 10000.0
beta_one = 0.9
beta_two = 0.95
adam_eps = 1e-08
decay_weight = 0.1
vector_rate = 0.5
masked_score = -1e30

K_AT = ATT
V_AT = K_AT + KVH * HD
Z_AT = V_AT + KVH * HD
X_AT = Z_AT + DSSM
BC_AT = X_AT + DSSM
DT_AT = BC_AT + 2 * NS
END = DT_AT + MH


def rows_by_rows(left, right):
    return lax.dot_general(
        left, right, (((0,), (0,)), ((), ())), preferred_element_type=jnp.float32
    )


def cols_by_cols(left, right):
    return lax.dot_general(
        left, right, (((1,), (1,)), ((), ())), preferred_element_type=jnp.float32
    )


def plain(left, right):
    return jnp.dot(left, right, preferred_element_type=jnp.float32)


def rms_norm(values, gain):
    factor = lax.rsqrt(jnp.mean(values * values, axis=-1, keepdims=True) + norm_eps)
    return values * factor * gain


def split_vectors(vectors):
    extents = (D, D, DSSM, CONVCH, CONV * CONVCH, MH, MH, MH)
    pieces = []
    offset = 0
    for extent in extents:
        pieces.append(lax.slice_in_dim(vectors, offset, offset + extent))
        offset = offset + extent
    pieces[4] = pieces[4].reshape(CONV, CONVCH)
    return pieces


def adamw(weight, moment, second, grad, rate, decay):
    moment = beta_one * moment + (1.0 - beta_one) * grad
    second = beta_two * second + (1.0 - beta_two) * grad * grad
    corrected = moment / (1.0 - beta_one**STEP)
    divisor = jnp.sqrt(second / (1.0 - beta_two**STEP)) + adam_eps
    return (weight - rate * (corrected / divisor + decay * weight), moment, second)


class Plan:
    def __init__(self, count):
        self.count = count
        self.R = MIXIN // count
        self.attn = ATT // self.R
        self.ha = self.R // HD
        self.hm = self.R // MP
        self.B = self.R
        self.A = self.R + max(self.R, 2 * HD)
        self.K = 2 * NS + PAD
        self.W = self.R + 2 * NS

    def kv_of(self, c):
        return c * self.ha // GROUP


def up_from_slabs(plan, slabs):
    G = FF // plan.count
    slabs = slabs.astype(jnp.float32)
    return jnp.concatenate(
        [slabs[c][:, :G] for c in range(plan.count)] + [slabs[c][:, G:] for c in range(plan.count)],
        axis=1,
    )


def ring_groups(n, ways):
    ring = list(range(0, n, 2)) + list(range(n - 1, 0, -2))
    return [[c * ways + w for c in (ring[::-1] if w % 2 else ring)] for w in range(ways)], ring


def gather_ctx(x, n, ways, odd):
    groups, ring = ring_groups(n, ways)
    blocks = lax.all_gather(x, ("ctx", "wshard"), axis_index_groups=groups)
    at = [ring.index(c) for c in range(n)]
    parts = [
        lax.dynamic_index_in_dim(blocks, jnp.where(odd, n - 1 - i, i), 0, False) for i in at
    ]
    return jnp.concatenate(parts)


def in_ring(blocks, n, ways, odd):
    ring = ring_groups(n, ways)[1]
    parts = [
        lax.dynamic_index_in_dim(blocks, jnp.where(odd, ring[n - 1 - i], ring[i]), 0, False)
        for i in range(n)
    ]
    return jnp.concatenate(parts)


def scatter_ctx(x, n, ways):
    return lax.psum_scatter(
        x.astype(jnp.bfloat16),
        ("ctx", "wshard"),
        scatter_dimension=0,
        axis_index_groups=ring_groups(n, ways)[0],
        tiled=True,
    ).astype(jnp.float32)


def adam_in_kernel(plan, rate, slabs, shared, w, m, v, new_w, new_m, new_v):
    R, B = plan.R, plan.B
    wide = jnp.float32
    heads, spaces = range(plan.attn), range(plan.attn, plan.count)

    def update(lo, hi, parts):
        grad = functools.reduce(lambda a, b: a + b, [part.astype(wide) for part in parts])
        new = adamw(w[:, lo:hi], m[:, lo:hi], v[:, lo:hi], grad, rate, decay_weight)
        new_w[:, lo:hi], new_m[:, lo:hi], new_v[:, lo:hi] = new

    for c in heads:
        update(c * R, (c + 1) * R, [slabs[c, :, :R]])
    for start, at in ((K_AT, B), (V_AT, B + HD)):
        for g in range(KVH):
            owners = [slabs[c, :, at : at + HD] for c in heads if plan.kv_of(c) == g]
            update(start + g * HD, start + (g + 1) * HD, owners)
    for c in spaces:
        j = c - plan.attn
        update(Z_AT + j * R, Z_AT + (j + 1) * R, [slabs[c, :, :R]])
        update(X_AT + j * R, X_AT + (j + 1) * R, [slabs[c, :, B : B + R]])
    update(BC_AT, END, [shared[c, :, : END - BC_AT] for c in spaces])


def adam_in(plan, slabs, shared, w, m, v, rate):
    rows = w.shape[0]
    block = 16
    flat = pl.BlockSpec((block, END), lambda i: (i, 0))
    return pl.pallas_call(
        functools.partial(adam_in_kernel, plan, rate),
        grid=(rows // block,),
        out_shape=(jax.ShapeDtypeStruct(w.shape, w.dtype),) * 3,
        in_specs=[
            pl.BlockSpec((plan.count, block, plan.A), lambda i: (0, i, 0)),
            pl.BlockSpec((plan.count, block, plan.K), lambda i: (0, i, 0)),
            flat,
            flat,
            flat,
        ],
        out_specs=(flat,) * 3,
        compiler_params=pltpu.CompilerParams(vmem_limit_bytes=VMEM),
    )(slabs, shared, w, m, v)


MESH = pl.DeviceIdType.MESH


def here():
    c, w = lax.axis_index("ctx"), lax.axis_index("wshard")
    return c, w, w + 1 - 2 * (w % 2), (w + 2) % 4


def greet(devices):
    barrier = pltpu.get_barrier_semaphore()
    for device in devices:
        pl.semaphore_signal(barrier, inc=1, device_id=device, device_id_type=MESH)
    pl.semaphore_wait(barrier, len(devices))


def remote(src, dst, send, recv, device):
    return pltpu.make_async_remote_copy(
        src_ref=src, dst_ref=dst, send_sem=send, recv_sem=recv, device_id=device, device_id_type=MESH
    )


class Collect:
    def __init__(self, n, kinds, sources, targets, extra):
        self.n = n
        self.c, self.w, self.sib, self.across = here()
        self.x, self.core = self.w // 2, self.w % 2
        self.pending = []
        self.jobs = []
        for j, kind in enumerate(kinds):
            self.jobs.append((kind, sources[j], targets[j]) + tuple(extra[10 * j : 10 * j + 10]))
        most = max(job[3].shape[1] for job in self.jobs)
        self.steps = [s % most for s in range(1, most + 1)]

    def due(self, s):
        for job in self.jobs:
            count = job[3].shape[1]
            if s < count:
                yield job, (self.c + s) % self.n if count > 1 else 0

    def send(self, s):
        for place, slot in ((1 - self.x, 0), (self.x, 1)):
            for job, q in self.due(s):
                _, src, _, kbuf, _, _, _, k_send, k_recv = job[:9]
                out = remote(
                    src.at[q, place * 2 + 1 - self.core],
                    kbuf.at[slot, q],
                    k_send.at[slot, s],
                    k_recv.at[slot, q],
                    (self.c, self.sib),
                )
                out.start()
                self.pending.append(out)

    def cross(self, s):
        wide = jnp.float32
        for job, q in self.due(s):
            _, src, _, kbuf, stage, xbuf, _, k_send, k_recv, x_send, x_recv = job[:11]
            got = kbuf.at[0, q]
            remote(got, got, k_send.at[0, s], k_recv.at[0, q], (self.c, self.sib)).wait_recv()
            mine = src[q, (1 - self.x) * 2 + self.core].astype(wide)
            stage[q] = (mine + kbuf[0, q].astype(wide)).astype(stage.dtype)
            out = remote(
                stage.at[q], xbuf.at[q], x_send.at[s], x_recv.at[q], (self.c, self.across)
            )
            out.start()
            self.pending.append(out)

    def close(self, s):
        wide = jnp.float32
        for job, q in self.due(s):
            kind, src, dst, kbuf, stage, xbuf, done, k_send, k_recv, x_send, x_recv = job[:11]
            got = kbuf.at[1, q]
            remote(got, got, k_send.at[1, s], k_recv.at[1, q], (self.c, self.sib)).wait_recv()
            got = xbuf.at[q]
            remote(got, got, x_send.at[s], x_recv.at[q], (self.c, self.across)).wait_recv()
            total = src[q, self.x * 2 + self.core].astype(wide) + kbuf[1, q].astype(wide)
            total = (total + xbuf[q].astype(wide)).astype(stage.dtype)
            if kind == "cols" and s > 0:
                done[q] = total
                out = remote(done.at[q], dst.at[self.c], job[11].at[s], job[12].at[self.c], (q, self.w))
                out.start()
                self.pending.append(out)
            else:
                dst[q] = total

    def end(self):
        for job in self.jobs:
            if job[0] == "cols":
                dst, a_send, a_recv = job[2], job[11], job[12]
                for s in range(1, self.n):
                    q = (self.c + self.n - s) % self.n
                    got = dst.at[q]
                    remote(got, got, a_send.at[s], a_recv.at[q], (q, self.w)).wait_recv()
        for out in self.pending:
            out.wait_send()


def home_job(n, source, target, send, recv):
    c, w = lax.axis_index("ctx"), lax.axis_index("wshard")
    target[c] = source[c]
    copies = [
        remote(source.at[(c + s) % n], target.at[c], send.at[s], recv.at[c], ((c + s) % n, w))
        for s in range(1, n)
    ]
    for copy in copies:
        copy.start()
    yield
    for s in range(1, n):
        q = (c + n - s) % n
        remote(source.at[q], target.at[q], send.at[s], recv.at[q], (q, w)).wait_recv()
    for copy in copies:
        copy.wait_send()


def collect_shapes(kinds, sources):
    shapes, scratch = [], []
    for kind, src in zip(kinds, sources):
        count, _, rows, size = src.shape
        block = (count, rows, size)
        shapes.append(jax.ShapeDtypeStruct(block, src.dtype))
        scratch += [
            pltpu.VMEM((2,) + block, src.dtype),
            pltpu.VMEM(block, src.dtype),
            pltpu.VMEM(block, src.dtype),
            pltpu.VMEM(block if kind == "cols" else (1, 16, 128), src.dtype),
            pltpu.SemaphoreType.DMA((2, count)),
            pltpu.SemaphoreType.DMA((2, count)),
            pltpu.SemaphoreType.DMA((count,)),
            pltpu.SemaphoreType.DMA((count,)),
            pltpu.SemaphoreType.DMA((count,)),
            pltpu.SemaphoreType.DMA((count,)),
        ]
    return shapes, scratch


def row_sum_kernel(n, x_ref, out_ref, got, send, recv):
    c, w = lax.axis_index("ctx"), lax.axis_index("wshard")
    greet([((c + s) % n, w) for s in range(1, n)])
    copies = [
        remote(x_ref, got.at[c], send.at[s], recv.at[c], ((c + s) % n, w)) for s in range(1, n)
    ]
    for copy in copies:
        copy.start()
    total = x_ref[...]
    for s in range(1, n):
        q = (c + n - s) % n
        remote(x_ref, got.at[q], send.at[s], recv.at[q], (q, w)).wait_recv()
        total = total + got[q]
    out_ref[...] = total
    for copy in copies:
        copy.wait_send()


def sum_rows(n, x, collective_id):
    block = x.reshape(-1, 128)
    return pl.pallas_call(
        functools.partial(row_sum_kernel, n),
        out_shape=jax.ShapeDtypeStruct(block.shape, x.dtype),
        in_specs=[pl.BlockSpec(memory_space=pltpu.VMEM)],
        out_specs=pl.BlockSpec(memory_space=pltpu.VMEM),
        scratch_shapes=[
            pltpu.VMEM((n,) + block.shape, x.dtype),
            pltpu.SemaphoreType.DMA((n,)),
            pltpu.SemaphoreType.DMA((n,)),
        ],
        compiler_params=pltpu.CompilerParams(
            collective_id=collective_id, has_side_effects=True, vmem_limit_bytes=VMEM
        ),
    )(block).reshape(x.shape)


def sum_job(n, x_ref, out_ref, kept, got, send, recv):
    c, w, sib, across = here()
    partners = [(c, sib), (c, across)]
    for level in list(range(1, n.bit_length() - 1)) + [0]:
        reach = 2**level
        partners.append((c + reach - 2 * reach * ((c // reach) % 2), w))
    out_ref[...] = x_ref[...]
    for i, partner in enumerate(partners):
        kept[i] = out_ref[...]
        swap = remote(kept.at[i], got.at[i], send.at[i], recv.at[i], partner)
        swap.start()
        yield
        swap.wait()
        out_ref[...] += got[i]


def sum_scratch(n, shape):
    stages = n.bit_length() + 1
    return [
        pltpu.VMEM((stages,) + shape, jnp.float32),
        pltpu.VMEM((stages,) + shape, jnp.float32),
        pltpu.SemaphoreType.DMA((stages,)),
        pltpu.SemaphoreType.DMA((stages,)),
    ]


def share_job(sources, targets, sems):
    c, w, sib, across = here()
    pending = []
    for j, (src, dst) in enumerate(zip(sources, targets)):
        x_send, x_recv, k_send, k_recv, own_sem = sems[5 * j : 5 * j + 5]
        for q in range(src.shape[0]):
            own = pltpu.make_async_copy(src.at[q], dst.at[q, w], own_sem.at[q])
            to_x = remote(src.at[q], dst.at[q, w], x_send.at[q], x_recv.at[q], (c, across))
            to_k = remote(src.at[q], dst.at[q, w], k_send.at[0, q], k_recv.at[0, q], (c, sib))
            for copy in (to_x, to_k, own):
                copy.start()
            pending += [to_x.wait_send, to_k.wait_send, own.wait]
    yield
    for j, dst in enumerate(targets):
        x_send, x_recv, k_send, k_recv, own_sem = sems[5 * j : 5 * j + 5]
        for q in range(dst.shape[0]):
            got = dst.at[q, across]
            remote(got, got, x_send.at[q], x_recv.at[q], (c, across)).wait_recv()
            out = remote(got, got, k_send.at[1, q], k_recv.at[1, q], (c, sib))
            out.start()
            pending.append(out.wait_send)
    yield
    for j, dst in enumerate(targets):
        x_send, x_recv, k_send, k_recv, own_sem = sems[5 * j : 5 * j + 5]
        for q in range(dst.shape[0]):
            for half, place in ((0, sib), (1, (sib + 2) % 4)):
                got = dst.at[q, place]
                remote(got, got, k_send.at[half, q], k_recv.at[half, q], (c, sib)).wait_recv()
    for wait in pending:
        wait()


def share_shapes(sources):
    shapes, sems = [], []
    for src in sources:
        count = src.shape[0]
        shapes.append(jax.ShapeDtypeStruct((count, 4) + src.shape[1:], src.dtype))
        sems += [
            pltpu.SemaphoreType.DMA((count,)),
            pltpu.SemaphoreType.DMA((count,)),
            pltpu.SemaphoreType.DMA((2, count)),
            pltpu.SemaphoreType.DMA((2, count)),
            pltpu.SemaphoreType.DMA((count,)),
        ]
    return shapes, sems


def advance(*jobs):
    jobs = list(jobs)
    while jobs:
        for job in list(jobs):
            try:
                next(job)
            except StopIteration:
                jobs.remove(job)


class Line:
    def __init__(self, n):
        self.c, self.w, self.sib, self.across = here()
        self.n, self.N = n, n // 2
        self.at, self.side = self.c // 2, self.c % 2
        self.pair = (self.c + 1 - 2 * self.side, self.w)
        self.left = (self.c - 2, self.w)
        self.right = (self.c + 2, self.w)
        self.has_left = self.at > 0
        self.has_right = self.at < self.N - 1

    def greet(self, others=()):
        barrier = pltpu.get_barrier_semaphore()
        signal = lambda d: pl.semaphore_signal(barrier, inc=1, device_id=d, device_id_type=MESH)
        sure = [self.pair] + list(others)
        for device in sure:
            signal(device)
        pl.when(self.has_left)(lambda: signal(self.left))
        pl.when(self.has_right)(lambda: signal(self.right))
        beside = (self.at + self.N - 1) // self.N + (2 * self.N - 2 - self.at) // self.N
        pl.semaphore_wait(barrier, len(sure) + beside)


def scatter_job(line, theirs, mine_of, total, ybuf, zbuf, sems):
    y_send, y_recv, r_send, r_recv, l_send, l_recv = sems
    N, at, side = line.N, line.at, line.side
    wide = jnp.float32

    def both_ways(d):
        return ((at + d, at + d < N), (at - d, at - d >= 0)) if d else ((at, None),)

    def guarded(keep, step):
        if keep is None:
            step()
        else:
            pl.when(keep)(step)

    def y_copy(b, src=None):
        src = ybuf.at[b] if src is None else src
        return remote(src, ybuf.at[b], y_send.at[b], y_recv.at[b], line.pair)

    def r_copy(b, slot):
        return remote(ybuf.at[b], zbuf.at[slot], r_send.at[b], r_recv.at[b], line.right)

    def l_copy(b, slot):
        return remote(ybuf.at[b], zbuf.at[slot], l_send.at[b], l_recv.at[b], line.left)

    for d in range(N - 1, -1, -1):
        for b, keep in both_ways(d):

            def first(b=b):
                y_copy(b, theirs(b)).start()

            guarded(keep, first)
        yield
    for d in range(N - 1, 0, -1):
        for b, keep, ahead in ((at + d, at + d < N, True), (at - d, at - d >= 0, False)):

            def relay(b=b, ahead=ahead):
                mine = mine_of(b)
                y_copy(b).wait_recv()
                mine = mine + ybuf[b].astype(wide)
                came = line.has_left if ahead else line.has_right

                @pl.when(came)
                def _():
                    (r_copy if ahead else l_copy)(b, b).wait_recv()
                    ybuf[b] = (mine + zbuf[b].astype(wide)).astype(ybuf.dtype)

                @pl.when(jnp.logical_not(came))
                def _():
                    ybuf[b] = mine.astype(ybuf.dtype)

                if ahead:
                    pl.when(b == at + 1)(lambda: r_copy(b, b).start())
                    pl.when(b > at + 1)(lambda: r_copy(b, b).start())
                else:
                    pl.when(b == at - 1)(lambda: l_copy(b, N).start())
                    pl.when(b < at - 1)(lambda: l_copy(b, b).start())

            guarded(keep, relay)
        yield
    mine = mine_of(at)
    y_copy(at).wait_recv()
    total[...] = mine + ybuf[at].astype(wide)

    @pl.when(line.has_left)
    def _():
        r_copy(at, at).wait_recv()
        total[...] += zbuf[at].astype(wide)

    @pl.when(line.has_right)
    def _():
        l_copy(at, N).wait_recv()
        total[...] += zbuf[N].astype(wide)

    for d in range(N):
        for b, keep in both_ways(d):
            guarded(keep, lambda b=b: y_copy(b).wait_send())
    for d in range(1, N):
        pl.when(at + d < N)(lambda d=d: r_copy(at + d, at + d).wait_send())
        pl.when(at - d >= 0)(lambda d=d: l_copy(at - d, at - d).wait_send())


def scatter_line_job(line, value, stage, slots, pair_slot, total, sems):
    r_send, r_recv, l_send, l_recv, p_send, p_recv = sems
    n, N, at, side = line.n, line.N, line.at, line.side
    wide = jnp.float32

    def copy(q, slot, ahead):
        send, recv = (r_send, r_recv) if ahead else (l_send, l_recv)
        device = line.right if ahead else line.left
        return remote(stage.at[q], slots.at[slot], send.at[q], recv.at[q], device)

    for d in range(N - 1, 0, -1):
        for b, keep, ahead in ((at + d, at + d < N, True), (at - d, at - d >= 0, False)):

            def relay(b=b, ahead=ahead):
                came = line.has_left if ahead else line.has_right
                for y in range(2):
                    q = 2 * b + y

                    @pl.when(came)
                    def _(q=q, y=y):
                        copy(q, q, ahead).wait_recv()
                        stage[q] = (value(b, y) + slots[q].astype(wide)).astype(stage.dtype)

                    @pl.when(jnp.logical_not(came))
                    def _(q=q, y=y):
                        stage[q] = value(b, y).astype(stage.dtype)

                    if ahead:
                        copy(q, q, True).start()
                    else:
                        pl.when(b == at - 1)(lambda q=q, y=y: copy(q, n + y, False).start())
                        pl.when(b < at - 1)(lambda q=q: copy(q, q, False).start())

            pl.when(keep)(relay)
        yield

    def reach(y):
        q, y_slot = 2 * at + y, n + y
        pl.when(line.has_left)(lambda: copy(q, q, True).wait_recv())
        pl.when(line.has_right)(lambda: copy(q, y_slot, False).wait_recv())
        left = jnp.where(line.has_left, slots[q].astype(wide), 0.0)
        right = jnp.where(line.has_right, slots[y_slot].astype(wide), 0.0)
        return value(at, y) + left + right

    other = 2 * at + 1 - side
    stage[other] = reach(1 - side).astype(stage.dtype)
    swap = remote(stage.at[other], pair_slot, p_send, p_recv, line.pair)
    swap.start()
    mine = reach(side)
    yield
    swap.wait()
    total[...] = mine + pair_slot[...].astype(wide)
    for d in range(1, N):
        for y in range(2):
            pl.when(at + d < N)(lambda d=d, y=y: copy(2 * (at + d) + y, 0, True).wait_send())
            pl.when(at - d >= 0)(lambda d=d, y=y: copy(2 * (at - d) + y, 0, False).wait_send())


def gather_job(line, own, out, sems, use=None):
    r_send, l_send, y_send, recv, own_sem = sems
    n, N, at, side, c = line.n, line.N, line.at, line.side, line.c
    local = pltpu.make_async_copy(own, out(c), own_sem)
    local.start()

    def send(src, q, sem, device):
        return remote(src, out(q), sem.at[q // 2], recv.at[q], device)

    use = use or (lambda q: None)
    pair = c + 1 - 2 * side

    def other(d):
        for q, keep in ((pair - 2 * d, at - d >= 0), (pair + 2 * d, at + d < N))[: 1 + (d > 0)]:

            def take(q=q):
                send(out(q), q, y_send, line.pair).wait_recv()
                use(q)

            pl.when(keep)(take)

    pl.when(line.has_right)(lambda: send(own, c, r_send, line.right).start())
    pl.when(line.has_left)(lambda: send(own, c, l_send, line.left).start())
    send(own, c, y_send, line.pair).start()
    yield
    local.wait()
    use(c)
    for d in range(1, N):
        for q, keep, ahead in ((c - 2 * d, at - d >= 0, True), (c + 2 * d, at + d < N, False)):

            def relay(q=q, ahead=ahead):
                got = out(q)
                send(got, q, y_send, line.pair).wait_recv()
                if ahead:
                    pl.when(line.has_right)(lambda: send(got, q, r_send, line.right).start())
                else:
                    pl.when(line.has_left)(lambda: send(got, q, l_send, line.left).start())
                send(got, q, y_send, line.pair).start()
                use(q)

            pl.when(keep)(relay)
        yield
    for d in range(N):
        other(d)
    for b in range(N):
        q = 2 * b + side
        got = out(q)
        send(got, q, y_send, line.pair).wait_send()
        pl.when(jnp.logical_and(b <= at, line.has_right))(
            lambda q=q, got=got: send(got, q, r_send, line.right).wait_send()
        )
        pl.when(jnp.logical_and(b >= at, line.has_left))(
            lambda q=q, got=got: send(got, q, l_send, line.left).wait_send()
        )


def gather_pair_job(line, own, out, sems):
    r_send, l_send, y_send, recv, own_sem = sems
    n, N, at, c = line.n, line.N, line.at, line.c
    local = pltpu.make_async_copy(own, out(c), own_sem)
    local.start()

    def send(src, q, sem, device):
        return remote(src, out(q), sem.at[q], recv.at[q], device)

    def ahead(src, q, act):
        pl.when(line.has_right)(lambda: act(send(src, q, r_send, line.right)))

    def back(src, q, act):
        pl.when(line.has_left)(lambda: act(send(src, q, l_send, line.left)))

    start = lambda copy: copy.start()
    to_pair = remote(own, out(c), y_send.at[0], recv.at[c], line.pair)
    to_pair.start()
    ahead(own, c, start)
    back(own, c, start)
    yield
    local.wait()
    q = line.pair[0]
    got = out(q)
    send(got, q, r_send, line.pair).wait_recv()
    ahead(got, q, start)
    back(got, q, start)
    yield
    for d in range(1, N):
        for b, keep, forward in ((at - d, at - d >= 0, True), (at + d, at + d < N, False)):

            def relay(b=b, forward=forward):
                for y in range(2):
                    got = out(2 * b + y)
                    send(got, 2 * b + y, r_send, line.pair).wait_recv()
                    (ahead if forward else back)(got, 2 * b + y, start)

            pl.when(keep)(relay)
        yield
    to_pair.wait_send()
    done = lambda copy: copy.wait_send()
    for b in range(N):
        for y in range(2):
            q = 2 * b + y
            pl.when(b <= at)(lambda q=q: ahead(out(q), q, done))
            pl.when(b >= at)(lambda q=q: back(out(q), q, done))


def minor_rows(rows):
    return rows // 8


def scatter_steps(line, product, rows, total, made, scratch):
    N, side = line.N, line.side
    if len(made.shape) == 3:

        def theirs(b):
            made[b] = product(2 * b * rows + (1 - side) * rows, rows).astype(made.dtype)
            return made.at[b]

        yield from scatter_job(
            line,
            theirs,
            lambda b: product(2 * b * rows + side * rows, rows),
            total,
            *scratch[:2],
            scratch[2:8],
        )
        return
    few = minor_rows(rows)
    many = rows - few
    ybuf, zbuf = scratch[:2]
    stage, slots, pair_slot = scratch[8:11]
    wide = jnp.float32

    def theirs(b):
        both = product(2 * b * rows, 2 * rows).astype(made.dtype)
        made[b] = both.reshape(2, rows, D)
        return made.at[b, 1 - side, pl.ds(0, many)]

    minor = scatter_line_job(
        line,
        lambda b, y: made[b, y, many:, :].astype(wide),
        stage,
        slots,
        pair_slot,
        total.at[pl.ds(many, few)],
        scratch[11:17],
    )
    main = scatter_job(
        line,
        theirs,
        lambda b: made[b, side, :many, :].astype(wide),
        total.at[pl.ds(0, many)],
        ybuf,
        zbuf,
        scratch[2:8],
    )
    for _ in range(N):
        next(main)
        yield
    next(minor)
    for _ in range(N - 1):
        next(minor, None)
        next(main)
        yield
    finish(minor)
    finish(main)


def gather_steps(line, own, out, rows, scratch, use=None):
    few = minor_rows(rows)
    many = rows - few
    minor = gather_pair_job(
        line, own.at[pl.ds(many, few)], lambda q: out(q, many, few), scratch[5:10]
    )
    main = gather_job(line, own.at[pl.ds(0, many)], lambda q: out(q, 0, many), scratch[:5], use)
    next(minor)
    next(main)
    yield
    next(minor)
    for _ in range(line.N - 1):
        next(minor)
        next(main)
        yield
    finish(minor)
    finish(main)


GATHER = 10


def scatter_shapes(n, rows, roomy):
    N = n // 2
    few = minor_rows(rows) if roomy else 0
    many = rows - few
    low, dma = jnp.bfloat16, pltpu.SemaphoreType.DMA
    made = pltpu.VMEM((N, 2, rows, D) if roomy else (N, rows, D), low)
    scratch = [
        pltpu.VMEM((N, many, D), low),
        pltpu.VMEM((N + 1, many, D), low),
    ] + [dma((N,))] * 6
    if roomy:
        scratch += [
            pltpu.VMEM((n, few, D), low),
            pltpu.VMEM((n + 2, few, D), low),
            pltpu.VMEM((few, D), low),
        ]
        scratch += [dma((n,))] * 4 + [dma, dma]
    return made, scratch


def gather_scratch(n):
    N = n // 2
    dma = pltpu.SemaphoreType.DMA
    return [dma((N,)), dma((N,)), dma((N,)), dma((n,)), dma] + [
        dma((n,)),
        dma((n,)),
        dma((1,)),
        dma((n,)),
        dma,
    ]


def rms_factor(values):
    return lax.rsqrt(jnp.mean(values * values, axis=1, keepdims=True) + norm_eps)


def rms_back(values, gain, grad):
    factor = rms_factor(values)
    scaled = grad * gain
    inner = jnp.mean(scaled * values, axis=1, keepdims=True)
    d_gain = jnp.sum(grad * (values * factor), axis=0, keepdims=True)
    return factor * scaled - values * (factor * factor * factor * inner), d_gain


def matmul_rows(*pairs):
    def product(first, count):
        total = 0.0
        for left, right in pairs:
            part = left[pl.ds(pl.multiple_of(first, 16), count), :]
            if right.shape[0] == left.shape[1]:
                total = total + plain(part, right[...])
            else:
                total = total + cols_by_cols(part, right[...])
        return total

    return product


def finish(job):
    for _ in job:
        pass


def start_kernel(plan, n, x, w_in, w_up, w_mix, w_down, *refs):
    tokens, in_all, shared_all, up_some, mix_all, down_some = refs[:6]
    in_low, shared_low, up_low, mix_low, down_low = refs[6:11]
    t_sems = refs[11 : 11 + GATHER]
    a_send, a_recv, x_send, x_recv, k_send, k_recv, own_sem = refs[11 + GATHER :]
    line = Line(n)
    c, w, sib, across = line.c, line.w, line.sib, line.across
    greet([((c + s) % n, w) for s in range(1, n)] + [(c, sib), (c, across)])
    R, B, G = plan.R, plan.B, FF // n
    low = jnp.bfloat16
    place = lambda q, first, count: tokens.at[q, pl.ds(first, count)]
    inputs = gather_steps(line, x, place, x.shape[0], t_sems)
    next(inputs)
    passed, pending = [], []

    def pass_on(number, view, src=None):
        src = view(w) if src is None else src
        to_x = remote(src, view(w), x_send.at[number], x_recv.at[number], (c, across))
        to_k = remote(src, view(w), k_send.at[0, number], k_recv.at[0, number], (c, sib))
        to_x.start()
        to_k.start()
        pending.append(to_x)
        pending.append(to_k)
        passed.append((number, view))

    mix_low[...] = w_mix[...].astype(low)
    pass_on(2 * n, lambda place: mix_all.at[0, place], mix_low)
    shared_low[...] = jnp.zeros_like(shared_low)
    shared_low[:, : END - BC_AT] = w_in[:, BC_AT:END].astype(low)
    for p in range(n):
        if p < plan.attn:
            g = plan.kv_of(p)
            in_low[p, :, :R] = w_in[:, p * R : (p + 1) * R].astype(low)
            in_low[p, :, B : B + HD] = w_in[:, K_AT + g * HD : K_AT + (g + 1) * HD].astype(low)
            in_low[p, :, B + HD : B + 2 * HD] = w_in[
                :, V_AT + g * HD : V_AT + (g + 1) * HD
            ].astype(low)
            if B + 2 * HD < plan.A:
                rest = plan.A - B - 2 * HD
                in_low[p, :, B + 2 * HD :] = jnp.zeros((in_low.shape[1], rest), low)
        else:
            j = p - plan.attn
            in_low[p, :, :R] = w_in[:, Z_AT + j * R : Z_AT + (j + 1) * R].astype(low)
            in_low[p, :, B : B + R] = w_in[:, X_AT + j * R : X_AT + (j + 1) * R].astype(low)
            if B + R < plan.A:
                in_low[p, :, B + R :] = jnp.zeros((in_low.shape[1], plan.A - B - R), low)

    def column_copies(s):
        p = (c + s) % n
        ends = ((in_low.at[p], in_all), (shared_low, shared_all))
        return [
            remote(src, dst.at[c, w], a_send.at[k, s], a_recv.at[k, c], (p, w))
            for k, (src, dst) in enumerate(ends)
        ]

    def send_columns(steps):
        for s in steps:
            for copy in column_copies(s):
                copy.start()
                pending.append(copy)

    in_view = lambda q: lambda place: in_all.at[q, place]
    shared_view = lambda q: lambda place: shared_all.at[q, place]

    def take_columns(steps):
        for s in steps:
            q = (c + n - s) % n
            for k, view in ((0, in_view), (1, shared_view)):
                got = view(q)(w)
                remote(got, got, a_send.at[k, s], a_recv.at[k, q], (q, w)).wait_recv()
                pass_on(k * n + q, view(q))

    done = [0]

    def seconds(upto):
        while done[0] < min(upto, len(passed)):
            number, view = passed[done[0]]
            got = view(across)
            remote(got, got, x_send.at[number], x_recv.at[number], (c, across)).wait_recv()
            out = remote(got, got, k_send.at[1, number], k_recv.at[1, number], (c, sib))
            out.start()
            pending.append(out)
            done[0] += 1

    cuts = [round(1 + (n - 1) * i / 3) for i in range(4)]
    parts = [range(cuts[i], cuts[i + 1]) for i in range(3)]
    send_columns(parts[0])
    pass_on(c, in_view(c), in_low.at[c])
    pass_on(n + c, shared_view(c), shared_low)
    down_low[...] = w_down[...].astype(low)
    for p in range(n):
        up_low[p, :, :G] = w_up[:, p * G : (p + 1) * G].astype(low)
        up_low[p, :, G:] = w_up[:, FF + p * G : FF + (p + 1) * G].astype(low)
    locals_started = []
    own = (
        (in_low.at[c], in_all.at[c, w]),
        (shared_low, shared_all.at[c, w]),
        (mix_low, mix_all.at[0, w]),
        (up_low.at[c], up_some.at[c]),
        (down_low, down_some.at[0]),
    )
    for i, (src, dst) in enumerate(own):
        copy = pltpu.make_async_copy(src, dst, own_sem.at[i])
        copy.start()
        locals_started.append(copy)
    for step in range(3):
        for _ in range(line.N // 4):
            next(inputs, None)
        if step < 2:
            send_columns(parts[step + 1])
        else:
            for s in range(1, n):
                p = (c + s) % n
                out = remote(
                    up_low.at[p], up_some.at[c], a_send.at[2, s], a_recv.at[2, c], (p, w)
                )
                out.start()
                pending.append(out)
        take_columns(parts[step])
        seconds(len(passed) - 4)
    finish(inputs)
    seconds(len(passed))
    for s in range(1, n):
        q = (c + n - s) % n
        got = up_some.at[q]
        remote(got, got, a_send.at[2, s], a_recv.at[2, q], (q, w)).wait_recv()
    for number, view in passed:
        for half, place in ((0, sib), (1, (sib + 2) % 4)):
            got = view(place)
            remote(got, got, k_send.at[half, number], k_recv.at[half, number], (c, sib)).wait_recv()
    for copy in locals_started:
        copy.wait()
    for out in pending:
        out.wait_send()


def branch_kernel(n, refs_in, refs_out, scratch):
    left, right, source, gain, up, down = refs_in
    middle, gates, normed, up_all, down_all = refs_out
    line = Line(n)
    line.greet([(line.c, line.sib), (line.c, line.across)])
    rows = source.shape[0]
    (total, own, made), (flow, gather, extra) = scratch[:3], scratch[3:]
    share = share_job((up, down), (up_all, down_all), extra)
    main = scatter_steps(line, matmul_rows((left, right)), rows, total, made, flow)
    next(main)
    next(share)
    finish(main)
    value = source[...].astype(jnp.float32) + total[...]
    middle[...] = value
    own[...] = (value * rms_factor(value) * gain[...]).astype(own.dtype)
    place = lambda q, first, count: normed.at[q, pl.ds(first, count)]

    def use(q):
        gates[pl.ds(pl.multiple_of(q * rows, rows), rows), :] = plain(
            normed[q], up_all[...].reshape(D, -1)
        )

    fused = gates.shape[0] == n * rows
    spread_out = gather_steps(
        line, own, place, rows, gather, use if fused else None
    )
    next(spread_out)
    next(share)
    finish(share)
    finish(spread_out)


def feed_back_kernel(n, refs_in, refs_out, scratch):
    left, right, cotangent, middle, gain, active, w_mix, normed, upstream, up, down = refs_in
    grad, d_gain, made, low_all, up_sum, down_sum = refs_out
    line = Line(n)
    line.greet([(line.c, line.sib), (line.c, line.across)])
    rows = cotangent.shape[0]
    (total, own, terms), (flow, gather, extra) = scratch[:3], scratch[3:]
    both = active.shape[0] == n * rows
    if both:
        (up, down, normed_part, upstream_part, part_sem), extra = extra[:5], extra[5:]
        width = D // n
        height = down.shape[2]

        def fetch(s):
            columns = pl.ds(pl.multiple_of((line.c + s) % n * width, 128), width)
            return [
                pltpu.make_async_copy(a.at[:, columns], b.at[s % 2], part_sem.at[i, s % 2])
                for i, (a, b) in enumerate(((normed, normed_part), (upstream, upstream_part)))
            ]

        def piece(s):
            q = (line.c + s) % n
            for copy in fetch(s):
                copy.wait()
            if s:
                for copy in fetch((s + 1) % n):
                    copy.start()
            part = rows_by_rows(normed_part[s % 2], left[...])
            up[q] = part.astype(up.dtype).reshape(up.shape[1:])
            part = rows_by_rows(active[...], upstream_part[s % 2]).astype(down.dtype)
            columns = pl.ds(pl.multiple_of(q * width, 128), width)
            for k in range(4):
                down[0, k, :, columns] = part[k * height : (k + 1) * height]

        for copy in fetch(1):
            copy.start()
    else:
        piece = lambda s: None
    sums = Collect(n, ("rows", "rows"), (up, down), (up_sum, down_sum), extra)
    main = scatter_steps(line, matmul_rows((left, right)), rows, total, terms, flow)
    for _ in range(line.N):
        next(main)
    steps = sums.steps
    per = -(-len(steps) // max(line.N - 1, 1))
    for i in range(line.N - 1):
        for at in range(i * per, min((i + 1) * per, len(steps))):
            piece(steps[at])
            sums.send(steps[at])
            if at:
                sums.cross(steps[at - 1])
        next(main)
    sums.cross(steps[-1])
    finish(main)
    back, gain_row = rms_back(middle[...], gain[...], total[...])
    value = cotangent[...].astype(jnp.float32) + back
    grad[...] = value
    d_gain[...] = jnp.broadcast_to(gain_row, d_gain.shape)
    own[...] = value.astype(own.dtype)
    place = lambda q, first, count: low_all.at[q, pl.ds(first, count)]

    def use(q):
        made[pl.ds(pl.multiple_of(q * rows, rows), rows), :] = cols_by_cols(
            low_all[q], w_mix[...]
        ).astype(made.dtype)

    spread_out = gather_steps(
        line, own, place, rows, gather, use if both else None
    )
    next(spread_out)
    finish(spread_out)
    for s in sums.steps:
        sums.close(s)
    sums.end()


SUMS = ("cols", "cols", "rows")


def source_back_kernel(n, refs_in, refs_out, scratch):
    (left, left_two, right, right_two, source, grad_middle, gain, vector, up) = refs_in[:9]
    mixed, gain_column, unit, branch, w_in, w_shared, w_mix = refs_in[9:]
    grad, vector_sum, up_home, in_sum, shared_sum, mix_sum = refs_out
    line = Line(n)
    others = [((line.c + s) % n, line.w) for s in range(1, n)]
    greet(others + [(line.c, line.sib), (line.c, line.across)])
    rows = source.shape[0]
    (total, _, made), (flow, _, extra) = scratch[:3], scratch[3:]
    both = unit.shape[0] == n * rows
    if both:
        (w_in, w_shared, w_mix, unit_part, branch_part, part_sem, local), extra = extra[:7], extra[7:]
        width = D // n
        height = w_mix.shape[2]
        local[...] = vector[...]

        def fetch(s):
            columns = pl.ds(pl.multiple_of((line.c + s) % n * width, 128), width)
            return [
                pltpu.make_async_copy(a.at[:, columns], b.at[s % 2], part_sem.at[i, s % 2])
                for i, (a, b) in enumerate(((unit, unit_part), (branch, branch_part)))
            ]

        def piece(s):
            q = (line.c + s) % n
            for copy in fetch(s):
                copy.wait()
            if s:
                for copy in fetch((s + 1) % n):
                    copy.start()
            place = pl.ds(pl.multiple_of(q * width, 128), width)
            scale = gain_column[place, :]
            part = rows_by_rows(unit_part[s % 2], left[...])
            w_in[q] = (part * scale).astype(w_in.dtype).reshape(w_in.shape[1:])
            two = rows_by_rows(unit_part[s % 2], left_two[...])
            w_shared[q] = (two * scale).astype(w_shared.dtype).reshape(w_shared.shape[1:])
            each = jnp.concatenate(
                [
                    part * right[place, :].astype(jnp.float32),
                    two * right_two[place, :].astype(jnp.float32),
                ],
                axis=1,
            )
            ones = jnp.ones((8, each.shape[1]), jnp.bfloat16)
            row = sum(cols_by_cols(ones, some) for some in pieces(each, 3))
            for i in range(width // 128):
                at = q * (width // 128) + i
                local[pl.ds(at, 1), :] = row[0:1, i * 128 : (i + 1) * 128]
            part = rows_by_rows(mixed[...], branch_part[s % 2]).astype(w_mix.dtype)
            for k in range(4):
                w_mix[0, k, :, place] = part[k * height : (k + 1) * height]

        for copy in fetch(1):
            copy.start()
    else:
        local = vector
        piece = lambda s: None
    sums = Collect(n, SUMS, (w_in, w_shared, w_mix), (in_sum, shared_sum, mix_sum), extra[:-6])
    vectors = sum_job(n, local, vector_sum, *extra[-6:-2])
    home = home_job(n, up, up_home, *extra[-2:])
    product = matmul_rows((left, right), (left_two, right_two))
    main = scatter_steps(line, product, rows, total, made, flow)
    steps = sums.steps
    next(home)
    per = -(-len(steps) // line.N)
    for i in range(line.N):
        next(main)
        for at in range(i * per, min((i + 1) * per, len(steps))):
            piece(steps[at])
            sums.send(steps[at])
            if at:
                sums.cross(steps[at - 1])
    next(vectors)
    sums.cross(steps[-1])
    closed = 0
    for _ in main:
        next(vectors, None)
        for s in steps[closed : closed + 2]:
            sums.close(s)
        closed += 2
    for s in steps[closed:]:
        sums.close(s)
        next(vectors, None)
    finish(vectors)
    back, _ = rms_back(source[...].astype(jnp.float32), gain[...], total[...])
    grad[...] = grad_middle[...] + back
    finish(home)
    sums.end()


def flow_call(
    kernel, n, rows, args, outs, gathers, away, extra, collective_id, near=False, far_args=()
):
    inside = pl.BlockSpec(memory_space=pltpu.VMEM)
    outside = pl.BlockSpec(memory_space=pl.ANY)
    side_args, side_shapes, side_scratch = extra
    shapes = list(outs)
    specs = [inside] * len(outs)
    scratch = [
        pltpu.VMEM((rows, D), jnp.float32),
        pltpu.VMEM((rows, D) if gathers else (16, 128), jnp.bfloat16),
    ]
    made, flow = scatter_shapes(n, rows, args[0].shape[0] <= 1024)
    gather = []
    if gathers:
        shapes.append(jax.ShapeDtypeStruct((n, rows, D), jnp.bfloat16))
        specs.append(inside if near else outside)
        gather = gather_scratch(n)
    scratch = scratch + [made] + flow + gather + list(side_scratch)
    ends = 3 + len(flow), 3 + len(flow) + len(gather)
    side = outside if away else inside
    in_specs = [inside] * len(args) + [outside] * len(far_args) + [side] * len(side_args)
    specs = specs + [inside if near else side] * len(side_shapes)
    shapes = shapes + list(side_shapes)
    first, second = len(in_specs), len(in_specs) + len(specs)

    def run(*refs):
        parts = refs[second:]
        groups = parts[3 : ends[0]], parts[ends[0] : ends[1]], parts[ends[1] :]
        kernel(n, refs[:first], refs[first:second], tuple(parts[:3]) + groups)

    return pl.pallas_call(
        run,
        out_shape=tuple(shapes),
        in_specs=in_specs,
        out_specs=tuple(specs),
        scratch_shapes=scratch,
        cost_estimate=pl.CostEstimate(flops=0, bytes_accessed=2 * 10**8, transcendentals=0),
        compiler_params=pltpu.CompilerParams(
            collective_id=collective_id, has_side_effects=True, vmem_limit_bytes=VMEM
        ),
    )(*args, *far_args, *side_args)


def start_call(plan, n, x, w_in, w_up, w_mix, w_down, collective_id):
    rows = w_in.shape[0]
    low = jnp.bfloat16
    G = FF // n
    shapes = (
        jax.ShapeDtypeStruct((n,) + x.shape, low),
        jax.ShapeDtypeStruct((n, 4, rows, plan.A), low),
        jax.ShapeDtypeStruct((n, 4, rows, plan.K), low),
        jax.ShapeDtypeStruct((n, rows, 2 * G), low),
        jax.ShapeDtypeStruct((1, 4) + w_mix.shape, low),
        jax.ShapeDtypeStruct((1,) + w_down.shape, low),
    )
    dma = pltpu.SemaphoreType.DMA
    outside = pl.BlockSpec(memory_space=pl.ANY)
    inside = pl.BlockSpec(memory_space=pltpu.VMEM)
    blocks = 2 * n + 1
    outs = pl.pallas_call(
        functools.partial(start_kernel, plan, n),
        out_shape=shapes,
        in_specs=[outside] + [inside] * 4,
        out_specs=(outside,) * 6,
        scratch_shapes=[
            pltpu.VMEM((n, rows, plan.A), low),
            pltpu.VMEM((rows, plan.K), low),
            pltpu.VMEM((n, rows, 2 * G), low),
            pltpu.VMEM(w_mix.shape, low),
            pltpu.VMEM(w_down.shape, low),
        ]
        + gather_scratch(n)
        + [dma((3, n)), dma((3, n))]
        + [dma((blocks,)), dma((blocks,)), dma((2, blocks)), dma((2, blocks))]
        + [dma((5,))],
        cost_estimate=pl.CostEstimate(flops=0, bytes_accessed=2 * 10**8, transcendentals=0),
        compiler_params=pltpu.CompilerParams(
            collective_id=collective_id, has_side_effects=True, vmem_limit_bytes=VMEM
        ),
    )(x, w_in, w_up, w_mix, w_down)
    flat = lambda o: o.reshape(-1, o.shape[-1])
    tokens, in_all, shared_all, up_some, mix_all, down_some = outs
    return flat(tokens), flat(in_all), flat(shared_all), up_some, flat(mix_all), down_some


def mm(left, right):
    return jnp.dot(
        left.astype(jnp.bfloat16), right.astype(jnp.bfloat16), preferred_element_type=jnp.float32
    )


def mm_nt(left, right):
    return cols_by_cols(left.astype(jnp.bfloat16), right.astype(jnp.bfloat16))


def mm_tn(left, right):
    return rows_by_rows(left.astype(jnp.bfloat16), right.astype(jnp.bfloat16))


def pieces(values, count):
    found = []
    for _ in range(count):
        part = values.astype(jnp.bfloat16)
        found.append(part)
        values = values - part.astype(jnp.float32)
    return found


def by_marks(values, marks, count=2):
    return plain(
        jnp.concatenate(pieces(values, count), axis=1), jnp.concatenate([marks] * count, axis=0)
    )


def marks_by(marks, values, count=3):
    return plain(
        jnp.concatenate([marks] * count, axis=1), jnp.concatenate(pieces(values, count), axis=0)
    )


def iota(shape, axis):
    return lax.broadcasted_iota(jnp.int32, shape, axis)


def rope_tables(length):
    half = HD // 2
    frequency = rope_base ** (-jnp.arange(half, dtype=jnp.float32) / half)
    angles = jnp.arange(length).astype(jnp.float32)[:, None] * frequency[None, :]
    cosine, sine = jnp.cos(angles), jnp.sin(angles)
    return (
        jnp.concatenate([cosine, cosine], axis=1),
        jnp.concatenate([-sine, sine], axis=1),
    )


def turned(values, cosine, sine):
    return values * cosine + pltpu.roll(values, HD // 2, 1) * sine


def attn_stack(plan, q_ref, cosine, sine):
    heads = [
        turned(q_ref[:, h * HD : (h + 1) * HD], cosine, sine).astype(jnp.bfloat16)
        for h in range(plan.ha)
    ]
    return jnp.concatenate(heads, axis=0)


def by_extent(step, length, run):
    parts = 4
    per = length // CHUNK // parts
    for part in range(parts):
        pl.when(step // per == part)(functools.partial(run, (part + 1) * per * CHUNK))


def attn_softmax(stack, keys, at):
    scores = cols_by_cols(stack, keys) * (1.0 / math.sqrt(HD))
    row = iota(scores.shape, 0) & (CHUNK - 1)
    scores = jnp.where(iota(scores.shape, 1) <= row + at, scores, masked_score)
    weights = jnp.exp(scores - jnp.max(scores, axis=1, keepdims=True))
    return weights * (1.0 / jnp.sum(weights, axis=1, keepdims=True))


def attn_fwd_kernel(plan, q_ref, k_ref, v_ref, cos_ref, sin_ref, out_ref, keys, values):
    step = pl.program_id(0)

    @pl.when(step == 0)
    def _():
        keys[...] = turned(k_ref[...], cos_ref[...], sin_ref[...]).astype(jnp.bfloat16)
        values[...] = v_ref[...].astype(jnp.bfloat16)

    at = pl.multiple_of(step * CHUNK, CHUNK)
    rows = pl.ds(at, CHUNK)
    stack = attn_stack(plan, q_ref, cos_ref[rows, :], sin_ref[rows, :])

    def run(extent):
        probs = attn_softmax(stack, keys[:extent, :], at)
        made = mm(probs, values[:extent, :])
        for h in range(plan.ha):
            out_ref[:, h * HD : (h + 1) * HD] = made[h * CHUNK : (h + 1) * CHUNK]

    by_extent(step, keys.shape[0], run)


def attn_fwd(plan, proj, tables):
    length = proj.shape[0]
    whole = lambda i: (0, 0)
    return pl.pallas_call(
        functools.partial(attn_fwd_kernel, plan),
        grid=(length // CHUNK,),
        out_shape=jax.ShapeDtypeStruct((length, plan.R), jnp.float32),
        in_specs=[
            pl.BlockSpec((CHUNK, plan.R), lambda i: (i, 0)),
            pl.BlockSpec((length, HD), lambda i: (0, plan.B // HD)),
            pl.BlockSpec((length, HD), lambda i: (0, plan.B // HD + 1)),
            pl.BlockSpec((length, HD), whole),
            pl.BlockSpec((length, HD), whole),
        ],
        out_specs=pl.BlockSpec((CHUNK, plan.R), lambda i: (i, 0)),
        scratch_shapes=[pltpu.VMEM((length, HD), jnp.bfloat16)] * 2,
        compiler_params=pltpu.CompilerParams(vmem_limit_bytes=VMEM),
    )(proj, proj, proj, *tables)


def attn_bwd_kernel(
    plan, q_ref, k_ref, v_ref, cos_ref, sin_ref, grad_ref, slab_ref, keys, values, grad_k, grad_v
):
    step = pl.program_id(0)
    scale = 1.0 / math.sqrt(HD)

    @pl.when(step == 0)
    def _():
        keys[...] = turned(k_ref[...], cos_ref[...], sin_ref[...]).astype(jnp.bfloat16)
        values[...] = v_ref[...].astype(jnp.bfloat16)
        grad_k[...] = jnp.zeros_like(grad_k)
        grad_v[...] = jnp.zeros_like(grad_v)
        slab_ref[...] = jnp.zeros_like(slab_ref)

    at = pl.multiple_of(step * CHUNK, CHUNK)
    rows = pl.ds(at, CHUNK)
    cosine, sine = cos_ref[rows, :], sin_ref[rows, :]
    stack = attn_stack(plan, q_ref, cosine, sine)
    grads = jnp.concatenate([grad_ref[:, h * HD : (h + 1) * HD] for h in range(plan.ha)], axis=0)

    def run(extent):
        probs = attn_softmax(stack, keys[:extent, :], at)
        grad_probs = cols_by_cols(grads, values[:extent, :])
        delta = jnp.sum(probs * grad_probs, axis=1, keepdims=True)
        grad_scores = (probs * (grad_probs - delta)).astype(jnp.bfloat16)
        grad_q = mm(grad_scores, keys[:extent, :]) * scale
        for h in range(plan.ha):
            slab_ref[rows, h * HD : (h + 1) * HD] = turned(
                grad_q[h * CHUNK : (h + 1) * CHUNK], cosine, -sine
            ).astype(jnp.bfloat16)
        grad_k[:extent, :] += mm_tn(grad_scores, stack)
        grad_v[:extent, :] += mm_tn(probs, grads)

    by_extent(step, keys.shape[0], run)

    @pl.when(step == pl.num_programs(0) - 1)
    def _():
        slab_ref[:, plan.B : plan.B + HD] = turned(
            grad_k[...] * scale, cos_ref[...], -sin_ref[...]
        ).astype(jnp.bfloat16)
        slab_ref[:, plan.B + HD : plan.B + 2 * HD] = grad_v[...].astype(jnp.bfloat16)


def attn_bwd(plan, proj, tables, grad):
    length = proj.shape[0]
    whole = lambda i: (0, 0)
    return pl.pallas_call(
        functools.partial(attn_bwd_kernel, plan),
        grid=(length // CHUNK,),
        out_shape=jax.ShapeDtypeStruct((length, plan.A), jnp.bfloat16),
        in_specs=[
            pl.BlockSpec((CHUNK, plan.R), lambda i: (i, 0)),
            pl.BlockSpec((length, HD), lambda i: (0, plan.B // HD)),
            pl.BlockSpec((length, HD), lambda i: (0, plan.B // HD + 1)),
            pl.BlockSpec((length, HD), whole),
            pl.BlockSpec((length, HD), whole),
            pl.BlockSpec((CHUNK, plan.R), lambda i: (i, 0)),
        ],
        out_specs=pl.BlockSpec((length, plan.A), whole),
        scratch_shapes=[pltpu.VMEM((length, HD), jnp.bfloat16)] * 2
        + [pltpu.VMEM((length, HD), jnp.float32)] * 2,
        compiler_params=pltpu.CompilerParams(vmem_limit_bytes=VMEM),
    )(proj, proj, proj, *tables, grad)


def head_spread(plan):
    return ((iota((PAD, plan.R), 1) >> 6) == iota((PAD, plan.R), 0)).astype(jnp.bfloat16)


def head_gather(plan):
    return ((iota((plan.R, PAD), 0) >> 6) == iota((plan.R, PAD), 1)).astype(jnp.bfloat16)


def lower_ones():
    shape = (CHUNK, CHUNK)
    return (iota(shape, 0) >= iota(shape, 1)).astype(jnp.bfloat16)


def space_parts(plan, dt_raw, window, conv_ref, head_ref, pick_ref):
    total = conv_ref[4:5, :]
    for k in range(CONV):
        at = 8 - CONV + 1 + k
        total = total + conv_ref[k : k + 1, :] * window[at : at + CHUNK, :]
    raw = by_marks(dt_raw, pick_ref[...], 3) + head_ref[1:2, :]
    steps = jnp.maximum(raw, 0.0) + jnp.log1p(jnp.exp(-jnp.abs(raw)))
    logs = -steps * jnp.exp(head_ref[0:1, :])
    cumul = marks_by(lower_ones(), logs)
    return total, raw, steps, logs, cumul


def decay_of(cumul, cumul_t, causal, h):
    gaps = cumul[:, h : h + 1] - cumul_t[h : h + 1, :]
    return jnp.exp(jnp.where(causal, gaps, masked_score))


def space_fwd_kernel(
    plan, proj_ref, shared_ref, conv_ref, head_ref, pick_ref, gated_ref, made_ref, before_ref, state, window
):
    R = plan.R
    step = pl.program_id(0)

    @pl.when(step == 0)
    def _():
        state[...] = jnp.zeros_like(state)
        window[0:8, :] = jnp.zeros((8, window.shape[1]), jnp.float32)

    @pl.when(step > 0)
    def _():
        window[0:8, :] = window[CHUNK : CHUNK + 8, :]

    window[8 : CHUNK + 8, :R] = proj_ref[:, plan.B : plan.B + R]
    window[8 : CHUNK + 8, R:] = shared_ref[:, : 2 * NS]
    total, _, steps, _, cumul = space_parts(
        plan, shared_ref[:, 2 * NS :], window, conv_ref, head_ref, pick_ref
    )
    post = total * jax.nn.sigmoid(total)
    x = post[:, :R]
    b = post[:, R : R + NS].astype(jnp.bfloat16)
    c = post[:, R + NS :].astype(jnp.bfloat16)
    spread_heads = head_spread(plan)
    cumul_t = cumul.T
    last = cumul[CHUNK - 1 : CHUNK, :]
    tail = jnp.exp(last - cumul)
    weighted = x * by_marks(steps, spread_heads)
    causal = iota((CHUNK, CHUNK), 0) >= iota((CHUNK, CHUNK), 1)
    inner = cols_by_cols(c, b)
    before = state[...]
    before_ref[0] = before.astype(jnp.bfloat16)
    made = mm(c, before) * by_marks(jnp.exp(cumul), spread_heads)
    made = made + by_marks(jnp.broadcast_to(head_ref[2:3, :], (8, PAD)), spread_heads)[0:1] * x
    left = iota((CHUNK, 2 * MP), 1) < MP
    weighted_low = weighted.astype(jnp.bfloat16)
    intra = []
    for pair in range(plan.hm // 2):
        lanes = weighted_low[:, pair * 2 * MP : (pair + 1) * 2 * MP]
        one = mm(inner * decay_of(cumul, cumul_t, causal, 2 * pair), lanes)
        two = mm(inner * decay_of(cumul, cumul_t, causal, 2 * pair + 1), lanes)
        intra.append(jnp.where(left, one, two))
    made = made + jnp.concatenate(intra, axis=1)
    state[...] = before * by_marks(
        jnp.broadcast_to(jnp.exp(last), (8, PAD)), spread_heads
    )[0:1] + mm_tn(b, weighted * by_marks(tail, spread_heads))
    z = proj_ref[:, :R]
    made_ref[...] = made
    gated_ref[...] = made * (z * jax.nn.sigmoid(z))


def space_fwd(plan, proj, shared, conv, heads, pick):
    length = proj.shape[0]
    chunks = length // CHUNK
    W = plan.W
    whole = lambda i: (0, 0)
    rows = lambda i: (i, 0)
    return pl.pallas_call(
        functools.partial(space_fwd_kernel, plan),
        grid=(chunks,),
        out_shape=(
            jax.ShapeDtypeStruct((length, plan.R), jnp.float32),
            jax.ShapeDtypeStruct((length, plan.R), jnp.float32),
            jax.ShapeDtypeStruct((chunks, NS, plan.R), jnp.bfloat16),
        ),
        in_specs=[
            pl.BlockSpec((CHUNK, plan.A), rows),
            pl.BlockSpec((CHUNK, plan.K), rows),
            pl.BlockSpec((8, W), whole),
            pl.BlockSpec((8, PAD), whole),
            pl.BlockSpec((PAD, PAD), whole),
        ],
        out_specs=(
            pl.BlockSpec((CHUNK, plan.R), rows),
            pl.BlockSpec((CHUNK, plan.R), rows),
            pl.BlockSpec((1, NS, plan.R), lambda i: (i, 0, 0)),
        ),
        scratch_shapes=[
            pltpu.VMEM((NS, plan.R), jnp.float32),
            pltpu.VMEM((CHUNK + 8, W), jnp.float32),
        ],
        compiler_params=pltpu.CompilerParams(vmem_limit_bytes=VMEM),
    )(proj, shared, conv, heads, pick)


def space_bwd_kernel(
    plan, proj_ref, shared_ref, prev_ref, prev_shared, conv_ref, head_ref, pick_ref, gain_ref, row_ref,
    grad_ref, made_ref, before_ref, slab_ref, slab_shared, conv_acc, head_acc, skip_acc, d_state, window, d_window,
):
    R = plan.R
    step = pl.program_id(0)
    chunk = pl.num_programs(0) - 1 - step

    @pl.when(step == 0)
    def _():
        d_state[...] = jnp.zeros_like(d_state)
        d_window[CHUNK : CHUNK + 8, :] = jnp.zeros((8, plan.W), jnp.float32)
        conv_acc[...] = jnp.zeros_like(conv_acc)
        head_acc[...] = jnp.zeros_like(head_acc)
        skip_acc[...] = jnp.zeros_like(skip_acc)

    @pl.when(step > 0)
    def _():
        d_window[CHUNK : CHUNK + 8, :] = d_window[0:8, :]

    window[0:8, :R] = jnp.where(chunk == 0, 0.0, prev_ref[:, plan.B : plan.B + R])
    window[0:8, R:] = jnp.where(chunk == 0, 0.0, prev_shared[:, : 2 * NS])
    window[8 : CHUNK + 8, :R] = proj_ref[:, plan.B : plan.B + R]
    window[8 : CHUNK + 8, R:] = shared_ref[:, : 2 * NS]
    total, raw, steps, logs, cumul = space_parts(
        plan, shared_ref[:, 2 * NS :], window, conv_ref, head_ref, pick_ref
    )
    sig = jax.nn.sigmoid(total)
    post = total * sig
    x = post[:, :R]
    b = post[:, R : R + NS].astype(jnp.bfloat16)
    c = post[:, R + NS :].astype(jnp.bfloat16)
    spread_heads = head_spread(plan)
    gather_heads = head_gather(plan)
    cumul_t = cumul.T
    last = cumul[CHUNK - 1 : CHUNK, :]
    steps_wide = by_marks(steps, spread_heads)
    tail_wide = by_marks(jnp.exp(last - cumul), spread_heads)
    grow_wide = by_marks(jnp.exp(cumul), spread_heads)
    last_wide = by_marks(jnp.broadcast_to(jnp.exp(last), (8, PAD)), spread_heads)[0:1]
    skip_wide = by_marks(jnp.broadcast_to(head_ref[2:3, :], (8, PAD)), spread_heads)[0:1]
    weighted = x * steps_wide
    causal = iota((CHUNK, CHUNK), 0) >= iota((CHUNK, CHUNK), 1)
    inner = cols_by_cols(c, b)

    z = proj_ref[:, :R]
    sig_z = jax.nn.sigmoid(z)
    grad = grad_ref[...].astype(jnp.float32)
    gate = z * sig_z
    gated = made_ref[...] * gate
    row_factor = row_ref[:, 0:1]
    skip_acc[1:2, :] += jnp.sum(grad * gated * row_factor, axis=0, keepdims=True)
    grad = grad * gain_ref[0:1, :] * row_factor - gated * row_ref[:, 1:2]
    d_made = grad * gate
    slab_ref[:, :R] = (grad * made_ref[...] * (sig_z * (1.0 + z * (1.0 - sig_z)))).astype(
        jnp.bfloat16
    )
    skip_acc[0:1, :] += jnp.sum(d_made * x, axis=0, keepdims=True)

    before = before_ref[0]
    d_after = d_state[...]
    d_after_low = d_after.astype(jnp.bfloat16)
    grown = d_made * grow_wide
    grown_low = grown.astype(jnp.bfloat16)
    carried = mm(c, before)
    d_c = mm_nt(grown_low, before)
    pulled = weighted * tail_wide
    d_pulled = mm(b, d_after_low)
    d_b = mm_nt(pulled, d_after_low)
    d_cumul = by_marks(grown * carried, gather_heads)
    kept = by_marks(d_pulled * pulled, gather_heads)
    d_cumul = d_cumul - kept
    decayed = jnp.sum(d_after * before.astype(jnp.float32), axis=0, keepdims=True) * last_wide
    d_last = jnp.sum(kept, axis=0, keepdims=True) + by_marks(
        jnp.broadcast_to(decayed, (8, R)), gather_heads
    )[0:1]
    d_state[...] = d_after * last_wide + mm_tn(c, grown_low)

    left = iota((CHUNK, 2 * MP), 1) < MP
    lane = iota((CHUNK, PAD), 1)
    sub = iota((8, CHUNK), 0)
    weighted_low = weighted.astype(jnp.bfloat16)
    d_made_low = d_made.astype(jnp.bfloat16)
    d_inner = jnp.zeros((CHUNK, CHUNK), jnp.float32)
    columns = jnp.zeros((8, CHUNK), jnp.float32)
    d_weighted = []
    for pair in range(plan.hm // 2):
        at = slice(pair * 2 * MP, (pair + 1) * 2 * MP)
        lanes, d_lanes = weighted_low[:, at], d_made_low[:, at]
        halves = []
        for which in range(2):
            h = 2 * pair + which
            decay = decay_of(cumul, cumul_t, causal, h)
            whole = inner * decay
            halves.append(mm_tn(whole, d_lanes))
            mine = jnp.where(left if which == 0 else ~left, d_lanes, jnp.zeros_like(d_lanes))
            d_whole = cols_by_cols(mine, lanes)
            d_inner = d_inner + d_whole * decay
            slope = d_whole * whole
            d_cumul = d_cumul + jnp.where(lane == h, jnp.sum(slope, axis=1, keepdims=True), 0.0)
            columns = columns + jnp.where(sub == h, jnp.sum(slope, axis=0, keepdims=True), 0.0)
        d_weighted.append(jnp.where(left, halves[0], halves[1]))
    d_weighted = jnp.concatenate(d_weighted, axis=1) + d_pulled * tail_wide
    columns = jnp.concatenate([columns, jnp.zeros((CHUNK - 8, CHUNK), jnp.float32)], axis=0).T
    d_cumul = d_cumul - columns
    d_inner_low = d_inner.astype(jnp.bfloat16)
    d_c = d_c + mm(d_inner_low, b)
    d_b = d_b + mm_tn(d_inner_low, c)
    d_x = d_weighted * steps_wide + skip_wide * d_made
    d_steps = by_marks(d_weighted * x, gather_heads)
    upper = (iota((CHUNK, CHUNK), 0) <= iota((CHUNK, CHUNK), 1)).astype(jnp.bfloat16)
    d_logs = marks_by(upper, d_cumul) + d_last
    d_steps = d_steps - jnp.exp(head_ref[0:1, :]) * d_logs
    d_raw = d_steps * jax.nn.sigmoid(raw)
    d_raw = jnp.where(lane < plan.hm, d_raw, 0.0)
    slab_shared[:, 2 * NS :] = cols_by_cols(d_raw.astype(jnp.bfloat16), pick_ref[...]).astype(
        jnp.bfloat16
    )
    head_acc[0:1, :] += jnp.sum(d_logs * logs, axis=0, keepdims=True)
    head_acc[1:2, :] += jnp.sum(d_raw, axis=0, keepdims=True)

    d_post = jnp.concatenate([d_x, d_b, d_c], axis=1)
    d_total = d_post * (sig * (1.0 + total * (1.0 - sig)))
    d_window[0:CHUNK, :] = d_total
    d_xbc = jnp.zeros((CHUNK, plan.W), jnp.float32)
    for k in range(CONV):
        shift = CONV - 1 - k
        d_xbc = d_xbc + conv_ref[k : k + 1, :] * d_window[shift : shift + CHUNK, :]
        at = 8 - CONV + 1 + k
        conv_acc[k : k + 1, :] += jnp.sum(
            d_total * window[at : at + CHUNK, :], axis=0, keepdims=True
        )
    conv_acc[4:5, :] += jnp.sum(d_total, axis=0, keepdims=True)
    slab_ref[:, plan.B : plan.B + R] = d_xbc[:, :R].astype(jnp.bfloat16)
    slab_shared[:, : 2 * NS] = d_xbc[:, R:].astype(jnp.bfloat16)
    if plan.B + R < plan.A:
        slab_ref[:, plan.B + R :] = jnp.zeros((CHUNK, plan.A - plan.B - R), jnp.bfloat16)


def space_bwd(plan, proj, shared, conv, heads, pick, gain, rows_of, grad, made, before):
    length = proj.shape[0]
    chunks = length // CHUNK
    W = plan.W
    whole = lambda i: (0, 0)
    rows = lambda i: (chunks - 1 - i, 0)
    per = CHUNK // 8
    return pl.pallas_call(
        functools.partial(space_bwd_kernel, plan),
        grid=(chunks,),
        out_shape=(
            jax.ShapeDtypeStruct((length, plan.A), jnp.bfloat16),
            jax.ShapeDtypeStruct((length, plan.K), jnp.bfloat16),
            jax.ShapeDtypeStruct((8, W), jnp.float32),
            jax.ShapeDtypeStruct((8, PAD), jnp.float32),
            jax.ShapeDtypeStruct((8, plan.R), jnp.float32),
        ),
        in_specs=[
            pl.BlockSpec((CHUNK, plan.A), rows),
            pl.BlockSpec((CHUNK, plan.K), rows),
            pl.BlockSpec((8, plan.A), lambda i: (jnp.maximum((chunks - 1 - i) * per - 1, 0), 0)),
            pl.BlockSpec((8, plan.K), lambda i: (jnp.maximum((chunks - 1 - i) * per - 1, 0), 0)),
            pl.BlockSpec((8, W), whole),
            pl.BlockSpec((8, PAD), whole),
            pl.BlockSpec((PAD, PAD), whole),
            pl.BlockSpec((8, plan.R), whole),
            pl.BlockSpec((CHUNK, 2), rows),
            pl.BlockSpec((CHUNK, plan.R), rows),
            pl.BlockSpec((CHUNK, plan.R), rows),
            pl.BlockSpec((1, NS, plan.R), lambda i: (chunks - 1 - i, 0, 0)),
        ],
        out_specs=(
            pl.BlockSpec((CHUNK, plan.A), rows),
            pl.BlockSpec((CHUNK, plan.K), rows),
            pl.BlockSpec((8, W), whole),
            pl.BlockSpec((8, PAD), whole),
            pl.BlockSpec((8, plan.R), whole),
        ),
        scratch_shapes=[
            pltpu.VMEM((NS, plan.R), jnp.float32),
            pltpu.VMEM((CHUNK + 8, W), jnp.float32),
            pltpu.VMEM((CHUNK + 8, W), jnp.float32),
        ],
        compiler_params=pltpu.CompilerParams(vmem_limit_bytes=VMEM),
    )(proj, shared, proj, shared, conv, heads, pick, gain, rows_of, grad, made, before)


def body(
    inputs,
    cotangent,
    w_in,
    w_in_m,
    w_in_v,
    w_mix,
    w_mix_m,
    w_mix_v,
    w_up,
    w_up_m,
    w_up_v,
    w_down,
    w_down_m,
    w_down_v,
    vectors,
    vectors_m,
    vectors_v,
):
    low = jnp.bfloat16
    count = lax.axis_size("ctx")
    ways = lax.axis_size("wshard")
    place = lax.axis_index("ctx")
    plan = Plan(count)
    R, hm = plan.R, plan.hm
    is_space = place >= plan.attn
    space = jnp.maximum(place - plan.attn, 0)

    gain_attn, gain_ffn, gain_ssm, conv_bias, conv_weight, a_log, dt_bias, d_skip = split_vectors(
        vectors
    )
    whole, in_own, shared_own, up_some, mix_own, down_some = start_call(
        plan, count, inputs[0], w_in, w_up, w_mix, w_down, 1
    )

    own = lambda a, size, axis=0: lax.dynamic_slice_in_dim(a, space * size, size, axis)
    gain_own = own(gain_ssm, R)
    W = plan.W
    conv = jnp.concatenate(
        [
            jnp.concatenate([own(conv_weight, R, 1), conv_weight[:, DSSM:]], axis=1),
            jnp.concatenate([own(conv_bias, R), conv_bias[DSSM:]])[None],
            jnp.zeros((8 - CONV - 1, W), jnp.float32),
        ]
    )
    heads = jnp.stack([own(v, hm) for v in (a_log, dt_bias, d_skip)])
    heads = jnp.pad(heads, ((0, 5), (0, PAD - hm)))
    column = lax.broadcasted_iota(jnp.int32, (PAD, PAD), 1)
    row = lax.broadcasted_iota(jnp.int32, (PAD, PAD), 0)
    pick = jnp.logical_and(row == column + space * hm, column < hm).astype(low)
    tables = rope_tables(count * inputs.shape[1])

    source = inputs[0].astype(jnp.float32)
    whole = whole.astype(jnp.float32)
    in_own, cotangent_late = lax.optimization_barrier((in_own, cotangent[0]))
    odd = lax.axis_index("wshard") % 2 == 1
    upstream_all = gather_ctx(cotangent_late, count, ways, odd)
    length = whole.shape[0]
    rows = inputs.shape[1]
    unit = whole * lax.rsqrt(jnp.mean(whole * whole, axis=-1, keepdims=True) + norm_eps)
    normed = (unit * gain_attn).astype(low)
    unit = unit.astype(low)
    proj = plain(normed, in_own)
    shared = plain(normed, shared_own)

    def space_ahead(proj, shared):
        return space_fwd(plan, proj, shared, conv, heads, pick)

    def attn_ahead(proj, shared):
        made = attn_fwd(plan, proj, tables)
        blank = jnp.zeros((length // CHUNK, NS, R), low)
        return made, jnp.zeros_like(made), blank

    made, raw_made, before = lax.cond(is_space, space_ahead, attn_ahead, proj, shared)
    square = jnp.where(is_space, jnp.sum(made * made, axis=1), 0.0)
    factor = lax.rsqrt(sum_rows(count, square, 5) / DSSM + norm_eps)
    mixed = jnp.where(is_space, made * factor[:, None] * gain_own, made).astype(low)
    wide = lambda *shape: jax.ShapeDtypeStruct(shape, jnp.float32)
    side = (up_some, down_some)
    roomy = length <= 1024
    middle, gate_up, two_all, up_own, down_own = flow_call(
        branch_kernel,
        count,
        rows,
        (mixed, mix_own, inputs[0], gain_ffn[None]),
        (wide(rows, D), wide(length if roomy else 8, 2 * FF // count)),
        True,
        True,
        (side, *share_shapes(side)),
        8,
        roomy,
    )
    two_all = two_all.reshape(length, D)
    up_own, down_own = up_own.reshape(D, -1), down_own.reshape(-1, D)

    if not roomy:
        gate_up = plain(two_all, up_own)
    half = FF // count
    swiglu = lambda g: jax.nn.silu(g[:, :half]) * g[:, half:]
    activated, act_pull = jax.vjp(swiglu, gate_up)
    activated = activated.astype(low)
    grad_act = cols_by_cols(upstream_all, down_own)
    grad_gate_up = act_pull(grad_act)[0].astype(low)
    cut = lambda g, blocks: g.astype(low).reshape(blocks, ways, -1, g.shape[1])
    blank = jnp.zeros((1, 1, 16, 128), low)
    if roomy:
        up_block = (count, ways, D // (count * ways), 2 * FF // count)
        down_block = (1, ways, FF // (count * ways), D)
        side = [jax.ShapeDtypeStruct(block, low) for block in (up_block, down_block)]
        side_shapes, side_scratch = collect_shapes(("rows", "rows"), side)
        side_scratch = (
            [pltpu.VMEM(block, low) for block in (up_block, down_block)]
            + [pltpu.VMEM((2, length, D // count), low)] * 2
            + [pltpu.SemaphoreType.DMA((2, 2))]
            + side_scratch
        )
        side = (blank, blank)
    else:
        side = (cut(rows_by_rows(two_all, grad_gate_up), count), cut(rows_by_rows(activated, upstream_all), 1))
        side_shapes, side_scratch = collect_shapes(("rows", "rows"), side)
    some = lambda a: a if roomy else a[:16]
    late = in_ring(activated.reshape(count, rows, -1), count, ways, odd)
    late = plain(late, down_own).astype(low)
    grad_gate_up, late = lax.optimization_barrier((grad_gate_up, late))
    grad_middle, grad_gain_ffn, grad_made, branch_all, up_mine, down_mine = flow_call(
        feed_back_kernel,
        count,
        rows,
        (
            grad_gate_up,
            up_own,
            cotangent[0],
            middle,
            gain_ffn[None],
            some(activated),
            some(mix_own),
        ),
        (
            wide(rows, D),
            wide(8, D),
            jax.ShapeDtypeStruct((length if roomy else 16, R), low),
        ),
        True,
        False,
        (side, side_shapes, side_scratch),
        9,
        roomy,
        (two_all, upstream_all),
    )
    grad_gain_ffn = grad_gain_ffn[0]
    branch_all = branch_all.reshape(length, D)
    branch_all, grad_made, late = lax.optimization_barrier((branch_all, grad_made, late))
    late = scatter_ctx(late, count, ways)
    if not roomy:
        grad_made = cols_by_cols(branch_all, mix_own).astype(low)
    made_wide = grad_made.astype(jnp.float32)
    dots = jnp.where(is_space, jnp.sum(made_wide * gain_own * made, axis=1), 0.0)
    dots = sum_rows(count, dots, 6)

    def space_back(proj, shared, grad_made):
        gain = jnp.broadcast_to(gain_own, (8, R))
        rows_of = jnp.stack([factor, factor**3 * dots / DSSM], axis=1)
        return space_bwd(
            plan, proj, shared, conv, heads, pick, gain, rows_of, grad_made, raw_made, before
        )

    def attn_back(proj, shared, grad_made):
        blank = lambda k: jnp.zeros((8, k), jnp.float32)
        none = jnp.zeros(shared.shape, low)
        return attn_bwd(plan, proj, tables, grad_made), none, blank(W), blank(PAD), blank(R)

    grad_proj, grad_shared, conv_acc, head_acc, skip_acc = lax.cond(
        is_space, space_back, attn_back, proj, shared, grad_made
    )
    if roomy:
        grad_gain_attn = jnp.zeros_like(gain_attn)
    else:
        grad_in = rows_by_rows(unit, grad_proj)
        grad_in_shared = rows_by_rows(unit, grad_shared)
        grad_gain_attn = jnp.sum(grad_in * in_own, axis=1)
        grad_gain_attn = grad_gain_attn + jnp.sum(grad_in_shared * shared_own, axis=1)
        grad_in = grad_in * gain_attn[:, None]
        grad_in_shared = grad_in_shared * gain_attn[:, None]
    def placed(piece, size, total, axis=0):
        shape = list(piece.shape)
        shape[axis] = total
        start = [0] * piece.ndim
        start[axis] = space * size
        return lax.dynamic_update_slice(jnp.zeros(shape, piece.dtype), piece, start)

    conv_w_grad, conv_b_grad = conv_acc[:CONV], conv_acc[CONV]
    a_grad, bias_grad = head_acc[0, :hm], head_acc[1, :hm]
    skip_grad = jnp.sum(skip_acc[0].reshape(hm, MP), axis=1)
    grad_gain_own = skip_acc[1]
    vector_local = jnp.concatenate(
        [
            grad_gain_attn,
            grad_gain_ffn,
            placed(grad_gain_own, R, DSSM),
            placed(conv_b_grad[:R], R, DSSM),
            conv_b_grad[R:],
            jnp.concatenate(
                [placed(conv_w_grad[:, :R], R, DSSM, 1), conv_w_grad[:, R:]], axis=1
            ).reshape(CONV * CONVCH),
            placed(a_grad, hm, MH),
            placed(bias_grad, hm, MH),
            placed(skip_grad, hm, MH),
        ]
    )
    grad_proj, late = lax.optimization_barrier((grad_proj, late))
    outputs = (middle + late).astype(low)[None]
    pad = -vectors.shape[0] % 1024
    vector_local = jnp.pad(vector_local, (0, pad)).reshape(-1, 128)
    if roomy:
        lines = D // (count * ways)
        blocks = (
            (count, ways, lines, plan.A),
            (count, ways, lines, plan.K),
            (1, ways, MIXIN // (count * ways), D),
        )
        side = [jax.ShapeDtypeStruct(block, low) for block in blocks]
        side_shapes, side_scratch = collect_shapes(SUMS, side)
        side_scratch = (
            [pltpu.VMEM(block, low) for block in blocks]
            + [pltpu.VMEM((2, length, D // count), low)] * 2
            + [pltpu.SemaphoreType.DMA((2, 2)), pltpu.VMEM(vector_local.shape, jnp.float32)]
            + side_scratch
        )
        side = (blank, blank, blank)
    else:
        grad_mix = rows_by_rows(mixed, branch_all)
        side = (cut(grad_in, count), cut(grad_in_shared, count), cut(grad_mix, 1))
        side_shapes, side_scratch = collect_shapes(SUMS, side)
    home_sems = [pltpu.SemaphoreType.DMA((count,))] * 2
    input_grad, vector_sum, up_mine, in_mine, shared_mine, mix_mine = flow_call(
        source_back_kernel,
        count,
        rows,
        (
            grad_proj,
            grad_shared,
            in_own,
            shared_own,
            inputs[0],
            grad_middle,
            gain_attn[None],
            vector_local,
            up_mine,
            some(mixed),
            some(gain_attn[:, None]),
        ),
        (wide(rows, D), wide(*vector_local.shape), jax.ShapeDtypeStruct(up_mine.shape, low)),
        False,
        False,
        (side, side_shapes, side_scratch + sum_scratch(count, vector_local.shape) + home_sems),
        10,
        far_args=(some(unit), some(branch_all)),
    )
    input_grad = input_grad[None]

    up_shard = up_from_slabs(plan, up_mine)
    mix_shard = mix_mine[0].astype(jnp.float32)
    down_shard = down_mine[0].astype(jnp.float32)

    vector_grad = vector_sum.reshape(-1)[: vectors.shape[0]]
    new_in = adam_in(plan, in_mine, shared_mine, w_in, w_in_m, w_in_v, 2.0 * D ** (-0.5))
    new_mix = adamw(w_mix, w_mix_m, w_mix_v, mix_shard, DSSM ** (-0.5), decay_weight)
    new_up = adamw(w_up, w_up_m, w_up_v, up_shard, D ** (-0.5), decay_weight)
    new_down = adamw(w_down, w_down_m, w_down_v, down_shard, FF ** (-0.5), decay_weight)
    new_vec = adamw(vectors, vectors_m, vectors_v, vector_grad, vector_rate, 0.0)
    return (outputs, input_grad, *new_in, *new_mix, *new_up, *new_down, *new_vec)


def solution(mesh):
    tokens = P("wshard", "ctx", None)
    weight = P(("ctx", "wshard"), None)
    return jax.shard_map(
        body,
        mesh=mesh,
        in_specs=(tokens,) * 2 + (weight,) * 12 + (P(),) * 3,
        out_specs=(tokens,) * 2 + (weight,) * 12 + (P(),) * 3,
        check_vma=False,
    )
```

```python
import functools
import math

import jax
import jax.numpy as jnp
from jax import lax
from jax.experimental import pallas as pl
from jax.experimental.pallas import tpu as pltpu
from jax.sharding import PartitionSpec as P

D = 2048
FF = 4096
AH = 8
KVH = 2
HD = 128
MH = 48
MP = 64
NS = 256
CONV = 4
STEP = 10
DSSM = 3072
CONVCH = 3584
ATT = AH * HD
MIXIN = ATT + DSSM
GROUP = AH // KVH
CHUNK = 128
PAD = 128
VMEM = 60 * 1024 * 1024


norm_eps = 1e-05
rope_base = 10000.0
beta_one = 0.9
beta_two = 0.95
adam_eps = 1e-08
decay_weight = 0.1
vector_rate = 0.5
masked_score = -1e30

K_AT = ATT
V_AT = K_AT + KVH * HD
Z_AT = V_AT + KVH * HD
X_AT = Z_AT + DSSM
BC_AT = X_AT + DSSM
DT_AT = BC_AT + 2 * NS
END = DT_AT + MH


def rows_by_rows(left, right):
    return lax.dot_general(
        left, right, (((0,), (0,)), ((), ())), preferred_element_type=jnp.float32
    )


def cols_by_cols(left, right):
    return lax.dot_general(
        left, right, (((1,), (1,)), ((), ())), preferred_element_type=jnp.float32
    )


def plain(left, right):
    return jnp.dot(left, right, preferred_element_type=jnp.float32)


def rms_norm(values, gain):
    factor = lax.rsqrt(jnp.mean(values * values, axis=-1, keepdims=True) + norm_eps)
    return values * factor * gain


def split_vectors(vectors):
    extents = (D, D, DSSM, CONVCH, CONV * CONVCH, MH, MH, MH)
    pieces = []
    offset = 0
    for extent in extents:
        pieces.append(lax.slice_in_dim(vectors, offset, offset + extent))
        offset = offset + extent
    pieces[4] = pieces[4].reshape(CONV, CONVCH)
    return pieces


def adamw(weight, moment, second, grad, rate, decay):
    moment = beta_one * moment + (1.0 - beta_one) * grad
    second = beta_two * second + (1.0 - beta_two) * grad * grad
    corrected = moment / (1.0 - beta_one**STEP)
    divisor = jnp.sqrt(second / (1.0 - beta_two**STEP)) + adam_eps
    return (weight - rate * (corrected / divisor + decay * weight), moment, second)


class Plan:
    def __init__(self, count):
        self.count = count
        self.R = MIXIN // count
        self.attn = ATT // self.R
        self.ha = self.R // HD
        self.hm = self.R // MP
        self.B = self.R
        self.A = self.R + max(self.R, 2 * HD)
        self.K = 2 * NS + PAD
        self.W = self.R + 2 * NS

    def kv_of(self, c):
        return c * self.ha // GROUP


def up_from_slabs(plan, slabs):
    G = FF // plan.count
    slabs = slabs.astype(jnp.float32)
    return jnp.concatenate(
        [slabs[c][:, :G] for c in range(plan.count)] + [slabs[c][:, G:] for c in range(plan.count)],
        axis=1,
    )


def ring_groups(n, ways):
    ring = list(range(0, n, 2)) + list(range(n - 1, 0, -2))
    return [[c * ways + w for c in (ring[::-1] if w % 2 else ring)] for w in range(ways)], ring


def ring_place(n, w, c):
    at = c // 2 + c % 2 * (n - 1 - c // 2 * 2)
    return at + w % 2 * (n - 1 - 2 * at)


def gather_ctx(x, n, ways):
    return lax.all_gather(x, ("ctx", "wshard"), axis_index_groups=ring_groups(n, ways)[0])


def from_ring(blocks, n, w):
    parts = [lax.dynamic_index_in_dim(blocks, ring_place(n, w, c), 0, False) for c in range(n)]
    return jnp.concatenate(parts)


def in_ring(blocks, n, ways, odd):
    ring = ring_groups(n, ways)[1]
    parts = [
        lax.dynamic_index_in_dim(blocks, jnp.where(odd, ring[n - 1 - i], ring[i]), 0, False)
        for i in range(n)
    ]
    return jnp.concatenate(parts)


def scatter_ctx(x, n, ways):
    return lax.psum_scatter(
        x.astype(jnp.bfloat16),
        ("ctx", "wshard"),
        scatter_dimension=0,
        axis_index_groups=ring_groups(n, ways)[0],
        tiled=True,
    ).astype(jnp.float32)


def adam_in_kernel(plan, rate, slabs, shared, w, m, v, new_w, new_m, new_v):
    R, B = plan.R, plan.B
    wide = jnp.float32
    heads, spaces = range(plan.attn), range(plan.attn, plan.count)

    def update(lo, hi, parts):
        grad = functools.reduce(lambda a, b: a + b, [part.astype(wide) for part in parts])
        new = adamw(w[:, lo:hi], m[:, lo:hi], v[:, lo:hi], grad, rate, decay_weight)
        new_w[:, lo:hi], new_m[:, lo:hi], new_v[:, lo:hi] = new

    for c in heads:
        update(c * R, (c + 1) * R, [slabs[c, :, :R]])
    for start, at in ((K_AT, B), (V_AT, B + HD)):
        for g in range(KVH):
            owners = [slabs[c, :, at : at + HD] for c in heads if plan.kv_of(c) == g]
            update(start + g * HD, start + (g + 1) * HD, owners)
    for c in spaces:
        j = c - plan.attn
        update(Z_AT + j * R, Z_AT + (j + 1) * R, [slabs[c, :, :R]])
        update(X_AT + j * R, X_AT + (j + 1) * R, [slabs[c, :, B : B + R]])
    update(BC_AT, END, [shared[c, :, : END - BC_AT] for c in spaces])


def adam_in(plan, slabs, shared, w, m, v, rate):
    rows = w.shape[0]
    block = 16
    flat = pl.BlockSpec((block, END), lambda i: (i, 0))
    return pl.pallas_call(
        functools.partial(adam_in_kernel, plan, rate),
        grid=(rows // block,),
        out_shape=(jax.ShapeDtypeStruct(w.shape, w.dtype),) * 3,
        in_specs=[
            pl.BlockSpec((plan.count, block, plan.A), lambda i: (0, i, 0)),
            pl.BlockSpec((plan.count, block, plan.K), lambda i: (0, i, 0)),
            flat,
            flat,
            flat,
        ],
        out_specs=(flat,) * 3,
        compiler_params=pltpu.CompilerParams(vmem_limit_bytes=VMEM),
    )(slabs, shared, w, m, v)


MESH = pl.DeviceIdType.MESH


def here():
    c, w = lax.axis_index("ctx"), lax.axis_index("wshard")
    return c, w, w + 1 - 2 * (w % 2), (w + 2) % 4


def greet(devices):
    barrier = pltpu.get_barrier_semaphore()
    for device in devices:
        pl.semaphore_signal(barrier, inc=1, device_id=device, device_id_type=MESH)
    pl.semaphore_wait(barrier, len(devices))


def remote(src, dst, send, recv, device):
    return pltpu.make_async_remote_copy(
        src_ref=src, dst_ref=dst, send_sem=send, recv_sem=recv, device_id=device, device_id_type=MESH
    )


class Collect:
    def __init__(self, n, kinds, sources, targets, extra):
        self.n = n
        self.c, self.w, self.sib, self.across = here()
        self.x, self.core = self.w // 2, self.w % 2
        self.pending = []
        self.jobs = []
        for j, kind in enumerate(kinds):
            self.jobs.append((kind, sources[j], targets[j]) + tuple(extra[10 * j : 10 * j + 10]))
        most = max(job[3].shape[1] for job in self.jobs)
        self.steps = [s % most for s in range(1, most + 1)]

    def due(self, s):
        for job in self.jobs:
            count = job[3].shape[1]
            if s < count:
                yield job, (self.c + s) % self.n if count > 1 else 0

    def send(self, s):
        for place, slot in ((1 - self.x, 0), (self.x, 1)):
            for job, q in self.due(s):
                _, src, _, kbuf, _, _, _, k_send, k_recv = job[:9]
                out = remote(
                    src.at[q, place * 2 + 1 - self.core],
                    kbuf.at[slot, q],
                    k_send.at[slot, s],
                    k_recv.at[slot, q],
                    (self.c, self.sib),
                )
                out.start()
                self.pending.append(out)

    def cross(self, s):
        wide = jnp.float32
        for job, q in self.due(s):
            _, src, _, kbuf, stage, xbuf, _, k_send, k_recv, x_send, x_recv = job[:11]
            got = kbuf.at[0, q]
            remote(got, got, k_send.at[0, s], k_recv.at[0, q], (self.c, self.sib)).wait_recv()
            mine = src[q, (1 - self.x) * 2 + self.core].astype(wide)
            stage[q] = (mine + kbuf[0, q].astype(wide)).astype(stage.dtype)
            out = remote(
                stage.at[q], xbuf.at[q], x_send.at[s], x_recv.at[q], (self.c, self.across)
            )
            out.start()
            self.pending.append(out)

    def close(self, s):
        wide = jnp.float32
        for job, q in self.due(s):
            kind, src, dst, kbuf, stage, xbuf, done, k_send, k_recv, x_send, x_recv = job[:11]
            got = kbuf.at[1, q]
            remote(got, got, k_send.at[1, s], k_recv.at[1, q], (self.c, self.sib)).wait_recv()
            got = xbuf.at[q]
            remote(got, got, x_send.at[s], x_recv.at[q], (self.c, self.across)).wait_recv()
            total = src[q, self.x * 2 + self.core].astype(wide) + kbuf[1, q].astype(wide)
            total = (total + xbuf[q].astype(wide)).astype(stage.dtype)
            if kind == "cols" and s > 0:
                done[q] = total
                out = remote(done.at[q], dst.at[self.c], job[11].at[s], job[12].at[self.c], (q, self.w))
                out.start()
                self.pending.append(out)
            else:
                dst[q] = total

    def end(self):
        for job in self.jobs:
            if job[0] == "cols":
                dst, a_send, a_recv = job[2], job[11], job[12]
                for s in range(1, self.n):
                    q = (self.c + self.n - s) % self.n
                    got = dst.at[q]
                    remote(got, got, a_send.at[s], a_recv.at[q], (q, self.w)).wait_recv()
        for out in self.pending:
            out.wait_send()


def home_job(n, source, target, send, recv):
    c, w = lax.axis_index("ctx"), lax.axis_index("wshard")
    target[c] = source[c]
    copies = [
        remote(source.at[(c + s) % n], target.at[c], send.at[s], recv.at[c], ((c + s) % n, w))
        for s in range(1, n)
    ]
    for copy in copies:
        copy.start()
    yield
    for s in range(1, n):
        q = (c + n - s) % n
        remote(source.at[q], target.at[q], send.at[s], recv.at[q], (q, w)).wait_recv()
    for copy in copies:
        copy.wait_send()


def collect_shapes(kinds, sources):
    shapes, scratch = [], []
    for kind, src in zip(kinds, sources):
        count, _, rows, size = src.shape
        block = (count, rows, size)
        shapes.append(jax.ShapeDtypeStruct(block, src.dtype))
        scratch += [
            pltpu.VMEM((2,) + block, src.dtype),
            pltpu.VMEM(block, src.dtype),
            pltpu.VMEM(block, src.dtype),
            pltpu.VMEM(block if kind == "cols" else (1, 16, 128), src.dtype),
            pltpu.SemaphoreType.DMA((2, count)),
            pltpu.SemaphoreType.DMA((2, count)),
            pltpu.SemaphoreType.DMA((count,)),
            pltpu.SemaphoreType.DMA((count,)),
            pltpu.SemaphoreType.DMA((count,)),
            pltpu.SemaphoreType.DMA((count,)),
        ]
    return shapes, scratch


def row_sum_kernel(n, x_ref, out_ref, got, send, recv):
    c, w = lax.axis_index("ctx"), lax.axis_index("wshard")
    greet([((c + s) % n, w) for s in range(1, n)])
    copies = [
        remote(x_ref, got.at[c], send.at[s], recv.at[c], ((c + s) % n, w)) for s in range(1, n)
    ]
    for copy in copies:
        copy.start()
    total = x_ref[...]
    for s in range(1, n):
        q = (c + n - s) % n
        remote(x_ref, got.at[q], send.at[s], recv.at[q], (q, w)).wait_recv()
        total = total + got[q]
    out_ref[...] = total
    for copy in copies:
        copy.wait_send()


def sum_rows(n, x, collective_id):
    block = x.reshape(-1, 128)
    return pl.pallas_call(
        functools.partial(row_sum_kernel, n),
        out_shape=jax.ShapeDtypeStruct(block.shape, x.dtype),
        in_specs=[pl.BlockSpec(memory_space=pltpu.VMEM)],
        out_specs=pl.BlockSpec(memory_space=pltpu.VMEM),
        scratch_shapes=[
            pltpu.VMEM((n,) + block.shape, x.dtype),
            pltpu.SemaphoreType.DMA((n,)),
            pltpu.SemaphoreType.DMA((n,)),
        ],
        compiler_params=pltpu.CompilerParams(
            collective_id=collective_id, has_side_effects=True, vmem_limit_bytes=VMEM
        ),
    )(block).reshape(x.shape)


def sum_job(n, x_ref, out_ref, kept, got, send, recv):
    c, w, sib, across = here()
    partners = [(c, sib), (c, across)]
    for level in list(range(1, n.bit_length() - 1)) + [0]:
        reach = 2**level
        partners.append((c + reach - 2 * reach * ((c // reach) % 2), w))
    out_ref[...] = x_ref[...]
    for i, partner in enumerate(partners):
        kept[i] = out_ref[...]
        swap = remote(kept.at[i], got.at[i], send.at[i], recv.at[i], partner)
        swap.start()
        yield
        swap.wait()
        out_ref[...] += got[i]


def sum_scratch(n, shape):
    stages = n.bit_length() + 1
    return [
        pltpu.VMEM((stages,) + shape, jnp.float32),
        pltpu.VMEM((stages,) + shape, jnp.float32),
        pltpu.SemaphoreType.DMA((stages,)),
        pltpu.SemaphoreType.DMA((stages,)),
    ]


def share_job(sources, targets, sems):
    c, w, sib, across = here()
    pending = []
    for j, (src, dst) in enumerate(zip(sources, targets)):
        x_send, x_recv, k_send, k_recv, own_sem = sems[5 * j : 5 * j + 5]
        for q in range(src.shape[0]):
            own = pltpu.make_async_copy(src.at[q], dst.at[q, w], own_sem.at[q])
            to_x = remote(src.at[q], dst.at[q, w], x_send.at[q], x_recv.at[q], (c, across))
            to_k = remote(src.at[q], dst.at[q, w], k_send.at[0, q], k_recv.at[0, q], (c, sib))
            for copy in (to_x, to_k, own):
                copy.start()
            pending += [to_x.wait_send, to_k.wait_send, own.wait]
    yield
    for j, dst in enumerate(targets):
        x_send, x_recv, k_send, k_recv, own_sem = sems[5 * j : 5 * j + 5]
        for q in range(dst.shape[0]):
            got = dst.at[q, across]
            remote(got, got, x_send.at[q], x_recv.at[q], (c, across)).wait_recv()
            out = remote(got, got, k_send.at[1, q], k_recv.at[1, q], (c, sib))
            out.start()
            pending.append(out.wait_send)
    yield
    for j, dst in enumerate(targets):
        x_send, x_recv, k_send, k_recv, own_sem = sems[5 * j : 5 * j + 5]
        for q in range(dst.shape[0]):
            for half, place in ((0, sib), (1, (sib + 2) % 4)):
                got = dst.at[q, place]
                remote(got, got, k_send.at[half, q], k_recv.at[half, q], (c, sib)).wait_recv()
    for wait in pending:
        wait()


def share_shapes(sources):
    shapes, sems = [], []
    for src in sources:
        count = src.shape[0]
        shapes.append(jax.ShapeDtypeStruct((count, 4) + src.shape[1:], src.dtype))
        sems += [
            pltpu.SemaphoreType.DMA((count,)),
            pltpu.SemaphoreType.DMA((count,)),
            pltpu.SemaphoreType.DMA((2, count)),
            pltpu.SemaphoreType.DMA((2, count)),
            pltpu.SemaphoreType.DMA((count,)),
        ]
    return shapes, sems


def advance(*jobs):
    jobs = list(jobs)
    while jobs:
        for job in list(jobs):
            try:
                next(job)
            except StopIteration:
                jobs.remove(job)


class Line:
    def __init__(self, n):
        self.c, self.w, self.sib, self.across = here()
        self.n, self.N = n, n // 2
        self.at, self.side = self.c // 2, self.c % 2
        self.pair = (self.c + 1 - 2 * self.side, self.w)
        self.left = (self.c - 2, self.w)
        self.right = (self.c + 2, self.w)
        self.has_left = self.at > 0
        self.has_right = self.at < self.N - 1

    def greet(self, others=()):
        barrier = pltpu.get_barrier_semaphore()
        signal = lambda d: pl.semaphore_signal(barrier, inc=1, device_id=d, device_id_type=MESH)
        sure = [self.pair] + list(others)
        for device in sure:
            signal(device)
        pl.when(self.has_left)(lambda: signal(self.left))
        pl.when(self.has_right)(lambda: signal(self.right))
        beside = (self.at + self.N - 1) // self.N + (2 * self.N - 2 - self.at) // self.N
        pl.semaphore_wait(barrier, len(sure) + beside)


def scatter_job(line, theirs, mine_of, total, ybuf, zbuf, sems):
    y_send, y_recv, r_send, r_recv, l_send, l_recv = sems
    N, at, side = line.N, line.at, line.side
    wide = jnp.float32

    def both_ways(d):
        return ((at + d, at + d < N), (at - d, at - d >= 0)) if d else ((at, None),)

    def guarded(keep, step):
        if keep is None:
            step()
        else:
            pl.when(keep)(step)

    def y_copy(b, src=None):
        src = ybuf.at[b] if src is None else src
        return remote(src, ybuf.at[b], y_send.at[b], y_recv.at[b], line.pair)

    def r_copy(b, slot):
        return remote(ybuf.at[b], zbuf.at[slot], r_send.at[b], r_recv.at[b], line.right)

    def l_copy(b, slot):
        return remote(ybuf.at[b], zbuf.at[slot], l_send.at[b], l_recv.at[b], line.left)

    for d in range(N - 1, -1, -1):
        for b, keep in both_ways(d):

            def first(b=b):
                y_copy(b, theirs(b)).start()

            guarded(keep, first)
        yield
    for d in range(N - 1, 0, -1):
        for b, keep, ahead in ((at + d, at + d < N, True), (at - d, at - d >= 0, False)):

            def relay(b=b, ahead=ahead):
                mine = mine_of(b)
                y_copy(b).wait_recv()
                mine = mine + ybuf[b].astype(wide)
                came = line.has_left if ahead else line.has_right

                @pl.when(came)
                def _():
                    (r_copy if ahead else l_copy)(b, b).wait_recv()
                    ybuf[b] = (mine + zbuf[b].astype(wide)).astype(ybuf.dtype)

                @pl.when(jnp.logical_not(came))
                def _():
                    ybuf[b] = mine.astype(ybuf.dtype)

                if ahead:
                    pl.when(b == at + 1)(lambda: r_copy(b, b).start())
                    pl.when(b > at + 1)(lambda: r_copy(b, b).start())
                else:
                    pl.when(b == at - 1)(lambda: l_copy(b, N).start())
                    pl.when(b < at - 1)(lambda: l_copy(b, b).start())

            guarded(keep, relay)
        yield
    mine = mine_of(at)
    y_copy(at).wait_recv()
    total[...] = mine + ybuf[at].astype(wide)

    @pl.when(line.has_left)
    def _():
        r_copy(at, at).wait_recv()
        total[...] += zbuf[at].astype(wide)

    @pl.when(line.has_right)
    def _():
        l_copy(at, N).wait_recv()
        total[...] += zbuf[N].astype(wide)

    for d in range(N):
        for b, keep in both_ways(d):
            guarded(keep, lambda b=b: y_copy(b).wait_send())
    for d in range(1, N):
        pl.when(at + d < N)(lambda d=d: r_copy(at + d, at + d).wait_send())
        pl.when(at - d >= 0)(lambda d=d: l_copy(at - d, at - d).wait_send())


def scatter_line_job(line, value, stage, slots, pair_slot, total, sems):
    r_send, r_recv, l_send, l_recv, p_send, p_recv = sems
    n, N, at, side = line.n, line.N, line.at, line.side
    wide = jnp.float32

    def copy(q, slot, ahead):
        send, recv = (r_send, r_recv) if ahead else (l_send, l_recv)
        device = line.right if ahead else line.left
        return remote(stage.at[q], slots.at[slot], send.at[q], recv.at[q], device)

    for d in range(N - 1, 0, -1):
        for b, keep, ahead in ((at + d, at + d < N, True), (at - d, at - d >= 0, False)):

            def relay(b=b, ahead=ahead):
                came = line.has_left if ahead else line.has_right
                for y in range(2):
                    q = 2 * b + y

                    @pl.when(came)
                    def _(q=q, y=y):
                        copy(q, q, ahead).wait_recv()
                        stage[q] = (value(b, y) + slots[q].astype(wide)).astype(stage.dtype)

                    @pl.when(jnp.logical_not(came))
                    def _(q=q, y=y):
                        stage[q] = value(b, y).astype(stage.dtype)

                    if ahead:
                        copy(q, q, True).start()
                    else:
                        pl.when(b == at - 1)(lambda q=q, y=y: copy(q, n + y, False).start())
                        pl.when(b < at - 1)(lambda q=q: copy(q, q, False).start())

            pl.when(keep)(relay)
        yield

    def reach(y):
        q, y_slot = 2 * at + y, n + y
        pl.when(line.has_left)(lambda: copy(q, q, True).wait_recv())
        pl.when(line.has_right)(lambda: copy(q, y_slot, False).wait_recv())
        left = jnp.where(line.has_left, slots[q].astype(wide), 0.0)
        right = jnp.where(line.has_right, slots[y_slot].astype(wide), 0.0)
        return value(at, y) + left + right

    other = 2 * at + 1 - side
    stage[other] = reach(1 - side).astype(stage.dtype)
    swap = remote(stage.at[other], pair_slot, p_send, p_recv, line.pair)
    swap.start()
    mine = reach(side)
    yield
    swap.wait()
    total[...] = mine + pair_slot[...].astype(wide)
    for d in range(1, N):
        for y in range(2):
            pl.when(at + d < N)(lambda d=d, y=y: copy(2 * (at + d) + y, 0, True).wait_send())
            pl.when(at - d >= 0)(lambda d=d, y=y: copy(2 * (at - d) + y, 0, False).wait_send())


def gather_job(line, own, out, sems, use=None):
    r_send, l_send, y_send, recv, own_sem = sems
    n, N, at, side, c = line.n, line.N, line.at, line.side, line.c
    local = pltpu.make_async_copy(own, out(c), own_sem)
    local.start()

    def send(src, q, sem, device):
        return remote(src, out(q), sem.at[q // 2], recv.at[q], device)

    use = use or (lambda q: None)
    pair = c + 1 - 2 * side

    def other(d):
        for q, keep in ((pair - 2 * d, at - d >= 0), (pair + 2 * d, at + d < N))[: 1 + (d > 0)]:

            def take(q=q):
                send(out(q), q, y_send, line.pair).wait_recv()
                use(q)

            pl.when(keep)(take)

    pl.when(line.has_right)(lambda: send(own, c, r_send, line.right).start())
    pl.when(line.has_left)(lambda: send(own, c, l_send, line.left).start())
    send(own, c, y_send, line.pair).start()
    yield
    local.wait()
    use(c)
    for d in range(1, N):
        for q, keep, ahead in ((c - 2 * d, at - d >= 0, True), (c + 2 * d, at + d < N, False)):

            def relay(q=q, ahead=ahead):
                got = out(q)
                send(got, q, y_send, line.pair).wait_recv()
                if ahead:
                    pl.when(line.has_right)(lambda: send(got, q, r_send, line.right).start())
                else:
                    pl.when(line.has_left)(lambda: send(got, q, l_send, line.left).start())
                send(got, q, y_send, line.pair).start()
                use(q)

            pl.when(keep)(relay)
        yield
    for d in range(N):
        other(d)
    for b in range(N):
        q = 2 * b + side
        got = out(q)
        send(got, q, y_send, line.pair).wait_send()
        pl.when(jnp.logical_and(b <= at, line.has_right))(
            lambda q=q, got=got: send(got, q, r_send, line.right).wait_send()
        )
        pl.when(jnp.logical_and(b >= at, line.has_left))(
            lambda q=q, got=got: send(got, q, l_send, line.left).wait_send()
        )


def gather_pair_job(line, own, out, sems):
    r_send, l_send, y_send, recv, own_sem = sems
    n, N, at, c = line.n, line.N, line.at, line.c
    local = pltpu.make_async_copy(own, out(c), own_sem)
    local.start()

    def send(src, q, sem, device):
        return remote(src, out(q), sem.at[q], recv.at[q], device)

    def ahead(src, q, act):
        pl.when(line.has_right)(lambda: act(send(src, q, r_send, line.right)))

    def back(src, q, act):
        pl.when(line.has_left)(lambda: act(send(src, q, l_send, line.left)))

    start = lambda copy: copy.start()
    to_pair = remote(own, out(c), y_send.at[0], recv.at[c], line.pair)
    to_pair.start()
    ahead(own, c, start)
    back(own, c, start)
    yield
    local.wait()
    q = line.pair[0]
    got = out(q)
    send(got, q, r_send, line.pair).wait_recv()
    ahead(got, q, start)
    back(got, q, start)
    yield
    for d in range(1, N):
        for b, keep, forward in ((at - d, at - d >= 0, True), (at + d, at + d < N, False)):

            def relay(b=b, forward=forward):
                for y in range(2):
                    got = out(2 * b + y)
                    send(got, 2 * b + y, r_send, line.pair).wait_recv()
                    (ahead if forward else back)(got, 2 * b + y, start)

            pl.when(keep)(relay)
        yield
    to_pair.wait_send()
    done = lambda copy: copy.wait_send()
    for b in range(N):
        for y in range(2):
            q = 2 * b + y
            pl.when(b <= at)(lambda q=q: ahead(out(q), q, done))
            pl.when(b >= at)(lambda q=q: back(out(q), q, done))


def minor_rows(rows):
    return rows // 8


def scatter_steps(line, product, rows, total, made, scratch):
    N, side = line.N, line.side
    if len(made.shape) == 3:

        def theirs(b):
            made[b] = product(2 * b * rows + (1 - side) * rows, rows).astype(made.dtype)
            return made.at[b]

        yield from scatter_job(
            line,
            theirs,
            lambda b: product(2 * b * rows + side * rows, rows),
            total,
            *scratch[:2],
            scratch[2:8],
        )
        return
    few = minor_rows(rows)
    many = rows - few
    ybuf, zbuf = scratch[:2]
    stage, slots, pair_slot = scratch[8:11]
    wide = jnp.float32

    def theirs(b):
        both = product(2 * b * rows, 2 * rows).astype(made.dtype)
        made[b] = both.reshape(2, rows, D)
        return made.at[b, 1 - side, pl.ds(0, many)]

    minor = scatter_line_job(
        line,
        lambda b, y: made[b, y, many:, :].astype(wide),
        stage,
        slots,
        pair_slot,
        total.at[pl.ds(many, few)],
        scratch[11:17],
    )
    main = scatter_job(
        line,
        theirs,
        lambda b: made[b, side, :many, :].astype(wide),
        total.at[pl.ds(0, many)],
        ybuf,
        zbuf,
        scratch[2:8],
    )
    for _ in range(N):
        next(main)
        yield
    next(minor)
    for _ in range(N - 1):
        next(minor, None)
        next(main)
        yield
    finish(minor)
    finish(main)


def gather_steps(line, own, out, rows, scratch, use=None):
    few = minor_rows(rows)
    many = rows - few
    minor = gather_pair_job(
        line, own.at[pl.ds(many, few)], lambda q: out(q, many, few), scratch[5:10]
    )
    main = gather_job(line, own.at[pl.ds(0, many)], lambda q: out(q, 0, many), scratch[:5], use)
    next(minor)
    next(main)
    yield
    next(minor)
    for _ in range(line.N - 1):
        next(minor)
        next(main)
        yield
    finish(minor)
    finish(main)


GATHER = 10


def scatter_shapes(n, rows, roomy):
    N = n // 2
    few = minor_rows(rows) if roomy else 0
    many = rows - few
    low, dma = jnp.bfloat16, pltpu.SemaphoreType.DMA
    made = pltpu.VMEM((N, 2, rows, D) if roomy else (N, rows, D), low)
    scratch = [
        pltpu.VMEM((N, many, D), low),
        pltpu.VMEM((N + 1, many, D), low),
    ] + [dma((N,))] * 6
    if roomy:
        scratch += [
            pltpu.VMEM((n, few, D), low),
            pltpu.VMEM((n + 2, few, D), low),
            pltpu.VMEM((few, D), low),
        ]
        scratch += [dma((n,))] * 4 + [dma, dma]
    return made, scratch


def gather_scratch(n):
    N = n // 2
    dma = pltpu.SemaphoreType.DMA
    return [dma((N,)), dma((N,)), dma((N,)), dma((n,)), dma] + [
        dma((n,)),
        dma((n,)),
        dma((1,)),
        dma((n,)),
        dma,
    ]


def rms_factor(values):
    return lax.rsqrt(jnp.mean(values * values, axis=1, keepdims=True) + norm_eps)


def rms_back(values, gain, grad):
    factor = rms_factor(values)
    scaled = grad * gain
    inner = jnp.mean(scaled * values, axis=1, keepdims=True)
    d_gain = jnp.sum(grad * (values * factor), axis=0, keepdims=True)
    return factor * scaled - values * (factor * factor * factor * inner), d_gain


def matmul_rows(*pairs):
    def product(first, count):
        total = 0.0
        for left, right in pairs:
            part = left[pl.ds(pl.multiple_of(first, 16), count), :]
            if right.shape[0] == left.shape[1]:
                total = total + plain(part, right[...])
            else:
                total = total + cols_by_cols(part, right[...])
        return total

    return product


def finish(job):
    for _ in job:
        pass


def start_kernel(plan, n, x, w_in, w_up, w_mix, w_down, *refs):
    tokens, in_all, shared_all, up_some, mix_all, down_some = refs[:6]
    in_low, shared_low, up_low, mix_low, down_low = refs[6:11]
    t_sems = refs[11 : 11 + GATHER]
    a_send, a_recv, x_send, x_recv, k_send, k_recv, own_sem = refs[11 + GATHER :]
    line = Line(n)
    c, w, sib, across = line.c, line.w, line.sib, line.across
    greet([((c + s) % n, w) for s in range(1, n)] + [(c, sib), (c, across)])
    R, B, G = plan.R, plan.B, FF // n
    low = jnp.bfloat16
    place = lambda q, first, count: tokens.at[q, pl.ds(first, count)]
    inputs = gather_steps(line, x, place, x.shape[0], t_sems)
    next(inputs)
    passed, pending = [], []

    def pass_on(number, view, src=None):
        src = view(w) if src is None else src
        to_x = remote(src, view(w), x_send.at[number], x_recv.at[number], (c, across))
        to_k = remote(src, view(w), k_send.at[0, number], k_recv.at[0, number], (c, sib))
        to_x.start()
        to_k.start()
        pending.append(to_x)
        pending.append(to_k)
        passed.append((number, view))

    mix_low[...] = w_mix[...].astype(low)
    pass_on(2 * n, lambda place: mix_all.at[0, place], mix_low)
    shared_low[...] = jnp.zeros_like(shared_low)
    shared_low[:, : END - BC_AT] = w_in[:, BC_AT:END].astype(low)
    for p in range(n):
        if p < plan.attn:
            g = plan.kv_of(p)
            in_low[p, :, :R] = w_in[:, p * R : (p + 1) * R].astype(low)
            in_low[p, :, B : B + HD] = w_in[:, K_AT + g * HD : K_AT + (g + 1) * HD].astype(low)
            in_low[p, :, B + HD : B + 2 * HD] = w_in[
                :, V_AT + g * HD : V_AT + (g + 1) * HD
            ].astype(low)
            if B + 2 * HD < plan.A:
                rest = plan.A - B - 2 * HD
                in_low[p, :, B + 2 * HD :] = jnp.zeros((in_low.shape[1], rest), low)
        else:
            j = p - plan.attn
            in_low[p, :, :R] = w_in[:, Z_AT + j * R : Z_AT + (j + 1) * R].astype(low)
            in_low[p, :, B : B + R] = w_in[:, X_AT + j * R : X_AT + (j + 1) * R].astype(low)
            if B + R < plan.A:
                in_low[p, :, B + R :] = jnp.zeros((in_low.shape[1], plan.A - B - R), low)

    def column_copies(s):
        p = (c + s) % n
        ends = ((in_low.at[p], in_all), (shared_low, shared_all))
        return [
            remote(src, dst.at[c, w], a_send.at[k, s], a_recv.at[k, c], (p, w))
            for k, (src, dst) in enumerate(ends)
        ]

    def send_columns(steps):
        for s in steps:
            for copy in column_copies(s):
                copy.start()
                pending.append(copy)

    in_view = lambda q: lambda place: in_all.at[q, place]
    shared_view = lambda q: lambda place: shared_all.at[q, place]

    def take_columns(steps):
        for s in steps:
            q = (c + n - s) % n
            for k, view in ((0, in_view), (1, shared_view)):
                got = view(q)(w)
                remote(got, got, a_send.at[k, s], a_recv.at[k, q], (q, w)).wait_recv()
                pass_on(k * n + q, view(q))

    done = [0]

    def seconds(upto):
        while done[0] < min(upto, len(passed)):
            number, view = passed[done[0]]
            got = view(across)
            remote(got, got, x_send.at[number], x_recv.at[number], (c, across)).wait_recv()
            out = remote(got, got, k_send.at[1, number], k_recv.at[1, number], (c, sib))
            out.start()
            pending.append(out)
            done[0] += 1

    cuts = [round(1 + (n - 1) * i / 3) for i in range(4)]
    parts = [range(cuts[i], cuts[i + 1]) for i in range(3)]
    send_columns(parts[0])
    pass_on(c, in_view(c), in_low.at[c])
    pass_on(n + c, shared_view(c), shared_low)
    down_low[...] = w_down[...].astype(low)
    for p in range(n):
        up_low[p, :, :G] = w_up[:, p * G : (p + 1) * G].astype(low)
        up_low[p, :, G:] = w_up[:, FF + p * G : FF + (p + 1) * G].astype(low)
    locals_started = []
    own = (
        (in_low.at[c], in_all.at[c, w]),
        (shared_low, shared_all.at[c, w]),
        (mix_low, mix_all.at[0, w]),
        (up_low.at[c], up_some.at[c]),
        (down_low, down_some.at[0]),
    )
    for i, (src, dst) in enumerate(own):
        copy = pltpu.make_async_copy(src, dst, own_sem.at[i])
        copy.start()
        locals_started.append(copy)
    for step in range(3):
        for _ in range(line.N // 4):
            next(inputs, None)
        if step < 2:
            send_columns(parts[step + 1])
        else:
            for s in range(1, n):
                p = (c + s) % n
                out = remote(
                    up_low.at[p], up_some.at[c], a_send.at[2, s], a_recv.at[2, c], (p, w)
                )
                out.start()
                pending.append(out)
        take_columns(parts[step])
        seconds(len(passed) - 4)
    finish(inputs)
    seconds(len(passed))
    for s in range(1, n):
        q = (c + n - s) % n
        got = up_some.at[q]
        remote(got, got, a_send.at[2, s], a_recv.at[2, q], (q, w)).wait_recv()
    for number, view in passed:
        for half, place in ((0, sib), (1, (sib + 2) % 4)):
            got = view(place)
            remote(got, got, k_send.at[half, number], k_recv.at[half, number], (c, sib)).wait_recv()
    for copy in locals_started:
        copy.wait()
    for out in pending:
        out.wait_send()


def branch_kernel(n, refs_in, refs_out, scratch):
    left, right, source, gain, upstream, up, down = refs_in
    middle, active, grad_gates, normed, up_all, down_all = refs_out
    line = Line(n)
    line.greet([(line.c, line.sib), (line.c, line.across)])
    rows = source.shape[0]
    (total, own, made), (flow, gather, extra) = scratch[:3], scratch[3:]
    share = share_job((up, down), (up_all, down_all), extra)
    main = scatter_steps(line, matmul_rows((left, right)), rows, total, made, flow)
    next(main)
    next(share)
    finish(main)
    value = source[...].astype(jnp.float32) + total[...]
    middle[...] = value
    own[...] = (value * rms_factor(value) * gain[...]).astype(own.dtype)
    place = lambda q, first, count: normed.at[q, pl.ds(first, count)]

    half = grad_gates.shape[1] // 2

    def use(q):
        low = active.dtype
        gate_up = plain(normed[q], up_all[...].reshape(D, -1))
        gate, other = gate_up[:, :half], gate_up[:, half:]
        at = ring_place(n, line.w, q)
        grad = cols_by_cols(upstream[at], down_all[...].reshape(-1, D))
        sig = jax.nn.sigmoid(gate)
        passed = gate * sig
        active[pl.ds(pl.multiple_of(at * rows, rows), rows), :] = (passed * other).astype(low)
        here_rows = pl.ds(pl.multiple_of(q * rows, rows), rows)
        grad_gates[here_rows, :half] = (grad * other * (sig * (1.0 + gate * (1.0 - sig)))).astype(low)
        grad_gates[here_rows, half:] = (grad * passed).astype(low)

    fused = active.shape[0] == n * rows
    spread_out = gather_steps(
        line, own, place, rows, gather, use if fused else None
    )
    next(spread_out)
    next(share)
    finish(share)
    finish(spread_out)


def feed_back_kernel(n, refs_in, refs_out, scratch):
    left, right, cotangent, middle, gain, active, w_mix, w_down, normed, upstream, up, down = refs_in
    grad, d_gain, made, late, low_all, up_sum, down_sum = refs_out
    line = Line(n)
    line.greet([(line.c, line.sib), (line.c, line.across)])
    rows = cotangent.shape[0]
    (total, own, terms), (flow, gather, extra) = scratch[:3], scratch[3:]
    both = active.shape[0] == n * rows
    if both:
        (up, down, normed_part, upstream_part, part_sem), extra = extra[:5], extra[5:]
        width = D // n
        height = down.shape[2]

        def fetch(s):
            columns = pl.ds(pl.multiple_of((line.c + s) % n * width, 128), width)
            return [
                pltpu.make_async_copy(a.at[:, columns], b.at[s % 2], part_sem.at[i, s % 2])
                for i, (a, b) in enumerate(((normed, normed_part), (upstream, upstream_part)))
            ]

        def piece(s):
            q = (line.c + s) % n
            for copy in fetch(s):
                copy.wait()
            if s:
                for copy in fetch((s + 1) % n):
                    copy.start()
            part = rows_by_rows(normed_part[s % 2], left[...])
            up[q] = part.astype(up.dtype).reshape(up.shape[1:])
            part = rows_by_rows(active[...], upstream_part[s % 2]).astype(down.dtype)
            columns = pl.ds(pl.multiple_of(q * width, 128), width)
            for k in range(4):
                down[0, k, :, columns] = part[k * height : (k + 1) * height]

        for copy in fetch(1):
            copy.start()
    else:
        piece = lambda s: None
    sums = Collect(n, ("rows", "rows"), (up, down), (up_sum, down_sum), extra)
    main = scatter_steps(line, matmul_rows((left, right)), rows, total, terms, flow)
    for _ in range(line.N):
        next(main)
    steps = sums.steps
    made_count = [0]

    def advance():
        at = made_count[0]
        if at < len(steps):
            piece(steps[at])
            sums.send(steps[at])
        if 0 <= at - 1 < len(steps):
            sums.cross(steps[at - 1])
        made_count[0] += 1

    for i in range(line.N - 1):
        advance()
        if i:
            advance()
        next(main)
    finish(main)
    back, gain_row = rms_back(middle[...], gain[...], total[...])
    value = cotangent[...].astype(jnp.float32) + back
    grad[...] = value
    d_gain[...] = jnp.broadcast_to(gain_row, d_gain.shape)
    own[...] = value.astype(own.dtype)
    place = lambda q, first, count: low_all.at[q, pl.ds(first, count)]

    def use(q):
        block = pl.ds(pl.multiple_of(q * rows, rows), rows)
        made[block, :] = cols_by_cols(low_all[q], w_mix[...]).astype(made.dtype)
        late[block, :] = plain(active[block, :], w_down[...]).astype(late.dtype)

    spread_out = gather_steps(
        line, own, place, rows, gather, use if both else None
    )
    next(spread_out)
    for _ in range(line.N - 1):
        advance()
        next(spread_out)
    while made_count[0] <= len(steps):
        advance()
    finish(spread_out)
    for s in sums.steps:
        sums.close(s)
    sums.end()


SUMS = ("cols", "cols", "rows")


def source_back_kernel(n, refs_in, refs_out, scratch):
    (left, left_two, right, right_two, source, grad_middle, gain, vector, up) = refs_in[:9]
    mixed, gain_column, unit, branch, w_in, w_shared, w_mix = refs_in[9:]
    grad, vector_sum, up_home, in_sum, shared_sum, mix_sum = refs_out
    line = Line(n)
    others = [((line.c + s) % n, line.w) for s in range(1, n)]
    greet(others + [(line.c, line.sib), (line.c, line.across)])
    rows = source.shape[0]
    (total, _, made), (flow, _, extra) = scratch[:3], scratch[3:]
    both = unit.shape[0] == n * rows
    if both:
        (w_in, w_shared, w_mix, unit_part, branch_part, part_sem, local), extra = extra[:7], extra[7:]
        width = D // n
        height = w_mix.shape[2]
        local[...] = vector[...]

        def fetch(s):
            columns = pl.ds(pl.multiple_of((line.c + s) % n * width, 128), width)
            return [
                pltpu.make_async_copy(a.at[:, columns], b.at[s % 2], part_sem.at[i, s % 2])
                for i, (a, b) in enumerate(((unit, unit_part), (branch, branch_part)))
            ]

        def piece(s):
            q = (line.c + s) % n
            for copy in fetch(s):
                copy.wait()
            if s:
                for copy in fetch((s + 1) % n):
                    copy.start()
            place = pl.ds(pl.multiple_of(q * width, 128), width)
            scale = gain_column[place, :]
            part = rows_by_rows(unit_part[s % 2], left[...])
            w_in[q] = (part * scale).astype(w_in.dtype).reshape(w_in.shape[1:])
            two = rows_by_rows(unit_part[s % 2], left_two[...])
            w_shared[q] = (two * scale).astype(w_shared.dtype).reshape(w_shared.shape[1:])
            each = jnp.concatenate(
                [
                    part * right[place, :].astype(jnp.float32),
                    two * right_two[place, :].astype(jnp.float32),
                ],
                axis=1,
            )
            ones = jnp.ones((8, each.shape[1]), jnp.bfloat16)
            row = sum(cols_by_cols(ones, some) for some in pieces(each, 3))
            for i in range(width // 128):
                at = q * (width // 128) + i
                local[pl.ds(at, 1), :] = row[0:1, i * 128 : (i + 1) * 128]
            part = rows_by_rows(mixed[...], branch_part[s % 2]).astype(w_mix.dtype)
            for k in range(4):
                w_mix[0, k, :, place] = part[k * height : (k + 1) * height]

        for copy in fetch(1):
            copy.start()
    else:
        local = vector
        piece = lambda s: None
    sums = Collect(n, SUMS, (w_in, w_shared, w_mix), (in_sum, shared_sum, mix_sum), extra[:-6])
    vectors = sum_job(n, local, vector_sum, *extra[-6:-2])
    home = home_job(n, up, up_home, *extra[-2:])
    product = matmul_rows((left, right), (left_two, right_two))
    main = scatter_steps(line, product, rows, total, made, flow)
    steps = sums.steps
    next(home)
    made_count = [0]

    def advance(more=1):
        for _ in range(more):
            at = made_count[0]
            if at < len(steps):
                piece(steps[at])
                sums.send(steps[at])
            if 0 <= at - 1 < len(steps):
                sums.cross(steps[at - 1])
            if 0 <= at - 4 < len(steps):
                sums.close(steps[at - 4])
            made_count[0] += 1

    for _ in range(line.N):
        next(main)
        advance(2)
    next(vectors)
    for _ in main:
        next(vectors, None)
        advance()
    advance(len(steps) + 4 - made_count[0])
    finish(vectors)
    back, _ = rms_back(source[...].astype(jnp.float32), gain[...], total[...])
    grad[...] = grad_middle[...] + back
    finish(home)
    sums.end()


def flow_call(
    kernel, n, rows, args, outs, gathers, away, extra, collective_id, near=False, far_args=()
):
    inside = pl.BlockSpec(memory_space=pltpu.VMEM)
    outside = pl.BlockSpec(memory_space=pl.ANY)
    side_args, side_shapes, side_scratch = extra
    shapes = list(outs)
    specs = [inside] * len(outs)
    scratch = [
        pltpu.VMEM((rows, D), jnp.float32),
        pltpu.VMEM((rows, D) if gathers else (16, 128), jnp.bfloat16),
    ]
    made, flow = scatter_shapes(n, rows, args[0].shape[0] <= 1024)
    gather = []
    if gathers:
        shapes.append(jax.ShapeDtypeStruct((n, rows, D), jnp.bfloat16))
        specs.append(inside if near else outside)
        gather = gather_scratch(n)
    scratch = scratch + [made] + flow + gather + list(side_scratch)
    ends = 3 + len(flow), 3 + len(flow) + len(gather)
    side = outside if away else inside
    in_specs = [inside] * len(args) + [outside] * len(far_args) + [side] * len(side_args)
    specs = specs + [inside if near else side] * len(side_shapes)
    shapes = shapes + list(side_shapes)
    first, second = len(in_specs), len(in_specs) + len(specs)

    def run(*refs):
        parts = refs[second:]
        groups = parts[3 : ends[0]], parts[ends[0] : ends[1]], parts[ends[1] :]
        kernel(n, refs[:first], refs[first:second], tuple(parts[:3]) + groups)

    return pl.pallas_call(
        run,
        out_shape=tuple(shapes),
        in_specs=in_specs,
        out_specs=tuple(specs),
        scratch_shapes=scratch,
        cost_estimate=pl.CostEstimate(flops=0, bytes_accessed=2 * 10**8, transcendentals=0),
        compiler_params=pltpu.CompilerParams(
            collective_id=collective_id, has_side_effects=True, vmem_limit_bytes=VMEM
        ),
    )(*args, *far_args, *side_args)


def start_call(plan, n, x, w_in, w_up, w_mix, w_down, collective_id):
    rows = w_in.shape[0]
    low = jnp.bfloat16
    G = FF // n
    shapes = (
        jax.ShapeDtypeStruct((n,) + x.shape, low),
        jax.ShapeDtypeStruct((n, 4, rows, plan.A), low),
        jax.ShapeDtypeStruct((n, 4, rows, plan.K), low),
        jax.ShapeDtypeStruct((n, rows, 2 * G), low),
        jax.ShapeDtypeStruct((1, 4) + w_mix.shape, low),
        jax.ShapeDtypeStruct((1,) + w_down.shape, low),
    )
    dma = pltpu.SemaphoreType.DMA
    outside = pl.BlockSpec(memory_space=pl.ANY)
    inside = pl.BlockSpec(memory_space=pltpu.VMEM)
    blocks = 2 * n + 1
    outs = pl.pallas_call(
        functools.partial(start_kernel, plan, n),
        out_shape=shapes,
        in_specs=[outside] + [inside] * 4,
        out_specs=(outside,) * 6,
        scratch_shapes=[
            pltpu.VMEM((n, rows, plan.A), low),
            pltpu.VMEM((rows, plan.K), low),
            pltpu.VMEM((n, rows, 2 * G), low),
            pltpu.VMEM(w_mix.shape, low),
            pltpu.VMEM(w_down.shape, low),
        ]
        + gather_scratch(n)
        + [dma((3, n)), dma((3, n))]
        + [dma((blocks,)), dma((blocks,)), dma((2, blocks)), dma((2, blocks))]
        + [dma((5,))],
        cost_estimate=pl.CostEstimate(flops=0, bytes_accessed=2 * 10**8, transcendentals=0),
        compiler_params=pltpu.CompilerParams(
            collective_id=collective_id, has_side_effects=True, vmem_limit_bytes=VMEM
        ),
    )(x, w_in, w_up, w_mix, w_down)
    flat = lambda o: o.reshape(-1, o.shape[-1])
    tokens, in_all, shared_all, up_some, mix_all, down_some = outs
    return flat(tokens), flat(in_all), flat(shared_all), up_some, flat(mix_all), down_some


def mm(left, right):
    return jnp.dot(
        left.astype(jnp.bfloat16), right.astype(jnp.bfloat16), preferred_element_type=jnp.float32
    )


def mm_nt(left, right):
    return cols_by_cols(left.astype(jnp.bfloat16), right.astype(jnp.bfloat16))


def mm_tn(left, right):
    return rows_by_rows(left.astype(jnp.bfloat16), right.astype(jnp.bfloat16))


def pieces(values, count):
    found = []
    for _ in range(count):
        part = values.astype(jnp.bfloat16)
        found.append(part)
        values = values - part.astype(jnp.float32)
    return found


def by_marks(values, marks, count=2):
    return plain(
        jnp.concatenate(pieces(values, count), axis=1), jnp.concatenate([marks] * count, axis=0)
    )


def marks_by(marks, values, count=3):
    return plain(
        jnp.concatenate([marks] * count, axis=1), jnp.concatenate(pieces(values, count), axis=0)
    )


def iota(shape, axis):
    return lax.broadcasted_iota(jnp.int32, shape, axis)


def rope_tables(length):
    half = HD // 2
    frequency = rope_base ** (-jnp.arange(half, dtype=jnp.float32) / half)
    angles = jnp.arange(length).astype(jnp.float32)[:, None] * frequency[None, :]
    cosine, sine = jnp.cos(angles), jnp.sin(angles)
    return (
        jnp.concatenate([cosine, cosine], axis=1),
        jnp.concatenate([-sine, sine], axis=1),
    )


def turned(values, cosine, sine):
    return values * cosine + pltpu.roll(values, HD // 2, 1) * sine


def attn_stack(plan, q_ref, cosine, sine):
    heads = [
        turned(q_ref[:, h * HD : (h + 1) * HD], cosine, sine).astype(jnp.bfloat16)
        for h in range(plan.ha)
    ]
    return jnp.concatenate(heads, axis=0)


def by_extent(step, length, run):
    parts = 4
    per = length // CHUNK // parts
    for part in range(parts):
        pl.when(step // per == part)(functools.partial(run, (part + 1) * per * CHUNK))


def attn_softmax(stack, keys, at):
    scores = cols_by_cols(stack, keys) * (1.0 / math.sqrt(HD))
    row = iota(scores.shape, 0) & (CHUNK - 1)
    scores = jnp.where(iota(scores.shape, 1) <= row + at, scores, masked_score)
    weights = jnp.exp(scores - jnp.max(scores, axis=1, keepdims=True))
    return weights * (1.0 / jnp.sum(weights, axis=1, keepdims=True))


def attn_fwd_kernel(plan, q_ref, k_ref, v_ref, cos_ref, sin_ref, out_ref, keys, values):
    step = pl.program_id(0)

    @pl.when(step == 0)
    def _():
        keys[...] = turned(k_ref[...], cos_ref[...], sin_ref[...]).astype(jnp.bfloat16)
        values[...] = v_ref[...].astype(jnp.bfloat16)

    at = pl.multiple_of(step * CHUNK, CHUNK)
    rows = pl.ds(at, CHUNK)
    stack = attn_stack(plan, q_ref, cos_ref[rows, :], sin_ref[rows, :])

    def run(extent):
        probs = attn_softmax(stack, keys[:extent, :], at)
        made = mm(probs, values[:extent, :])
        for h in range(plan.ha):
            out_ref[:, h * HD : (h + 1) * HD] = made[h * CHUNK : (h + 1) * CHUNK]

    by_extent(step, keys.shape[0], run)


def attn_fwd(plan, proj, tables):
    length = proj.shape[0]
    whole = lambda i: (0, 0)
    return pl.pallas_call(
        functools.partial(attn_fwd_kernel, plan),
        grid=(length // CHUNK,),
        out_shape=jax.ShapeDtypeStruct((length, plan.R), jnp.float32),
        in_specs=[
            pl.BlockSpec((CHUNK, plan.R), lambda i: (i, 0)),
            pl.BlockSpec((length, HD), lambda i: (0, plan.B // HD)),
            pl.BlockSpec((length, HD), lambda i: (0, plan.B // HD + 1)),
            pl.BlockSpec((length, HD), whole),
            pl.BlockSpec((length, HD), whole),
        ],
        out_specs=pl.BlockSpec((CHUNK, plan.R), lambda i: (i, 0)),
        scratch_shapes=[pltpu.VMEM((length, HD), jnp.bfloat16)] * 2,
        compiler_params=pltpu.CompilerParams(vmem_limit_bytes=VMEM),
    )(proj, proj, proj, *tables)


def attn_bwd_kernel(
    plan, q_ref, k_ref, v_ref, cos_ref, sin_ref, grad_ref, slab_ref, keys, values, grad_k, grad_v
):
    step = pl.program_id(0)
    scale = 1.0 / math.sqrt(HD)

    @pl.when(step == 0)
    def _():
        keys[...] = turned(k_ref[...], cos_ref[...], sin_ref[...]).astype(jnp.bfloat16)
        values[...] = v_ref[...].astype(jnp.bfloat16)
        grad_k[...] = jnp.zeros_like(grad_k)
        grad_v[...] = jnp.zeros_like(grad_v)
        slab_ref[...] = jnp.zeros_like(slab_ref)

    at = pl.multiple_of(step * CHUNK, CHUNK)
    rows = pl.ds(at, CHUNK)
    cosine, sine = cos_ref[rows, :], sin_ref[rows, :]
    stack = attn_stack(plan, q_ref, cosine, sine)
    grads = jnp.concatenate([grad_ref[:, h * HD : (h + 1) * HD] for h in range(plan.ha)], axis=0)

    def run(extent):
        probs = attn_softmax(stack, keys[:extent, :], at)
        grad_probs = cols_by_cols(grads, values[:extent, :])
        delta = jnp.sum(probs * grad_probs, axis=1, keepdims=True)
        grad_scores = (probs * (grad_probs - delta)).astype(jnp.bfloat16)
        grad_q = mm(grad_scores, keys[:extent, :]) * scale
        for h in range(plan.ha):
            slab_ref[rows, h * HD : (h + 1) * HD] = turned(
                grad_q[h * CHUNK : (h + 1) * CHUNK], cosine, -sine
            ).astype(jnp.bfloat16)
        grad_k[:extent, :] += mm_tn(grad_scores, stack)
        grad_v[:extent, :] += mm_tn(probs, grads)

    by_extent(step, keys.shape[0], run)

    @pl.when(step == pl.num_programs(0) - 1)
    def _():
        slab_ref[:, plan.B : plan.B + HD] = turned(
            grad_k[...] * scale, cos_ref[...], -sin_ref[...]
        ).astype(jnp.bfloat16)
        slab_ref[:, plan.B + HD : plan.B + 2 * HD] = grad_v[...].astype(jnp.bfloat16)


def attn_bwd(plan, proj, tables, grad):
    length = proj.shape[0]
    whole = lambda i: (0, 0)
    return pl.pallas_call(
        functools.partial(attn_bwd_kernel, plan),
        grid=(length // CHUNK,),
        out_shape=jax.ShapeDtypeStruct((length, plan.A), jnp.bfloat16),
        in_specs=[
            pl.BlockSpec((CHUNK, plan.R), lambda i: (i, 0)),
            pl.BlockSpec((length, HD), lambda i: (0, plan.B // HD)),
            pl.BlockSpec((length, HD), lambda i: (0, plan.B // HD + 1)),
            pl.BlockSpec((length, HD), whole),
            pl.BlockSpec((length, HD), whole),
            pl.BlockSpec((CHUNK, plan.R), lambda i: (i, 0)),
        ],
        out_specs=pl.BlockSpec((length, plan.A), whole),
        scratch_shapes=[pltpu.VMEM((length, HD), jnp.bfloat16)] * 2
        + [pltpu.VMEM((length, HD), jnp.float32)] * 2,
        compiler_params=pltpu.CompilerParams(vmem_limit_bytes=VMEM),
    )(proj, proj, proj, *tables, grad)


def head_spread(plan):
    return ((iota((PAD, plan.R), 1) >> 6) == iota((PAD, plan.R), 0)).astype(jnp.bfloat16)


def head_gather(plan):
    return ((iota((plan.R, PAD), 0) >> 6) == iota((plan.R, PAD), 1)).astype(jnp.bfloat16)


def lower_ones():
    shape = (CHUNK, CHUNK)
    return (iota(shape, 0) >= iota(shape, 1)).astype(jnp.bfloat16)


def space_parts(plan, dt_raw, window, conv_ref, head_ref, pick_ref):
    total = conv_ref[4:5, :]
    for k in range(CONV):
        at = 8 - CONV + 1 + k
        total = total + conv_ref[k : k + 1, :] * window[at : at + CHUNK, :]
    raw = by_marks(dt_raw, pick_ref[...], 3) + head_ref[1:2, :]
    steps = jnp.maximum(raw, 0.0) + jnp.log1p(jnp.exp(-jnp.abs(raw)))
    logs = -steps * jnp.exp(head_ref[0:1, :])
    cumul = marks_by(lower_ones(), logs)
    return total, raw, steps, logs, cumul


def decay_of(cumul, cumul_t, causal, h):
    gaps = cumul[:, h : h + 1] - cumul_t[h : h + 1, :]
    return jnp.exp(jnp.where(causal, gaps, masked_score))


def space_fwd_kernel(
    plan, proj_ref, shared_ref, conv_ref, head_ref, pick_ref, gated_ref, made_ref, before_ref, state, window
):
    R = plan.R
    step = pl.program_id(0)

    @pl.when(step == 0)
    def _():
        state[...] = jnp.zeros_like(state)
        window[0:8, :] = jnp.zeros((8, window.shape[1]), jnp.float32)

    @pl.when(step > 0)
    def _():
        window[0:8, :] = window[CHUNK : CHUNK + 8, :]

    window[8 : CHUNK + 8, :R] = proj_ref[:, plan.B : plan.B + R]
    window[8 : CHUNK + 8, R:] = shared_ref[:, : 2 * NS]
    total, _, steps, _, cumul = space_parts(
        plan, shared_ref[:, 2 * NS :], window, conv_ref, head_ref, pick_ref
    )
    post = total * jax.nn.sigmoid(total)
    x = post[:, :R]
    b = post[:, R : R + NS].astype(jnp.bfloat16)
    c = post[:, R + NS :].astype(jnp.bfloat16)
    spread_heads = head_spread(plan)
    cumul_t = cumul.T
    last = cumul[CHUNK - 1 : CHUNK, :]
    tail = jnp.exp(last - cumul)
    weighted = x * by_marks(steps, spread_heads)
    causal = iota((CHUNK, CHUNK), 0) >= iota((CHUNK, CHUNK), 1)
    inner = cols_by_cols(c, b)
    before = state[...]
    before_ref[0] = before.astype(jnp.bfloat16)
    made = mm(c, before) * by_marks(jnp.exp(cumul), spread_heads)
    made = made + by_marks(jnp.broadcast_to(head_ref[2:3, :], (8, PAD)), spread_heads)[0:1] * x
    left = iota((CHUNK, 2 * MP), 1) < MP
    weighted_low = weighted.astype(jnp.bfloat16)
    intra = []
    for pair in range(plan.hm // 2):
        lanes = weighted_low[:, pair * 2 * MP : (pair + 1) * 2 * MP]
        one = mm(inner * decay_of(cumul, cumul_t, causal, 2 * pair), lanes)
        two = mm(inner * decay_of(cumul, cumul_t, causal, 2 * pair + 1), lanes)
        intra.append(jnp.where(left, one, two))
    made = made + jnp.concatenate(intra, axis=1)
    state[...] = before * by_marks(
        jnp.broadcast_to(jnp.exp(last), (8, PAD)), spread_heads
    )[0:1] + mm_tn(b, weighted * by_marks(tail, spread_heads))
    z = proj_ref[:, :R]
    made_ref[...] = made
    gated_ref[...] = made * (z * jax.nn.sigmoid(z))


def space_fwd(plan, proj, shared, conv, heads, pick):
    length = proj.shape[0]
    chunks = length // CHUNK
    W = plan.W
    whole = lambda i: (0, 0)
    rows = lambda i: (i, 0)
    return pl.pallas_call(
        functools.partial(space_fwd_kernel, plan),
        grid=(chunks,),
        out_shape=(
            jax.ShapeDtypeStruct((length, plan.R), jnp.float32),
            jax.ShapeDtypeStruct((length, plan.R), jnp.float32),
            jax.ShapeDtypeStruct((chunks, NS, plan.R), jnp.bfloat16),
        ),
        in_specs=[
            pl.BlockSpec((CHUNK, plan.A), rows),
            pl.BlockSpec((CHUNK, plan.K), rows),
            pl.BlockSpec((8, W), whole),
            pl.BlockSpec((8, PAD), whole),
            pl.BlockSpec((PAD, PAD), whole),
        ],
        out_specs=(
            pl.BlockSpec((CHUNK, plan.R), rows),
            pl.BlockSpec((CHUNK, plan.R), rows),
            pl.BlockSpec((1, NS, plan.R), lambda i: (i, 0, 0)),
        ),
        scratch_shapes=[
            pltpu.VMEM((NS, plan.R), jnp.float32),
            pltpu.VMEM((CHUNK + 8, W), jnp.float32),
        ],
        compiler_params=pltpu.CompilerParams(vmem_limit_bytes=VMEM),
    )(proj, shared, conv, heads, pick)


def space_bwd_kernel(
    plan, proj_ref, shared_ref, prev_ref, prev_shared, conv_ref, head_ref, pick_ref, gain_ref, row_ref,
    grad_ref, made_ref, before_ref, slab_ref, slab_shared, conv_acc, head_acc, skip_acc, d_state, window, d_window,
):
    R = plan.R
    step = pl.program_id(0)
    chunk = pl.num_programs(0) - 1 - step

    @pl.when(step == 0)
    def _():
        d_state[...] = jnp.zeros_like(d_state)
        d_window[CHUNK : CHUNK + 8, :] = jnp.zeros((8, plan.W), jnp.float32)
        conv_acc[...] = jnp.zeros_like(conv_acc)
        head_acc[...] = jnp.zeros_like(head_acc)
        skip_acc[...] = jnp.zeros_like(skip_acc)

    @pl.when(step > 0)
    def _():
        d_window[CHUNK : CHUNK + 8, :] = d_window[0:8, :]

    window[0:8, :R] = jnp.where(chunk == 0, 0.0, prev_ref[:, plan.B : plan.B + R])
    window[0:8, R:] = jnp.where(chunk == 0, 0.0, prev_shared[:, : 2 * NS])
    window[8 : CHUNK + 8, :R] = proj_ref[:, plan.B : plan.B + R]
    window[8 : CHUNK + 8, R:] = shared_ref[:, : 2 * NS]
    total, raw, steps, logs, cumul = space_parts(
        plan, shared_ref[:, 2 * NS :], window, conv_ref, head_ref, pick_ref
    )
    sig = jax.nn.sigmoid(total)
    post = total * sig
    x = post[:, :R]
    b = post[:, R : R + NS].astype(jnp.bfloat16)
    c = post[:, R + NS :].astype(jnp.bfloat16)
    spread_heads = head_spread(plan)
    gather_heads = head_gather(plan)
    cumul_t = cumul.T
    last = cumul[CHUNK - 1 : CHUNK, :]
    steps_wide = by_marks(steps, spread_heads)
    tail_wide = by_marks(jnp.exp(last - cumul), spread_heads)
    grow_wide = by_marks(jnp.exp(cumul), spread_heads)
    last_wide = by_marks(jnp.broadcast_to(jnp.exp(last), (8, PAD)), spread_heads)[0:1]
    skip_wide = by_marks(jnp.broadcast_to(head_ref[2:3, :], (8, PAD)), spread_heads)[0:1]
    weighted = x * steps_wide
    causal = iota((CHUNK, CHUNK), 0) >= iota((CHUNK, CHUNK), 1)
    inner = cols_by_cols(c, b)

    z = proj_ref[:, :R]
    sig_z = jax.nn.sigmoid(z)
    grad = grad_ref[...].astype(jnp.float32)
    gate = z * sig_z
    gated = made_ref[...] * gate
    row_factor = row_ref[:, 0:1]
    skip_acc[1:2, :] += jnp.sum(grad * gated * row_factor, axis=0, keepdims=True)
    grad = grad * gain_ref[0:1, :] * row_factor - gated * row_ref[:, 1:2]
    d_made = grad * gate
    slab_ref[:, :R] = (grad * made_ref[...] * (sig_z * (1.0 + z * (1.0 - sig_z)))).astype(
        jnp.bfloat16
    )
    skip_acc[0:1, :] += jnp.sum(d_made * x, axis=0, keepdims=True)

    before = before_ref[0]
    d_after = d_state[...]
    d_after_low = d_after.astype(jnp.bfloat16)
    grown = d_made * grow_wide
    grown_low = grown.astype(jnp.bfloat16)
    carried = mm(c, before)
    d_c = mm_nt(grown_low, before)
    pulled = weighted * tail_wide
    d_pulled = mm(b, d_after_low)
    d_b = mm_nt(pulled, d_after_low)
    d_cumul = by_marks(grown * carried, gather_heads)
    kept = by_marks(d_pulled * pulled, gather_heads)
    d_cumul = d_cumul - kept
    decayed = jnp.sum(d_after * before.astype(jnp.float32), axis=0, keepdims=True) * last_wide
    d_last = jnp.sum(kept, axis=0, keepdims=True) + by_marks(
        jnp.broadcast_to(decayed, (8, R)), gather_heads
    )[0:1]
    d_state[...] = d_after * last_wide + mm_tn(c, grown_low)

    left = iota((CHUNK, 2 * MP), 1) < MP
    lane = iota((CHUNK, PAD), 1)
    sub = iota((8, CHUNK), 0)
    weighted_low = weighted.astype(jnp.bfloat16)
    d_made_low = d_made.astype(jnp.bfloat16)
    d_inner = jnp.zeros((CHUNK, CHUNK), jnp.float32)
    columns = jnp.zeros((8, CHUNK), jnp.float32)
    d_weighted = []
    for pair in range(plan.hm // 2):
        at = slice(pair * 2 * MP, (pair + 1) * 2 * MP)
        lanes, d_lanes = weighted_low[:, at], d_made_low[:, at]
        halves = []
        for which in range(2):
            h = 2 * pair + which
            decay = decay_of(cumul, cumul_t, causal, h)
            whole = inner * decay
            halves.append(mm_tn(whole, d_lanes))
            mine = jnp.where(left if which == 0 else ~left, d_lanes, jnp.zeros_like(d_lanes))
            d_whole = cols_by_cols(mine, lanes)
            d_inner = d_inner + d_whole * decay
            slope = d_whole * whole
            d_cumul = d_cumul + jnp.where(lane == h, jnp.sum(slope, axis=1, keepdims=True), 0.0)
            columns = columns + jnp.where(sub == h, jnp.sum(slope, axis=0, keepdims=True), 0.0)
        d_weighted.append(jnp.where(left, halves[0], halves[1]))
    d_weighted = jnp.concatenate(d_weighted, axis=1) + d_pulled * tail_wide
    columns = jnp.concatenate([columns, jnp.zeros((CHUNK - 8, CHUNK), jnp.float32)], axis=0).T
    d_cumul = d_cumul - columns
    d_inner_low = d_inner.astype(jnp.bfloat16)
    d_c = d_c + mm(d_inner_low, b)
    d_b = d_b + mm_tn(d_inner_low, c)
    d_x = d_weighted * steps_wide + skip_wide * d_made
    d_steps = by_marks(d_weighted * x, gather_heads)
    upper = (iota((CHUNK, CHUNK), 0) <= iota((CHUNK, CHUNK), 1)).astype(jnp.bfloat16)
    d_logs = marks_by(upper, d_cumul) + d_last
    d_steps = d_steps - jnp.exp(head_ref[0:1, :]) * d_logs
    d_raw = d_steps * jax.nn.sigmoid(raw)
    d_raw = jnp.where(lane < plan.hm, d_raw, 0.0)
    slab_shared[:, 2 * NS :] = cols_by_cols(d_raw.astype(jnp.bfloat16), pick_ref[...]).astype(
        jnp.bfloat16
    )
    head_acc[0:1, :] += jnp.sum(d_logs * logs, axis=0, keepdims=True)
    head_acc[1:2, :] += jnp.sum(d_raw, axis=0, keepdims=True)

    d_post = jnp.concatenate([d_x, d_b, d_c], axis=1)
    d_total = d_post * (sig * (1.0 + total * (1.0 - sig)))
    d_window[0:CHUNK, :] = d_total
    d_xbc = jnp.zeros((CHUNK, plan.W), jnp.float32)
    for k in range(CONV):
        shift = CONV - 1 - k
        d_xbc = d_xbc + conv_ref[k : k + 1, :] * d_window[shift : shift + CHUNK, :]
        at = 8 - CONV + 1 + k
        conv_acc[k : k + 1, :] += jnp.sum(
            d_total * window[at : at + CHUNK, :], axis=0, keepdims=True
        )
    conv_acc[4:5, :] += jnp.sum(d_total, axis=0, keepdims=True)
    slab_ref[:, plan.B : plan.B + R] = d_xbc[:, :R].astype(jnp.bfloat16)
    slab_shared[:, : 2 * NS] = d_xbc[:, R:].astype(jnp.bfloat16)
    if plan.B + R < plan.A:
        slab_ref[:, plan.B + R :] = jnp.zeros((CHUNK, plan.A - plan.B - R), jnp.bfloat16)


def space_bwd(plan, proj, shared, conv, heads, pick, gain, rows_of, grad, made, before):
    length = proj.shape[0]
    chunks = length // CHUNK
    W = plan.W
    whole = lambda i: (0, 0)
    rows = lambda i: (chunks - 1 - i, 0)
    per = CHUNK // 8
    return pl.pallas_call(
        functools.partial(space_bwd_kernel, plan),
        grid=(chunks,),
        out_shape=(
            jax.ShapeDtypeStruct((length, plan.A), jnp.bfloat16),
            jax.ShapeDtypeStruct((length, plan.K), jnp.bfloat16),
            jax.ShapeDtypeStruct((8, W), jnp.float32),
            jax.ShapeDtypeStruct((8, PAD), jnp.float32),
            jax.ShapeDtypeStruct((8, plan.R), jnp.float32),
        ),
        in_specs=[
            pl.BlockSpec((CHUNK, plan.A), rows),
            pl.BlockSpec((CHUNK, plan.K), rows),
            pl.BlockSpec((8, plan.A), lambda i: (jnp.maximum((chunks - 1 - i) * per - 1, 0), 0)),
            pl.BlockSpec((8, plan.K), lambda i: (jnp.maximum((chunks - 1 - i) * per - 1, 0), 0)),
            pl.BlockSpec((8, W), whole),
            pl.BlockSpec((8, PAD), whole),
            pl.BlockSpec((PAD, PAD), whole),
            pl.BlockSpec((8, plan.R), whole),
            pl.BlockSpec((CHUNK, 2), rows),
            pl.BlockSpec((CHUNK, plan.R), rows),
            pl.BlockSpec((CHUNK, plan.R), rows),
            pl.BlockSpec((1, NS, plan.R), lambda i: (chunks - 1 - i, 0, 0)),
        ],
        out_specs=(
            pl.BlockSpec((CHUNK, plan.A), rows),
            pl.BlockSpec((CHUNK, plan.K), rows),
            pl.BlockSpec((8, W), whole),
            pl.BlockSpec((8, PAD), whole),
            pl.BlockSpec((8, plan.R), whole),
        ),
        scratch_shapes=[
            pltpu.VMEM((NS, plan.R), jnp.float32),
            pltpu.VMEM((CHUNK + 8, W), jnp.float32),
            pltpu.VMEM((CHUNK + 8, W), jnp.float32),
        ],
        compiler_params=pltpu.CompilerParams(vmem_limit_bytes=VMEM),
    )(proj, shared, proj, shared, conv, heads, pick, gain, rows_of, grad, made, before)


def body(
    inputs,
    cotangent,
    w_in,
    w_in_m,
    w_in_v,
    w_mix,
    w_mix_m,
    w_mix_v,
    w_up,
    w_up_m,
    w_up_v,
    w_down,
    w_down_m,
    w_down_v,
    vectors,
    vectors_m,
    vectors_v,
):
    low = jnp.bfloat16
    count = lax.axis_size("ctx")
    ways = lax.axis_size("wshard")
    place = lax.axis_index("ctx")
    plan = Plan(count)
    R, hm = plan.R, plan.hm
    is_space = place >= plan.attn
    space = jnp.maximum(place - plan.attn, 0)

    gain_attn, gain_ffn, gain_ssm, conv_bias, conv_weight, a_log, dt_bias, d_skip = split_vectors(
        vectors
    )
    whole, in_own, shared_own, up_some, mix_own, down_some = start_call(
        plan, count, inputs[0], w_in, w_up, w_mix, w_down, 1
    )

    own = lambda a, size, axis=0: lax.dynamic_slice_in_dim(a, space * size, size, axis)
    gain_own = own(gain_ssm, R)
    W = plan.W
    conv = jnp.concatenate(
        [
            jnp.concatenate([own(conv_weight, R, 1), conv_weight[:, DSSM:]], axis=1),
            jnp.concatenate([own(conv_bias, R), conv_bias[DSSM:]])[None],
            jnp.zeros((8 - CONV - 1, W), jnp.float32),
        ]
    )
    heads = jnp.stack([own(v, hm) for v in (a_log, dt_bias, d_skip)])
    heads = jnp.pad(heads, ((0, 5), (0, PAD - hm)))
    column = lax.broadcasted_iota(jnp.int32, (PAD, PAD), 1)
    row = lax.broadcasted_iota(jnp.int32, (PAD, PAD), 0)
    pick = jnp.logical_and(row == column + space * hm, column < hm).astype(low)
    tables = rope_tables(count * inputs.shape[1])

    source = inputs[0].astype(jnp.float32)
    whole = whole.astype(jnp.float32)
    in_own, cotangent_late = lax.optimization_barrier((in_own, cotangent[0]))
    odd = lax.axis_index("wshard") % 2 == 1
    upstream_all = gather_ctx(cotangent_late, count, ways)
    length = whole.shape[0]
    rows = inputs.shape[1]
    unit = whole * lax.rsqrt(jnp.mean(whole * whole, axis=-1, keepdims=True) + norm_eps)
    normed = (unit * gain_attn).astype(low)
    unit = unit.astype(low)
    proj = plain(normed, in_own)
    shared = plain(normed, shared_own)

    def space_ahead(proj, shared):
        return space_fwd(plan, proj, shared, conv, heads, pick)

    def attn_ahead(proj, shared):
        made = attn_fwd(plan, proj, tables)
        blank = jnp.zeros((length // CHUNK, NS, R), low)
        return made, jnp.zeros_like(made), blank

    made, raw_made, before = lax.cond(is_space, space_ahead, attn_ahead, proj, shared)
    square = jnp.where(is_space, jnp.sum(made * made, axis=1), 0.0)
    factor = lax.rsqrt(sum_rows(count, square, 5) / DSSM + norm_eps)
    mixed = jnp.where(is_space, made * factor[:, None] * gain_own, made).astype(low)
    wide = lambda *shape: jax.ShapeDtypeStruct(shape, jnp.float32)
    side = (up_some, down_some)
    roomy = length <= 1024
    middle, activated, grad_gate_up, two_all, up_own, down_own = flow_call(
        branch_kernel,
        count,
        rows,
        (mixed, mix_own, inputs[0], gain_ffn[None], upstream_all if roomy else upstream_all[:, :16]),
        (
            wide(rows, D),
            jax.ShapeDtypeStruct((length if roomy else 16, FF // count), low),
            jax.ShapeDtypeStruct((length if roomy else 16, 2 * FF // count), low),
        ),
        True,
        True,
        (side, *share_shapes(side)),
        8,
        roomy,
    )
    two_all = two_all.reshape(length, D)
    up_own, down_own = up_own.reshape(D, -1), down_own.reshape(-1, D)

    if not roomy:
        gate_up = plain(two_all, up_own)
        half = FF // count
        swiglu = lambda g: jax.nn.silu(g[:, :half]) * g[:, half:]
        activated, act_pull = jax.vjp(swiglu, gate_up)
        activated = in_ring(activated.astype(low).reshape(count, rows, -1), count, ways, odd)
        grad_act = cols_by_cols(from_ring(upstream_all, count, lax.axis_index("wshard")), down_own)
        grad_gate_up = act_pull(grad_act)[0].astype(low)
    upstream_all = upstream_all.reshape(length, D)
    cut = lambda g, blocks: g.astype(low).reshape(blocks, ways, -1, g.shape[1])
    blank = jnp.zeros((1, 1, 16, 128), low)
    if roomy:
        up_block = (count, ways, D // (count * ways), 2 * FF // count)
        down_block = (1, ways, FF // (count * ways), D)
        side = [jax.ShapeDtypeStruct(block, low) for block in (up_block, down_block)]
        side_shapes, side_scratch = collect_shapes(("rows", "rows"), side)
        side_scratch = (
            [pltpu.VMEM(block, low) for block in (up_block, down_block)]
            + [pltpu.VMEM((2, length, D // count), low)] * 2
            + [pltpu.SemaphoreType.DMA((2, 2))]
            + side_scratch
        )
        side = (blank, blank)
    else:
        side = (cut(rows_by_rows(two_all, grad_gate_up), count), cut(rows_by_rows(activated, upstream_all), 1))
        side_shapes, side_scratch = collect_shapes(("rows", "rows"), side)
    some = lambda a: a if roomy else a[:16]
    grad_middle, grad_gain_ffn, grad_made, late, branch_all, up_mine, down_mine = flow_call(
        feed_back_kernel,
        count,
        rows,
        (
            grad_gate_up,
            up_own,
            cotangent[0],
            middle,
            gain_ffn[None],
            some(activated),
            some(mix_own),
            some(down_own),
        ),
        (
            wide(rows, D),
            wide(8, D),
            jax.ShapeDtypeStruct((length if roomy else 16, R), low),
            jax.ShapeDtypeStruct((length if roomy else 16, D), low),
        ),
        True,
        False,
        (side, side_shapes, side_scratch),
        9,
        roomy,
        (two_all, upstream_all),
    )
    grad_gain_ffn = grad_gain_ffn[0]
    branch_all = branch_all.reshape(length, D)
    if not roomy:
        late = plain(activated, down_own).astype(low)
    branch_all, grad_made, late = lax.optimization_barrier((branch_all, grad_made, late))
    late = scatter_ctx(late, count, ways)
    if not roomy:
        grad_made = cols_by_cols(branch_all, mix_own).astype(low)
    made_wide = grad_made.astype(jnp.float32)
    dots = jnp.where(is_space, jnp.sum(made_wide * gain_own * made, axis=1), 0.0)
    dots = sum_rows(count, dots, 6)

    def space_back(proj, shared, grad_made):
        gain = jnp.broadcast_to(gain_own, (8, R))
        rows_of = jnp.stack([factor, factor**3 * dots / DSSM], axis=1)
        return space_bwd(
            plan, proj, shared, conv, heads, pick, gain, rows_of, grad_made, raw_made, before
        )

    def attn_back(proj, shared, grad_made):
        blank = lambda k: jnp.zeros((8, k), jnp.float32)
        none = jnp.zeros(shared.shape, low)
        return attn_bwd(plan, proj, tables, grad_made), none, blank(W), blank(PAD), blank(R)

    grad_proj, grad_shared, conv_acc, head_acc, skip_acc = lax.cond(
        is_space, space_back, attn_back, proj, shared, grad_made
    )
    if roomy:
        grad_gain_attn = jnp.zeros_like(gain_attn)
    else:
        grad_in = rows_by_rows(unit, grad_proj)
        grad_in_shared = rows_by_rows(unit, grad_shared)
        grad_gain_attn = jnp.sum(grad_in * in_own, axis=1)
        grad_gain_attn = grad_gain_attn + jnp.sum(grad_in_shared * shared_own, axis=1)
        grad_in = grad_in * gain_attn[:, None]
        grad_in_shared = grad_in_shared * gain_attn[:, None]
    def placed(piece, size, total, axis=0):
        shape = list(piece.shape)
        shape[axis] = total
        start = [0] * piece.ndim
        start[axis] = space * size
        return lax.dynamic_update_slice(jnp.zeros(shape, piece.dtype), piece, start)

    conv_w_grad, conv_b_grad = conv_acc[:CONV], conv_acc[CONV]
    a_grad, bias_grad = head_acc[0, :hm], head_acc[1, :hm]
    skip_grad = jnp.sum(skip_acc[0].reshape(hm, MP), axis=1)
    grad_gain_own = skip_acc[1]
    vector_local = jnp.concatenate(
        [
            grad_gain_attn,
            grad_gain_ffn,
            placed(grad_gain_own, R, DSSM),
            placed(conv_b_grad[:R], R, DSSM),
            conv_b_grad[R:],
            jnp.concatenate(
                [placed(conv_w_grad[:, :R], R, DSSM, 1), conv_w_grad[:, R:]], axis=1
            ).reshape(CONV * CONVCH),
            placed(a_grad, hm, MH),
            placed(bias_grad, hm, MH),
            placed(skip_grad, hm, MH),
        ]
    )
    grad_proj, late = lax.optimization_barrier((grad_proj, late))
    outputs = (middle + late).astype(low)[None]
    pad = -vectors.shape[0] % 1024
    vector_local = jnp.pad(vector_local, (0, pad)).reshape(-1, 128)
    if roomy:
        lines = D // (count * ways)
        blocks = (
            (count, ways, lines, plan.A),
            (count, ways, lines, plan.K),
            (1, ways, MIXIN // (count * ways), D),
        )
        side = [jax.ShapeDtypeStruct(block, low) for block in blocks]
        side_shapes, side_scratch = collect_shapes(SUMS, side)
        side_scratch = (
            [pltpu.VMEM(block, low) for block in blocks]
            + [pltpu.VMEM((2, length, D // count), low)] * 2
            + [pltpu.SemaphoreType.DMA((2, 2)), pltpu.VMEM(vector_local.shape, jnp.float32)]
            + side_scratch
        )
        side = (blank, blank, blank)
    else:
        grad_mix = rows_by_rows(mixed, branch_all)
        side = (cut(grad_in, count), cut(grad_in_shared, count), cut(grad_mix, 1))
        side_shapes, side_scratch = collect_shapes(SUMS, side)
    home_sems = [pltpu.SemaphoreType.DMA((count,))] * 2
    input_grad, vector_sum, up_mine, in_mine, shared_mine, mix_mine = flow_call(
        source_back_kernel,
        count,
        rows,
        (
            grad_proj,
            grad_shared,
            in_own,
            shared_own,
            inputs[0],
            grad_middle,
            gain_attn[None],
            vector_local,
            up_mine,
            some(mixed),
            some(gain_attn[:, None]),
        ),
        (wide(rows, D), wide(*vector_local.shape), jax.ShapeDtypeStruct(up_mine.shape, low)),
        False,
        False,
        (side, side_shapes, side_scratch + sum_scratch(count, vector_local.shape) + home_sems),
        10,
        far_args=(some(unit), some(branch_all)),
    )
    input_grad = input_grad[None]

    up_shard = up_from_slabs(plan, up_mine)
    mix_shard = mix_mine[0].astype(jnp.float32)
    down_shard = down_mine[0].astype(jnp.float32)

    vector_grad = vector_sum.reshape(-1)[: vectors.shape[0]]
    new_in = adam_in(plan, in_mine, shared_mine, w_in, w_in_m, w_in_v, 2.0 * D ** (-0.5))
    new_mix = adamw(w_mix, w_mix_m, w_mix_v, mix_shard, DSSM ** (-0.5), decay_weight)
    new_up = adamw(w_up, w_up_m, w_up_v, up_shard, D ** (-0.5), decay_weight)
    new_down = adamw(w_down, w_down_m, w_down_v, down_shard, FF ** (-0.5), decay_weight)
    new_vec = adamw(vectors, vectors_m, vectors_v, vector_grad, vector_rate, 0.0)
    return (outputs, input_grad, *new_in, *new_mix, *new_up, *new_down, *new_vec)


def solution(mesh):
    tokens = P("wshard", "ctx", None)
    weight = P(("ctx", "wshard"), None)
    return jax.shard_map(
        body,
        mesh=mesh,
        in_specs=(tokens,) * 2 + (weight,) * 12 + (P(),) * 3,
        out_specs=(tokens,) * 2 + (weight,) * 12 + (P(),) * 3,
        check_vma=False,
    )
```

```python
import functools
import math

import jax
import jax.numpy as jnp
from jax import lax
from jax.experimental import pallas as pl
from jax.experimental.pallas import tpu as pltpu
from jax.sharding import PartitionSpec as P

D = 2048
FF = 4096
AH = 8
KVH = 2
HD = 128
MH = 48
MP = 64
NS = 256
CONV = 4
STEP = 10
DSSM = 3072
CONVCH = 3584
ATT = AH * HD
MIXIN = ATT + DSSM
GROUP = AH // KVH
CHUNK = 128
PAD = 128
VMEM = 60 * 1024 * 1024


norm_eps = 1e-05
rope_base = 10000.0
beta_one = 0.9
beta_two = 0.95
adam_eps = 1e-08
decay_weight = 0.1
vector_rate = 0.5
masked_score = -1e30

K_AT = ATT
V_AT = K_AT + KVH * HD
Z_AT = V_AT + KVH * HD
X_AT = Z_AT + DSSM
BC_AT = X_AT + DSSM
DT_AT = BC_AT + 2 * NS
END = DT_AT + MH


def rows_by_rows(left, right):
    return lax.dot_general(
        left, right, (((0,), (0,)), ((), ())), preferred_element_type=jnp.float32
    )


def cols_by_cols(left, right):
    return lax.dot_general(
        left, right, (((1,), (1,)), ((), ())), preferred_element_type=jnp.float32
    )


def plain(left, right):
    return jnp.dot(left, right, preferred_element_type=jnp.float32)


def rms_norm(values, gain):
    factor = lax.rsqrt(jnp.mean(values * values, axis=-1, keepdims=True) + norm_eps)
    return values * factor * gain


def split_vectors(vectors):
    extents = (D, D, DSSM, CONVCH, CONV * CONVCH, MH, MH, MH)
    pieces = []
    offset = 0
    for extent in extents:
        pieces.append(lax.slice_in_dim(vectors, offset, offset + extent))
        offset = offset + extent
    pieces[4] = pieces[4].reshape(CONV, CONVCH)
    return pieces


def adamw(weight, moment, second, grad, rate, decay):
    moment = beta_one * moment + (1.0 - beta_one) * grad
    second = beta_two * second + (1.0 - beta_two) * grad * grad
    corrected = moment / (1.0 - beta_one**STEP)
    divisor = jnp.sqrt(second / (1.0 - beta_two**STEP)) + adam_eps
    return (weight - rate * (corrected / divisor + decay * weight), moment, second)


class Plan:
    def __init__(self, count):
        self.count = count
        self.R = MIXIN // count
        self.attn = ATT // self.R
        self.ha = self.R // HD
        self.hm = self.R // MP
        self.B = self.R
        self.A = self.R + max(self.R, 2 * HD)
        self.K = 2 * NS + PAD
        self.W = self.R + 2 * NS

    def kv_of(self, c):
        return c * self.ha // GROUP


def up_from_slabs(plan, slabs):
    G = FF // plan.count
    slabs = slabs.astype(jnp.float32)
    return jnp.concatenate(
        [slabs[c][:, :G] for c in range(plan.count)] + [slabs[c][:, G:] for c in range(plan.count)],
        axis=1,
    )


def ring_groups(n, ways):
    ring = list(range(0, n, 2)) + list(range(n - 1, 0, -2))
    return [[c * ways + w for c in (ring[::-1] if w % 2 else ring)] for w in range(ways)], ring


def ring_place(n, w, c):
    at = c // 2 + c % 2 * (n - 1 - c // 2 * 2)
    return at + w % 2 * (n - 1 - 2 * at)


def gather_ctx(x, n, ways):
    return lax.all_gather(x, ("ctx", "wshard"), axis_index_groups=ring_groups(n, ways)[0])


def from_ring(blocks, n, w):
    parts = [lax.dynamic_index_in_dim(blocks, ring_place(n, w, c), 0, False) for c in range(n)]
    return jnp.concatenate(parts)


def in_ring(blocks, n, ways, odd):
    ring = ring_groups(n, ways)[1]
    parts = [
        lax.dynamic_index_in_dim(blocks, jnp.where(odd, ring[n - 1 - i], ring[i]), 0, False)
        for i in range(n)
    ]
    return jnp.concatenate(parts)


def scatter_ctx(x, n, ways):
    return lax.psum_scatter(
        x.astype(jnp.bfloat16),
        ("ctx", "wshard"),
        scatter_dimension=0,
        axis_index_groups=ring_groups(n, ways)[0],
        tiled=True,
    ).astype(jnp.float32)


def adam_in_kernel(plan, rate, slabs, shared, w, m, v, new_w, new_m, new_v):
    R, B = plan.R, plan.B
    wide = jnp.float32
    heads, spaces = range(plan.attn), range(plan.attn, plan.count)

    def update(lo, hi, parts):
        grad = functools.reduce(lambda a, b: a + b, [part.astype(wide) for part in parts])
        new = adamw(w[:, lo:hi], m[:, lo:hi], v[:, lo:hi], grad, rate, decay_weight)
        new_w[:, lo:hi], new_m[:, lo:hi], new_v[:, lo:hi] = new

    for c in heads:
        update(c * R, (c + 1) * R, [slabs[c, :, :R]])
    for start, at in ((K_AT, B), (V_AT, B + HD)):
        for g in range(KVH):
            owners = [slabs[c, :, at : at + HD] for c in heads if plan.kv_of(c) == g]
            update(start + g * HD, start + (g + 1) * HD, owners)
    for c in spaces:
        j = c - plan.attn
        update(Z_AT + j * R, Z_AT + (j + 1) * R, [slabs[c, :, :R]])
        update(X_AT + j * R, X_AT + (j + 1) * R, [slabs[c, :, B : B + R]])
    update(BC_AT, END, [shared[c, :, : END - BC_AT] for c in spaces])


def adam_in(plan, slabs, shared, w, m, v, rate):
    rows = w.shape[0]
    block = 16
    flat = pl.BlockSpec((block, END), lambda i: (i, 0))
    return pl.pallas_call(
        functools.partial(adam_in_kernel, plan, rate),
        grid=(rows // block,),
        out_shape=(jax.ShapeDtypeStruct(w.shape, w.dtype),) * 3,
        in_specs=[
            pl.BlockSpec((plan.count, block, plan.A), lambda i: (0, i, 0)),
            pl.BlockSpec((plan.count, block, plan.K), lambda i: (0, i, 0)),
            flat,
            flat,
            flat,
        ],
        out_specs=(flat,) * 3,
        compiler_params=pltpu.CompilerParams(vmem_limit_bytes=VMEM),
    )(slabs, shared, w, m, v)


MESH = pl.DeviceIdType.MESH


def here():
    c, w = lax.axis_index("ctx"), lax.axis_index("wshard")
    return c, w, w + 1 - 2 * (w % 2), (w + 2) % 4


def greet(devices):
    barrier = pltpu.get_barrier_semaphore()
    for device in devices:
        pl.semaphore_signal(barrier, inc=1, device_id=device, device_id_type=MESH)
    pl.semaphore_wait(barrier, len(devices))


def remote(src, dst, send, recv, device):
    return pltpu.make_async_remote_copy(
        src_ref=src, dst_ref=dst, send_sem=send, recv_sem=recv, device_id=device, device_id_type=MESH
    )


class Collect:
    def __init__(self, n, kinds, sources, targets, extra):
        self.n = n
        self.c, self.w, self.sib, self.across = here()
        self.x, self.core = self.w // 2, self.w % 2
        self.pending = []
        self.jobs = []
        for j, kind in enumerate(kinds):
            self.jobs.append((kind, sources[j], targets[j]) + tuple(extra[10 * j : 10 * j + 10]))
        most = max(job[3].shape[1] for job in self.jobs)
        self.steps = [s % most for s in range(1, most + 1)]

    def due(self, s):
        for job in self.jobs:
            count = job[3].shape[1]
            if s < count:
                yield job, (self.c + s) % self.n if count > 1 else 0

    def send(self, s):
        for place, slot in ((1 - self.x, 0), (self.x, 1)):
            for job, q in self.due(s):
                _, src, _, kbuf, _, _, _, k_send, k_recv = job[:9]
                out = remote(
                    src.at[q, place * 2 + 1 - self.core],
                    kbuf.at[slot, q],
                    k_send.at[slot, s],
                    k_recv.at[slot, q],
                    (self.c, self.sib),
                )
                out.start()
                self.pending.append(out)

    def cross(self, s):
        wide = jnp.float32
        for job, q in self.due(s):
            _, src, _, kbuf, stage, xbuf, _, k_send, k_recv, x_send, x_recv = job[:11]
            got = kbuf.at[0, q]
            remote(got, got, k_send.at[0, s], k_recv.at[0, q], (self.c, self.sib)).wait_recv()
            mine = src[q, (1 - self.x) * 2 + self.core].astype(wide)
            stage[q] = (mine + kbuf[0, q].astype(wide)).astype(stage.dtype)
            out = remote(
                stage.at[q], xbuf.at[q], x_send.at[s], x_recv.at[q], (self.c, self.across)
            )
            out.start()
            self.pending.append(out)

    def close(self, s):
        wide = jnp.float32
        for job, q in self.due(s):
            kind, src, dst, kbuf, stage, xbuf, done, k_send, k_recv, x_send, x_recv = job[:11]
            got = kbuf.at[1, q]
            remote(got, got, k_send.at[1, s], k_recv.at[1, q], (self.c, self.sib)).wait_recv()
            got = xbuf.at[q]
            remote(got, got, x_send.at[s], x_recv.at[q], (self.c, self.across)).wait_recv()
            total = src[q, self.x * 2 + self.core].astype(wide) + kbuf[1, q].astype(wide)
            total = (total + xbuf[q].astype(wide)).astype(stage.dtype)
            if kind == "cols" and s > 0:
                done[q] = total
                out = remote(done.at[q], dst.at[self.c], job[11].at[s], job[12].at[self.c], (q, self.w))
                out.start()
                self.pending.append(out)
            else:
                dst[q] = total

    def end(self):
        for job in self.jobs:
            if job[0] == "cols":
                dst, a_send, a_recv = job[2], job[11], job[12]
                for s in range(1, self.n):
                    q = (self.c + self.n - s) % self.n
                    got = dst.at[q]
                    remote(got, got, a_send.at[s], a_recv.at[q], (q, self.w)).wait_recv()
        for out in self.pending:
            out.wait_send()


def home_job(n, source, target, send, recv):
    c, w = lax.axis_index("ctx"), lax.axis_index("wshard")
    target[c] = source[c]
    copies = [
        remote(source.at[(c + s) % n], target.at[c], send.at[s], recv.at[c], ((c + s) % n, w))
        for s in range(1, n)
    ]
    for copy in copies:
        copy.start()
    yield
    for s in range(1, n):
        q = (c + n - s) % n
        remote(source.at[q], target.at[q], send.at[s], recv.at[q], (q, w)).wait_recv()
    for copy in copies:
        copy.wait_send()


def collect_shapes(kinds, sources):
    shapes, scratch = [], []
    for kind, src in zip(kinds, sources):
        count, _, rows, size = src.shape
        block = (count, rows, size)
        shapes.append(jax.ShapeDtypeStruct(block, src.dtype))
        scratch += [
            pltpu.VMEM((2,) + block, src.dtype),
            pltpu.VMEM(block, src.dtype),
            pltpu.VMEM(block, src.dtype),
            pltpu.VMEM(block if kind == "cols" else (1, 16, 128), src.dtype),
            pltpu.SemaphoreType.DMA((2, count)),
            pltpu.SemaphoreType.DMA((2, count)),
            pltpu.SemaphoreType.DMA((count,)),
            pltpu.SemaphoreType.DMA((count,)),
            pltpu.SemaphoreType.DMA((count,)),
            pltpu.SemaphoreType.DMA((count,)),
        ]
    return shapes, scratch


def row_sum_kernel(n, x_ref, out_ref, got, send, recv):
    c, w = lax.axis_index("ctx"), lax.axis_index("wshard")
    greet([((c + s) % n, w) for s in range(1, n)])
    copies = [
        remote(x_ref, got.at[c], send.at[s], recv.at[c], ((c + s) % n, w)) for s in range(1, n)
    ]
    for copy in copies:
        copy.start()
    total = x_ref[...]
    for s in range(1, n):
        q = (c + n - s) % n
        remote(x_ref, got.at[q], send.at[s], recv.at[q], (q, w)).wait_recv()
        total = total + got[q]
    out_ref[...] = total
    for copy in copies:
        copy.wait_send()


def sum_rows(n, x, collective_id):
    block = x.reshape(-1, 128)
    return pl.pallas_call(
        functools.partial(row_sum_kernel, n),
        out_shape=jax.ShapeDtypeStruct(block.shape, x.dtype),
        in_specs=[pl.BlockSpec(memory_space=pltpu.VMEM)],
        out_specs=pl.BlockSpec(memory_space=pltpu.VMEM),
        scratch_shapes=[
            pltpu.VMEM((n,) + block.shape, x.dtype),
            pltpu.SemaphoreType.DMA((n,)),
            pltpu.SemaphoreType.DMA((n,)),
        ],
        compiler_params=pltpu.CompilerParams(
            collective_id=collective_id, has_side_effects=True, vmem_limit_bytes=VMEM
        ),
    )(block).reshape(x.shape)


def sum_job(n, x_ref, out_ref, kept, got, send, recv):
    c, w, sib, across = here()
    partners = [(c, sib), (c, across)]
    for level in list(range(1, n.bit_length() - 1)) + [0]:
        reach = 2**level
        partners.append((c + reach - 2 * reach * ((c // reach) % 2), w))
    out_ref[...] = x_ref[...]
    for i, partner in enumerate(partners):
        kept[i] = out_ref[...]
        swap = remote(kept.at[i], got.at[i], send.at[i], recv.at[i], partner)
        swap.start()
        yield
        swap.wait()
        out_ref[...] += got[i]


def sum_scratch(n, shape):
    stages = n.bit_length() + 1
    return [
        pltpu.VMEM((stages,) + shape, jnp.float32),
        pltpu.VMEM((stages,) + shape, jnp.float32),
        pltpu.SemaphoreType.DMA((stages,)),
        pltpu.SemaphoreType.DMA((stages,)),
    ]


def share_job(sources, targets, sems):
    c, w, sib, across = here()
    pending = []
    for j, (src, dst) in enumerate(zip(sources, targets)):
        x_send, x_recv, k_send, k_recv, own_sem = sems[5 * j : 5 * j + 5]
        for q in range(src.shape[0]):
            own = pltpu.make_async_copy(src.at[q], dst.at[q, w], own_sem.at[q])
            to_x = remote(src.at[q], dst.at[q, w], x_send.at[q], x_recv.at[q], (c, across))
            to_k = remote(src.at[q], dst.at[q, w], k_send.at[0, q], k_recv.at[0, q], (c, sib))
            for copy in (to_x, to_k, own):
                copy.start()
            pending += [to_x.wait_send, to_k.wait_send, own.wait]
    yield
    for j, dst in enumerate(targets):
        x_send, x_recv, k_send, k_recv, own_sem = sems[5 * j : 5 * j + 5]
        for q in range(dst.shape[0]):
            got = dst.at[q, across]
            remote(got, got, x_send.at[q], x_recv.at[q], (c, across)).wait_recv()
            out = remote(got, got, k_send.at[1, q], k_recv.at[1, q], (c, sib))
            out.start()
            pending.append(out.wait_send)
    yield
    for j, dst in enumerate(targets):
        x_send, x_recv, k_send, k_recv, own_sem = sems[5 * j : 5 * j + 5]
        for q in range(dst.shape[0]):
            for half, place in ((0, sib), (1, (sib + 2) % 4)):
                got = dst.at[q, place]
                remote(got, got, k_send.at[half, q], k_recv.at[half, q], (c, sib)).wait_recv()
    for wait in pending:
        wait()


def share_shapes(sources):
    shapes, sems = [], []
    for src in sources:
        count = src.shape[0]
        shapes.append(jax.ShapeDtypeStruct((count, 4) + src.shape[1:], src.dtype))
        sems += [
            pltpu.SemaphoreType.DMA((count,)),
            pltpu.SemaphoreType.DMA((count,)),
            pltpu.SemaphoreType.DMA((2, count)),
            pltpu.SemaphoreType.DMA((2, count)),
            pltpu.SemaphoreType.DMA((count,)),
        ]
    return shapes, sems


def advance(*jobs):
    jobs = list(jobs)
    while jobs:
        for job in list(jobs):
            try:
                next(job)
            except StopIteration:
                jobs.remove(job)


class Line:
    def __init__(self, n):
        self.c, self.w, self.sib, self.across = here()
        self.n, self.N = n, n // 2
        self.at, self.side = self.c // 2, self.c % 2
        self.pair = (self.c + 1 - 2 * self.side, self.w)
        self.left = (self.c - 2, self.w)
        self.right = (self.c + 2, self.w)
        self.has_left = self.at > 0
        self.has_right = self.at < self.N - 1

    def greet(self, others=()):
        barrier = pltpu.get_barrier_semaphore()
        signal = lambda d: pl.semaphore_signal(barrier, inc=1, device_id=d, device_id_type=MESH)
        sure = [self.pair] + list(others)
        for device in sure:
            signal(device)
        pl.when(self.has_left)(lambda: signal(self.left))
        pl.when(self.has_right)(lambda: signal(self.right))
        beside = (self.at + self.N - 1) // self.N + (2 * self.N - 2 - self.at) // self.N
        pl.semaphore_wait(barrier, len(sure) + beside)


def scatter_job(line, theirs, mine_of, total, ybuf, zbuf, sems):
    y_send, y_recv, r_send, r_recv, l_send, l_recv = sems
    N, at, side = line.N, line.at, line.side
    wide = jnp.float32

    def both_ways(d):
        return ((at + d, at + d < N), (at - d, at - d >= 0)) if d else ((at, None),)

    def guarded(keep, step):
        if keep is None:
            step()
        else:
            pl.when(keep)(step)

    def y_copy(b, src=None):
        src = ybuf.at[b] if src is None else src
        return remote(src, ybuf.at[b], y_send.at[b], y_recv.at[b], line.pair)

    def r_copy(b, slot):
        return remote(ybuf.at[b], zbuf.at[slot], r_send.at[b], r_recv.at[b], line.right)

    def l_copy(b, slot):
        return remote(ybuf.at[b], zbuf.at[slot], l_send.at[b], l_recv.at[b], line.left)

    for d in range(N - 1, -1, -1):
        for b, keep in both_ways(d):

            def first(b=b):
                y_copy(b, theirs(b)).start()

            guarded(keep, first)
        yield
    for d in range(N - 1, 0, -1):
        for b, keep, ahead in ((at + d, at + d < N, True), (at - d, at - d >= 0, False)):

            def relay(b=b, ahead=ahead):
                mine = mine_of(b)
                y_copy(b).wait_recv()
                mine = mine + ybuf[b].astype(wide)
                came = line.has_left if ahead else line.has_right

                @pl.when(came)
                def _():
                    (r_copy if ahead else l_copy)(b, b).wait_recv()
                    ybuf[b] = (mine + zbuf[b].astype(wide)).astype(ybuf.dtype)

                @pl.when(jnp.logical_not(came))
                def _():
                    ybuf[b] = mine.astype(ybuf.dtype)

                if ahead:
                    pl.when(b == at + 1)(lambda: r_copy(b, b).start())
                    pl.when(b > at + 1)(lambda: r_copy(b, b).start())
                else:
                    pl.when(b == at - 1)(lambda: l_copy(b, N).start())
                    pl.when(b < at - 1)(lambda: l_copy(b, b).start())

            guarded(keep, relay)
        yield
    mine = mine_of(at)
    y_copy(at).wait_recv()
    total[...] = mine + ybuf[at].astype(wide)

    @pl.when(line.has_left)
    def _():
        r_copy(at, at).wait_recv()
        total[...] += zbuf[at].astype(wide)

    @pl.when(line.has_right)
    def _():
        l_copy(at, N).wait_recv()
        total[...] += zbuf[N].astype(wide)

    for d in range(N):
        for b, keep in both_ways(d):
            guarded(keep, lambda b=b: y_copy(b).wait_send())
    for d in range(1, N):
        pl.when(at + d < N)(lambda d=d: r_copy(at + d, at + d).wait_send())
        pl.when(at - d >= 0)(lambda d=d: l_copy(at - d, at - d).wait_send())


def scatter_line_job(line, value, stage, slots, pair_slot, total, sems):
    r_send, r_recv, l_send, l_recv, p_send, p_recv = sems
    n, N, at, side = line.n, line.N, line.at, line.side
    wide = jnp.float32

    def copy(q, slot, ahead):
        send, recv = (r_send, r_recv) if ahead else (l_send, l_recv)
        device = line.right if ahead else line.left
        return remote(stage.at[q], slots.at[slot], send.at[q], recv.at[q], device)

    for d in range(N - 1, 0, -1):
        for b, keep, ahead in ((at + d, at + d < N, True), (at - d, at - d >= 0, False)):

            def relay(b=b, ahead=ahead):
                came = line.has_left if ahead else line.has_right
                for y in range(2):
                    q = 2 * b + y

                    @pl.when(came)
                    def _(q=q, y=y):
                        copy(q, q, ahead).wait_recv()
                        stage[q] = (value(b, y) + slots[q].astype(wide)).astype(stage.dtype)

                    @pl.when(jnp.logical_not(came))
                    def _(q=q, y=y):
                        stage[q] = value(b, y).astype(stage.dtype)

                    if ahead:
                        copy(q, q, True).start()
                    else:
                        pl.when(b == at - 1)(lambda q=q, y=y: copy(q, n + y, False).start())
                        pl.when(b < at - 1)(lambda q=q: copy(q, q, False).start())

            pl.when(keep)(relay)
        yield

    def reach(y):
        q, y_slot = 2 * at + y, n + y
        pl.when(line.has_left)(lambda: copy(q, q, True).wait_recv())
        pl.when(line.has_right)(lambda: copy(q, y_slot, False).wait_recv())
        left = jnp.where(line.has_left, slots[q].astype(wide), 0.0)
        right = jnp.where(line.has_right, slots[y_slot].astype(wide), 0.0)
        return value(at, y) + left + right

    other = 2 * at + 1 - side
    stage[other] = reach(1 - side).astype(stage.dtype)
    swap = remote(stage.at[other], pair_slot, p_send, p_recv, line.pair)
    swap.start()
    mine = reach(side)
    yield
    swap.wait()
    total[...] = mine + pair_slot[...].astype(wide)
    for d in range(1, N):
        for y in range(2):
            pl.when(at + d < N)(lambda d=d, y=y: copy(2 * (at + d) + y, 0, True).wait_send())
            pl.when(at - d >= 0)(lambda d=d, y=y: copy(2 * (at - d) + y, 0, False).wait_send())


def gather_job(line, own, out, sems, use=None):
    r_send, l_send, y_send, recv, own_sem = sems
    n, N, at, side, c = line.n, line.N, line.at, line.side, line.c
    local = pltpu.make_async_copy(own, out(c), own_sem)
    local.start()

    def send(src, q, sem, device):
        return remote(src, out(q), sem.at[q // 2], recv.at[q], device)

    use = use or (lambda q: None)
    pair = c + 1 - 2 * side

    def other(d):
        for q, keep in ((pair - 2 * d, at - d >= 0), (pair + 2 * d, at + d < N))[: 1 + (d > 0)]:

            def take(q=q):
                send(out(q), q, y_send, line.pair).wait_recv()
                use(q)

            pl.when(keep)(take)

    pl.when(line.has_right)(lambda: send(own, c, r_send, line.right).start())
    pl.when(line.has_left)(lambda: send(own, c, l_send, line.left).start())
    send(own, c, y_send, line.pair).start()
    yield
    local.wait()
    use(c)
    for d in range(1, N):
        for q, keep, ahead in ((c - 2 * d, at - d >= 0, True), (c + 2 * d, at + d < N, False)):

            def relay(q=q, ahead=ahead):
                got = out(q)
                send(got, q, y_send, line.pair).wait_recv()
                if ahead:
                    pl.when(line.has_right)(lambda: send(got, q, r_send, line.right).start())
                else:
                    pl.when(line.has_left)(lambda: send(got, q, l_send, line.left).start())
                send(got, q, y_send, line.pair).start()
                use(q)

            pl.when(keep)(relay)
        yield
    for d in range(N):
        other(d)
    for b in range(N):
        q = 2 * b + side
        got = out(q)
        send(got, q, y_send, line.pair).wait_send()
        pl.when(jnp.logical_and(b <= at, line.has_right))(
            lambda q=q, got=got: send(got, q, r_send, line.right).wait_send()
        )
        pl.when(jnp.logical_and(b >= at, line.has_left))(
            lambda q=q, got=got: send(got, q, l_send, line.left).wait_send()
        )


def gather_pair_job(line, own, out, sems):
    r_send, l_send, y_send, recv, own_sem = sems
    n, N, at, c = line.n, line.N, line.at, line.c
    local = pltpu.make_async_copy(own, out(c), own_sem)
    local.start()

    def send(src, q, sem, device):
        return remote(src, out(q), sem.at[q], recv.at[q], device)

    def ahead(src, q, act):
        pl.when(line.has_right)(lambda: act(send(src, q, r_send, line.right)))

    def back(src, q, act):
        pl.when(line.has_left)(lambda: act(send(src, q, l_send, line.left)))

    start = lambda copy: copy.start()
    to_pair = remote(own, out(c), y_send.at[0], recv.at[c], line.pair)
    to_pair.start()
    ahead(own, c, start)
    back(own, c, start)
    yield
    local.wait()
    q = line.pair[0]
    got = out(q)
    send(got, q, r_send, line.pair).wait_recv()
    ahead(got, q, start)
    back(got, q, start)
    yield
    for d in range(1, N):
        for b, keep, forward in ((at - d, at - d >= 0, True), (at + d, at + d < N, False)):

            def relay(b=b, forward=forward):
                for y in range(2):
                    got = out(2 * b + y)
                    send(got, 2 * b + y, r_send, line.pair).wait_recv()
                    (ahead if forward else back)(got, 2 * b + y, start)

            pl.when(keep)(relay)
        yield
    to_pair.wait_send()
    done = lambda copy: copy.wait_send()
    for b in range(N):
        for y in range(2):
            q = 2 * b + y
            pl.when(b <= at)(lambda q=q: ahead(out(q), q, done))
            pl.when(b >= at)(lambda q=q: back(out(q), q, done))


def minor_rows(rows):
    return rows // 8


def scatter_steps(line, product, rows, total, made, scratch):
    N, side = line.N, line.side
    if len(made.shape) == 3:

        def theirs(b):
            made[b] = product(2 * b * rows + (1 - side) * rows, rows).astype(made.dtype)
            return made.at[b]

        yield from scatter_job(
            line,
            theirs,
            lambda b: product(2 * b * rows + side * rows, rows),
            total,
            *scratch[:2],
            scratch[2:8],
        )
        return
    few = minor_rows(rows)
    many = rows - few
    ybuf, zbuf = scratch[:2]
    stage, slots, pair_slot = scratch[8:11]
    wide = jnp.float32

    def theirs(b):
        both = product(2 * b * rows, 2 * rows).astype(made.dtype)
        made[b] = both.reshape(2, rows, D)
        return made.at[b, 1 - side, pl.ds(0, many)]

    minor = scatter_line_job(
        line,
        lambda b, y: made[b, y, many:, :].astype(wide),
        stage,
        slots,
        pair_slot,
        total.at[pl.ds(many, few)],
        scratch[11:17],
    )
    main = scatter_job(
        line,
        theirs,
        lambda b: made[b, side, :many, :].astype(wide),
        total.at[pl.ds(0, many)],
        ybuf,
        zbuf,
        scratch[2:8],
    )
    for _ in range(N):
        next(main)
        yield
    next(minor)
    for _ in range(N - 1):
        next(minor, None)
        next(main)
        yield
    finish(minor)
    finish(main)


def gather_steps(line, own, out, rows, scratch, use=None):
    few = minor_rows(rows)
    many = rows - few
    minor = gather_pair_job(
        line, own.at[pl.ds(many, few)], lambda q: out(q, many, few), scratch[5:10]
    )
    main = gather_job(line, own.at[pl.ds(0, many)], lambda q: out(q, 0, many), scratch[:5], use)
    next(minor)
    next(main)
    yield
    next(minor)
    for _ in range(line.N - 1):
        next(minor)
        next(main)
        yield
    finish(minor)
    finish(main)


GATHER = 10


def scatter_shapes(n, rows, roomy):
    N = n // 2
    few = minor_rows(rows) if roomy else 0
    many = rows - few
    low, dma = jnp.bfloat16, pltpu.SemaphoreType.DMA
    made = pltpu.VMEM((N, 2, rows, D) if roomy else (N, rows, D), low)
    scratch = [
        pltpu.VMEM((N, many, D), low),
        pltpu.VMEM((N + 1, many, D), low),
    ] + [dma((N,))] * 6
    if roomy:
        scratch += [
            pltpu.VMEM((n, few, D), low),
            pltpu.VMEM((n + 2, few, D), low),
            pltpu.VMEM((few, D), low),
        ]
        scratch += [dma((n,))] * 4 + [dma, dma]
    return made, scratch


def gather_scratch(n):
    N = n // 2
    dma = pltpu.SemaphoreType.DMA
    return [dma((N,)), dma((N,)), dma((N,)), dma((n,)), dma] + [
        dma((n,)),
        dma((n,)),
        dma((1,)),
        dma((n,)),
        dma,
    ]


def rms_factor(values):
    return lax.rsqrt(jnp.mean(values * values, axis=1, keepdims=True) + norm_eps)


def rms_back(values, gain, grad):
    factor = rms_factor(values)
    scaled = grad * gain
    inner = jnp.mean(scaled * values, axis=1, keepdims=True)
    d_gain = jnp.sum(grad * (values * factor), axis=0, keepdims=True)
    return factor * scaled - values * (factor * factor * factor * inner), d_gain


def matmul_rows(*pairs):
    def product(first, count):
        total = 0.0
        for left, right in pairs:
            part = left[pl.ds(pl.multiple_of(first, 16), count), :]
            if right.shape[0] == left.shape[1]:
                total = total + plain(part, right[...])
            else:
                total = total + cols_by_cols(part, right[...])
        return total

    return product


def finish(job):
    for _ in job:
        pass


def start_kernel(plan, n, x, w_in, w_up, w_mix, w_down, *refs):
    tokens, in_all, shared_all, up_some, mix_all, down_some = refs[:6]
    in_low, shared_low, up_low, mix_low, down_low = refs[6:11]
    t_sems, s_sems = refs[11 : 11 + GATHER], refs[11 + GATHER : 16 + GATHER]
    a_send, a_recv, x_send, x_recv, k_send, k_recv, own_sem = refs[16 + GATHER :]
    line = Line(n)
    c, w, sib, across = line.c, line.w, line.sib, line.across
    greet([((c + s) % n, w) for s in range(1, n)] + [(c, sib), (c, across)])
    R, B, G = plan.R, plan.B, FF // n
    low = jnp.bfloat16
    place = lambda q, first, count: tokens.at[q, pl.ds(first, count)]
    inputs = gather_steps(line, x, place, x.shape[0], t_sems)
    next(inputs)
    passed, pending = [], []

    def pass_on(number, view, src=None):
        src = view(w) if src is None else src
        to_x = remote(src, view(w), x_send.at[number], x_recv.at[number], (c, across))
        to_k = remote(src, view(w), k_send.at[0, number], k_recv.at[0, number], (c, sib))
        to_x.start()
        to_k.start()
        pending.append(to_x)
        pending.append(to_k)
        passed.append((number, view))

    mix_low[...] = w_mix[...].astype(low)
    pass_on(2 * n, lambda place: mix_all.at[0, place], mix_low)
    shared_low[...] = jnp.zeros_like(shared_low)
    shared_low[:, : END - BC_AT] = w_in[:, BC_AT:END].astype(low)
    for p in range(n):
        if p < plan.attn:
            g = plan.kv_of(p)
            in_low[p, :, :R] = w_in[:, p * R : (p + 1) * R].astype(low)
            in_low[p, :, B : B + HD] = w_in[:, K_AT + g * HD : K_AT + (g + 1) * HD].astype(low)
            in_low[p, :, B + HD : B + 2 * HD] = w_in[
                :, V_AT + g * HD : V_AT + (g + 1) * HD
            ].astype(low)
            if B + 2 * HD < plan.A:
                rest = plan.A - B - 2 * HD
                in_low[p, :, B + 2 * HD :] = jnp.zeros((in_low.shape[1], rest), low)
        else:
            j = p - plan.attn
            in_low[p, :, :R] = w_in[:, Z_AT + j * R : Z_AT + (j + 1) * R].astype(low)
            in_low[p, :, B : B + R] = w_in[:, X_AT + j * R : X_AT + (j + 1) * R].astype(low)
            if B + R < plan.A:
                in_low[p, :, B + R :] = jnp.zeros((in_low.shape[1], plan.A - B - R), low)

    common = gather_job(line, shared_low, lambda q: shared_all.at[q, w], s_sems)
    next(common)

    def send_columns(steps):
        for s in steps:
            p = (c + s) % n
            copy = remote(
                in_low.at[p], in_all.at[c, w], a_send.at[0, s], a_recv.at[0, c], (p, w)
            )
            copy.start()
            pending.append(copy)

    in_view = lambda q: lambda place: in_all.at[q, place]
    shared_view = lambda q: lambda place: shared_all.at[q, place]

    def take_columns(steps):
        for s in steps:
            q = (c + n - s) % n
            got = in_all.at[q, w]
            remote(got, got, a_send.at[0, s], a_recv.at[0, q], (q, w)).wait_recv()
            pass_on(q, in_view(q))

    done = [0]

    def seconds(upto):
        while done[0] < min(upto, len(passed)):
            number, view = passed[done[0]]
            got = view(across)
            remote(got, got, x_send.at[number], x_recv.at[number], (c, across)).wait_recv()
            out = remote(got, got, k_send.at[1, number], k_recv.at[1, number], (c, sib))
            out.start()
            pending.append(out)
            done[0] += 1

    cuts = [round(1 + (n - 1) * i / 3) for i in range(4)]
    parts = [range(cuts[i], cuts[i + 1]) for i in range(3)]
    send_columns(parts[0])
    pass_on(c, in_view(c), in_low.at[c])
    pass_on(n + c, shared_view(c), shared_low)
    down_low[...] = w_down[...].astype(low)
    for p in range(n):
        up_low[p, :, :G] = w_up[:, p * G : (p + 1) * G].astype(low)
        up_low[p, :, G:] = w_up[:, FF + p * G : FF + (p + 1) * G].astype(low)
    locals_started = []
    own = (
        (in_low.at[c], in_all.at[c, w]),
        (mix_low, mix_all.at[0, w]),
        (up_low.at[c], up_some.at[c]),
        (down_low, down_some.at[0]),
    )
    for i, (src, dst) in enumerate(own):
        copy = pltpu.make_async_copy(src, dst, own_sem.at[i])
        copy.start()
        locals_started.append(copy)
    for step in range(3):
        for _ in range(line.N // 4):
            next(common, None)
            next(inputs, None)
        if step < 2:
            send_columns(parts[step + 1])
        else:
            for s in range(1, n):
                p = (c + s) % n
                out = remote(
                    up_low.at[p], up_some.at[c], a_send.at[1, s], a_recv.at[1, c], (p, w)
                )
                out.start()
                pending.append(out)
        take_columns(parts[step])
        if step == 2:
            finish(common)
            for s in range(1, n):
                pass_on(n + (c + s) % n, shared_view((c + s) % n))
        seconds(len(passed) - 4)
    finish(inputs)
    seconds(len(passed))
    for s in range(1, n):
        q = (c + n - s) % n
        got = up_some.at[q]
        remote(got, got, a_send.at[1, s], a_recv.at[1, q], (q, w)).wait_recv()
    for number, view in passed:
        for half, place in ((0, sib), (1, (sib + 2) % 4)):
            got = view(place)
            remote(got, got, k_send.at[half, number], k_recv.at[half, number], (c, sib)).wait_recv()
    for copy in locals_started:
        copy.wait()
    for out in pending:
        out.wait_send()


def branch_kernel(n, refs_in, refs_out, scratch):
    left, right, source, gain, upstream, up, down = refs_in
    middle, active, grad_gates, normed, up_all, down_all = refs_out
    line = Line(n)
    line.greet([(line.c, line.sib), (line.c, line.across)])
    rows = source.shape[0]
    (total, own, made), (flow, gather, extra) = scratch[:3], scratch[3:]
    share = share_job((up, down), (up_all, down_all), extra)
    main = scatter_steps(line, matmul_rows((left, right)), rows, total, made, flow)
    next(main)
    next(share)
    finish(main)
    value = source[...].astype(jnp.float32) + total[...]
    middle[...] = value
    own[...] = (value * rms_factor(value) * gain[...]).astype(own.dtype)
    place = lambda q, first, count: normed.at[q, pl.ds(first, count)]

    half = grad_gates.shape[1] // 2

    def use(q):
        low = active.dtype
        gate_up = plain(normed[q], up_all[...].reshape(D, -1))
        gate, other = gate_up[:, :half], gate_up[:, half:]
        at = ring_place(n, line.w, q)
        grad = cols_by_cols(upstream[at], down_all[...].reshape(-1, D))
        sig = jax.nn.sigmoid(gate)
        passed = gate * sig
        active[pl.ds(pl.multiple_of(at * rows, rows), rows), :] = (passed * other).astype(low)
        here_rows = pl.ds(pl.multiple_of(q * rows, rows), rows)
        grad_gates[here_rows, :half] = (grad * other * (sig * (1.0 + gate * (1.0 - sig)))).astype(low)
        grad_gates[here_rows, half:] = (grad * passed).astype(low)

    fused = active.shape[0] == n * rows
    spread_out = gather_steps(
        line, own, place, rows, gather, use if fused else None
    )
    next(spread_out)
    next(share)
    finish(share)
    finish(spread_out)


def feed_back_kernel(n, refs_in, refs_out, scratch):
    left, right, cotangent, middle, gain, active, w_mix, w_down, normed, upstream, up, down = refs_in
    grad, d_gain, made, late, low_all, up_sum, down_sum = refs_out
    line = Line(n)
    line.greet([(line.c, line.sib), (line.c, line.across)])
    rows = cotangent.shape[0]
    (total, own, terms), (flow, gather, extra) = scratch[:3], scratch[3:]
    both = active.shape[0] == n * rows
    if both:
        (up, down, normed_part, upstream_part, part_sem), extra = extra[:5], extra[5:]
        width = D // n
        height = down.shape[2]

        def fetch(s):
            columns = pl.ds(pl.multiple_of((line.c + s) % n * width, 128), width)
            return [
                pltpu.make_async_copy(a.at[:, columns], b.at[s % 2], part_sem.at[i, s % 2])
                for i, (a, b) in enumerate(((normed, normed_part), (upstream, upstream_part)))
            ]

        def piece(s):
            q = (line.c + s) % n
            for copy in fetch(s):
                copy.wait()
            if s:
                for copy in fetch((s + 1) % n):
                    copy.start()
            part = rows_by_rows(normed_part[s % 2], left[...])
            up[q] = part.astype(up.dtype).reshape(up.shape[1:])
            part = rows_by_rows(active[...], upstream_part[s % 2]).astype(down.dtype)
            columns = pl.ds(pl.multiple_of(q * width, 128), width)
            for k in range(4):
                down[0, k, :, columns] = part[k * height : (k + 1) * height]

        for copy in fetch(1):
            copy.start()
    else:
        piece = lambda s: None
    sums = Collect(n, ("rows", "rows"), (up, down), (up_sum, down_sum), extra)
    main = scatter_steps(line, matmul_rows((left, right)), rows, total, terms, flow)
    for _ in range(line.N):
        next(main)
    steps = sums.steps
    made_count = [0]

    def advance():
        at = made_count[0]
        if at < len(steps):
            piece(steps[at])
            sums.send(steps[at])
        if 0 <= at - 1 < len(steps):
            sums.cross(steps[at - 1])
        made_count[0] += 1

    for i in range(line.N - 1):
        advance()
        if i:
            advance()
        next(main)
    finish(main)
    back, gain_row = rms_back(middle[...], gain[...], total[...])
    value = cotangent[...].astype(jnp.float32) + back
    grad[...] = value
    d_gain[...] = jnp.broadcast_to(gain_row, d_gain.shape)
    own[...] = value.astype(own.dtype)
    place = lambda q, first, count: low_all.at[q, pl.ds(first, count)]

    def use(q):
        block = pl.ds(pl.multiple_of(q * rows, rows), rows)
        made[block, :] = cols_by_cols(low_all[q], w_mix[...]).astype(made.dtype)
        late[block, :] = plain(active[block, :], w_down[...]).astype(late.dtype)

    spread_out = gather_steps(
        line, own, place, rows, gather, use if both else None
    )
    next(spread_out)
    for _ in range(line.N - 1):
        advance()
        next(spread_out)
    while made_count[0] <= len(steps):
        advance()
    finish(spread_out)
    for s in sums.steps:
        sums.close(s)
    sums.end()


SUMS = ("cols", "cols", "rows")


def source_back_kernel(n, refs_in, refs_out, scratch):
    (left, left_two, right, right_two, source, grad_middle, gain, vector, up) = refs_in[:9]
    mixed, gain_column, unit, branch, w_in, w_shared, w_mix = refs_in[9:]
    grad, vector_sum, up_home, in_sum, shared_sum, mix_sum = refs_out
    line = Line(n)
    others = [((line.c + s) % n, line.w) for s in range(1, n)]
    greet(others + [(line.c, line.sib), (line.c, line.across)])
    rows = source.shape[0]
    (total, _, made), (flow, _, extra) = scratch[:3], scratch[3:]
    both = unit.shape[0] == n * rows
    if both:
        (w_in, w_shared, w_mix, unit_part, branch_part, part_sem, local), extra = extra[:7], extra[7:]
        width = D // n
        height = w_mix.shape[2]
        local[...] = vector[...]

        def fetch(s):
            columns = pl.ds(pl.multiple_of((line.c + s) % n * width, 128), width)
            return [
                pltpu.make_async_copy(a.at[:, columns], b.at[s % 2], part_sem.at[i, s % 2])
                for i, (a, b) in enumerate(((unit, unit_part), (branch, branch_part)))
            ]

        def piece(s):
            q = (line.c + s) % n
            for copy in fetch(s):
                copy.wait()
            if s:
                for copy in fetch((s + 1) % n):
                    copy.start()
            place = pl.ds(pl.multiple_of(q * width, 128), width)
            scale = gain_column[place, :]
            part = rows_by_rows(unit_part[s % 2], left[...])
            w_in[q] = (part * scale).astype(w_in.dtype).reshape(w_in.shape[1:])
            two = rows_by_rows(unit_part[s % 2], left_two[...])
            w_shared[q] = (two * scale).astype(w_shared.dtype).reshape(w_shared.shape[1:])
            each = jnp.concatenate(
                [
                    part * right[place, :].astype(jnp.float32),
                    two * right_two[place, :].astype(jnp.float32),
                ],
                axis=1,
            )
            ones = jnp.ones((8, each.shape[1]), jnp.bfloat16)
            row = sum(cols_by_cols(ones, some) for some in pieces(each, 3))
            for i in range(width // 128):
                at = q * (width // 128) + i
                local[pl.ds(at, 1), :] = row[0:1, i * 128 : (i + 1) * 128]
            part = rows_by_rows(mixed[...], branch_part[s % 2]).astype(w_mix.dtype)
            for k in range(4):
                w_mix[0, k, :, place] = part[k * height : (k + 1) * height]

        for copy in fetch(1):
            copy.start()
    else:
        local = vector
        piece = lambda s: None
    sums = Collect(n, SUMS, (w_in, w_shared, w_mix), (in_sum, shared_sum, mix_sum), extra[:-6])
    vectors = sum_job(n, local, vector_sum, *extra[-6:-2])
    home = home_job(n, up, up_home, *extra[-2:])
    product = matmul_rows((left, right), (left_two, right_two))
    main = scatter_steps(line, product, rows, total, made, flow)
    steps = sums.steps
    next(home)
    made_count = [0]

    def advance(more=1):
        for _ in range(more):
            at = made_count[0]
            if at < len(steps):
                piece(steps[at])
                sums.send(steps[at])
            if 0 <= at - 1 < len(steps):
                sums.cross(steps[at - 1])
            if 0 <= at - 4 < len(steps):
                sums.close(steps[at - 4])
            made_count[0] += 1

    for _ in range(line.N):
        next(main)
        advance(2)
    next(vectors)
    for _ in main:
        next(vectors, None)
        advance()
    advance(len(steps) + 4 - made_count[0])
    finish(vectors)
    back, _ = rms_back(source[...].astype(jnp.float32), gain[...], total[...])
    grad[...] = grad_middle[...] + back
    finish(home)
    sums.end()


def flow_call(
    kernel, n, rows, args, outs, gathers, away, extra, collective_id, near=False, far_args=()
):
    inside = pl.BlockSpec(memory_space=pltpu.VMEM)
    outside = pl.BlockSpec(memory_space=pl.ANY)
    side_args, side_shapes, side_scratch = extra
    shapes = list(outs)
    specs = [inside] * len(outs)
    scratch = [
        pltpu.VMEM((rows, D), jnp.float32),
        pltpu.VMEM((rows, D) if gathers else (16, 128), jnp.bfloat16),
    ]
    made, flow = scatter_shapes(n, rows, args[0].shape[0] <= 1024)
    gather = []
    if gathers:
        shapes.append(jax.ShapeDtypeStruct((n, rows, D), jnp.bfloat16))
        specs.append(inside if near else outside)
        gather = gather_scratch(n)
    scratch = scratch + [made] + flow + gather + list(side_scratch)
    ends = 3 + len(flow), 3 + len(flow) + len(gather)
    side = outside if away else inside
    in_specs = [inside] * len(args) + [outside] * len(far_args) + [side] * len(side_args)
    specs = specs + [inside if near else side] * len(side_shapes)
    shapes = shapes + list(side_shapes)
    first, second = len(in_specs), len(in_specs) + len(specs)

    def run(*refs):
        parts = refs[second:]
        groups = parts[3 : ends[0]], parts[ends[0] : ends[1]], parts[ends[1] :]
        kernel(n, refs[:first], refs[first:second], tuple(parts[:3]) + groups)

    return pl.pallas_call(
        run,
        out_shape=tuple(shapes),
        in_specs=in_specs,
        out_specs=tuple(specs),
        scratch_shapes=scratch,
        cost_estimate=pl.CostEstimate(flops=0, bytes_accessed=2 * 10**8, transcendentals=0),
        compiler_params=pltpu.CompilerParams(
            collective_id=collective_id, has_side_effects=True, vmem_limit_bytes=VMEM
        ),
    )(*args, *far_args, *side_args)


def start_call(plan, n, x, w_in, w_up, w_mix, w_down, collective_id):
    rows = w_in.shape[0]
    low = jnp.bfloat16
    G = FF // n
    shapes = (
        jax.ShapeDtypeStruct((n,) + x.shape, low),
        jax.ShapeDtypeStruct((n, 4, rows, plan.A), low),
        jax.ShapeDtypeStruct((n, 4, rows, plan.K), low),
        jax.ShapeDtypeStruct((n, rows, 2 * G), low),
        jax.ShapeDtypeStruct((1, 4) + w_mix.shape, low),
        jax.ShapeDtypeStruct((1,) + w_down.shape, low),
    )
    dma = pltpu.SemaphoreType.DMA
    outside = pl.BlockSpec(memory_space=pl.ANY)
    inside = pl.BlockSpec(memory_space=pltpu.VMEM)
    blocks = 2 * n + 1
    outs = pl.pallas_call(
        functools.partial(start_kernel, plan, n),
        out_shape=shapes,
        in_specs=[outside] + [inside] * 4,
        out_specs=(outside,) * 6,
        scratch_shapes=[
            pltpu.VMEM((n, rows, plan.A), low),
            pltpu.VMEM((rows, plan.K), low),
            pltpu.VMEM((n, rows, 2 * G), low),
            pltpu.VMEM(w_mix.shape, low),
            pltpu.VMEM(w_down.shape, low),
        ]
        + gather_scratch(n)
        + gather_scratch(n)[:5]
        + [dma((2, n)), dma((2, n))]
        + [dma((blocks,)), dma((blocks,)), dma((2, blocks)), dma((2, blocks))]
        + [dma((4,))],
        cost_estimate=pl.CostEstimate(flops=0, bytes_accessed=2 * 10**8, transcendentals=0),
        compiler_params=pltpu.CompilerParams(
            collective_id=collective_id, has_side_effects=True, vmem_limit_bytes=VMEM
        ),
    )(x, w_in, w_up, w_mix, w_down)
    flat = lambda o: o.reshape(-1, o.shape[-1])
    tokens, in_all, shared_all, up_some, mix_all, down_some = outs
    return flat(tokens), flat(in_all), flat(shared_all), up_some, flat(mix_all), down_some


def mm(left, right):
    return jnp.dot(
        left.astype(jnp.bfloat16), right.astype(jnp.bfloat16), preferred_element_type=jnp.float32
    )


def mm_nt(left, right):
    return cols_by_cols(left.astype(jnp.bfloat16), right.astype(jnp.bfloat16))


def mm_tn(left, right):
    return rows_by_rows(left.astype(jnp.bfloat16), right.astype(jnp.bfloat16))


def pieces(values, count):
    found = []
    for _ in range(count):
        part = values.astype(jnp.bfloat16)
        found.append(part)
        values = values - part.astype(jnp.float32)
    return found


def by_marks(values, marks, count=2):
    return plain(
        jnp.concatenate(pieces(values, count), axis=1), jnp.concatenate([marks] * count, axis=0)
    )


def marks_by(marks, values, count=3):
    return plain(
        jnp.concatenate([marks] * count, axis=1), jnp.concatenate(pieces(values, count), axis=0)
    )


def iota(shape, axis):
    return lax.broadcasted_iota(jnp.int32, shape, axis)


def rope_tables(length):
    half = HD // 2
    frequency = rope_base ** (-jnp.arange(half, dtype=jnp.float32) / half)
    angles = jnp.arange(length).astype(jnp.float32)[:, None] * frequency[None, :]
    cosine, sine = jnp.cos(angles), jnp.sin(angles)
    return (
        jnp.concatenate([cosine, cosine], axis=1),
        jnp.concatenate([-sine, sine], axis=1),
    )


def turned(values, cosine, sine):
    return values * cosine + pltpu.roll(values, HD // 2, 1) * sine


def attn_stack(plan, q_ref, cosine, sine):
    heads = [
        turned(q_ref[:, h * HD : (h + 1) * HD], cosine, sine).astype(jnp.bfloat16)
        for h in range(plan.ha)
    ]
    return jnp.concatenate(heads, axis=0)


def by_extent(step, length, run):
    parts = 4
    per = length // CHUNK // parts
    for part in range(parts):
        pl.when(step // per == part)(functools.partial(run, (part + 1) * per * CHUNK))


def attn_softmax(stack, keys, at):
    scores = cols_by_cols(stack, keys) * (1.0 / math.sqrt(HD))
    row = iota(scores.shape, 0) & (CHUNK - 1)
    scores = jnp.where(iota(scores.shape, 1) <= row + at, scores, masked_score)
    weights = jnp.exp(scores - jnp.max(scores, axis=1, keepdims=True))
    return weights * (1.0 / jnp.sum(weights, axis=1, keepdims=True))


def attn_fwd_kernel(plan, q_ref, k_ref, v_ref, cos_ref, sin_ref, out_ref, keys, values):
    step = pl.program_id(0)

    @pl.when(step == 0)
    def _():
        keys[...] = turned(k_ref[...], cos_ref[...], sin_ref[...]).astype(jnp.bfloat16)
        values[...] = v_ref[...].astype(jnp.bfloat16)

    at = pl.multiple_of(step * CHUNK, CHUNK)
    rows = pl.ds(at, CHUNK)
    stack = attn_stack(plan, q_ref, cos_ref[rows, :], sin_ref[rows, :])

    def run(extent):
        probs = attn_softmax(stack, keys[:extent, :], at)
        made = mm(probs, values[:extent, :])
        for h in range(plan.ha):
            out_ref[:, h * HD : (h + 1) * HD] = made[h * CHUNK : (h + 1) * CHUNK]

    by_extent(step, keys.shape[0], run)


def attn_fwd(plan, proj, tables):
    length = proj.shape[0]
    whole = lambda i: (0, 0)
    return pl.pallas_call(
        functools.partial(attn_fwd_kernel, plan),
        grid=(length // CHUNK,),
        out_shape=jax.ShapeDtypeStruct((length, plan.R), jnp.float32),
        in_specs=[
            pl.BlockSpec((CHUNK, plan.R), lambda i: (i, 0)),
            pl.BlockSpec((length, HD), lambda i: (0, plan.B // HD)),
            pl.BlockSpec((length, HD), lambda i: (0, plan.B // HD + 1)),
            pl.BlockSpec((length, HD), whole),
            pl.BlockSpec((length, HD), whole),
        ],
        out_specs=pl.BlockSpec((CHUNK, plan.R), lambda i: (i, 0)),
        scratch_shapes=[pltpu.VMEM((length, HD), jnp.bfloat16)] * 2,
        compiler_params=pltpu.CompilerParams(vmem_limit_bytes=VMEM),
    )(proj, proj, proj, *tables)


def attn_bwd_kernel(
    plan, q_ref, k_ref, v_ref, cos_ref, sin_ref, grad_ref, slab_ref, keys, values, grad_k, grad_v
):
    step = pl.program_id(0)
    scale = 1.0 / math.sqrt(HD)

    @pl.when(step == 0)
    def _():
        keys[...] = turned(k_ref[...], cos_ref[...], sin_ref[...]).astype(jnp.bfloat16)
        values[...] = v_ref[...].astype(jnp.bfloat16)
        grad_k[...] = jnp.zeros_like(grad_k)
        grad_v[...] = jnp.zeros_like(grad_v)
        slab_ref[...] = jnp.zeros_like(slab_ref)

    at = pl.multiple_of(step * CHUNK, CHUNK)
    rows = pl.ds(at, CHUNK)
    cosine, sine = cos_ref[rows, :], sin_ref[rows, :]
    stack = attn_stack(plan, q_ref, cosine, sine)
    grads = jnp.concatenate([grad_ref[:, h * HD : (h + 1) * HD] for h in range(plan.ha)], axis=0)

    def run(extent):
        probs = attn_softmax(stack, keys[:extent, :], at)
        grad_probs = cols_by_cols(grads, values[:extent, :])
        delta = jnp.sum(probs * grad_probs, axis=1, keepdims=True)
        grad_scores = (probs * (grad_probs - delta)).astype(jnp.bfloat16)
        grad_q = mm(grad_scores, keys[:extent, :]) * scale
        for h in range(plan.ha):
            slab_ref[rows, h * HD : (h + 1) * HD] = turned(
                grad_q[h * CHUNK : (h + 1) * CHUNK], cosine, -sine
            ).astype(jnp.bfloat16)
        grad_k[:extent, :] += mm_tn(grad_scores, stack)
        grad_v[:extent, :] += mm_tn(probs, grads)

    by_extent(step, keys.shape[0], run)

    @pl.when(step == pl.num_programs(0) - 1)
    def _():
        slab_ref[:, plan.B : plan.B + HD] = turned(
            grad_k[...] * scale, cos_ref[...], -sin_ref[...]
        ).astype(jnp.bfloat16)
        slab_ref[:, plan.B + HD : plan.B + 2 * HD] = grad_v[...].astype(jnp.bfloat16)


def attn_bwd(plan, proj, tables, grad):
    length = proj.shape[0]
    whole = lambda i: (0, 0)
    return pl.pallas_call(
        functools.partial(attn_bwd_kernel, plan),
        grid=(length // CHUNK,),
        out_shape=jax.ShapeDtypeStruct((length, plan.A), jnp.bfloat16),
        in_specs=[
            pl.BlockSpec((CHUNK, plan.R), lambda i: (i, 0)),
            pl.BlockSpec((length, HD), lambda i: (0, plan.B // HD)),
            pl.BlockSpec((length, HD), lambda i: (0, plan.B // HD + 1)),
            pl.BlockSpec((length, HD), whole),
            pl.BlockSpec((length, HD), whole),
            pl.BlockSpec((CHUNK, plan.R), lambda i: (i, 0)),
        ],
        out_specs=pl.BlockSpec((length, plan.A), whole),
        scratch_shapes=[pltpu.VMEM((length, HD), jnp.bfloat16)] * 2
        + [pltpu.VMEM((length, HD), jnp.float32)] * 2,
        compiler_params=pltpu.CompilerParams(vmem_limit_bytes=VMEM),
    )(proj, proj, proj, *tables, grad)


def head_spread(plan):
    return ((iota((PAD, plan.R), 1) >> 6) == iota((PAD, plan.R), 0)).astype(jnp.bfloat16)


def head_gather(plan):
    return ((iota((plan.R, PAD), 0) >> 6) == iota((plan.R, PAD), 1)).astype(jnp.bfloat16)


def lower_ones():
    shape = (CHUNK, CHUNK)
    return (iota(shape, 0) >= iota(shape, 1)).astype(jnp.bfloat16)


def space_parts(plan, dt_raw, window, conv_ref, head_ref, pick_ref):
    total = conv_ref[4:5, :]
    for k in range(CONV):
        at = 8 - CONV + 1 + k
        total = total + conv_ref[k : k + 1, :] * window[at : at + CHUNK, :]
    raw = by_marks(dt_raw, pick_ref[...], 3) + head_ref[1:2, :]
    steps = jnp.maximum(raw, 0.0) + jnp.log1p(jnp.exp(-jnp.abs(raw)))
    logs = -steps * jnp.exp(head_ref[0:1, :])
    cumul = marks_by(lower_ones(), logs)
    return total, raw, steps, logs, cumul


def decay_of(cumul, cumul_t, causal, h):
    gaps = cumul[:, h : h + 1] - cumul_t[h : h + 1, :]
    return jnp.exp(jnp.where(causal, gaps, masked_score))


def space_fwd_kernel(
    plan, proj_ref, shared_ref, conv_ref, head_ref, pick_ref, gated_ref, made_ref, before_ref, state, window
):
    R = plan.R
    step = pl.program_id(0)

    @pl.when(step == 0)
    def _():
        state[...] = jnp.zeros_like(state)
        window[0:8, :] = jnp.zeros((8, window.shape[1]), jnp.float32)

    @pl.when(step > 0)
    def _():
        window[0:8, :] = window[CHUNK : CHUNK + 8, :]

    window[8 : CHUNK + 8, :R] = proj_ref[:, plan.B : plan.B + R]
    window[8 : CHUNK + 8, R:] = shared_ref[:, : 2 * NS]
    total, _, steps, _, cumul = space_parts(
        plan, shared_ref[:, 2 * NS :], window, conv_ref, head_ref, pick_ref
    )
    post = total * jax.nn.sigmoid(total)
    x = post[:, :R]
    b = post[:, R : R + NS].astype(jnp.bfloat16)
    c = post[:, R + NS :].astype(jnp.bfloat16)
    spread_heads = head_spread(plan)
    cumul_t = cumul.T
    last = cumul[CHUNK - 1 : CHUNK, :]
    tail = jnp.exp(last - cumul)
    weighted = x * by_marks(steps, spread_heads)
    causal = iota((CHUNK, CHUNK), 0) >= iota((CHUNK, CHUNK), 1)
    inner = cols_by_cols(c, b)
    before = state[...]
    before_ref[0] = before.astype(jnp.bfloat16)
    made = mm(c, before) * by_marks(jnp.exp(cumul), spread_heads)
    made = made + by_marks(jnp.broadcast_to(head_ref[2:3, :], (8, PAD)), spread_heads)[0:1] * x
    left = iota((CHUNK, 2 * MP), 1) < MP
    weighted_low = weighted.astype(jnp.bfloat16)
    intra = []
    for pair in range(plan.hm // 2):
        lanes = weighted_low[:, pair * 2 * MP : (pair + 1) * 2 * MP]
        one = mm(inner * decay_of(cumul, cumul_t, causal, 2 * pair), lanes)
        two = mm(inner * decay_of(cumul, cumul_t, causal, 2 * pair + 1), lanes)
        intra.append(jnp.where(left, one, two))
    made = made + jnp.concatenate(intra, axis=1)
    state[...] = before * by_marks(
        jnp.broadcast_to(jnp.exp(last), (8, PAD)), spread_heads
    )[0:1] + mm_tn(b, weighted * by_marks(tail, spread_heads))
    z = proj_ref[:, :R]
    made_ref[...] = made
    gated_ref[...] = made * (z * jax.nn.sigmoid(z))


def space_fwd(plan, proj, shared, conv, heads, pick):
    length = proj.shape[0]
    chunks = length // CHUNK
    W = plan.W
    whole = lambda i: (0, 0)
    rows = lambda i: (i, 0)
    return pl.pallas_call(
        functools.partial(space_fwd_kernel, plan),
        grid=(chunks,),
        out_shape=(
            jax.ShapeDtypeStruct((length, plan.R), jnp.float32),
            jax.ShapeDtypeStruct((length, plan.R), jnp.float32),
            jax.ShapeDtypeStruct((chunks, NS, plan.R), jnp.bfloat16),
        ),
        in_specs=[
            pl.BlockSpec((CHUNK, plan.A), rows),
            pl.BlockSpec((CHUNK, plan.K), rows),
            pl.BlockSpec((8, W), whole),
            pl.BlockSpec((8, PAD), whole),
            pl.BlockSpec((PAD, PAD), whole),
        ],
        out_specs=(
            pl.BlockSpec((CHUNK, plan.R), rows),
            pl.BlockSpec((CHUNK, plan.R), rows),
            pl.BlockSpec((1, NS, plan.R), lambda i: (i, 0, 0)),
        ),
        scratch_shapes=[
            pltpu.VMEM((NS, plan.R), jnp.float32),
            pltpu.VMEM((CHUNK + 8, W), jnp.float32),
        ],
        compiler_params=pltpu.CompilerParams(vmem_limit_bytes=VMEM),
    )(proj, shared, conv, heads, pick)


def space_bwd_kernel(
    plan, proj_ref, shared_ref, prev_ref, prev_shared, conv_ref, head_ref, pick_ref, gain_ref, row_ref,
    grad_ref, made_ref, before_ref, slab_ref, slab_shared, conv_acc, head_acc, skip_acc, d_state, window, d_window,
):
    R = plan.R
    step = pl.program_id(0)
    chunk = pl.num_programs(0) - 1 - step

    @pl.when(step == 0)
    def _():
        d_state[...] = jnp.zeros_like(d_state)
        d_window[CHUNK : CHUNK + 8, :] = jnp.zeros((8, plan.W), jnp.float32)
        conv_acc[...] = jnp.zeros_like(conv_acc)
        head_acc[...] = jnp.zeros_like(head_acc)
        skip_acc[...] = jnp.zeros_like(skip_acc)

    @pl.when(step > 0)
    def _():
        d_window[CHUNK : CHUNK + 8, :] = d_window[0:8, :]

    window[0:8, :R] = jnp.where(chunk == 0, 0.0, prev_ref[:, plan.B : plan.B + R])
    window[0:8, R:] = jnp.where(chunk == 0, 0.0, prev_shared[:, : 2 * NS])
    window[8 : CHUNK + 8, :R] = proj_ref[:, plan.B : plan.B + R]
    window[8 : CHUNK + 8, R:] = shared_ref[:, : 2 * NS]
    total, raw, steps, logs, cumul = space_parts(
        plan, shared_ref[:, 2 * NS :], window, conv_ref, head_ref, pick_ref
    )
    sig = jax.nn.sigmoid(total)
    post = total * sig
    x = post[:, :R]
    b = post[:, R : R + NS].astype(jnp.bfloat16)
    c = post[:, R + NS :].astype(jnp.bfloat16)
    spread_heads = head_spread(plan)
    gather_heads = head_gather(plan)
    cumul_t = cumul.T
    last = cumul[CHUNK - 1 : CHUNK, :]
    steps_wide = by_marks(steps, spread_heads)
    tail_wide = by_marks(jnp.exp(last - cumul), spread_heads)
    grow_wide = by_marks(jnp.exp(cumul), spread_heads)
    last_wide = by_marks(jnp.broadcast_to(jnp.exp(last), (8, PAD)), spread_heads)[0:1]
    skip_wide = by_marks(jnp.broadcast_to(head_ref[2:3, :], (8, PAD)), spread_heads)[0:1]
    weighted = x * steps_wide
    causal = iota((CHUNK, CHUNK), 0) >= iota((CHUNK, CHUNK), 1)
    inner = cols_by_cols(c, b)

    z = proj_ref[:, :R]
    sig_z = jax.nn.sigmoid(z)
    grad = grad_ref[...].astype(jnp.float32)
    gate = z * sig_z
    gated = made_ref[...] * gate
    row_factor = row_ref[:, 0:1]
    skip_acc[1:2, :] += jnp.sum(grad * gated * row_factor, axis=0, keepdims=True)
    grad = grad * gain_ref[0:1, :] * row_factor - gated * row_ref[:, 1:2]
    d_made = grad * gate
    slab_ref[:, :R] = (grad * made_ref[...] * (sig_z * (1.0 + z * (1.0 - sig_z)))).astype(
        jnp.bfloat16
    )
    skip_acc[0:1, :] += jnp.sum(d_made * x, axis=0, keepdims=True)

    before = before_ref[0]
    d_after = d_state[...]
    d_after_low = d_after.astype(jnp.bfloat16)
    grown = d_made * grow_wide
    grown_low = grown.astype(jnp.bfloat16)
    carried = mm(c, before)
    d_c = mm_nt(grown_low, before)
    pulled = weighted * tail_wide
    d_pulled = mm(b, d_after_low)
    d_b = mm_nt(pulled, d_after_low)
    d_cumul = by_marks(grown * carried, gather_heads)
    kept = by_marks(d_pulled * pulled, gather_heads)
    d_cumul = d_cumul - kept
    decayed = jnp.sum(d_after * before.astype(jnp.float32), axis=0, keepdims=True) * last_wide
    d_last = jnp.sum(kept, axis=0, keepdims=True) + by_marks(
        jnp.broadcast_to(decayed, (8, R)), gather_heads
    )[0:1]
    d_state[...] = d_after * last_wide + mm_tn(c, grown_low)

    left = iota((CHUNK, 2 * MP), 1) < MP
    lane = iota((CHUNK, PAD), 1)
    sub = iota((8, CHUNK), 0)
    weighted_low = weighted.astype(jnp.bfloat16)
    d_made_low = d_made.astype(jnp.bfloat16)
    d_inner = jnp.zeros((CHUNK, CHUNK), jnp.float32)
    columns = jnp.zeros((8, CHUNK), jnp.float32)
    d_weighted = []
    for pair in range(plan.hm // 2):
        at = slice(pair * 2 * MP, (pair + 1) * 2 * MP)
        lanes, d_lanes = weighted_low[:, at], d_made_low[:, at]
        halves = []
        for which in range(2):
            h = 2 * pair + which
            decay = decay_of(cumul, cumul_t, causal, h)
            whole = inner * decay
            halves.append(mm_tn(whole, d_lanes))
            mine = jnp.where(left if which == 0 else ~left, d_lanes, jnp.zeros_like(d_lanes))
            d_whole = cols_by_cols(mine, lanes)
            d_inner = d_inner + d_whole * decay
            slope = d_whole * whole
            d_cumul = d_cumul + jnp.where(lane == h, jnp.sum(slope, axis=1, keepdims=True), 0.0)
            columns = columns + jnp.where(sub == h, jnp.sum(slope, axis=0, keepdims=True), 0.0)
        d_weighted.append(jnp.where(left, halves[0], halves[1]))
    d_weighted = jnp.concatenate(d_weighted, axis=1) + d_pulled * tail_wide
    columns = jnp.concatenate([columns, jnp.zeros((CHUNK - 8, CHUNK), jnp.float32)], axis=0).T
    d_cumul = d_cumul - columns
    d_inner_low = d_inner.astype(jnp.bfloat16)
    d_c = d_c + mm(d_inner_low, b)
    d_b = d_b + mm_tn(d_inner_low, c)
    d_x = d_weighted * steps_wide + skip_wide * d_made
    d_steps = by_marks(d_weighted * x, gather_heads)
    upper = (iota((CHUNK, CHUNK), 0) <= iota((CHUNK, CHUNK), 1)).astype(jnp.bfloat16)
    d_logs = marks_by(upper, d_cumul) + d_last
    d_steps = d_steps - jnp.exp(head_ref[0:1, :]) * d_logs
    d_raw = d_steps * jax.nn.sigmoid(raw)
    d_raw = jnp.where(lane < plan.hm, d_raw, 0.0)
    slab_shared[:, 2 * NS :] = cols_by_cols(d_raw.astype(jnp.bfloat16), pick_ref[...]).astype(
        jnp.bfloat16
    )
    head_acc[0:1, :] += jnp.sum(d_logs * logs, axis=0, keepdims=True)
    head_acc[1:2, :] += jnp.sum(d_raw, axis=0, keepdims=True)

    d_post = jnp.concatenate([d_x, d_b, d_c], axis=1)
    d_total = d_post * (sig * (1.0 + total * (1.0 - sig)))
    d_window[0:CHUNK, :] = d_total
    d_xbc = jnp.zeros((CHUNK, plan.W), jnp.float32)
    for k in range(CONV):
        shift = CONV - 1 - k
        d_xbc = d_xbc + conv_ref[k : k + 1, :] * d_window[shift : shift + CHUNK, :]
        at = 8 - CONV + 1 + k
        conv_acc[k : k + 1, :] += jnp.sum(
            d_total * window[at : at + CHUNK, :], axis=0, keepdims=True
        )
    conv_acc[4:5, :] += jnp.sum(d_total, axis=0, keepdims=True)
    slab_ref[:, plan.B : plan.B + R] = d_xbc[:, :R].astype(jnp.bfloat16)
    slab_shared[:, : 2 * NS] = d_xbc[:, R:].astype(jnp.bfloat16)
    if plan.B + R < plan.A:
        slab_ref[:, plan.B + R :] = jnp.zeros((CHUNK, plan.A - plan.B - R), jnp.bfloat16)


def space_bwd(plan, proj, shared, conv, heads, pick, gain, rows_of, grad, made, before):
    length = proj.shape[0]
    chunks = length // CHUNK
    W = plan.W
    whole = lambda i: (0, 0)
    rows = lambda i: (chunks - 1 - i, 0)
    per = CHUNK // 8
    return pl.pallas_call(
        functools.partial(space_bwd_kernel, plan),
        grid=(chunks,),
        out_shape=(
            jax.ShapeDtypeStruct((length, plan.A), jnp.bfloat16),
            jax.ShapeDtypeStruct((length, plan.K), jnp.bfloat16),
            jax.ShapeDtypeStruct((8, W), jnp.float32),
            jax.ShapeDtypeStruct((8, PAD), jnp.float32),
            jax.ShapeDtypeStruct((8, plan.R), jnp.float32),
        ),
        in_specs=[
            pl.BlockSpec((CHUNK, plan.A), rows),
            pl.BlockSpec((CHUNK, plan.K), rows),
            pl.BlockSpec((8, plan.A), lambda i: (jnp.maximum((chunks - 1 - i) * per - 1, 0), 0)),
            pl.BlockSpec((8, plan.K), lambda i: (jnp.maximum((chunks - 1 - i) * per - 1, 0), 0)),
            pl.BlockSpec((8, W), whole),
            pl.BlockSpec((8, PAD), whole),
            pl.BlockSpec((PAD, PAD), whole),
            pl.BlockSpec((8, plan.R), whole),
            pl.BlockSpec((CHUNK, 2), rows),
            pl.BlockSpec((CHUNK, plan.R), rows),
            pl.BlockSpec((CHUNK, plan.R), rows),
            pl.BlockSpec((1, NS, plan.R), lambda i: (chunks - 1 - i, 0, 0)),
        ],
        out_specs=(
            pl.BlockSpec((CHUNK, plan.A), rows),
            pl.BlockSpec((CHUNK, plan.K), rows),
            pl.BlockSpec((8, W), whole),
            pl.BlockSpec((8, PAD), whole),
            pl.BlockSpec((8, plan.R), whole),
        ),
        scratch_shapes=[
            pltpu.VMEM((NS, plan.R), jnp.float32),
            pltpu.VMEM((CHUNK + 8, W), jnp.float32),
            pltpu.VMEM((CHUNK + 8, W), jnp.float32),
        ],
        compiler_params=pltpu.CompilerParams(vmem_limit_bytes=VMEM),
    )(proj, shared, proj, shared, conv, heads, pick, gain, rows_of, grad, made, before)


def body(
    inputs,
    cotangent,
    w_in,
    w_in_m,
    w_in_v,
    w_mix,
    w_mix_m,
    w_mix_v,
    w_up,
    w_up_m,
    w_up_v,
    w_down,
    w_down_m,
    w_down_v,
    vectors,
    vectors_m,
    vectors_v,
):
    low = jnp.bfloat16
    count = lax.axis_size("ctx")
    ways = lax.axis_size("wshard")
    place = lax.axis_index("ctx")
    plan = Plan(count)
    R, hm = plan.R, plan.hm
    is_space = place >= plan.attn
    space = jnp.maximum(place - plan.attn, 0)

    gain_attn, gain_ffn, gain_ssm, conv_bias, conv_weight, a_log, dt_bias, d_skip = split_vectors(
        vectors
    )
    whole, in_own, shared_own, up_some, mix_own, down_some = start_call(
        plan, count, inputs[0], w_in, w_up, w_mix, w_down, 1
    )

    own = lambda a, size, axis=0: lax.dynamic_slice_in_dim(a, space * size, size, axis)
    gain_own = own(gain_ssm, R)
    W = plan.W
    conv = jnp.concatenate(
        [
            jnp.concatenate([own(conv_weight, R, 1), conv_weight[:, DSSM:]], axis=1),
            jnp.concatenate([own(conv_bias, R), conv_bias[DSSM:]])[None],
            jnp.zeros((8 - CONV - 1, W), jnp.float32),
        ]
    )
    heads = jnp.stack([own(v, hm) for v in (a_log, dt_bias, d_skip)])
    heads = jnp.pad(heads, ((0, 5), (0, PAD - hm)))
    column = lax.broadcasted_iota(jnp.int32, (PAD, PAD), 1)
    row = lax.broadcasted_iota(jnp.int32, (PAD, PAD), 0)
    pick = jnp.logical_and(row == column + space * hm, column < hm).astype(low)
    tables = rope_tables(count * inputs.shape[1])

    source = inputs[0].astype(jnp.float32)
    whole = whole.astype(jnp.float32)
    in_own, cotangent_late = lax.optimization_barrier((in_own, cotangent[0]))
    odd = lax.axis_index("wshard") % 2 == 1
    upstream_all = gather_ctx(cotangent_late, count, ways)
    length = whole.shape[0]
    rows = inputs.shape[1]
    unit = whole * lax.rsqrt(jnp.mean(whole * whole, axis=-1, keepdims=True) + norm_eps)
    normed = (unit * gain_attn).astype(low)
    unit = unit.astype(low)
    proj = plain(normed, in_own)
    shared = plain(normed, shared_own)

    def space_ahead(proj, shared):
        return space_fwd(plan, proj, shared, conv, heads, pick)

    def attn_ahead(proj, shared):
        made = attn_fwd(plan, proj, tables)
        blank = jnp.zeros((length // CHUNK, NS, R), low)
        return made, jnp.zeros_like(made), blank

    made, raw_made, before = lax.cond(is_space, space_ahead, attn_ahead, proj, shared)
    square = jnp.where(is_space, jnp.sum(made * made, axis=1), 0.0)
    factor = lax.rsqrt(sum_rows(count, square, 5) / DSSM + norm_eps)
    mixed = jnp.where(is_space, made * factor[:, None] * gain_own, made).astype(low)
    wide = lambda *shape: jax.ShapeDtypeStruct(shape, jnp.float32)
    side = (up_some, down_some)
    roomy = length <= 1024
    middle, activated, grad_gate_up, two_all, up_own, down_own = flow_call(
        branch_kernel,
        count,
        rows,
        (mixed, mix_own, inputs[0], gain_ffn[None], upstream_all if roomy else upstream_all[:, :16]),
        (
            wide(rows, D),
            jax.ShapeDtypeStruct((length if roomy else 16, FF // count), low),
            jax.ShapeDtypeStruct((length if roomy else 16, 2 * FF // count), low),
        ),
        True,
        True,
        (side, *share_shapes(side)),
        8,
        roomy,
    )
    two_all = two_all.reshape(length, D)
    up_own, down_own = up_own.reshape(D, -1), down_own.reshape(-1, D)

    if not roomy:
        gate_up = plain(two_all, up_own)
        half = FF // count
        swiglu = lambda g: jax.nn.silu(g[:, :half]) * g[:, half:]
        activated, act_pull = jax.vjp(swiglu, gate_up)
        activated = in_ring(activated.astype(low).reshape(count, rows, -1), count, ways, odd)
        grad_act = cols_by_cols(from_ring(upstream_all, count, lax.axis_index("wshard")), down_own)
        grad_gate_up = act_pull(grad_act)[0].astype(low)
    upstream_all = upstream_all.reshape(length, D)
    cut = lambda g, blocks: g.astype(low).reshape(blocks, ways, -1, g.shape[1])
    blank = jnp.zeros((1, 1, 16, 128), low)
    if roomy:
        up_block = (count, ways, D // (count * ways), 2 * FF // count)
        down_block = (1, ways, FF // (count * ways), D)
        side = [jax.ShapeDtypeStruct(block, low) for block in (up_block, down_block)]
        side_shapes, side_scratch = collect_shapes(("rows", "rows"), side)
        side_scratch = (
            [pltpu.VMEM(block, low) for block in (up_block, down_block)]
            + [pltpu.VMEM((2, length, D // count), low)] * 2
            + [pltpu.SemaphoreType.DMA((2, 2))]
            + side_scratch
        )
        side = (blank, blank)
    else:
        side = (cut(rows_by_rows(two_all, grad_gate_up), count), cut(rows_by_rows(activated, upstream_all), 1))
        side_shapes, side_scratch = collect_shapes(("rows", "rows"), side)
    some = lambda a: a if roomy else a[:16]
    grad_middle, grad_gain_ffn, grad_made, late, branch_all, up_mine, down_mine = flow_call(
        feed_back_kernel,
        count,
        rows,
        (
            grad_gate_up,
            up_own,
            cotangent[0],
            middle,
            gain_ffn[None],
            some(activated),
            some(mix_own),
            some(down_own),
        ),
        (
            wide(rows, D),
            wide(8, D),
            jax.ShapeDtypeStruct((length if roomy else 16, R), low),
            jax.ShapeDtypeStruct((length if roomy else 16, D), low),
        ),
        True,
        False,
        (side, side_shapes, side_scratch),
        9,
        roomy,
        (two_all, upstream_all),
    )
    grad_gain_ffn = grad_gain_ffn[0]
    branch_all = branch_all.reshape(length, D)
    if not roomy:
        late = plain(activated, down_own).astype(low)
    branch_all, grad_made, late = lax.optimization_barrier((branch_all, grad_made, late))
    late = scatter_ctx(late, count, ways)
    if not roomy:
        grad_made = cols_by_cols(branch_all, mix_own).astype(low)
    made_wide = grad_made.astype(jnp.float32)
    dots = jnp.where(is_space, jnp.sum(made_wide * gain_own * made, axis=1), 0.0)
    dots = sum_rows(count, dots, 6)

    def space_back(proj, shared, grad_made):
        gain = jnp.broadcast_to(gain_own, (8, R))
        rows_of = jnp.stack([factor, factor**3 * dots / DSSM], axis=1)
        return space_bwd(
            plan, proj, shared, conv, heads, pick, gain, rows_of, grad_made, raw_made, before
        )

    def attn_back(proj, shared, grad_made):
        blank = lambda k: jnp.zeros((8, k), jnp.float32)
        none = jnp.zeros(shared.shape, low)
        return attn_bwd(plan, proj, tables, grad_made), none, blank(W), blank(PAD), blank(R)

    grad_proj, grad_shared, conv_acc, head_acc, skip_acc = lax.cond(
        is_space, space_back, attn_back, proj, shared, grad_made
    )
    if roomy:
        grad_gain_attn = jnp.zeros_like(gain_attn)
    else:
        grad_in = rows_by_rows(unit, grad_proj)
        grad_in_shared = rows_by_rows(unit, grad_shared)
        grad_gain_attn = jnp.sum(grad_in * in_own, axis=1)
        grad_gain_attn = grad_gain_attn + jnp.sum(grad_in_shared * shared_own, axis=1)
        grad_in = grad_in * gain_attn[:, None]
        grad_in_shared = grad_in_shared * gain_attn[:, None]
    def placed(piece, size, total, axis=0):
        shape = list(piece.shape)
        shape[axis] = total
        start = [0] * piece.ndim
        start[axis] = space * size
        return lax.dynamic_update_slice(jnp.zeros(shape, piece.dtype), piece, start)

    conv_w_grad, conv_b_grad = conv_acc[:CONV], conv_acc[CONV]
    a_grad, bias_grad = head_acc[0, :hm], head_acc[1, :hm]
    skip_grad = jnp.sum(skip_acc[0].reshape(hm, MP), axis=1)
    grad_gain_own = skip_acc[1]
    vector_local = jnp.concatenate(
        [
            grad_gain_attn,
            grad_gain_ffn,
            placed(grad_gain_own, R, DSSM),
            placed(conv_b_grad[:R], R, DSSM),
            conv_b_grad[R:],
            jnp.concatenate(
                [placed(conv_w_grad[:, :R], R, DSSM, 1), conv_w_grad[:, R:]], axis=1
            ).reshape(CONV * CONVCH),
            placed(a_grad, hm, MH),
            placed(bias_grad, hm, MH),
            placed(skip_grad, hm, MH),
        ]
    )
    grad_proj, late = lax.optimization_barrier((grad_proj, late))
    outputs = (middle + late).astype(low)[None]
    pad = -vectors.shape[0] % 1024
    vector_local = jnp.pad(vector_local, (0, pad)).reshape(-1, 128)
    if roomy:
        lines = D // (count * ways)
        blocks = (
            (count, ways, lines, plan.A),
            (count, ways, lines, plan.K),
            (1, ways, MIXIN // (count * ways), D),
        )
        side = [jax.ShapeDtypeStruct(block, low) for block in blocks]
        side_shapes, side_scratch = collect_shapes(SUMS, side)
        side_scratch = (
            [pltpu.VMEM(block, low) for block in blocks]
            + [pltpu.VMEM((2, length, D // count), low)] * 2
            + [pltpu.SemaphoreType.DMA((2, 2)), pltpu.VMEM(vector_local.shape, jnp.float32)]
            + side_scratch
        )
        side = (blank, blank, blank)
    else:
        grad_mix = rows_by_rows(mixed, branch_all)
        side = (cut(grad_in, count), cut(grad_in_shared, count), cut(grad_mix, 1))
        side_shapes, side_scratch = collect_shapes(SUMS, side)
    home_sems = [pltpu.SemaphoreType.DMA((count,))] * 2
    input_grad, vector_sum, up_mine, in_mine, shared_mine, mix_mine = flow_call(
        source_back_kernel,
        count,
        rows,
        (
            grad_proj,
            grad_shared,
            in_own,
            shared_own,
            inputs[0],
            grad_middle,
            gain_attn[None],
            vector_local,
            up_mine,
            some(mixed),
            some(gain_attn[:, None]),
        ),
        (wide(rows, D), wide(*vector_local.shape), jax.ShapeDtypeStruct(up_mine.shape, low)),
        False,
        False,
        (side, side_shapes, side_scratch + sum_scratch(count, vector_local.shape) + home_sems),
        10,
        far_args=(some(unit), some(branch_all)),
    )
    input_grad = input_grad[None]

    up_shard = up_from_slabs(plan, up_mine)
    mix_shard = mix_mine[0].astype(jnp.float32)
    down_shard = down_mine[0].astype(jnp.float32)

    vector_grad = vector_sum.reshape(-1)[: vectors.shape[0]]
    new_in = adam_in(plan, in_mine, shared_mine, w_in, w_in_m, w_in_v, 2.0 * D ** (-0.5))
    new_mix = adamw(w_mix, w_mix_m, w_mix_v, mix_shard, DSSM ** (-0.5), decay_weight)
    new_up = adamw(w_up, w_up_m, w_up_v, up_shard, D ** (-0.5), decay_weight)
    new_down = adamw(w_down, w_down_m, w_down_v, down_shard, FF ** (-0.5), decay_weight)
    new_vec = adamw(vectors, vectors_m, vectors_v, vector_grad, vector_rate, 0.0)
    return (outputs, input_grad, *new_in, *new_mix, *new_up, *new_down, *new_vec)


def solution(mesh):
    tokens = P("wshard", "ctx", None)
    weight = P(("ctx", "wshard"), None)
    return jax.shard_map(
        body,
        mesh=mesh,
        in_specs=(tokens,) * 2 + (weight,) * 12 + (P(),) * 3,
        out_specs=(tokens,) * 2 + (weight,) * 12 + (P(),) * 3,
        check_vma=False,
    )
```

```python
import functools
import math

import jax
import jax.numpy as jnp
from jax import lax
from jax.experimental import pallas as pl
from jax.experimental.pallas import tpu as pltpu
from jax.sharding import PartitionSpec as P

D = 2048
FF = 4096
AH = 8
KVH = 2
HD = 128
MH = 48
MP = 64
NS = 256
CONV = 4
STEP = 10
DSSM = 3072
CONVCH = 3584
ATT = AH * HD
MIXIN = ATT + DSSM
GROUP = AH // KVH
CHUNK = 128
PAD = 128
VMEM = 60 * 1024 * 1024


norm_eps = 1e-05
rope_base = 10000.0
beta_one = 0.9
beta_two = 0.95
adam_eps = 1e-08
decay_weight = 0.1
vector_rate = 0.5
masked_score = -1e30

K_AT = ATT
V_AT = K_AT + KVH * HD
Z_AT = V_AT + KVH * HD
X_AT = Z_AT + DSSM
BC_AT = X_AT + DSSM
DT_AT = BC_AT + 2 * NS
END = DT_AT + MH


def rows_by_rows(left, right):
    return lax.dot_general(
        left, right, (((0,), (0,)), ((), ())), preferred_element_type=jnp.float32
    )


def cols_by_cols(left, right):
    return lax.dot_general(
        left, right, (((1,), (1,)), ((), ())), preferred_element_type=jnp.float32
    )


def plain(left, right):
    return jnp.dot(left, right, preferred_element_type=jnp.float32)


def rms_norm(values, gain):
    factor = lax.rsqrt(jnp.mean(values * values, axis=-1, keepdims=True) + norm_eps)
    return values * factor * gain


def split_vectors(vectors):
    extents = (D, D, DSSM, CONVCH, CONV * CONVCH, MH, MH, MH)
    pieces = []
    offset = 0
    for extent in extents:
        pieces.append(lax.slice_in_dim(vectors, offset, offset + extent))
        offset = offset + extent
    pieces[4] = pieces[4].reshape(CONV, CONVCH)
    return pieces


def adamw(weight, moment, second, grad, rate, decay):
    moment = beta_one * moment + (1.0 - beta_one) * grad
    second = beta_two * second + (1.0 - beta_two) * grad * grad
    corrected = moment / (1.0 - beta_one**STEP)
    divisor = jnp.sqrt(second / (1.0 - beta_two**STEP)) + adam_eps
    return (weight - rate * (corrected / divisor + decay * weight), moment, second)


class Plan:
    def __init__(self, count):
        self.count = count
        self.R = MIXIN // count
        self.attn = ATT // self.R
        self.ha = self.R // HD
        self.hm = self.R // MP
        self.B = self.R
        self.A = self.R + max(self.R, 2 * HD)
        self.K = 2 * NS + PAD
        self.W = self.R + 2 * NS

    def kv_of(self, c):
        return c * self.ha // GROUP


def up_from_slabs(plan, slabs):
    G = FF // plan.count
    slabs = slabs.astype(jnp.float32)
    return jnp.concatenate(
        [slabs[c][:, :G] for c in range(plan.count)] + [slabs[c][:, G:] for c in range(plan.count)],
        axis=1,
    )


def ring_groups(n, ways):
    ring = list(range(0, n, 2)) + list(range(n - 1, 0, -2))
    return [[c * ways + w for c in (ring[::-1] if w % 2 else ring)] for w in range(ways)], ring


def ring_place(n, w, c):
    at = c // 2 + c % 2 * (n - 1 - c // 2 * 2)
    return at + w % 2 * (n - 1 - 2 * at)


def gather_ctx(x, n, ways):
    return lax.all_gather(x, ("ctx", "wshard"), axis_index_groups=ring_groups(n, ways)[0])


def from_ring(blocks, n, w):
    parts = [lax.dynamic_index_in_dim(blocks, ring_place(n, w, c), 0, False) for c in range(n)]
    return jnp.concatenate(parts)


def in_ring(blocks, n, ways, odd):
    ring = ring_groups(n, ways)[1]
    parts = [
        lax.dynamic_index_in_dim(blocks, jnp.where(odd, ring[n - 1 - i], ring[i]), 0, False)
        for i in range(n)
    ]
    return jnp.concatenate(parts)


def scatter_ctx(x, n, ways):
    return lax.psum_scatter(
        x.astype(jnp.bfloat16),
        ("ctx", "wshard"),
        scatter_dimension=0,
        axis_index_groups=ring_groups(n, ways)[0],
        tiled=True,
    ).astype(jnp.float32)


def adam_in_kernel(plan, rate, slabs, shared, w, m, v, new_w, new_m, new_v):
    R, B = plan.R, plan.B
    wide = jnp.float32
    heads, spaces = range(plan.attn), range(plan.attn, plan.count)

    def update(lo, hi, parts):
        grad = functools.reduce(lambda a, b: a + b, [part.astype(wide) for part in parts])
        new = adamw(w[:, lo:hi], m[:, lo:hi], v[:, lo:hi], grad, rate, decay_weight)
        new_w[:, lo:hi], new_m[:, lo:hi], new_v[:, lo:hi] = new

    for c in heads:
        update(c * R, (c + 1) * R, [slabs[c, :, :R]])
    for start, at in ((K_AT, B), (V_AT, B + HD)):
        for g in range(KVH):
            owners = [slabs[c, :, at : at + HD] for c in heads if plan.kv_of(c) == g]
            update(start + g * HD, start + (g + 1) * HD, owners)
    for c in spaces:
        j = c - plan.attn
        update(Z_AT + j * R, Z_AT + (j + 1) * R, [slabs[c, :, :R]])
        update(X_AT + j * R, X_AT + (j + 1) * R, [slabs[c, :, B : B + R]])
    update(BC_AT, END, [shared[c, :, : END - BC_AT] for c in spaces])


def adam_in(plan, slabs, shared, w, m, v, rate):
    rows = w.shape[0]
    block = 16
    flat = pl.BlockSpec((block, END), lambda i: (i, 0))
    return pl.pallas_call(
        functools.partial(adam_in_kernel, plan, rate),
        grid=(rows // block,),
        out_shape=(jax.ShapeDtypeStruct(w.shape, w.dtype),) * 3,
        in_specs=[
            pl.BlockSpec((plan.count, block, plan.A), lambda i: (0, i, 0)),
            pl.BlockSpec((plan.count, block, plan.K), lambda i: (0, i, 0)),
            flat,
            flat,
            flat,
        ],
        out_specs=(flat,) * 3,
        compiler_params=pltpu.CompilerParams(vmem_limit_bytes=VMEM),
    )(slabs, shared, w, m, v)


MESH = pl.DeviceIdType.MESH


def here():
    c, w = lax.axis_index("ctx"), lax.axis_index("wshard")
    return c, w, w + 1 - 2 * (w % 2), (w + 2) % 4


def greet(devices):
    barrier = pltpu.get_barrier_semaphore()
    for device in devices:
        pl.semaphore_signal(barrier, inc=1, device_id=device, device_id_type=MESH)
    pl.semaphore_wait(barrier, len(devices))


def remote(src, dst, send, recv, device):
    return pltpu.make_async_remote_copy(
        src_ref=src, dst_ref=dst, send_sem=send, recv_sem=recv, device_id=device, device_id_type=MESH
    )


class Collect:
    def __init__(self, n, kinds, sources, targets, extra):
        self.n = n
        self.c, self.w, self.sib, self.across = here()
        self.x, self.core = self.w // 2, self.w % 2
        self.pending = []
        self.jobs = []
        for j, kind in enumerate(kinds):
            self.jobs.append((kind, sources[j], targets[j]) + tuple(extra[10 * j : 10 * j + 10]))
        most = max(job[3].shape[1] for job in self.jobs)
        self.steps = [s % most for s in range(1, most + 1)]

    def due(self, s):
        for job in self.jobs:
            count = job[3].shape[1]
            if s < count:
                yield job, (self.c + s) % self.n if count > 1 else 0

    def send(self, s):
        for place, slot in ((1 - self.x, 0), (self.x, 1)):
            for job, q in self.due(s):
                _, src, _, kbuf, _, _, _, k_send, k_recv = job[:9]
                out = remote(
                    src.at[q, place * 2 + 1 - self.core],
                    kbuf.at[slot, q],
                    k_send.at[slot, s],
                    k_recv.at[slot, q],
                    (self.c, self.sib),
                )
                out.start()
                self.pending.append(out)

    def cross(self, s):
        wide = jnp.float32
        for job, q in self.due(s):
            _, src, _, kbuf, stage, xbuf, _, k_send, k_recv, x_send, x_recv = job[:11]
            got = kbuf.at[0, q]
            remote(got, got, k_send.at[0, s], k_recv.at[0, q], (self.c, self.sib)).wait_recv()
            mine = src[q, (1 - self.x) * 2 + self.core].astype(wide)
            stage[q] = (mine + kbuf[0, q].astype(wide)).astype(stage.dtype)
            out = remote(
                stage.at[q], xbuf.at[q], x_send.at[s], x_recv.at[q], (self.c, self.across)
            )
            out.start()
            self.pending.append(out)

    def close(self, s):
        wide = jnp.float32
        for job, q in self.due(s):
            kind, src, dst, kbuf, stage, xbuf, done, k_send, k_recv, x_send, x_recv = job[:11]
            got = kbuf.at[1, q]
            remote(got, got, k_send.at[1, s], k_recv.at[1, q], (self.c, self.sib)).wait_recv()
            got = xbuf.at[q]
            remote(got, got, x_send.at[s], x_recv.at[q], (self.c, self.across)).wait_recv()
            total = src[q, self.x * 2 + self.core].astype(wide) + kbuf[1, q].astype(wide)
            total = (total + xbuf[q].astype(wide)).astype(stage.dtype)
            if kind == "cols" and s > 0:
                done[q] = total
                out = remote(done.at[q], dst.at[self.c], job[11].at[s], job[12].at[self.c], (q, self.w))
                out.start()
                self.pending.append(out)
            else:
                dst[q] = total

    def end(self):
        for job in self.jobs:
            if job[0] == "cols":
                dst, a_send, a_recv = job[2], job[11], job[12]
                for s in range(1, self.n):
                    q = (self.c + self.n - s) % self.n
                    got = dst.at[q]
                    remote(got, got, a_send.at[s], a_recv.at[q], (q, self.w)).wait_recv()
        for out in self.pending:
            out.wait_send()


def home_job(n, source, target, send, recv):
    c, w = lax.axis_index("ctx"), lax.axis_index("wshard")
    target[c] = source[c]
    copies = [
        remote(source.at[(c + s) % n], target.at[c], send.at[s], recv.at[c], ((c + s) % n, w))
        for s in range(1, n)
    ]
    for copy in copies:
        copy.start()
    yield
    for s in range(1, n):
        q = (c + n - s) % n
        remote(source.at[q], target.at[q], send.at[s], recv.at[q], (q, w)).wait_recv()
    for copy in copies:
        copy.wait_send()


def collect_shapes(kinds, sources):
    shapes, scratch = [], []
    for kind, src in zip(kinds, sources):
        count, _, rows, size = src.shape
        block = (count, rows, size)
        shapes.append(jax.ShapeDtypeStruct(block, src.dtype))
        scratch += [
            pltpu.VMEM((2,) + block, src.dtype),
            pltpu.VMEM(block, src.dtype),
            pltpu.VMEM(block, src.dtype),
            pltpu.VMEM(block if kind == "cols" else (1, 16, 128), src.dtype),
            pltpu.SemaphoreType.DMA((2, count)),
            pltpu.SemaphoreType.DMA((2, count)),
            pltpu.SemaphoreType.DMA((count,)),
            pltpu.SemaphoreType.DMA((count,)),
            pltpu.SemaphoreType.DMA((count,)),
            pltpu.SemaphoreType.DMA((count,)),
        ]
    return shapes, scratch


def row_sum_kernel(n, x_ref, out_ref, got, send, recv):
    c, w = lax.axis_index("ctx"), lax.axis_index("wshard")
    greet([((c + s) % n, w) for s in range(1, n)])
    copies = [
        remote(x_ref, got.at[c], send.at[s], recv.at[c], ((c + s) % n, w)) for s in range(1, n)
    ]
    for copy in copies:
        copy.start()
    total = x_ref[...]
    for s in range(1, n):
        q = (c + n - s) % n
        remote(x_ref, got.at[q], send.at[s], recv.at[q], (q, w)).wait_recv()
        total = total + got[q]
    out_ref[...] = total
    for copy in copies:
        copy.wait_send()


def sum_rows(n, x, collective_id):
    block = x.reshape(-1, 128)
    return pl.pallas_call(
        functools.partial(row_sum_kernel, n),
        out_shape=jax.ShapeDtypeStruct(block.shape, x.dtype),
        in_specs=[pl.BlockSpec(memory_space=pltpu.VMEM)],
        out_specs=pl.BlockSpec(memory_space=pltpu.VMEM),
        scratch_shapes=[
            pltpu.VMEM((n,) + block.shape, x.dtype),
            pltpu.SemaphoreType.DMA((n,)),
            pltpu.SemaphoreType.DMA((n,)),
        ],
        compiler_params=pltpu.CompilerParams(
            collective_id=collective_id, has_side_effects=True, vmem_limit_bytes=VMEM
        ),
    )(block).reshape(x.shape)


def sum_job(n, x_ref, out_ref, kept, got, send, recv):
    c, w, sib, across = here()
    partners = [(c, sib), (c, across)]
    for level in list(range(1, n.bit_length() - 1)) + [0]:
        reach = 2**level
        partners.append((c + reach - 2 * reach * ((c // reach) % 2), w))
    out_ref[...] = x_ref[...]
    for i, partner in enumerate(partners):
        kept[i] = out_ref[...]
        swap = remote(kept.at[i], got.at[i], send.at[i], recv.at[i], partner)
        swap.start()
        yield
        swap.wait()
        out_ref[...] += got[i]


def sum_scratch(n, shape):
    stages = n.bit_length() + 1
    return [
        pltpu.VMEM((stages,) + shape, jnp.float32),
        pltpu.VMEM((stages,) + shape, jnp.float32),
        pltpu.SemaphoreType.DMA((stages,)),
        pltpu.SemaphoreType.DMA((stages,)),
    ]


def share_job(sources, targets, sems):
    c, w, sib, across = here()
    pending = []
    for j, (src, dst) in enumerate(zip(sources, targets)):
        x_send, x_recv, k_send, k_recv, own_sem = sems[5 * j : 5 * j + 5]
        for q in range(src.shape[0]):
            own = pltpu.make_async_copy(src.at[q], dst.at[q, w], own_sem.at[q])
            to_x = remote(src.at[q], dst.at[q, w], x_send.at[q], x_recv.at[q], (c, across))
            to_k = remote(src.at[q], dst.at[q, w], k_send.at[0, q], k_recv.at[0, q], (c, sib))
            for copy in (to_x, to_k, own):
                copy.start()
            pending += [to_x.wait_send, to_k.wait_send, own.wait]
    yield
    for j, dst in enumerate(targets):
        x_send, x_recv, k_send, k_recv, own_sem = sems[5 * j : 5 * j + 5]
        for q in range(dst.shape[0]):
            got = dst.at[q, across]
            remote(got, got, x_send.at[q], x_recv.at[q], (c, across)).wait_recv()
            out = remote(got, got, k_send.at[1, q], k_recv.at[1, q], (c, sib))
            out.start()
            pending.append(out.wait_send)
    yield
    for j, dst in enumerate(targets):
        x_send, x_recv, k_send, k_recv, own_sem = sems[5 * j : 5 * j + 5]
        for q in range(dst.shape[0]):
            for half, place in ((0, sib), (1, (sib + 2) % 4)):
                got = dst.at[q, place]
                remote(got, got, k_send.at[half, q], k_recv.at[half, q], (c, sib)).wait_recv()
    for wait in pending:
        wait()


def share_shapes(sources):
    shapes, sems = [], []
    for src in sources:
        count = src.shape[0]
        shapes.append(jax.ShapeDtypeStruct((count, 4) + src.shape[1:], src.dtype))
        sems += [
            pltpu.SemaphoreType.DMA((count,)),
            pltpu.SemaphoreType.DMA((count,)),
            pltpu.SemaphoreType.DMA((2, count)),
            pltpu.SemaphoreType.DMA((2, count)),
            pltpu.SemaphoreType.DMA((count,)),
        ]
    return shapes, sems


def advance(*jobs):
    jobs = list(jobs)
    while jobs:
        for job in list(jobs):
            try:
                next(job)
            except StopIteration:
                jobs.remove(job)


class Line:
    def __init__(self, n):
        self.c, self.w, self.sib, self.across = here()
        self.n, self.N = n, n // 2
        self.at, self.side = self.c // 2, self.c % 2
        self.pair = (self.c + 1 - 2 * self.side, self.w)
        self.left = (self.c - 2, self.w)
        self.right = (self.c + 2, self.w)
        self.has_left = self.at > 0
        self.has_right = self.at < self.N - 1

    def greet(self, others=()):
        barrier = pltpu.get_barrier_semaphore()
        signal = lambda d: pl.semaphore_signal(barrier, inc=1, device_id=d, device_id_type=MESH)
        sure = [self.pair] + list(others)
        for device in sure:
            signal(device)
        pl.when(self.has_left)(lambda: signal(self.left))
        pl.when(self.has_right)(lambda: signal(self.right))
        beside = (self.at + self.N - 1) // self.N + (2 * self.N - 2 - self.at) // self.N
        pl.semaphore_wait(barrier, len(sure) + beside)


def scatter_job(line, theirs, mine_of, total, ybuf, zbuf, sems):
    y_send, y_recv, r_send, r_recv, l_send, l_recv = sems
    N, at, side = line.N, line.at, line.side
    wide = jnp.float32

    def both_ways(d):
        return ((at + d, at + d < N), (at - d, at - d >= 0)) if d else ((at, None),)

    def guarded(keep, step):
        if keep is None:
            step()
        else:
            pl.when(keep)(step)

    def y_copy(b, src=None):
        src = ybuf.at[b] if src is None else src
        return remote(src, ybuf.at[b], y_send.at[b], y_recv.at[b], line.pair)

    def r_copy(b, slot):
        return remote(ybuf.at[b], zbuf.at[slot], r_send.at[b], r_recv.at[b], line.right)

    def l_copy(b, slot):
        return remote(ybuf.at[b], zbuf.at[slot], l_send.at[b], l_recv.at[b], line.left)

    for d in range(N - 1, -1, -1):
        for b, keep in both_ways(d):

            def first(b=b):
                y_copy(b, theirs(b)).start()

            guarded(keep, first)
        yield
    for d in range(N - 1, 0, -1):
        for b, keep, ahead in ((at + d, at + d < N, True), (at - d, at - d >= 0, False)):

            def relay(b=b, ahead=ahead):
                mine = mine_of(b)
                y_copy(b).wait_recv()
                mine = mine + ybuf[b].astype(wide)
                came = line.has_left if ahead else line.has_right

                @pl.when(came)
                def _():
                    (r_copy if ahead else l_copy)(b, b).wait_recv()
                    ybuf[b] = (mine + zbuf[b].astype(wide)).astype(ybuf.dtype)

                @pl.when(jnp.logical_not(came))
                def _():
                    ybuf[b] = mine.astype(ybuf.dtype)

                if ahead:
                    pl.when(b == at + 1)(lambda: r_copy(b, b).start())
                    pl.when(b > at + 1)(lambda: r_copy(b, b).start())
                else:
                    pl.when(b == at - 1)(lambda: l_copy(b, N).start())
                    pl.when(b < at - 1)(lambda: l_copy(b, b).start())

            guarded(keep, relay)
        yield
    mine = mine_of(at)
    y_copy(at).wait_recv()
    total[...] = mine + ybuf[at].astype(wide)

    @pl.when(line.has_left)
    def _():
        r_copy(at, at).wait_recv()
        total[...] += zbuf[at].astype(wide)

    @pl.when(line.has_right)
    def _():
        l_copy(at, N).wait_recv()
        total[...] += zbuf[N].astype(wide)

    for d in range(N):
        for b, keep in both_ways(d):
            guarded(keep, lambda b=b: y_copy(b).wait_send())
    for d in range(1, N):
        pl.when(at + d < N)(lambda d=d: r_copy(at + d, at + d).wait_send())
        pl.when(at - d >= 0)(lambda d=d: l_copy(at - d, at - d).wait_send())


def scatter_line_job(line, value, stage, slots, pair_slot, total, sems):
    r_send, r_recv, l_send, l_recv, p_send, p_recv = sems
    n, N, at, side = line.n, line.N, line.at, line.side
    wide = jnp.float32

    def copy(q, slot, ahead):
        send, recv = (r_send, r_recv) if ahead else (l_send, l_recv)
        device = line.right if ahead else line.left
        return remote(stage.at[q], slots.at[slot], send.at[q], recv.at[q], device)

    for d in range(N - 1, 0, -1):
        for b, keep, ahead in ((at + d, at + d < N, True), (at - d, at - d >= 0, False)):

            def relay(b=b, ahead=ahead):
                came = line.has_left if ahead else line.has_right
                for y in range(2):
                    q = 2 * b + y

                    @pl.when(came)
                    def _(q=q, y=y):
                        copy(q, q, ahead).wait_recv()
                        stage[q] = (value(b, y) + slots[q].astype(wide)).astype(stage.dtype)

                    @pl.when(jnp.logical_not(came))
                    def _(q=q, y=y):
                        stage[q] = value(b, y).astype(stage.dtype)

                    if ahead:
                        copy(q, q, True).start()
                    else:
                        pl.when(b == at - 1)(lambda q=q, y=y: copy(q, n + y, False).start())
                        pl.when(b < at - 1)(lambda q=q: copy(q, q, False).start())

            pl.when(keep)(relay)
        yield

    def reach(y):
        q, y_slot = 2 * at + y, n + y
        pl.when(line.has_left)(lambda: copy(q, q, True).wait_recv())
        pl.when(line.has_right)(lambda: copy(q, y_slot, False).wait_recv())
        left = jnp.where(line.has_left, slots[q].astype(wide), 0.0)
        right = jnp.where(line.has_right, slots[y_slot].astype(wide), 0.0)
        return value(at, y) + left + right

    other = 2 * at + 1 - side
    stage[other] = reach(1 - side).astype(stage.dtype)
    swap = remote(stage.at[other], pair_slot, p_send, p_recv, line.pair)
    swap.start()
    mine = reach(side)
    yield
    swap.wait()
    total[...] = mine + pair_slot[...].astype(wide)
    for d in range(1, N):
        for y in range(2):
            pl.when(at + d < N)(lambda d=d, y=y: copy(2 * (at + d) + y, 0, True).wait_send())
            pl.when(at - d >= 0)(lambda d=d, y=y: copy(2 * (at - d) + y, 0, False).wait_send())


def gather_job(line, own, out, sems, use=None):
    r_send, l_send, y_send, recv, own_sem = sems
    n, N, at, side, c = line.n, line.N, line.at, line.side, line.c
    local = pltpu.make_async_copy(own, out(c), own_sem)
    local.start()

    def send(src, q, sem, device):
        return remote(src, out(q), sem.at[q // 2], recv.at[q], device)

    use = use or (lambda q: None)
    pair = c + 1 - 2 * side

    def other(d):
        for q, keep in ((pair - 2 * d, at - d >= 0), (pair + 2 * d, at + d < N))[: 1 + (d > 0)]:

            def take(q=q):
                send(out(q), q, y_send, line.pair).wait_recv()
                use(q)

            pl.when(keep)(take)

    pl.when(line.has_right)(lambda: send(own, c, r_send, line.right).start())
    pl.when(line.has_left)(lambda: send(own, c, l_send, line.left).start())
    send(own, c, y_send, line.pair).start()
    yield
    local.wait()
    use(c)
    for d in range(1, N):
        for q, keep, ahead in ((c - 2 * d, at - d >= 0, True), (c + 2 * d, at + d < N, False)):

            def relay(q=q, ahead=ahead):
                got = out(q)
                send(got, q, y_send, line.pair).wait_recv()
                if ahead:
                    pl.when(line.has_right)(lambda: send(got, q, r_send, line.right).start())
                else:
                    pl.when(line.has_left)(lambda: send(got, q, l_send, line.left).start())
                send(got, q, y_send, line.pair).start()
                use(q)

            pl.when(keep)(relay)
        yield
    for d in range(N):
        other(d)
    for b in range(N):
        q = 2 * b + side
        got = out(q)
        send(got, q, y_send, line.pair).wait_send()
        pl.when(jnp.logical_and(b <= at, line.has_right))(
            lambda q=q, got=got: send(got, q, r_send, line.right).wait_send()
        )
        pl.when(jnp.logical_and(b >= at, line.has_left))(
            lambda q=q, got=got: send(got, q, l_send, line.left).wait_send()
        )


def gather_pair_job(line, own, out, sems):
    r_send, l_send, y_send, recv, own_sem = sems
    n, N, at, c = line.n, line.N, line.at, line.c
    local = pltpu.make_async_copy(own, out(c), own_sem)
    local.start()

    def send(src, q, sem, device):
        return remote(src, out(q), sem.at[q], recv.at[q], device)

    def ahead(src, q, act):
        pl.when(line.has_right)(lambda: act(send(src, q, r_send, line.right)))

    def back(src, q, act):
        pl.when(line.has_left)(lambda: act(send(src, q, l_send, line.left)))

    start = lambda copy: copy.start()
    to_pair = remote(own, out(c), y_send.at[0], recv.at[c], line.pair)
    to_pair.start()
    ahead(own, c, start)
    back(own, c, start)
    yield
    local.wait()
    q = line.pair[0]
    got = out(q)
    send(got, q, r_send, line.pair).wait_recv()
    ahead(got, q, start)
    back(got, q, start)
    yield
    for d in range(1, N):
        for b, keep, forward in ((at - d, at - d >= 0, True), (at + d, at + d < N, False)):

            def relay(b=b, forward=forward):
                for y in range(2):
                    got = out(2 * b + y)
                    send(got, 2 * b + y, r_send, line.pair).wait_recv()
                    (ahead if forward else back)(got, 2 * b + y, start)

            pl.when(keep)(relay)
        yield
    to_pair.wait_send()
    done = lambda copy: copy.wait_send()
    for b in range(N):
        for y in range(2):
            q = 2 * b + y
            pl.when(b <= at)(lambda q=q: ahead(out(q), q, done))
            pl.when(b >= at)(lambda q=q: back(out(q), q, done))


def minor_rows(rows):
    return rows // 8


def scatter_steps(line, product, rows, total, made, scratch):
    N, side = line.N, line.side
    if len(made.shape) == 3:

        def theirs(b):
            made[b] = product(2 * b * rows + (1 - side) * rows, rows).astype(made.dtype)
            return made.at[b]

        yield from scatter_job(
            line,
            theirs,
            lambda b: product(2 * b * rows + side * rows, rows),
            total,
            *scratch[:2],
            scratch[2:8],
        )
        return
    few = minor_rows(rows)
    many = rows - few
    ybuf, zbuf = scratch[:2]
    stage, slots, pair_slot = scratch[8:11]
    wide = jnp.float32

    def theirs(b):
        both = product(2 * b * rows, 2 * rows).astype(made.dtype)
        made[b] = both.reshape(2, rows, D)
        return made.at[b, 1 - side, pl.ds(0, many)]

    minor = scatter_line_job(
        line,
        lambda b, y: made[b, y, many:, :].astype(wide),
        stage,
        slots,
        pair_slot,
        total.at[pl.ds(many, few)],
        scratch[11:17],
    )
    main = scatter_job(
        line,
        theirs,
        lambda b: made[b, side, :many, :].astype(wide),
        total.at[pl.ds(0, many)],
        ybuf,
        zbuf,
        scratch[2:8],
    )
    for _ in range(N):
        next(main)
        yield
    next(minor)
    for _ in range(N - 1):
        next(minor, None)
        next(main)
        yield
    finish(minor)
    finish(main)


def gather_steps(line, own, out, rows, scratch, use=None):
    few = minor_rows(rows)
    many = rows - few
    minor = gather_pair_job(
        line, own.at[pl.ds(many, few)], lambda q: out(q, many, few), scratch[5:10]
    )
    main = gather_job(line, own.at[pl.ds(0, many)], lambda q: out(q, 0, many), scratch[:5], use)
    next(minor)
    next(main)
    yield
    next(minor)
    for _ in range(line.N - 1):
        next(minor)
        next(main)
        yield
    finish(minor)
    finish(main)


GATHER = 10


def scatter_shapes(n, rows, roomy):
    N = n // 2
    few = minor_rows(rows) if roomy else 0
    many = rows - few
    low, dma = jnp.bfloat16, pltpu.SemaphoreType.DMA
    made = pltpu.VMEM((N, 2, rows, D) if roomy else (N, rows, D), low)
    scratch = [
        pltpu.VMEM((N, many, D), low),
        pltpu.VMEM((N + 1, many, D), low),
    ] + [dma((N,))] * 6
    if roomy:
        scratch += [
            pltpu.VMEM((n, few, D), low),
            pltpu.VMEM((n + 2, few, D), low),
            pltpu.VMEM((few, D), low),
        ]
        scratch += [dma((n,))] * 4 + [dma, dma]
    return made, scratch


def gather_scratch(n):
    N = n // 2
    dma = pltpu.SemaphoreType.DMA
    return [dma((N,)), dma((N,)), dma((N,)), dma((n,)), dma] + [
        dma((n,)),
        dma((n,)),
        dma((1,)),
        dma((n,)),
        dma,
    ]


def rms_factor(values):
    return lax.rsqrt(jnp.mean(values * values, axis=1, keepdims=True) + norm_eps)


def rms_back(values, gain, grad):
    factor = rms_factor(values)
    scaled = grad * gain
    inner = jnp.mean(scaled * values, axis=1, keepdims=True)
    d_gain = jnp.sum(grad * (values * factor), axis=0, keepdims=True)
    return factor * scaled - values * (factor * factor * factor * inner), d_gain


def matmul_rows(*pairs):
    def product(first, count):
        total = 0.0
        for left, right in pairs:
            part = left[pl.ds(pl.multiple_of(first, 16), count), :]
            if right.shape[0] == left.shape[1]:
                total = total + plain(part, right[...])
            else:
                total = total + cols_by_cols(part, right[...])
        return total

    return product


def finish(job):
    for _ in job:
        pass


def start_kernel(plan, n, x, w_in, w_up, w_mix, w_down, *refs):
    tokens, in_all, shared_all, up_some, mix_all, down_some = refs[:6]
    in_low, shared_low, up_low, mix_low, down_low = refs[6:11]
    t_sems, s_sems = refs[11 : 11 + GATHER], refs[11 + GATHER : 16 + GATHER]
    a_send, a_recv, x_send, x_recv, k_send, k_recv, own_sem = refs[16 + GATHER :]
    line = Line(n)
    c, w, sib, across = line.c, line.w, line.sib, line.across
    greet([((c + s) % n, w) for s in range(1, n)] + [(c, sib), (c, across)])
    R, B, G = plan.R, plan.B, FF // n
    low = jnp.bfloat16
    place = lambda q, first, count: tokens.at[q, pl.ds(first, count)]
    inputs = gather_steps(line, x, place, x.shape[0], t_sems)
    next(inputs)
    passed, pending = [], []

    def pass_on(number, view, src=None):
        src = view(w) if src is None else src
        to_x = remote(src, view(w), x_send.at[number], x_recv.at[number], (c, across))
        to_k = remote(src, view(w), k_send.at[0, number], k_recv.at[0, number], (c, sib))
        to_x.start()
        to_k.start()
        pending.append(to_x)
        pending.append(to_k)
        passed.append((number, view))

    mix_low[...] = w_mix[...].astype(low)
    pass_on(2 * n, lambda place: mix_all.at[0, place], mix_low)
    shared_low[...] = jnp.zeros_like(shared_low)
    shared_low[:, : END - BC_AT] = w_in[:, BC_AT:END].astype(low)
    for p in range(n):
        if p < plan.attn:
            g = plan.kv_of(p)
            in_low[p, :, :R] = w_in[:, p * R : (p + 1) * R].astype(low)
            in_low[p, :, B : B + HD] = w_in[:, K_AT + g * HD : K_AT + (g + 1) * HD].astype(low)
            in_low[p, :, B + HD : B + 2 * HD] = w_in[
                :, V_AT + g * HD : V_AT + (g + 1) * HD
            ].astype(low)
            if B + 2 * HD < plan.A:
                rest = plan.A - B - 2 * HD
                in_low[p, :, B + 2 * HD :] = jnp.zeros((in_low.shape[1], rest), low)
        else:
            j = p - plan.attn
            in_low[p, :, :R] = w_in[:, Z_AT + j * R : Z_AT + (j + 1) * R].astype(low)
            in_low[p, :, B : B + R] = w_in[:, X_AT + j * R : X_AT + (j + 1) * R].astype(low)
            if B + R < plan.A:
                in_low[p, :, B + R :] = jnp.zeros((in_low.shape[1], plan.A - B - R), low)

    common = gather_job(line, shared_low, lambda q: shared_all.at[q, w], s_sems)
    next(common)

    def send_columns(steps):
        for s in steps:
            p = (c + s) % n
            copy = remote(
                in_low.at[p], in_all.at[c, w], a_send.at[0, s], a_recv.at[0, c], (p, w)
            )
            copy.start()
            pending.append(copy)

    in_view = lambda q: lambda place: in_all.at[q, place]
    shared_view = lambda q: lambda place: shared_all.at[q, place]

    def take_columns(steps):
        for s in steps:
            q = (c + n - s) % n
            got = in_all.at[q, w]
            remote(got, got, a_send.at[0, s], a_recv.at[0, q], (q, w)).wait_recv()
            pass_on(q, in_view(q))

    done = [0]

    def seconds(upto):
        while done[0] < min(upto, len(passed)):
            number, view = passed[done[0]]
            got = view(across)
            remote(got, got, x_send.at[number], x_recv.at[number], (c, across)).wait_recv()
            out = remote(got, got, k_send.at[1, number], k_recv.at[1, number], (c, sib))
            out.start()
            pending.append(out)
            done[0] += 1

    cuts = [round(1 + (n - 1) * i / 3) for i in range(4)]
    parts = [range(cuts[i], cuts[i + 1]) for i in range(3)]
    send_columns(parts[0])
    pass_on(c, in_view(c), in_low.at[c])
    pass_on(n + c, shared_view(c), shared_low)
    down_low[...] = w_down[...].astype(low)
    for p in range(n):
        up_low[p, :, :G] = w_up[:, p * G : (p + 1) * G].astype(low)
        up_low[p, :, G:] = w_up[:, FF + p * G : FF + (p + 1) * G].astype(low)
    locals_started = []
    own = (
        (in_low.at[c], in_all.at[c, w]),
        (mix_low, mix_all.at[0, w]),
        (up_low.at[c], up_some.at[c]),
        (down_low, down_some.at[0]),
    )
    for i, (src, dst) in enumerate(own):
        copy = pltpu.make_async_copy(src, dst, own_sem.at[i])
        copy.start()
        locals_started.append(copy)
    for step in range(3):
        for _ in range(line.N // 4):
            next(common, None)
            next(inputs, None)
        if step < 2:
            send_columns(parts[step + 1])
        else:
            for s in range(1, n):
                p = (c + s) % n
                out = remote(
                    up_low.at[p], up_some.at[c], a_send.at[1, s], a_recv.at[1, c], (p, w)
                )
                out.start()
                pending.append(out)
        take_columns(parts[step])
        if step == 2:
            finish(common)
            for s in range(1, n):
                pass_on(n + (c + s) % n, shared_view((c + s) % n))
        seconds(len(passed) - 4)
    finish(inputs)
    seconds(len(passed))
    for s in range(1, n):
        q = (c + n - s) % n
        got = up_some.at[q]
        remote(got, got, a_send.at[1, s], a_recv.at[1, q], (q, w)).wait_recv()
    for number, view in passed:
        for half, place in ((0, sib), (1, (sib + 2) % 4)):
            got = view(place)
            remote(got, got, k_send.at[half, number], k_recv.at[half, number], (c, sib)).wait_recv()
    for copy in locals_started:
        copy.wait()
    for out in pending:
        out.wait_send()


def branch_kernel(n, refs_in, refs_out, scratch):
    left, right, source, gain, upstream, up, down = refs_in
    middle, active, grad_gates, normed, up_all, down_all = refs_out
    line = Line(n)
    line.greet([(line.c, line.sib), (line.c, line.across)])
    rows = source.shape[0]
    (total, own, made), (flow, gather, extra, kept) = scratch[:3], scratch[3:]
    fused = active.shape[0] == n * rows
    writes = []
    if fused:
        outs = normed, up_all, down_all
        normed, normed_sem, up_all, down_all, side_sem = kept
        writes = [
            pltpu.make_async_copy(a, b, side_sem.at[i])
            for i, (a, b) in enumerate(((up_all, outs[1]), (down_all, outs[2])))
        ]
        token_writes = [
            pltpu.make_async_copy(normed.at[q], outs[0].at[q], normed_sem.at[q]) for q in range(n)
        ]
    share = share_job((up, down), (up_all, down_all), extra)
    main = scatter_steps(line, matmul_rows((left, right)), rows, total, made, flow)
    next(main)
    next(share)
    finish(main)
    value = source[...].astype(jnp.float32) + total[...]
    middle[...] = value
    own[...] = (value * rms_factor(value) * gain[...]).astype(own.dtype)
    place = lambda q, first, count: normed.at[q, pl.ds(first, count)]

    half = grad_gates.shape[1] // 2

    def use(q):
        pltpu.make_async_copy(normed.at[q], outs[0].at[q], normed_sem.at[q]).start()
        low = active.dtype
        gate_up = plain(normed[q], up_all[...].reshape(D, -1))
        gate, other = gate_up[:, :half], gate_up[:, half:]
        at = ring_place(n, line.w, q)
        grad = cols_by_cols(upstream[at], down_all[...].reshape(-1, D))
        sig = jax.nn.sigmoid(gate)
        passed = gate * sig
        active[pl.ds(pl.multiple_of(at * rows, rows), rows), :] = (passed * other).astype(low)
        here_rows = pl.ds(pl.multiple_of(q * rows, rows), rows)
        grad_gates[here_rows, :half] = (grad * other * (sig * (1.0 + gate * (1.0 - sig)))).astype(low)
        grad_gates[here_rows, half:] = (grad * passed).astype(low)

    spread_out = gather_steps(
        line, own, place, rows, gather, use if fused else None
    )
    next(spread_out)
    next(share)
    finish(share)
    for copy in writes:
        copy.start()
    finish(spread_out)
    for copy in writes + (token_writes if fused else []):
        copy.wait()


def feed_back_kernel(n, refs_in, refs_out, scratch):
    left, right, cotangent, middle, gain, active, w_mix, w_down, normed, upstream, up, down = refs_in
    grad, d_gain, made, late, low_all, up_sum, down_sum = refs_out
    line = Line(n)
    line.greet([(line.c, line.sib), (line.c, line.across)])
    rows = cotangent.shape[0]
    (total, own, terms), (flow, gather, extra, kept) = scratch[:3], scratch[3:]
    both = active.shape[0] == n * rows
    if both:
        (up, down, normed_part, upstream_part, part_sem), extra = extra[:5], extra[5:]
        width = D // n
        height = down.shape[2]

        def fetch(s):
            columns = pl.ds(pl.multiple_of((line.c + s) % n * width, 128), width)
            return [
                pltpu.make_async_copy(a.at[:, columns], b.at[s % 2], part_sem.at[i, s % 2])
                for i, (a, b) in enumerate(((normed, normed_part), (upstream, upstream_part)))
            ]

        def piece(s):
            q = (line.c + s) % n
            for copy in fetch(s):
                copy.wait()
            if s:
                for copy in fetch((s + 1) % n):
                    copy.start()
            part = rows_by_rows(normed_part[s % 2], left[...])
            up[q] = part.astype(up.dtype).reshape(up.shape[1:])
            part = rows_by_rows(active[...], upstream_part[s % 2]).astype(down.dtype)
            columns = pl.ds(pl.multiple_of(q * width, 128), width)
            for k in range(4):
                down[0, k, :, columns] = part[k * height : (k + 1) * height]

        for copy in fetch(1):
            copy.start()
    else:
        piece = lambda s: None
    sums = Collect(n, ("rows", "rows"), (up, down), (up_sum, down_sum), extra)
    main = scatter_steps(line, matmul_rows((left, right)), rows, total, terms, flow)
    for _ in range(line.N):
        next(main)
    steps = sums.steps
    made_count = [0]

    def advance():
        at = made_count[0]
        if at < len(steps):
            piece(steps[at])
            sums.send(steps[at])
        if 0 <= at - 1 < len(steps):
            sums.cross(steps[at - 1])
        made_count[0] += 1

    for i in range(line.N - 1):
        advance()
        if i:
            advance()
        next(main)
    finish(main)
    back, gain_row = rms_back(middle[...], gain[...], total[...])
    value = cotangent[...].astype(jnp.float32) + back
    grad[...] = value
    d_gain[...] = jnp.broadcast_to(gain_row, d_gain.shape)
    own[...] = value.astype(own.dtype)
    token_writes = []
    if both:
        low_out = low_all
        low_all, low_sem = kept
        token_writes = [
            pltpu.make_async_copy(low_all.at[q], low_out.at[q], low_sem.at[q]) for q in range(n)
        ]
    place = lambda q, first, count: low_all.at[q, pl.ds(first, count)]

    def use(q):
        pltpu.make_async_copy(low_all.at[q], low_out.at[q], low_sem.at[q]).start()
        block = pl.ds(pl.multiple_of(q * rows, rows), rows)
        made[block, :] = cols_by_cols(low_all[q], w_mix[...]).astype(made.dtype)
        late[block, :] = plain(active[block, :], w_down[...]).astype(late.dtype)

    spread_out = gather_steps(
        line, own, place, rows, gather, use if both else None
    )
    next(spread_out)
    for _ in range(line.N - 1):
        advance()
        next(spread_out)
    while made_count[0] <= len(steps):
        advance()
    finish(spread_out)
    for copy in token_writes:
        copy.wait()
    for s in sums.steps:
        sums.close(s)
    sums.end()


SUMS = ("cols", "cols", "rows")


def source_back_kernel(n, refs_in, refs_out, scratch):
    (left, left_two, right, right_two, source, grad_middle, gain, vector, up) = refs_in[:9]
    mixed, gain_column, unit, branch, w_in, w_shared, w_mix = refs_in[9:]
    grad, vector_sum, up_home, in_sum, shared_sum, mix_sum = refs_out
    line = Line(n)
    others = [((line.c + s) % n, line.w) for s in range(1, n)]
    greet(others + [(line.c, line.sib), (line.c, line.across)])
    rows = source.shape[0]
    (total, _, made), (flow, _, extra, _) = scratch[:3], scratch[3:]
    both = unit.shape[0] == n * rows
    if both:
        (w_in, w_shared, w_mix, unit_part, branch_part, part_sem, local), extra = extra[:7], extra[7:]
        width = D // n
        height = w_mix.shape[2]
        local[...] = vector[...]

        def fetch(s):
            columns = pl.ds(pl.multiple_of((line.c + s) % n * width, 128), width)
            return [
                pltpu.make_async_copy(a.at[:, columns], b.at[s % 2], part_sem.at[i, s % 2])
                for i, (a, b) in enumerate(((unit, unit_part), (branch, branch_part)))
            ]

        def piece(s):
            q = (line.c + s) % n
            for copy in fetch(s):
                copy.wait()
            if s:
                for copy in fetch((s + 1) % n):
                    copy.start()
            place = pl.ds(pl.multiple_of(q * width, 128), width)
            scale = gain_column[place, :]
            part = rows_by_rows(unit_part[s % 2], left[...])
            w_in[q] = (part * scale).astype(w_in.dtype).reshape(w_in.shape[1:])
            two = rows_by_rows(unit_part[s % 2], left_two[...])
            w_shared[q] = (two * scale).astype(w_shared.dtype).reshape(w_shared.shape[1:])
            each = jnp.concatenate(
                [
                    part * right[place, :].astype(jnp.float32),
                    two * right_two[place, :].astype(jnp.float32),
                ],
                axis=1,
            )
            ones = jnp.ones((8, each.shape[1]), jnp.bfloat16)
            row = sum(cols_by_cols(ones, some) for some in pieces(each, 3))
            for i in range(width // 128):
                at = q * (width // 128) + i
                local[pl.ds(at, 1), :] = row[0:1, i * 128 : (i + 1) * 128]
            part = rows_by_rows(mixed[...], branch_part[s % 2]).astype(w_mix.dtype)
            for k in range(4):
                w_mix[0, k, :, place] = part[k * height : (k + 1) * height]

        for copy in fetch(1):
            copy.start()
    else:
        local = vector
        piece = lambda s: None
    sums = Collect(n, SUMS, (w_in, w_shared, w_mix), (in_sum, shared_sum, mix_sum), extra[:-6])
    vectors = sum_job(n, local, vector_sum, *extra[-6:-2])
    home = home_job(n, up, up_home, *extra[-2:])
    product = matmul_rows((left, right), (left_two, right_two))
    main = scatter_steps(line, product, rows, total, made, flow)
    steps = sums.steps
    next(home)
    made_count = [0]

    def advance(more=1):
        for _ in range(more):
            at = made_count[0]
            if at < len(steps):
                piece(steps[at])
                sums.send(steps[at])
            if 0 <= at - 1 < len(steps):
                sums.cross(steps[at - 1])
            if 0 <= at - 4 < len(steps):
                sums.close(steps[at - 4])
            made_count[0] += 1

    for _ in range(line.N):
        next(main)
        advance(2)
    next(vectors)
    for _ in main:
        next(vectors, None)
        advance()
    advance(len(steps) + 4 - made_count[0])
    finish(vectors)
    back, _ = rms_back(source[...].astype(jnp.float32), gain[...], total[...])
    grad[...] = grad_middle[...] + back
    finish(home)
    sums.end()


def flow_call(
    kernel, n, rows, args, outs, gathers, away, extra, collective_id, near=False, far_args=()
):
    inside = pl.BlockSpec(memory_space=pltpu.VMEM)
    outside = pl.BlockSpec(memory_space=pl.ANY)
    side_args, side_shapes, side_scratch = extra
    shapes = list(outs)
    specs = [inside] * len(outs)
    scratch = [
        pltpu.VMEM((rows, D), jnp.float32),
        pltpu.VMEM((rows, D) if gathers else (16, 128), jnp.bfloat16),
    ]
    made, flow = scatter_shapes(n, rows, args[0].shape[0] <= 1024)
    gather = []
    if gathers:
        shapes.append(jax.ShapeDtypeStruct((n, rows, D), jnp.bfloat16))
        specs.append(outside)
        gather = gather_scratch(n)
    scratch = scratch + [made] + flow + gather + list(side_scratch)
    ends = 3 + len(flow), 3 + len(flow) + len(gather), len(scratch)
    side = outside if away else inside
    in_specs = [inside] * len(args) + [outside] * len(far_args) + [side] * len(side_args)
    specs = specs + [side] * len(side_shapes)
    kept = []
    if near:
        kept = [pltpu.VMEM((n, rows, D), jnp.bfloat16), pltpu.SemaphoreType.DMA((n,))]
        if away:
            kept += [pltpu.VMEM(shape.shape, shape.dtype) for shape in side_shapes]
            kept.append(pltpu.SemaphoreType.DMA((len(side_shapes),)))
    shapes = shapes + list(side_shapes)
    first, second = len(in_specs), len(in_specs) + len(specs)

    def run(*refs):
        parts = refs[second:]
        groups = parts[3 : ends[0]], parts[ends[0] : ends[1]], parts[ends[1] : ends[2]], parts[ends[2] :]
        kernel(n, refs[:first], refs[first:second], tuple(parts[:3]) + groups)

    return pl.pallas_call(
        run,
        out_shape=tuple(shapes),
        in_specs=in_specs,
        out_specs=tuple(specs),
        scratch_shapes=scratch + kept,
        cost_estimate=pl.CostEstimate(flops=0, bytes_accessed=2 * 10**8, transcendentals=0),
        compiler_params=pltpu.CompilerParams(
            collective_id=collective_id, has_side_effects=True, vmem_limit_bytes=VMEM
        ),
    )(*args, *far_args, *side_args)


def start_call(plan, n, x, w_in, w_up, w_mix, w_down, collective_id):
    rows = w_in.shape[0]
    low = jnp.bfloat16
    G = FF // n
    shapes = (
        jax.ShapeDtypeStruct((n,) + x.shape, low),
        jax.ShapeDtypeStruct((n, 4, rows, plan.A), low),
        jax.ShapeDtypeStruct((n, 4, rows, plan.K), low),
        jax.ShapeDtypeStruct((n, rows, 2 * G), low),
        jax.ShapeDtypeStruct((1, 4) + w_mix.shape, low),
        jax.ShapeDtypeStruct((1,) + w_down.shape, low),
    )
    dma = pltpu.SemaphoreType.DMA
    outside = pl.BlockSpec(memory_space=pl.ANY)
    inside = pl.BlockSpec(memory_space=pltpu.VMEM)
    blocks = 2 * n + 1
    outs = pl.pallas_call(
        functools.partial(start_kernel, plan, n),
        out_shape=shapes,
        in_specs=[outside] + [inside] * 4,
        out_specs=(outside,) * 6,
        scratch_shapes=[
            pltpu.VMEM((n, rows, plan.A), low),
            pltpu.VMEM((rows, plan.K), low),
            pltpu.VMEM((n, rows, 2 * G), low),
            pltpu.VMEM(w_mix.shape, low),
            pltpu.VMEM(w_down.shape, low),
        ]
        + gather_scratch(n)
        + gather_scratch(n)[:5]
        + [dma((2, n)), dma((2, n))]
        + [dma((blocks,)), dma((blocks,)), dma((2, blocks)), dma((2, blocks))]
        + [dma((4,))],
        cost_estimate=pl.CostEstimate(flops=0, bytes_accessed=2 * 10**8, transcendentals=0),
        compiler_params=pltpu.CompilerParams(
            collective_id=collective_id, has_side_effects=True, vmem_limit_bytes=VMEM
        ),
    )(x, w_in, w_up, w_mix, w_down)
    flat = lambda o: o.reshape(-1, o.shape[-1])
    tokens, in_all, shared_all, up_some, mix_all, down_some = outs
    return flat(tokens), flat(in_all), flat(shared_all), up_some, flat(mix_all), down_some


def mm(left, right):
    return jnp.dot(
        left.astype(jnp.bfloat16), right.astype(jnp.bfloat16), preferred_element_type=jnp.float32
    )


def mm_nt(left, right):
    return cols_by_cols(left.astype(jnp.bfloat16), right.astype(jnp.bfloat16))


def mm_tn(left, right):
    return rows_by_rows(left.astype(jnp.bfloat16), right.astype(jnp.bfloat16))


def pieces(values, count):
    found = []
    for _ in range(count):
        part = values.astype(jnp.bfloat16)
        found.append(part)
        values = values - part.astype(jnp.float32)
    return found


def by_marks(values, marks, count=2):
    return plain(
        jnp.concatenate(pieces(values, count), axis=1), jnp.concatenate([marks] * count, axis=0)
    )


def marks_by(marks, values, count=3):
    return plain(
        jnp.concatenate([marks] * count, axis=1), jnp.concatenate(pieces(values, count), axis=0)
    )


def iota(shape, axis):
    return lax.broadcasted_iota(jnp.int32, shape, axis)


def rope_tables(length):
    half = HD // 2
    frequency = rope_base ** (-jnp.arange(half, dtype=jnp.float32) / half)
    angles = jnp.arange(length).astype(jnp.float32)[:, None] * frequency[None, :]
    cosine, sine = jnp.cos(angles), jnp.sin(angles)
    return (
        jnp.concatenate([cosine, cosine], axis=1),
        jnp.concatenate([-sine, sine], axis=1),
    )


def turned(values, cosine, sine):
    return values * cosine + pltpu.roll(values, HD // 2, 1) * sine


def attn_stack(plan, q_ref, cosine, sine):
    heads = [
        turned(q_ref[:, h * HD : (h + 1) * HD], cosine, sine).astype(jnp.bfloat16)
        for h in range(plan.ha)
    ]
    return jnp.concatenate(heads, axis=0)


def by_extent(step, length, run):
    parts = 4
    per = length // CHUNK // parts
    for part in range(parts):
        pl.when(step // per == part)(functools.partial(run, (part + 1) * per * CHUNK))


def attn_softmax(stack, keys, at):
    scores = cols_by_cols(stack, keys) * (1.0 / math.sqrt(HD))
    row = iota(scores.shape, 0) & (CHUNK - 1)
    scores = jnp.where(iota(scores.shape, 1) <= row + at, scores, masked_score)
    weights = jnp.exp(scores - jnp.max(scores, axis=1, keepdims=True))
    return weights * (1.0 / jnp.sum(weights, axis=1, keepdims=True))


def attn_fwd_kernel(plan, q_ref, k_ref, v_ref, cos_ref, sin_ref, out_ref, keys, values):
    step = pl.program_id(0)

    @pl.when(step == 0)
    def _():
        keys[...] = turned(k_ref[...], cos_ref[...], sin_ref[...]).astype(jnp.bfloat16)
        values[...] = v_ref[...].astype(jnp.bfloat16)

    at = pl.multiple_of(step * CHUNK, CHUNK)
    rows = pl.ds(at, CHUNK)
    stack = attn_stack(plan, q_ref, cos_ref[rows, :], sin_ref[rows, :])

    def run(extent):
        probs = attn_softmax(stack, keys[:extent, :], at)
        made = mm(probs, values[:extent, :])
        for h in range(plan.ha):
            out_ref[:, h * HD : (h + 1) * HD] = made[h * CHUNK : (h + 1) * CHUNK]

    by_extent(step, keys.shape[0], run)


def attn_fwd(plan, proj, tables):
    length = proj.shape[0]
    whole = lambda i: (0, 0)
    return pl.pallas_call(
        functools.partial(attn_fwd_kernel, plan),
        grid=(length // CHUNK,),
        out_shape=jax.ShapeDtypeStruct((length, plan.R), jnp.float32),
        in_specs=[
            pl.BlockSpec((CHUNK, plan.R), lambda i: (i, 0)),
            pl.BlockSpec((length, HD), lambda i: (0, plan.B // HD)),
            pl.BlockSpec((length, HD), lambda i: (0, plan.B // HD + 1)),
            pl.BlockSpec((length, HD), whole),
            pl.BlockSpec((length, HD), whole),
        ],
        out_specs=pl.BlockSpec((CHUNK, plan.R), lambda i: (i, 0)),
        scratch_shapes=[pltpu.VMEM((length, HD), jnp.bfloat16)] * 2,
        compiler_params=pltpu.CompilerParams(vmem_limit_bytes=VMEM),
    )(proj, proj, proj, *tables)


def attn_bwd_kernel(
    plan, q_ref, k_ref, v_ref, cos_ref, sin_ref, grad_ref, slab_ref, keys, values, grad_k, grad_v
):
    step = pl.program_id(0)
    scale = 1.0 / math.sqrt(HD)

    @pl.when(step == 0)
    def _():
        keys[...] = turned(k_ref[...], cos_ref[...], sin_ref[...]).astype(jnp.bfloat16)
        values[...] = v_ref[...].astype(jnp.bfloat16)
        grad_k[...] = jnp.zeros_like(grad_k)
        grad_v[...] = jnp.zeros_like(grad_v)
        slab_ref[...] = jnp.zeros_like(slab_ref)

    at = pl.multiple_of(step * CHUNK, CHUNK)
    rows = pl.ds(at, CHUNK)
    cosine, sine = cos_ref[rows, :], sin_ref[rows, :]
    stack = attn_stack(plan, q_ref, cosine, sine)
    grads = jnp.concatenate([grad_ref[:, h * HD : (h + 1) * HD] for h in range(plan.ha)], axis=0)

    def run(extent):
        probs = attn_softmax(stack, keys[:extent, :], at)
        grad_probs = cols_by_cols(grads, values[:extent, :])
        delta = jnp.sum(probs * grad_probs, axis=1, keepdims=True)
        grad_scores = (probs * (grad_probs - delta)).astype(jnp.bfloat16)
        grad_q = mm(grad_scores, keys[:extent, :]) * scale
        for h in range(plan.ha):
            slab_ref[rows, h * HD : (h + 1) * HD] = turned(
                grad_q[h * CHUNK : (h + 1) * CHUNK], cosine, -sine
            ).astype(jnp.bfloat16)
        grad_k[:extent, :] += mm_tn(grad_scores, stack)
        grad_v[:extent, :] += mm_tn(probs, grads)

    by_extent(step, keys.shape[0], run)

    @pl.when(step == pl.num_programs(0) - 1)
    def _():
        slab_ref[:, plan.B : plan.B + HD] = turned(
            grad_k[...] * scale, cos_ref[...], -sin_ref[...]
        ).astype(jnp.bfloat16)
        slab_ref[:, plan.B + HD : plan.B + 2 * HD] = grad_v[...].astype(jnp.bfloat16)


def attn_bwd(plan, proj, tables, grad):
    length = proj.shape[0]
    whole = lambda i: (0, 0)
    return pl.pallas_call(
        functools.partial(attn_bwd_kernel, plan),
        grid=(length // CHUNK,),
        out_shape=jax.ShapeDtypeStruct((length, plan.A), jnp.bfloat16),
        in_specs=[
            pl.BlockSpec((CHUNK, plan.R), lambda i: (i, 0)),
            pl.BlockSpec((length, HD), lambda i: (0, plan.B // HD)),
            pl.BlockSpec((length, HD), lambda i: (0, plan.B // HD + 1)),
            pl.BlockSpec((length, HD), whole),
            pl.BlockSpec((length, HD), whole),
            pl.BlockSpec((CHUNK, plan.R), lambda i: (i, 0)),
        ],
        out_specs=pl.BlockSpec((length, plan.A), whole),
        scratch_shapes=[pltpu.VMEM((length, HD), jnp.bfloat16)] * 2
        + [pltpu.VMEM((length, HD), jnp.float32)] * 2,
        compiler_params=pltpu.CompilerParams(vmem_limit_bytes=VMEM),
    )(proj, proj, proj, *tables, grad)


def head_spread(plan):
    return ((iota((PAD, plan.R), 1) >> 6) == iota((PAD, plan.R), 0)).astype(jnp.bfloat16)


def head_gather(plan):
    return ((iota((plan.R, PAD), 0) >> 6) == iota((plan.R, PAD), 1)).astype(jnp.bfloat16)


def lower_ones():
    shape = (CHUNK, CHUNK)
    return (iota(shape, 0) >= iota(shape, 1)).astype(jnp.bfloat16)


def space_parts(plan, dt_raw, window, conv_ref, head_ref, pick_ref):
    total = conv_ref[4:5, :]
    for k in range(CONV):
        at = 8 - CONV + 1 + k
        total = total + conv_ref[k : k + 1, :] * window[at : at + CHUNK, :]
    raw = by_marks(dt_raw, pick_ref[...], 3) + head_ref[1:2, :]
    steps = jnp.maximum(raw, 0.0) + jnp.log1p(jnp.exp(-jnp.abs(raw)))
    logs = -steps * jnp.exp(head_ref[0:1, :])
    cumul = marks_by(lower_ones(), logs)
    return total, raw, steps, logs, cumul


def decay_of(cumul, cumul_t, causal, h):
    gaps = cumul[:, h : h + 1] - cumul_t[h : h + 1, :]
    return jnp.exp(jnp.where(causal, gaps, masked_score))


def space_fwd_kernel(
    plan, proj_ref, shared_ref, conv_ref, head_ref, pick_ref, gated_ref, made_ref, before_ref, state, window
):
    R = plan.R
    step = pl.program_id(0)

    @pl.when(step == 0)
    def _():
        state[...] = jnp.zeros_like(state)
        window[0:8, :] = jnp.zeros((8, window.shape[1]), jnp.float32)

    @pl.when(step > 0)
    def _():
        window[0:8, :] = window[CHUNK : CHUNK + 8, :]

    window[8 : CHUNK + 8, :R] = proj_ref[:, plan.B : plan.B + R]
    window[8 : CHUNK + 8, R:] = shared_ref[:, : 2 * NS]
    total, _, steps, _, cumul = space_parts(
        plan, shared_ref[:, 2 * NS :], window, conv_ref, head_ref, pick_ref
    )
    post = total * jax.nn.sigmoid(total)
    x = post[:, :R]
    b = post[:, R : R + NS].astype(jnp.bfloat16)
    c = post[:, R + NS :].astype(jnp.bfloat16)
    spread_heads = head_spread(plan)
    cumul_t = cumul.T
    last = cumul[CHUNK - 1 : CHUNK, :]
    tail = jnp.exp(last - cumul)
    weighted = x * by_marks(steps, spread_heads)
    causal = iota((CHUNK, CHUNK), 0) >= iota((CHUNK, CHUNK), 1)
    inner = cols_by_cols(c, b)
    before = state[...]
    before_ref[0] = before.astype(jnp.bfloat16)
    made = mm(c, before) * by_marks(jnp.exp(cumul), spread_heads)
    made = made + by_marks(jnp.broadcast_to(head_ref[2:3, :], (8, PAD)), spread_heads)[0:1] * x
    left = iota((CHUNK, 2 * MP), 1) < MP
    weighted_low = weighted.astype(jnp.bfloat16)
    intra = []
    for pair in range(plan.hm // 2):
        lanes = weighted_low[:, pair * 2 * MP : (pair + 1) * 2 * MP]
        one = mm(inner * decay_of(cumul, cumul_t, causal, 2 * pair), lanes)
        two = mm(inner * decay_of(cumul, cumul_t, causal, 2 * pair + 1), lanes)
        intra.append(jnp.where(left, one, two))
    made = made + jnp.concatenate(intra, axis=1)
    state[...] = before * by_marks(
        jnp.broadcast_to(jnp.exp(last), (8, PAD)), spread_heads
    )[0:1] + mm_tn(b, weighted * by_marks(tail, spread_heads))
    z = proj_ref[:, :R]
    made_ref[...] = made
    gated_ref[...] = made * (z * jax.nn.sigmoid(z))


def space_fwd(plan, proj, shared, conv, heads, pick):
    length = proj.shape[0]
    chunks = length // CHUNK
    W = plan.W
    whole = lambda i: (0, 0)
    rows = lambda i: (i, 0)
    return pl.pallas_call(
        functools.partial(space_fwd_kernel, plan),
        grid=(chunks,),
        out_shape=(
            jax.ShapeDtypeStruct((length, plan.R), jnp.float32),
            jax.ShapeDtypeStruct((length, plan.R), jnp.float32),
            jax.ShapeDtypeStruct((chunks, NS, plan.R), jnp.bfloat16),
        ),
        in_specs=[
            pl.BlockSpec((CHUNK, plan.A), rows),
            pl.BlockSpec((CHUNK, plan.K), rows),
            pl.BlockSpec((8, W), whole),
            pl.BlockSpec((8, PAD), whole),
            pl.BlockSpec((PAD, PAD), whole),
        ],
        out_specs=(
            pl.BlockSpec((CHUNK, plan.R), rows),
            pl.BlockSpec((CHUNK, plan.R), rows),
            pl.BlockSpec((1, NS, plan.R), lambda i: (i, 0, 0)),
        ),
        scratch_shapes=[
            pltpu.VMEM((NS, plan.R), jnp.float32),
            pltpu.VMEM((CHUNK + 8, W), jnp.float32),
        ],
        compiler_params=pltpu.CompilerParams(vmem_limit_bytes=VMEM),
    )(proj, shared, conv, heads, pick)


def space_bwd_kernel(
    plan, proj_ref, shared_ref, prev_ref, prev_shared, conv_ref, head_ref, pick_ref, gain_ref, row_ref,
    grad_ref, made_ref, before_ref, slab_ref, slab_shared, conv_acc, head_acc, skip_acc, d_state, window, d_window,
):
    R = plan.R
    step = pl.program_id(0)
    chunk = pl.num_programs(0) - 1 - step

    @pl.when(step == 0)
    def _():
        d_state[...] = jnp.zeros_like(d_state)
        d_window[CHUNK : CHUNK + 8, :] = jnp.zeros((8, plan.W), jnp.float32)
        conv_acc[...] = jnp.zeros_like(conv_acc)
        head_acc[...] = jnp.zeros_like(head_acc)
        skip_acc[...] = jnp.zeros_like(skip_acc)

    @pl.when(step > 0)
    def _():
        d_window[CHUNK : CHUNK + 8, :] = d_window[0:8, :]

    window[0:8, :R] = jnp.where(chunk == 0, 0.0, prev_ref[:, plan.B : plan.B + R])
    window[0:8, R:] = jnp.where(chunk == 0, 0.0, prev_shared[:, : 2 * NS])
    window[8 : CHUNK + 8, :R] = proj_ref[:, plan.B : plan.B + R]
    window[8 : CHUNK + 8, R:] = shared_ref[:, : 2 * NS]
    total, raw, steps, logs, cumul = space_parts(
        plan, shared_ref[:, 2 * NS :], window, conv_ref, head_ref, pick_ref
    )
    sig = jax.nn.sigmoid(total)
    post = total * sig
    x = post[:, :R]
    b = post[:, R : R + NS].astype(jnp.bfloat16)
    c = post[:, R + NS :].astype(jnp.bfloat16)
    spread_heads = head_spread(plan)
    gather_heads = head_gather(plan)
    cumul_t = cumul.T
    last = cumul[CHUNK - 1 : CHUNK, :]
    steps_wide = by_marks(steps, spread_heads)
    tail_wide = by_marks(jnp.exp(last - cumul), spread_heads)
    grow_wide = by_marks(jnp.exp(cumul), spread_heads)
    last_wide = by_marks(jnp.broadcast_to(jnp.exp(last), (8, PAD)), spread_heads)[0:1]
    skip_wide = by_marks(jnp.broadcast_to(head_ref[2:3, :], (8, PAD)), spread_heads)[0:1]
    weighted = x * steps_wide
    causal = iota((CHUNK, CHUNK), 0) >= iota((CHUNK, CHUNK), 1)
    inner = cols_by_cols(c, b)

    z = proj_ref[:, :R]
    sig_z = jax.nn.sigmoid(z)
    grad = grad_ref[...].astype(jnp.float32)
    gate = z * sig_z
    gated = made_ref[...] * gate
    row_factor = row_ref[:, 0:1]
    skip_acc[1:2, :] += jnp.sum(grad * gated * row_factor, axis=0, keepdims=True)
    grad = grad * gain_ref[0:1, :] * row_factor - gated * row_ref[:, 1:2]
    d_made = grad * gate
    slab_ref[:, :R] = (grad * made_ref[...] * (sig_z * (1.0 + z * (1.0 - sig_z)))).astype(
        jnp.bfloat16
    )
    skip_acc[0:1, :] += jnp.sum(d_made * x, axis=0, keepdims=True)

    before = before_ref[0]
    d_after = d_state[...]
    d_after_low = d_after.astype(jnp.bfloat16)
    grown = d_made * grow_wide
    grown_low = grown.astype(jnp.bfloat16)
    carried = mm(c, before)
    d_c = mm_nt(grown_low, before)
    pulled = weighted * tail_wide
    d_pulled = mm(b, d_after_low)
    d_b = mm_nt(pulled, d_after_low)
    d_cumul = by_marks(grown * carried, gather_heads)
    kept = by_marks(d_pulled * pulled, gather_heads)
    d_cumul = d_cumul - kept
    decayed = jnp.sum(d_after * before.astype(jnp.float32), axis=0, keepdims=True) * last_wide
    d_last = jnp.sum(kept, axis=0, keepdims=True) + by_marks(
        jnp.broadcast_to(decayed, (8, R)), gather_heads
    )[0:1]
    d_state[...] = d_after * last_wide + mm_tn(c, grown_low)

    left = iota((CHUNK, 2 * MP), 1) < MP
    lane = iota((CHUNK, PAD), 1)
    sub = iota((8, CHUNK), 0)
    weighted_low = weighted.astype(jnp.bfloat16)
    d_made_low = d_made.astype(jnp.bfloat16)
    d_inner = jnp.zeros((CHUNK, CHUNK), jnp.float32)
    columns = jnp.zeros((8, CHUNK), jnp.float32)
    d_weighted = []
    for pair in range(plan.hm // 2):
        at = slice(pair * 2 * MP, (pair + 1) * 2 * MP)
        lanes, d_lanes = weighted_low[:, at], d_made_low[:, at]
        halves = []
        for which in range(2):
            h = 2 * pair + which
            decay = decay_of(cumul, cumul_t, causal, h)
            whole = inner * decay
            halves.append(mm_tn(whole, d_lanes))
            mine = jnp.where(left if which == 0 else ~left, d_lanes, jnp.zeros_like(d_lanes))
            d_whole = cols_by_cols(mine, lanes)
            d_inner = d_inner + d_whole * decay
            slope = d_whole * whole
            d_cumul = d_cumul + jnp.where(lane == h, jnp.sum(slope, axis=1, keepdims=True), 0.0)
            columns = columns + jnp.where(sub == h, jnp.sum(slope, axis=0, keepdims=True), 0.0)
        d_weighted.append(jnp.where(left, halves[0], halves[1]))
    d_weighted = jnp.concatenate(d_weighted, axis=1) + d_pulled * tail_wide
    columns = jnp.concatenate([columns, jnp.zeros((CHUNK - 8, CHUNK), jnp.float32)], axis=0).T
    d_cumul = d_cumul - columns
    d_inner_low = d_inner.astype(jnp.bfloat16)
    d_c = d_c + mm(d_inner_low, b)
    d_b = d_b + mm_tn(d_inner_low, c)
    d_x = d_weighted * steps_wide + skip_wide * d_made
    d_steps = by_marks(d_weighted * x, gather_heads)
    upper = (iota((CHUNK, CHUNK), 0) <= iota((CHUNK, CHUNK), 1)).astype(jnp.bfloat16)
    d_logs = marks_by(upper, d_cumul) + d_last
    d_steps = d_steps - jnp.exp(head_ref[0:1, :]) * d_logs
    d_raw = d_steps * jax.nn.sigmoid(raw)
    d_raw = jnp.where(lane < plan.hm, d_raw, 0.0)
    slab_shared[:, 2 * NS :] = cols_by_cols(d_raw.astype(jnp.bfloat16), pick_ref[...]).astype(
        jnp.bfloat16
    )
    head_acc[0:1, :] += jnp.sum(d_logs * logs, axis=0, keepdims=True)
    head_acc[1:2, :] += jnp.sum(d_raw, axis=0, keepdims=True)

    d_post = jnp.concatenate([d_x, d_b, d_c], axis=1)
    d_total = d_post * (sig * (1.0 + total * (1.0 - sig)))
    d_window[0:CHUNK, :] = d_total
    d_xbc = jnp.zeros((CHUNK, plan.W), jnp.float32)
    for k in range(CONV):
        shift = CONV - 1 - k
        d_xbc = d_xbc + conv_ref[k : k + 1, :] * d_window[shift : shift + CHUNK, :]
        at = 8 - CONV + 1 + k
        conv_acc[k : k + 1, :] += jnp.sum(
            d_total * window[at : at + CHUNK, :], axis=0, keepdims=True
        )
    conv_acc[4:5, :] += jnp.sum(d_total, axis=0, keepdims=True)
    slab_ref[:, plan.B : plan.B + R] = d_xbc[:, :R].astype(jnp.bfloat16)
    slab_shared[:, : 2 * NS] = d_xbc[:, R:].astype(jnp.bfloat16)
    if plan.B + R < plan.A:
        slab_ref[:, plan.B + R :] = jnp.zeros((CHUNK, plan.A - plan.B - R), jnp.bfloat16)


def space_bwd(plan, proj, shared, conv, heads, pick, gain, rows_of, grad, made, before):
    length = proj.shape[0]
    chunks = length // CHUNK
    W = plan.W
    whole = lambda i: (0, 0)
    rows = lambda i: (chunks - 1 - i, 0)
    per = CHUNK // 8
    return pl.pallas_call(
        functools.partial(space_bwd_kernel, plan),
        grid=(chunks,),
        out_shape=(
            jax.ShapeDtypeStruct((length, plan.A), jnp.bfloat16),
            jax.ShapeDtypeStruct((length, plan.K), jnp.bfloat16),
            jax.ShapeDtypeStruct((8, W), jnp.float32),
            jax.ShapeDtypeStruct((8, PAD), jnp.float32),
            jax.ShapeDtypeStruct((8, plan.R), jnp.float32),
        ),
        in_specs=[
            pl.BlockSpec((CHUNK, plan.A), rows),
            pl.BlockSpec((CHUNK, plan.K), rows),
            pl.BlockSpec((8, plan.A), lambda i: (jnp.maximum((chunks - 1 - i) * per - 1, 0), 0)),
            pl.BlockSpec((8, plan.K), lambda i: (jnp.maximum((chunks - 1 - i) * per - 1, 0), 0)),
            pl.BlockSpec((8, W), whole),
            pl.BlockSpec((8, PAD), whole),
            pl.BlockSpec((PAD, PAD), whole),
            pl.BlockSpec((8, plan.R), whole),
            pl.BlockSpec((CHUNK, 2), rows),
            pl.BlockSpec((CHUNK, plan.R), rows),
            pl.BlockSpec((CHUNK, plan.R), rows),
            pl.BlockSpec((1, NS, plan.R), lambda i: (chunks - 1 - i, 0, 0)),
        ],
        out_specs=(
            pl.BlockSpec((CHUNK, plan.A), rows),
            pl.BlockSpec((CHUNK, plan.K), rows),
            pl.BlockSpec((8, W), whole),
            pl.BlockSpec((8, PAD), whole),
            pl.BlockSpec((8, plan.R), whole),
        ),
        scratch_shapes=[
            pltpu.VMEM((NS, plan.R), jnp.float32),
            pltpu.VMEM((CHUNK + 8, W), jnp.float32),
            pltpu.VMEM((CHUNK + 8, W), jnp.float32),
        ],
        compiler_params=pltpu.CompilerParams(vmem_limit_bytes=VMEM),
    )(proj, shared, proj, shared, conv, heads, pick, gain, rows_of, grad, made, before)


def body(
    inputs,
    cotangent,
    w_in,
    w_in_m,
    w_in_v,
    w_mix,
    w_mix_m,
    w_mix_v,
    w_up,
    w_up_m,
    w_up_v,
    w_down,
    w_down_m,
    w_down_v,
    vectors,
    vectors_m,
    vectors_v,
):
    low = jnp.bfloat16
    count = lax.axis_size("ctx")
    ways = lax.axis_size("wshard")
    place = lax.axis_index("ctx")
    plan = Plan(count)
    R, hm = plan.R, plan.hm
    is_space = place >= plan.attn
    space = jnp.maximum(place - plan.attn, 0)

    gain_attn, gain_ffn, gain_ssm, conv_bias, conv_weight, a_log, dt_bias, d_skip = split_vectors(
        vectors
    )
    whole, in_own, shared_own, up_some, mix_own, down_some = start_call(
        plan, count, inputs[0], w_in, w_up, w_mix, w_down, 1
    )

    own = lambda a, size, axis=0: lax.dynamic_slice_in_dim(a, space * size, size, axis)
    gain_own = own(gain_ssm, R)
    W = plan.W
    conv = jnp.concatenate(
        [
            jnp.concatenate([own(conv_weight, R, 1), conv_weight[:, DSSM:]], axis=1),
            jnp.concatenate([own(conv_bias, R), conv_bias[DSSM:]])[None],
            jnp.zeros((8 - CONV - 1, W), jnp.float32),
        ]
    )
    heads = jnp.stack([own(v, hm) for v in (a_log, dt_bias, d_skip)])
    heads = jnp.pad(heads, ((0, 5), (0, PAD - hm)))
    column = lax.broadcasted_iota(jnp.int32, (PAD, PAD), 1)
    row = lax.broadcasted_iota(jnp.int32, (PAD, PAD), 0)
    pick = jnp.logical_and(row == column + space * hm, column < hm).astype(low)
    tables = rope_tables(count * inputs.shape[1])

    source = inputs[0].astype(jnp.float32)
    whole = whole.astype(jnp.float32)
    in_own, cotangent_late = lax.optimization_barrier((in_own, cotangent[0]))
    odd = lax.axis_index("wshard") % 2 == 1
    upstream_all = gather_ctx(cotangent_late, count, ways)
    length = whole.shape[0]
    rows = inputs.shape[1]
    unit = whole * lax.rsqrt(jnp.mean(whole * whole, axis=-1, keepdims=True) + norm_eps)
    normed = (unit * gain_attn).astype(low)
    unit = unit.astype(low)
    proj = plain(normed, in_own)
    shared = plain(normed, shared_own)

    def space_ahead(proj, shared):
        return space_fwd(plan, proj, shared, conv, heads, pick)

    def attn_ahead(proj, shared):
        made = attn_fwd(plan, proj, tables)
        blank = jnp.zeros((length // CHUNK, NS, R), low)
        return made, jnp.zeros_like(made), blank

    made, raw_made, before = lax.cond(is_space, space_ahead, attn_ahead, proj, shared)
    square = jnp.where(is_space, jnp.sum(made * made, axis=1), 0.0)
    factor = lax.rsqrt(sum_rows(count, square, 5) / DSSM + norm_eps)
    mixed = jnp.where(is_space, made * factor[:, None] * gain_own, made).astype(low)
    wide = lambda *shape: jax.ShapeDtypeStruct(shape, jnp.float32)
    side = (up_some, down_some)
    roomy = length <= 1024
    middle, activated, grad_gate_up, two_all, up_own, down_own = flow_call(
        branch_kernel,
        count,
        rows,
        (mixed, mix_own, inputs[0], gain_ffn[None], upstream_all if roomy else upstream_all[:, :16]),
        (
            wide(rows, D),
            jax.ShapeDtypeStruct((length if roomy else 16, FF // count), low),
            jax.ShapeDtypeStruct((length if roomy else 16, 2 * FF // count), low),
        ),
        True,
        True,
        (side, *share_shapes(side)),
        8,
        roomy,
    )
    two_all = two_all.reshape(length, D)
    up_own, down_own = up_own.reshape(D, -1), down_own.reshape(-1, D)

    if not roomy:
        gate_up = plain(two_all, up_own)
        half = FF // count
        swiglu = lambda g: jax.nn.silu(g[:, :half]) * g[:, half:]
        activated, act_pull = jax.vjp(swiglu, gate_up)
        activated = in_ring(activated.astype(low).reshape(count, rows, -1), count, ways, odd)
        grad_act = cols_by_cols(from_ring(upstream_all, count, lax.axis_index("wshard")), down_own)
        grad_gate_up = act_pull(grad_act)[0].astype(low)
    upstream_all = upstream_all.reshape(length, D)
    cut = lambda g, blocks: g.astype(low).reshape(blocks, ways, -1, g.shape[1])
    blank = jnp.zeros((1, 1, 16, 128), low)
    if roomy:
        up_block = (count, ways, D // (count * ways), 2 * FF // count)
        down_block = (1, ways, FF // (count * ways), D)
        side = [jax.ShapeDtypeStruct(block, low) for block in (up_block, down_block)]
        side_shapes, side_scratch = collect_shapes(("rows", "rows"), side)
        side_scratch = (
            [pltpu.VMEM(block, low) for block in (up_block, down_block)]
            + [pltpu.VMEM((2, length, D // count), low)] * 2
            + [pltpu.SemaphoreType.DMA((2, 2))]
            + side_scratch
        )
        side = (blank, blank)
    else:
        side = (cut(rows_by_rows(two_all, grad_gate_up), count), cut(rows_by_rows(activated, upstream_all), 1))
        side_shapes, side_scratch = collect_shapes(("rows", "rows"), side)
    some = lambda a: a if roomy else a[:16]
    grad_middle, grad_gain_ffn, grad_made, late, branch_all, up_mine, down_mine = flow_call(
        feed_back_kernel,
        count,
        rows,
        (
            grad_gate_up,
            up_own,
            cotangent[0],
            middle,
            gain_ffn[None],
            some(activated),
            some(mix_own),
            some(down_own),
        ),
        (
            wide(rows, D),
            wide(8, D),
            jax.ShapeDtypeStruct((length if roomy else 16, R), low),
            jax.ShapeDtypeStruct((length if roomy else 16, D), low),
        ),
        True,
        False,
        (side, side_shapes, side_scratch),
        9,
        roomy,
        (two_all, upstream_all),
    )
    grad_gain_ffn = grad_gain_ffn[0]
    branch_all = branch_all.reshape(length, D)
    if not roomy:
        late = plain(activated, down_own).astype(low)
    branch_all, grad_made, late = lax.optimization_barrier((branch_all, grad_made, late))
    late = scatter_ctx(late, count, ways)
    if not roomy:
        grad_made = cols_by_cols(branch_all, mix_own).astype(low)
    made_wide = grad_made.astype(jnp.float32)
    dots = jnp.where(is_space, jnp.sum(made_wide * gain_own * made, axis=1), 0.0)
    dots = sum_rows(count, dots, 6)

    def space_back(proj, shared, grad_made):
        gain = jnp.broadcast_to(gain_own, (8, R))
        rows_of = jnp.stack([factor, factor**3 * dots / DSSM], axis=1)
        return space_bwd(
            plan, proj, shared, conv, heads, pick, gain, rows_of, grad_made, raw_made, before
        )

    def attn_back(proj, shared, grad_made):
        blank = lambda k: jnp.zeros((8, k), jnp.float32)
        none = jnp.zeros(shared.shape, low)
        return attn_bwd(plan, proj, tables, grad_made), none, blank(W), blank(PAD), blank(R)

    grad_proj, grad_shared, conv_acc, head_acc, skip_acc = lax.cond(
        is_space, space_back, attn_back, proj, shared, grad_made
    )
    if roomy:
        grad_gain_attn = jnp.zeros_like(gain_attn)
    else:
        grad_in = rows_by_rows(unit, grad_proj)
        grad_in_shared = rows_by_rows(unit, grad_shared)
        grad_gain_attn = jnp.sum(grad_in * in_own, axis=1)
        grad_gain_attn = grad_gain_attn + jnp.sum(grad_in_shared * shared_own, axis=1)
        grad_in = grad_in * gain_attn[:, None]
        grad_in_shared = grad_in_shared * gain_attn[:, None]
    def placed(piece, size, total, axis=0):
        shape = list(piece.shape)
        shape[axis] = total
        start = [0] * piece.ndim
        start[axis] = space * size
        return lax.dynamic_update_slice(jnp.zeros(shape, piece.dtype), piece, start)

    conv_w_grad, conv_b_grad = conv_acc[:CONV], conv_acc[CONV]
    a_grad, bias_grad = head_acc[0, :hm], head_acc[1, :hm]
    skip_grad = jnp.sum(skip_acc[0].reshape(hm, MP), axis=1)
    grad_gain_own = skip_acc[1]
    vector_local = jnp.concatenate(
        [
            grad_gain_attn,
            grad_gain_ffn,
            placed(grad_gain_own, R, DSSM),
            placed(conv_b_grad[:R], R, DSSM),
            conv_b_grad[R:],
            jnp.concatenate(
                [placed(conv_w_grad[:, :R], R, DSSM, 1), conv_w_grad[:, R:]], axis=1
            ).reshape(CONV * CONVCH),
            placed(a_grad, hm, MH),
            placed(bias_grad, hm, MH),
            placed(skip_grad, hm, MH),
        ]
    )
    grad_proj, late = lax.optimization_barrier((grad_proj, late))
    outputs = (middle + late).astype(low)[None]
    pad = -vectors.shape[0] % 1024
    vector_local = jnp.pad(vector_local, (0, pad)).reshape(-1, 128)
    if roomy:
        lines = D // (count * ways)
        blocks = (
            (count, ways, lines, plan.A),
            (count, ways, lines, plan.K),
            (1, ways, MIXIN // (count * ways), D),
        )
        side = [jax.ShapeDtypeStruct(block, low) for block in blocks]
        side_shapes, side_scratch = collect_shapes(SUMS, side)
        side_scratch = (
            [pltpu.VMEM(block, low) for block in blocks]
            + [pltpu.VMEM((2, length, D // count), low)] * 2
            + [pltpu.SemaphoreType.DMA((2, 2)), pltpu.VMEM(vector_local.shape, jnp.float32)]
            + side_scratch
        )
        side = (blank, blank, blank)
    else:
        grad_mix = rows_by_rows(mixed, branch_all)
        side = (cut(grad_in, count), cut(grad_in_shared, count), cut(grad_mix, 1))
        side_shapes, side_scratch = collect_shapes(SUMS, side)
    home_sems = [pltpu.SemaphoreType.DMA((count,))] * 2
    input_grad, vector_sum, up_mine, in_mine, shared_mine, mix_mine = flow_call(
        source_back_kernel,
        count,
        rows,
        (
            grad_proj,
            grad_shared,
            in_own,
            shared_own,
            inputs[0],
            grad_middle,
            gain_attn[None],
            vector_local,
            up_mine,
            some(mixed),
            some(gain_attn[:, None]),
        ),
        (wide(rows, D), wide(*vector_local.shape), jax.ShapeDtypeStruct(up_mine.shape, low)),
        False,
        False,
        (side, side_shapes, side_scratch + sum_scratch(count, vector_local.shape) + home_sems),
        10,
        far_args=(some(unit), some(branch_all)),
    )
    input_grad = input_grad[None]

    up_shard = up_from_slabs(plan, up_mine)
    mix_shard = mix_mine[0].astype(jnp.float32)
    down_shard = down_mine[0].astype(jnp.float32)

    vector_grad = vector_sum.reshape(-1)[: vectors.shape[0]]
    new_in = adam_in(plan, in_mine, shared_mine, w_in, w_in_m, w_in_v, 2.0 * D ** (-0.5))
    new_mix = adamw(w_mix, w_mix_m, w_mix_v, mix_shard, DSSM ** (-0.5), decay_weight)
    new_up = adamw(w_up, w_up_m, w_up_v, up_shard, D ** (-0.5), decay_weight)
    new_down = adamw(w_down, w_down_m, w_down_v, down_shard, FF ** (-0.5), decay_weight)
    new_vec = adamw(vectors, vectors_m, vectors_v, vector_grad, vector_rate, 0.0)
    return (outputs, input_grad, *new_in, *new_mix, *new_up, *new_down, *new_vec)


def solution(mesh):
    tokens = P("wshard", "ctx", None)
    weight = P(("ctx", "wshard"), None)
    return jax.shard_map(
        body,
        mesh=mesh,
        in_specs=(tokens,) * 2 + (weight,) * 12 + (P(),) * 3,
        out_specs=(tokens,) * 2 + (weight,) * 12 + (P(),) * 3,
        check_vma=False,
    )
```
